32 devices in a mesh: tm: 16 (over z, x, core), head: 2 (over y).
Axes of the slice: x: 2, y: 2, z: 4, core: 2. Of those that a mesh axis runs over, the one named last changes fastest.
Arguments:
- frames_in: bfloat16 [16, 1024, 1024], P('tm', 'head'), may hold values from -400 to 400
- in_weight: bfloat16 [1024, 5120], P('tm', 'head'), may hold values from -0.1875 to 0.1875
- out_weight: bfloat16 [1024, 1024], replicated, may hold values from -0.1875 to 0.1875
- block_ids: int32 [1024], replicated, may hold values from 0 to 15, as said below
- block_lists: int32 [16, 4], replicated, may hold values from 0 to 15, as said below
- decays: float32 [16, 16, 16], P('tm', 'head'), may hold values from 0.3 to 1
Outputs:
- layer_out: bfloat16 [16, 1024, 1024], P('tm', 'head')
The draws below stay inside these ranges and needn't reach their ends.
Inputs may be any that keep to these rules, and one draw needn't show every extreme that they name: `block_ids`: each of the 16 block ids is held by exactly 64 tokens. `block_lists`: row g starts with g itself, followed by 4 - 1 further blocks, all different.
All inputs are finite; a program needn't handle non-finite values.
Results may differ from the reference program's by a relative error of at most 0.0069.
Values may be sent and summed in bfloat16 or wider, within the bound.
No kernel may reach another device: no remote copies, remote signals or barrier semaphores. Data moves between devices by JAX's collectives and lax.ppermute only.
A program may use at most 192 MiB of HBM per device.

```python
import math
import jax
import jax.numpy as jnp
from jax import lax

D = 1024
H = 16
HD = 64
N = 64
TOKS = 1024
NB = 16
K_SEL = 4
CLIP_IMAGE_COUNT = 16


def draw_frames_in(key, part):
    key_base, key_rows, key_cols = jax.random.split(key, 3)
    row_scale = jnp.exp(jax.random.uniform(key_rows, (CLIP_IMAGE_COUNT, TOKS, 1), jnp.float32) * math.log(10.0))
    col_scale = jnp.exp(jax.random.uniform(key_cols, (1, 1, D), jnp.float32) * math.log(10.0))
    base = jnp.clip(jax.random.normal(key_base, (CLIP_IMAGE_COUNT, TOKS, D), jnp.float32), -4.0, 4.0)
    return jnp.clip(base * row_scale * col_scale, -400.0, 400.0).astype(jnp.bfloat16)


def draw_block_ids(key, part):
    order = jax.random.permutation(jax.random.fold_in(key, 11), TOKS)
    return (order // (TOKS // NB)).astype(jnp.int32)


def draw_block_lists(key, part):
    base_key = jax.random.fold_in(key, 23)

    def one_row(index):
        others = jax.random.permutation(jax.random.fold_in(base_key, index), NB - 1)[:K_SEL - 1]
        chosen = (index + 1 + others) % NB
        return jnp.concatenate([jnp.full((1,), index, jnp.int32), chosen.astype(jnp.int32)])
    return jax.vmap(one_row)(jnp.arange(NB, dtype=jnp.int32)).astype(jnp.int32)


def draw_decays(key, part):
    variety_seed, gradual_seed, quick_seed, scatter_seed, spike_seed, strength_seed = jax.random.split(key, 6)
    share_fast = 0.5
    fast_head = jax.random.uniform(variety_seed, (1, H, 1), jnp.float32) < share_fast
    slow_rate = jnp.exp(jax.random.uniform(gradual_seed, (1, H, 1), jnp.float32, math.log(0.05), math.log(0.5))) / CLIP_IMAGE_COUNT
    fast_rate = jnp.exp(jax.random.uniform(quick_seed, (1, H, 1), jnp.float32, math.log(math.log(10.0) / 50.0), math.log(math.log(10.0) / 30.0)))
    resting_level = jnp.where(fast_head, fast_rate, slow_rate)
    level_variation = jnp.exp(jax.random.uniform(scatter_seed, (CLIP_IMAGE_COUNT, 1, NB), jnp.float32, math.log(0.5), math.log(2.0)))
    spike_beginning = jax.random.randint(spike_seed, (2,), 0, CLIP_IMAGE_COUNT)
    image_index_along_clip = jnp.arange(CLIP_IMAGE_COUNT, dtype=jnp.int32)[:, None, None]
    within_spike_window = (image_index_along_clip == spike_beginning[0]) | (image_index_along_clip == spike_beginning[1])
    fading_strength = jax.random.uniform(strength_seed, (CLIP_IMAGE_COUNT, H, NB), jnp.float32, 0.5, 0.8)
    kept_share = jnp.exp(-resting_level * level_variation) * jnp.where(within_spike_window, fading_strength, 1.0)
    return kept_share.astype(jnp.float32)


def steps_of(key, dims, cuts, low, high):
    level = 1.0
    for dim, blocks in cuts:
        steps = jax.random.uniform(jax.random.fold_in(jax.random.fold_in(key, 6), dim), (blocks,), jnp.float32, low / len(cuts), high / len(cuts))
        level = level * jnp.repeat(jnp.exp(steps), dims[dim] // blocks).reshape((-1,) + (1,) * (len(dims) - 1 - dim))
    return level


def scatter_about(stream_key, dims, scale, limit, pieces=(), kind=jnp.bfloat16):
    array = jax.random.normal(stream_key, dims, jnp.float32) * scale
    if len(pieces) > 0:
        array = steps_of(stream_key, dims, pieces, -0.22, 0.18) * array
    return jnp.clip(array, min=-limit, max=limit).astype(kind)


def setup_inputs(seed: int = 0) -> dict:
    streams_of = jax.random.split(jax.random.key(seed), 7)
    frames_in = draw_frames_in(jax.random.fold_in(streams_of[6], 71), 0)
    in_weight = scatter_about(streams_of[1], (D, 5 * H * HD), D ** -0.5, 0.1875, ((0, 16), (1, 2)))
    out_weight = scatter_about(streams_of[2], (H * HD, D), (H * HD) ** -0.5, 0.1875)
    block_ids = draw_block_ids(jax.random.fold_in(streams_of[6], 71), 0)
    block_lists = draw_block_lists(jax.random.fold_in(streams_of[6], 71), 0)
    decays = draw_decays(jax.random.fold_in(streams_of[6], 71), 0)
    return dict(frames_in=frames_in, in_weight=in_weight, out_weight=out_weight, block_ids=block_ids, block_lists=block_lists, decays=decays)


epsilon = 1e-06
highest = lax.Precision.HIGHEST

def head_norm(values):
    wide = values.astype(jnp.float32)
    return (wide * lax.rsqrt(lax.optimization_barrier(jnp.mean(wide * wide, axis=-1, keepdims=True)) + epsilon)).astype(jnp.bfloat16)

def reference(frames_in, in_weight, out_weight, block_ids, block_lists, decays):
    labels = jnp.arange(NB, dtype=jnp.int32)
    onehot = (block_ids[:, None] == labels[None, :]).astype(jnp.float32)
    adjacent = jnp.any(block_lists[:, :, None] == labels[None, None, :], axis=1).astype(jnp.float32)
    allowed = jnp.dot(jnp.dot(onehot, adjacent, precision=highest), onehot.T, precision=highest)
    ssm_scale = 1.0 / (N * math.sqrt(TOKS // NB))

    def frame_step(carry_state, inputs):
        frame_rows, frame_decay = inputs
        inputs_wide = frame_rows.astype(jnp.float32)
        normed = (inputs_wide * lax.rsqrt(lax.optimization_barrier(jnp.mean(inputs_wide * inputs_wide, axis=-1, keepdims=True)) + epsilon)).astype(jnp.bfloat16)
        projected = jnp.dot(normed, in_weight, preferred_element_type=jnp.float32).astype(jnp.bfloat16)
        projected = projected.reshape(TOKS, H, 5, HD)
        queries = head_norm(projected[:, :, 0]).astype(jnp.float32)
        key_rows = head_norm(projected[:, :, 1]).astype(jnp.float32)
        values = projected[:, :, 2].astype(jnp.float32)
        input_map = projected[:, :, 3, :N].astype(jnp.float32)
        output_map = projected[:, :, 4, :N].astype(jnp.float32)
        scores = jnp.einsum('shd,thd->hst', queries, key_rows, precision=highest) / math.sqrt(HD)
        exponent = jnp.exp(scores) * allowed[None]
        weights = (exponent / lax.optimization_barrier(jnp.sum(exponent, axis=-1, keepdims=True))).astype(jnp.bfloat16)
        attended = jnp.einsum('hst,thd->shd', weights.astype(jnp.float32), values, precision=highest)
        update = jnp.einsum('sb,shn,shd->hbnd', onehot, input_map, values, precision=highest)
        carry_state = frame_decay[:, :, None, None] * carry_state + update
        readout = jnp.einsum('sb,shn,hbnd->shd', onehot, output_map, carry_state, precision=highest) * ssm_scale
        mixed = (attended + readout).astype(jnp.bfloat16).reshape(TOKS, H * HD)
        result = jnp.dot(mixed, out_weight, preferred_element_type=jnp.float32).astype(jnp.bfloat16)
        return (carry_state, result)
    start_state = jnp.zeros((H, NB, N, HD), jnp.float32)
    final_state, frame_outs = lax.scan(frame_step, start_state, (frames_in, decays))
    return frame_outs
```

```python
import functools
import math

import jax
import jax.numpy as jnp
from jax import lax
from jax.experimental import pallas as pl
from jax.experimental.pallas import tpu as pltpu
from jax.sharding import PartitionSpec as P

HD = 64
N = 64
LANES = 2 * HD
PIECES = 5
EARLY = (2, 3)
LATE = (0, 1, 4)

epsilon = 1e-06

f32 = jnp.float32
bf16 = jnp.bfloat16


def params(mib=48):
    return pltpu.CompilerParams(vmem_limit_bytes=mib << 20)


def cost(flops, nbytes, transcendentals=0):
    return pl.CostEstimate(
        flops=int(flops), bytes_accessed=int(nbytes), transcendentals=int(transcendentals)
    )


def first_half(shape):
    return lax.broadcasted_iota(jnp.int32, shape, len(shape) - 1) < HD


def reorder_kernel(w_ref, early_ref, late_ref):
    pairs = w_ref.shape[1] // (2 * PIECES * HD)

    def piece(head, i):
        at = (head * PIECES + i) * HD
        return w_ref[:, at : at + HD]

    for p in range(pairs):
        for out_ref, kinds in ((early_ref, EARLY), (late_ref, LATE)):
            for j, i in enumerate(kinds):
                at = (p * len(kinds) + j) * LANES
                out_ref[:, at : at + LANES] = jnp.concatenate(
                    [piece(2 * p, i), piece(2 * p + 1, i)], axis=1
                )


def reorder(w):
    rows, cols = w.shape
    base = cols // PIECES
    return pl.pallas_call(
        reorder_kernel,
        out_shape=(
            jax.ShapeDtypeStruct((rows, base * len(EARLY)), bf16),
            jax.ShapeDtypeStruct((rows, base * len(LATE)), bf16),
        ),
        compiler_params=params(),
        cost_estimate=cost(0, 4 * rows * cols),
        name="reorder",
    )(w)


def sort_kernel(groups, ids_row_ref, ids_col_ref, *refs):
    part_refs = refs[:-3]
    sorted_ref, back_ref, normed = refs[-3:]
    local, width = part_refs[0].shape
    tokens = normed.shape[0]
    block = tokens // groups
    step = 128

    for k, part in enumerate(part_refs):

        def norm(c, _, part=part, k=k):
            at = pl.multiple_of(c * step, step)
            wide = part[pl.ds(at, step), :].astype(f32)
            scale = lax.rsqrt(jnp.mean(wide * wide, axis=-1, keepdims=True) + epsilon)
            normed[pl.ds(k * local + at, step), :] = (wide * scale).astype(bf16)
            return 0

        lax.fori_loop(0, local // step, norm, 0)

    ids_row = ids_row_ref[...]
    label = lax.broadcasted_iota(jnp.int32, (groups, tokens), 0)
    held = label == ids_row
    held_bf = jnp.where(held, 1.0, 0.0).astype(bf16)
    counts = []
    for c in range(tokens // 256):
        before = lax.broadcasted_iota(jnp.int32, (tokens, 256), 0) < (
            lax.broadcasted_iota(jnp.int32, (tokens, 256), 1) + c * 256
        )
        counts.append(
            jnp.dot(held_bf, jnp.where(before, 1.0, 0.0).astype(bf16), preferred_element_type=f32)
        )
    count = jnp.concatenate(counts, axis=1)
    rank_row = jnp.sum(
        jnp.where(held, count + (label * block).astype(f32), 0.0), axis=0, keepdims=True
    ).astype(jnp.int32)

    def place(c, _):
        at = pl.multiple_of(c * step, step)
        pick = (lax.broadcasted_iota(jnp.int32, (step, tokens), 0) + at) == rank_row
        pick = jnp.where(pick, 1.0, 0.0).astype(bf16)
        sorted_ref[pl.ds(at, step), :] = jnp.dot(
            pick, normed[...], preferred_element_type=f32
        ).astype(bf16)
        return 0

    lax.fori_loop(0, tokens // step, place, 0)

    lane = lax.broadcasted_iota(jnp.int32, (tokens, 128), 1)
    held_col = jnp.where(lane == ids_col_ref[...], 1.0, 0.0).astype(bf16)

    def place_back(c, _):
        at = pl.multiple_of(c * step, step)
        before = lax.broadcasted_iota(jnp.int32, (step, tokens), 1) < (
            lax.broadcasted_iota(jnp.int32, (step, tokens), 0) + at
        )
        count = jnp.dot(
            jnp.where(before, 1.0, 0.0).astype(bf16), held_col, preferred_element_type=f32
        )
        lane = lax.broadcasted_iota(jnp.int32, (step, 128), 1)
        mine = lane == ids_col_ref[pl.ds(at, step), :]
        rank = jnp.sum(
            jnp.where(mine, count + (lane * block).astype(f32), 0.0), axis=1, keepdims=True
        ).astype(jnp.int32)
        pick = lax.broadcasted_iota(jnp.int32, (step, tokens), 1) == rank
        back_ref[pl.ds(at, step), :] = jnp.where(pick, 1.0, 0.0).astype(bf16)
        return 0

    lax.fori_loop(0, tokens // step, place_back, 0)


def sort_tokens(ids, parts, groups):
    tokens = ids.shape[0]
    width = parts[0].shape[1]
    return pl.pallas_call(
        functools.partial(sort_kernel, groups),
        out_shape=(
            jax.ShapeDtypeStruct((tokens, width), bf16),
            jax.ShapeDtypeStruct((tokens, tokens), bf16),
        ),
        scratch_shapes=[pltpu.VMEM((tokens, width), bf16)],
        compiler_params=params(),
        cost_estimate=cost(2 * tokens * tokens * width, 6 * tokens * width),
        name="sort_tokens",
    )(ids.reshape(1, tokens), ids.reshape(tokens, 1), *parts)


def update_kernel(groups, x_ref, w_ref, v_ref, u_ref, b_ref):
    tokens = x_ref.shape[0]
    block = tokens // groups
    step = 256

    def project(c, _):
        at = pl.multiple_of(c * step, step)
        both = jnp.dot(
            x_ref[pl.ds(at, step), :], w_ref[...], preferred_element_type=f32
        ).astype(bf16)
        v_ref[pl.ds(at, step), :] = both[:, :LANES]
        b_ref[pl.ds(at, step), :] = both[:, LANES:]
        return 0

    lax.fori_loop(0, tokens // step, project, 0)
    for g in range(groups):
        rows = slice(g * block, (g + 1) * block)
        outer = lax.dot_general(
            b_ref[rows, :], v_ref[rows, :], (((0,), (0,)), ((), ())), preferred_element_type=f32
        )
        u_ref[g * N : (g + 1) * N, :] = jnp.where(
            first_half((N, LANES)), outer[:HD], outer[HD:]
        ).astype(bf16)


def project_updates(x, w, groups):
    tokens, width = x.shape
    pairs = w.shape[1] // (2 * LANES)
    return pl.pallas_call(
        functools.partial(update_kernel, groups),
        grid=(pairs,),
        in_specs=[
            pl.BlockSpec((tokens, width), lambda p: (0, 0)),
            pl.BlockSpec((width, 2 * LANES), lambda p: (0, p)),
        ],
        out_specs=(
            pl.BlockSpec((tokens, LANES), lambda p: (0, p)),
            pl.BlockSpec((groups * N, LANES), lambda p: (p, 0)),
        ),
        out_shape=(
            jax.ShapeDtypeStruct((tokens, pairs * LANES), bf16),
            jax.ShapeDtypeStruct((pairs * groups * N, LANES), bf16),
        ),
        scratch_shapes=[pltpu.VMEM((tokens, LANES), bf16)],
        compiler_params=params(),
        cost_estimate=cost(2 * tokens * width * w.shape[1], 2 * (tokens * width + w.size * 2)),
        name="project_updates",
    )(x, w)


def scan_kernel(d_ref, u_ref, s_ref):
    frames = u_ref.shape[0]
    state = jnp.zeros(u_ref.shape[1:], f32)
    for t in range(frames):
        state = d_ref[t] * state + u_ref[t].astype(f32)
        s_ref[t] = state.astype(bf16)


def scan_states(decay, update):
    return pl.pallas_call(
        scan_kernel,
        out_shape=jax.ShapeDtypeStruct(update.shape, bf16),
        compiler_params=params(),
        cost_estimate=cost(2 * update.size, 4 * update.size),
        name="scan_states",
    )(decay, update)


def attend_kernel(lists_ref, x_ref, w_ref, v_ref, a_ref, c_ref, q_ref, k_ref):
    tokens = x_ref.shape[0]
    groups, chosen = lists_ref.shape
    block = tokens // groups
    step = 256
    per = step // block

    def project(c, _):
        at = pl.multiple_of(c * step, step)
        three = jnp.dot(
            x_ref[pl.ds(at, step), :], w_ref[...], preferred_element_type=f32
        ).astype(bf16)
        c_ref[pl.ds(at, step), :] = three[:, 2 * LANES :]
        half = first_half((step, LANES))

        def head_norm(wide):
            square = wide * wide
            one = jnp.sum(jnp.where(half, square, 0.0), axis=-1, keepdims=True)
            two = jnp.sum(jnp.where(half, 0.0, square), axis=-1, keepdims=True)
            return wide * lax.rsqrt(jnp.where(half, one, two) * (1.0 / HD) + epsilon)

        q = head_norm(three[:, :LANES].astype(f32))
        k_ref[pl.ds(at, step), :] = head_norm(three[:, LANES : 2 * LANES].astype(f32)).astype(bf16)
        one = jnp.where(half, q, 0.0).astype(bf16)
        two = jnp.where(half, 0.0, q).astype(bf16)
        for i in range(per):
            rows = slice(i * block, (i + 1) * block)
            q_ref[c * per + i] = jnp.concatenate([one[rows], two[rows]], axis=0)
        return 0

    lax.fori_loop(0, tokens // step, project, 0)

    scale = math.log2(math.e) / math.sqrt(HD)
    for g in range(groups):
        starts = [pl.multiple_of(lists_ref[g, j] * block, block) for j in range(chosen)]
        keys = jnp.concatenate([k_ref[pl.ds(s, block), :] for s in starts], axis=0)
        values = jnp.concatenate([v_ref[pl.ds(s, block), :] for s in starts], axis=0)
        score = lax.dot_general(
            q_ref[g], keys, (((1,), (1,)), ((), ())), preferred_element_type=f32
        )
        e = jnp.exp2(score * scale)
        weight = (e * (1.0 / jnp.sum(e, axis=-1, keepdims=True))).astype(bf16)
        both = jnp.dot(weight, values, preferred_element_type=f32)
        a_ref[g * block : (g + 1) * block, :] = jnp.where(
            first_half((block, LANES)), both[:block], both[block:]
        )


def attend(lists, x, w, v):
    tokens, width = x.shape
    groups, chosen = lists.shape
    pairs = w.shape[1] // (3 * LANES)
    block = tokens // groups
    return pl.pallas_call(
        attend_kernel,
        grid_spec=pltpu.PrefetchScalarGridSpec(
            num_scalar_prefetch=1,
            grid=(pairs,),
            in_specs=[
                pl.BlockSpec((tokens, width), lambda p, _: (0, 0)),
                pl.BlockSpec((width, 3 * LANES), lambda p, _: (0, p)),
                pl.BlockSpec((tokens, LANES), lambda p, _: (0, p)),
            ],
            out_specs=(
                pl.BlockSpec((tokens, LANES), lambda p, _: (0, p)),
                pl.BlockSpec((tokens, LANES), lambda p, _: (0, p)),
            ),
            scratch_shapes=[
                pltpu.VMEM((groups, 2 * block, LANES), bf16),
                pltpu.VMEM((tokens, LANES), bf16),
            ],
        ),
        out_shape=(
            jax.ShapeDtypeStruct((tokens, pairs * LANES), f32),
            jax.ShapeDtypeStruct((tokens, pairs * LANES), bf16),
        ),
        compiler_params=params(),
        cost_estimate=cost(
            4 * tokens * width * w.shape[1],
            2 * (tokens * width + w.size + 4 * tokens * pairs * LANES),
            2 * pairs * tokens * chosen * block,
        ),
        name="attend",
    )(lists, x, w, v)


def mix_kernel(groups, a_ref, c_ref, s_ref, back_ref, out_ref, mixed):
    tokens = a_ref.shape[0]
    block = tokens // groups
    pairs = a_ref.shape[1] // LANES
    scale = 1.0 / (N * math.sqrt(block))
    for p in range(pairs):
        cols = slice(p * LANES, (p + 1) * LANES)
        for g in range(groups):
            rows = slice(g * block, (g + 1) * block)
            at = (p * groups + g) * N
            state = s_ref[at : at + N, :].astype(f32)
            half = first_half((N, LANES))
            wide = jnp.concatenate(
                [jnp.where(half, state, 0.0), jnp.where(half, 0.0, state)], axis=0
            ).astype(bf16)
            read = jnp.dot(c_ref[rows, cols], wide, preferred_element_type=f32)
            mixed[rows, cols] = (a_ref[rows, cols] + read * scale).astype(bf16)
    step = 256

    def place(c, _):
        at = pl.multiple_of(c * step, step)
        out_ref[pl.ds(at, step), :] = jnp.dot(
            back_ref[pl.ds(at, step), :], mixed[...], preferred_element_type=f32
        ).astype(bf16)
        return 0

    lax.fori_loop(0, tokens // step, place, 0)


def mix(attended, readers, state, back, groups):
    tokens, width = attended.shape
    return pl.pallas_call(
        functools.partial(mix_kernel, groups),
        out_shape=jax.ShapeDtypeStruct((tokens, width), bf16),
        scratch_shapes=[pltpu.VMEM((tokens, width), bf16)],
        compiler_params=params(),
        cost_estimate=cost(2 * tokens * tokens * width, 2 * tokens * tokens + 8 * tokens * width),
        name="mix",
    )(attended, readers, state, back)


def out_kernel(me_ref, w_ref, *refs):
    part_refs, out_ref = refs[:-1], refs[-1]
    peers = len(part_refs)
    depth = part_refs[0].shape[1]
    total = None
    for k, part in enumerate(part_refs):
        owner = lax.rem(me_ref[0] - k + peers, peers)
        rows = pl.ds(pl.multiple_of(owner * depth, depth), depth)
        term = jnp.dot(part[...], w_ref[rows, :], preferred_element_type=f32)
        total = term if total is None else total + term
    out_ref[...] = total.astype(bf16)


def project_out(me, w, parts):
    local = parts[0].shape[0]
    width = w.shape[1]
    vmem = pl.BlockSpec(memory_space=pltpu.VMEM)
    return pl.pallas_call(
        out_kernel,
        in_specs=[pl.BlockSpec(memory_space=pltpu.SMEM)] + [vmem] * (1 + len(parts)),
        out_specs=vmem,
        out_shape=jax.ShapeDtypeStruct((local, width), bf16),
        compiler_params=params(),
        cost_estimate=cost(2 * local * w.size, 2 * (w.size + 2 * local * width)),
        name="project_out",
    )(me.reshape(1), w, *parts)


def body(frames_in, in_weight, out_weight, block_ids, block_lists, decays):
    local_tokens = frames_in.shape[1]
    heads_here = decays.shape[1]
    groups = block_lists.shape[0]
    tokens = block_ids.shape[0]
    pairs = heads_here // 2
    frames, peers = lax.axis_size("tm"), lax.axis_size("head")
    frame, me = lax.axis_index("tm"), lax.axis_index("head")

    own = frames_in[0]
    parts = [own] + [
        lax.ppermute(own, "head", [(j, (j - k) % peers) for j in range(peers)])
        for k in range(1, peers)
    ]
    early, late = reorder(in_weight)
    w_early = lax.all_gather(early, "tm", axis=0, tiled=True)
    w_late = lax.all_gather(late, "tm", axis=0, tiled=True)

    ids = jnp.roll(block_ids, -me * local_tokens)
    x, back = sort_tokens(ids, parts, groups)
    v, update = project_updates(x, w_early, groups)

    rows = update.shape[0] // frames
    arrived = lax.all_to_all(
        update.reshape(frames, rows, LANES), "tm", split_axis=0, concat_axis=0, tiled=True
    )
    items = max(1, rows // N)
    per = rows // items
    all_decays = lax.all_gather(decays[0], "tm", axis=0)
    by_item = all_decays.reshape(frames, pairs, 2, groups).transpose(0, 1, 3, 2)
    by_item = by_item.reshape(frames, pairs * groups, 2)
    mine = lax.dynamic_slice_in_dim(by_item, frame * rows // N, items, axis=1)
    decay = jnp.repeat(mine, HD, axis=2).reshape(frames, items, 1, LANES)
    states = scan_states(decay, arrived.reshape(frames, items, per, LANES))
    state = lax.all_to_all(
        states.reshape(frames, rows, LANES), "tm", split_axis=0, concat_axis=0, tiled=True
    ).reshape(frames * rows, LANES)

    attended, readers = attend(block_lists, x, w_late, v)
    mixed = mix(attended, readers, state, back, groups)
    mixed = mixed.reshape(peers, local_tokens, heads_here * HD)
    features = [mixed[0]] + [
        lax.ppermute(mixed[k], "head", [(j, (j + k) % peers) for j in range(peers)])
        for k in range(1, peers)
    ]
    return project_out(me, out_weight, features)[None]


def solution(mesh):
    return jax.shard_map(
        body,
        mesh=mesh,
        in_specs=(P("tm", "head", None), P("tm", "head"), P(), P(), P(), P("tm", "head", None)),
        out_specs=P("tm", "head", None),
        check_vma=False,
    )
```

```python
import functools
import math

import jax
import jax.numpy as jnp
from jax import lax
from jax.experimental import pallas as pl
from jax.experimental.pallas import tpu as pltpu
from jax.sharding import PartitionSpec as P

HD = 64
N = 64
LANES = 2 * HD
PIECES = 5
EARLY = (2, 3)
LATE = (0, 1, 4)

epsilon = 1e-06

f32 = jnp.float32
bf16 = jnp.bfloat16


def params(mib=32):
    return pltpu.CompilerParams(vmem_limit_bytes=mib << 20)


def cost(flops, nbytes, transcendentals=0):
    return pl.CostEstimate(
        flops=int(flops), bytes_accessed=int(nbytes), transcendentals=int(transcendentals)
    )


def first_half(shape):
    return lax.broadcasted_iota(jnp.int32, shape, len(shape) - 1) < HD


class Plan:
    def __init__(self, frames, peers, heads_here):
        self.merge = 2 if frames % 2 == 0 and heads_here % 4 == 0 else 1
        self.frames, self.peers = frames, peers
        self.heads = heads_here // self.merge
        self.pairs = self.heads // 2
        self.chips = frames // self.merge
        self.across = 2 if self.chips % 2 == 0 else 1
        self.along = self.chips // self.across
        self.chained = self.along <= 4
        if self.chained:
            moves = [0] + [s * k for k in range(1, self.along) for s in (-1, 1)]
            self.sources = [(m, f) for f in range(self.across) for m in moves]
        else:
            self.sources = [None]

    def core(self):
        return lax.rem(lax.axis_index("tm"), self.merge)

    def chip(self):
        return lax.div(lax.axis_index("tm"), self.merge)

    def at(self, a, b, c):
        return (a * self.across + b) * self.merge + c

    def move(self, block, step, valid):
        pairs = [
            (self.at(a, b, c), self.at(a + step, b, c))
            for a in valid
            if 0 <= a + step < self.along
            for b in range(self.across)
            for c in range(self.merge)
        ]
        return lax.ppermute(block, "tm", pairs)

    def cross(self, block, valid):
        pairs = [
            (self.at(a, b, c), self.at(a, 1 - b, c))
            for a in valid
            for b in range(2)
            for c in range(self.merge)
        ]
        return lax.ppermute(block, "tm", pairs)

    def swap(self, block):
        return lax.ppermute(block, "tm", [(t, t ^ 1) for t in range(self.frames)])

    def to_peer(self, block, k, other):
        if not other:
            pairs = [(j, (j + k) % self.peers) for j in range(self.peers)]
            return lax.ppermute(block, "head", pairs)
        if k == 0:
            return self.swap(block)
        pairs = [
            (t * self.peers + j, (t ^ 1) * self.peers + (j + k) % self.peers)
            for t in range(self.frames)
            for j in range(self.peers)
        ]
        return lax.ppermute(block, ("tm", "head"), pairs)

    def groups(self):
        if self.merge == 1:
            return None
        return [[j * self.merge + c for j in range(self.chips)] for c in range(self.merge)]

    def gather(self, block, gate=None):
        if not self.chained:
            whole = lax.all_gather(
                block, "tm", axis=0, tiled=True, axis_index_groups=self.groups()
            )
            return [whole], None
        n = self.along
        found = {(0, 0): block}
        for k in range(1, n):
            found[-k, 0] = self.move(found[1 - k, 0], 1, range(k - 1, n))
            found[k, 0] = self.move(found[k - 1, 0], -1, range(0, n - k + 1))
        if self.across == 2:
            for m in [0] + [s * k for k in range(1, n) for s in (-1, 1)]:
                valid = range(max(0, -m), min(n, n - m))
                found[m, 1] = self.cross(found[m, 0], valid)
        return [found[s] for s in self.sources], (found.get((-1, 0)), found.get((1, 0)))

    def assemble(self, refs, out):
        if not self.chained:
            out[...] = refs[0][...]
            return
        rows = refs[0].shape[0]
        chip = self.chip()
        a, b = lax.div(chip, self.across), lax.rem(chip, self.across)
        for ref, (m, flip) in zip(refs, self.sources):
            there = jnp.clip(a + m, 0, self.along - 1)
            side = 1 - b if flip else b
            at = pl.multiple_of((there * self.across + side) * rows, rows)

            @pl.when((a + m >= 0) & (a + m < self.along))
            def _(ref=ref, at=at):
                out[pl.ds(at, rows), :] = ref[...]


def halves(shape, one, two):
    return jnp.where(first_half(shape), one, two)


def reorder_kernel(plan, *refs):
    w_refs, (early_ref, late_ref) = refs[: plan.merge], refs[plan.merge :]
    rows = w_refs[0].shape[0]
    width = plan.heads * PIECES * HD
    first = plan.core() == 0

    def chosen(ref, at):
        one = ref[:, at : at + HD]
        return one if plan.merge == 1 else jnp.where(first, one, ref[:, width + at : width + at + HD])

    for p in range(plan.pairs):
        for out_ref, kinds in ((early_ref, EARLY), (late_ref, LATE)):
            for j, i in enumerate(kinds):
                to = (p * len(kinds) + j) * LANES
                blocks = []
                for ref in w_refs:
                    one, two = (
                        chosen(ref, ((2 * p + h) * PIECES + i) * HD) for h in range(2)
                    )
                    blocks.append(jnp.concatenate([one, two], axis=1))
                for s, block in enumerate(blocks):
                    if plan.merge == 2:
                        block = jnp.where(first, block, blocks[1 - s])
                    out_ref[s * rows : (s + 1) * rows, to : to + LANES] = block


def reorder(plan, weights):
    rows = weights[0].shape[0]
    base = plan.heads * HD
    return pl.pallas_call(
        functools.partial(reorder_kernel, plan),
        out_shape=(
            jax.ShapeDtypeStruct((plan.merge * rows, base * len(EARLY)), bf16),
            jax.ShapeDtypeStruct((plan.merge * rows, base * len(LATE)), bf16),
        ),
        compiler_params=params(),
        cost_estimate=cost(0, 4 * weights[0].size),
        name="reorder",
    )(*weights)


def normalise(part, out, at):
    step = min(128, part.shape[0])

    def norm(c, _):
        start = pl.multiple_of(c * step, step)
        wide = part[pl.ds(start, step), :].astype(f32)
        scale = lax.rsqrt(jnp.mean(wide * wide, axis=-1, keepdims=True) + epsilon)
        out[pl.ds(at + start, step), :] = (wide * scale).astype(bf16)
        return 0

    lax.fori_loop(0, part.shape[0] // step, norm, 0)


def order_kernel(plan, groups, ids_row_ref, ids_col_ref, *refs):
    own_refs = refs[: plan.merge]
    x_ref, rest_ref, back_ref, normed = refs[plan.merge :]
    local = own_refs[0].shape[0]
    tokens = back_ref.shape[0]
    block = tokens // groups
    step = 128
    for s, own in enumerate(own_refs):
        normalise(own, normed, s * local)

    label = lax.broadcasted_iota(jnp.int32, (groups, tokens), 0)
    held = label == ids_row_ref[...]
    held_bf = jnp.where(held, 1.0, 0.0).astype(bf16)
    counts = []
    for c in range(tokens // 256):
        before = lax.broadcasted_iota(jnp.int32, (tokens, 256), 0) < (
            lax.broadcasted_iota(jnp.int32, (tokens, 256), 1) + c * 256
        )
        counts.append(
            jnp.dot(held_bf, jnp.where(before, 1.0, 0.0).astype(bf16), preferred_element_type=f32)
        )
    count = jnp.concatenate(counts, axis=1)
    rank_row = jnp.sum(
        jnp.where(held, count + (label * block).astype(f32), 0.0), axis=0, keepdims=True
    ).astype(jnp.int32)

    def place(c, _):
        at = pl.multiple_of(c * step, step)
        pick = (lax.broadcasted_iota(jnp.int32, (step, tokens), 0) + at) == rank_row
        pick = jnp.where(pick, 1.0, 0.0).astype(bf16)
        rest_ref[pl.ds(at, step), :] = pick[:, local:]
        for s in range(plan.merge):
            x_ref[pl.ds(s * tokens + at, step), :] = jnp.dot(
                pick[:, :local], normed[s * local : (s + 1) * local], preferred_element_type=f32
            ).astype(bf16)
        return 0

    lax.fori_loop(0, tokens // step, place, 0)

    lane = lax.broadcasted_iota(jnp.int32, (tokens, 128), 1)
    held_col = jnp.where(lane == ids_col_ref[...], 1.0, 0.0).astype(bf16)

    def place_back(c, _):
        at = pl.multiple_of(c * step, step)
        before = lax.broadcasted_iota(jnp.int32, (step, tokens), 1) < (
            lax.broadcasted_iota(jnp.int32, (step, tokens), 0) + at
        )
        count = jnp.dot(
            jnp.where(before, 1.0, 0.0).astype(bf16), held_col, preferred_element_type=f32
        )
        lane = lax.broadcasted_iota(jnp.int32, (step, 128), 1)
        mine = lane == ids_col_ref[pl.ds(at, step), :]
        rank = jnp.sum(
            jnp.where(mine, count + (lane * block).astype(f32), 0.0), axis=1, keepdims=True
        ).astype(jnp.int32)
        pick = lax.broadcasted_iota(jnp.int32, (step, tokens), 1) == rank
        back_ref[pl.ds(at, step), :] = jnp.where(pick, 1.0, 0.0).astype(bf16)
        return 0

    lax.fori_loop(0, tokens // step, place_back, 0)


def order(plan, ids, owns, groups):
    tokens = ids.shape[0]
    local, width = owns[0].shape
    return pl.pallas_call(
        functools.partial(order_kernel, plan, groups),
        out_shape=(
            jax.ShapeDtypeStruct((plan.merge * tokens, width), bf16),
            jax.ShapeDtypeStruct((tokens, tokens - local), bf16),
            jax.ShapeDtypeStruct((tokens, tokens), bf16),
        ),
        scratch_shapes=[pltpu.VMEM((plan.merge * local, width), bf16)],
        compiler_params=params(),
        cost_estimate=cost(2 * tokens * tokens * width, 6 * tokens * width),
        name="order",
    )(ids.reshape(1, tokens), ids.reshape(tokens, 1), *owns)


def decay_row(plan, ref, frame, pair, g, groups):
    heads_here = plan.heads * plan.merge
    at = (frame * heads_here + plan.core() * plan.heads + 2 * pair) * groups + g
    return halves((1, LANES), ref[at], ref[at + groups])


def update_kernel(plan, groups, parts, decay_ref, part_ref, rest_ref, *refs):
    n = plan.merge * parts
    frame_refs, w_refs = refs[:n], refs[n : n + len(plan.sources)]
    x_ref, v_ref, u_ref, total_ref, normed, w_scr, b_scr = refs[n + len(plan.sources) :]
    tokens = rest_ref.shape[0]
    block = tokens // groups
    step = 256
    plan.assemble(w_refs, w_scr)

    for s in range(plan.merge):
        at = 0
        for ref in frame_refs[s * parts : (s + 1) * parts]:
            normalise(ref, normed, at)
            at += ref.shape[0]

        def place(c, _, s=s):
            at = pl.multiple_of(c * step, step)
            there = pl.ds(s * tokens + at, step)
            more = jnp.dot(rest_ref[pl.ds(at, step), :], normed[...], preferred_element_type=f32)
            x_ref[there, :] = part_ref[there, :] + more.astype(bf16)
            return 0

        lax.fori_loop(0, tokens // step, place, 0)

    def project(c, _):
        at = pl.ds(pl.multiple_of(c * step, step), step)
        both = jnp.dot(x_ref[at, :], w_scr[...], preferred_element_type=f32).astype(bf16)
        for p in range(plan.pairs):
            cols = slice(p * LANES, (p + 1) * LANES)
            v_ref[at, cols] = both[:, 2 * p * LANES : (2 * p + 1) * LANES]
            b_scr[at, cols] = both[:, (2 * p + 1) * LANES : (2 * p + 2) * LANES]
        return 0

    lax.fori_loop(0, plan.merge * tokens // step, project, 0)

    for s in range(plan.merge):
        for p in range(plan.pairs):
            cols = slice(p * LANES, (p + 1) * LANES)
            for g in range(0, groups, 2):
                rows = slice(s * tokens + g * block, s * tokens + (g + 2) * block)
                turned = b_scr[rows, cols].astype(f32).T
                half = lax.broadcasted_iota(jnp.int32, turned.shape, 1) < block
                wide = jnp.concatenate(
                    [jnp.where(half, turned, 0.0), jnp.where(half, 0.0, turned)], axis=0
                ).astype(bf16)
                outer = jnp.dot(wide, v_ref[rows, cols], preferred_element_type=f32)
                for i in range(2):
                    at = (p * groups + g + i) * N
                    m = outer[i * 2 * N : (i + 1) * 2 * N]
                    u_ref[s, at : at + N, :] = halves((N, LANES), m[:N], m[N:])

    core = plan.core()
    for p in range(plan.pairs):
        for g in range(groups):
            rows = slice((p * groups + g) * N, (p * groups + g + 1) * N)
            total = u_ref[core, rows, :]
            if plan.merge == 2:
                last = plan.chip() * plan.merge + 1
                decay = decay_row(plan, decay_ref, last, p, g, groups)
                total = decay * total + u_ref[1 - core, rows, :]
            total_ref[rows, :] = total.astype(bf16)


def project_updates(plan, decays, part, rest, frames, weights, groups):
    tokens, width = rest.shape[0], part.shape[1]
    cols = weights[0].shape[1]
    rows = plan.pairs * groups * N
    vmem = pl.BlockSpec(memory_space=pltpu.VMEM)
    every = plan.merge * tokens
    return pl.pallas_call(
        functools.partial(update_kernel, plan, groups, len(frames) // plan.merge),
        in_specs=[pl.BlockSpec(memory_space=pltpu.SMEM)]
        + [vmem] * (2 + len(frames) + len(weights)),
        out_shape=(
            jax.ShapeDtypeStruct((every, width), bf16),
            jax.ShapeDtypeStruct((every, plan.pairs * LANES), bf16),
            jax.ShapeDtypeStruct((plan.merge, rows, LANES), f32),
            jax.ShapeDtypeStruct((rows, LANES), bf16),
        ),
        scratch_shapes=[
            pltpu.VMEM((rest.shape[1], width), bf16),
            pltpu.VMEM((width, cols), bf16),
            pltpu.VMEM((every, plan.pairs * LANES), bf16),
        ],
        compiler_params=params(),
        cost_estimate=cost(2 * every * width * (cols + rest.shape[1]), 6 * every * width),
        name="project_updates",
    )(decays, part, rest, *frames, *weights)


def scan_kernel(plan, groups, decay_ref, u_ref, s_ref):
    rows = u_ref.shape[1]
    step = min(rows, N)
    for i in range(rows // step):
        at = slice(i * step, (i + 1) * step)
        item = lax.div(plan.chip() * rows + i * step, N)
        pair, g = lax.div(item, groups), lax.rem(item, groups)
        state = jnp.zeros((step, LANES), f32)
        for j in range(plan.chips):
            s_ref[j, at, :] = state.astype(bf16)
            decay = decay_row(plan, decay_ref, j * plan.merge, pair, g, groups)
            for t in range(1, plan.merge):
                decay = decay * decay_row(plan, decay_ref, j * plan.merge + t, pair, g, groups)
            state = decay * state + u_ref[j, at, :].astype(f32)


def scan_states(plan, decays, update, groups):
    return pl.pallas_call(
        functools.partial(scan_kernel, plan, groups),
        in_specs=[
            pl.BlockSpec(memory_space=pltpu.SMEM),
            pl.BlockSpec(memory_space=pltpu.VMEM),
        ],
        out_shape=jax.ShapeDtypeStruct(update.shape, bf16),
        compiler_params=params(),
        cost_estimate=cost(2 * update.size, 4 * update.size),
        name="scan_states",
    )(decays, update)


def attend_kernel(plan, lists_ref, x_ref, v_ref, *refs):
    w_refs = refs[: len(plan.sources)]
    a_ref, c_ref, w_scr, q_ref, k_ref = refs[len(plan.sources) :]
    tokens = x_ref.shape[0]
    groups, chosen = lists_ref.shape
    block = tokens // groups
    step = 256
    per = step // block

    @pl.when(pl.program_id(0) == 0)
    def _():
        plan.assemble(w_refs, w_scr)

    def project(c, _):
        at = pl.multiple_of(c * step, step)
        rows = pl.ds(at, step)
        every = jnp.dot(x_ref[rows, :], w_scr[...], preferred_element_type=f32).astype(bf16)
        half = first_half((step, LANES))

        def head_norm(wide):
            square = wide * wide
            one = jnp.sum(jnp.where(half, square, 0.0), axis=-1, keepdims=True)
            two = jnp.sum(jnp.where(half, 0.0, square), axis=-1, keepdims=True)
            return wide * lax.rsqrt(jnp.where(half, one, two) * (1.0 / HD) + epsilon)

        for p in range(plan.pairs):
            cols = slice(p * LANES, (p + 1) * LANES)
            q, k, reader = (
                every[:, (3 * p + i) * LANES : (3 * p + i + 1) * LANES] for i in range(3)
            )
            c_ref[rows, cols] = reader
            k_ref[rows, cols] = head_norm(k.astype(f32)).astype(bf16)
            q = head_norm(q.astype(f32))
            one = jnp.where(half, q, 0.0).astype(bf16)
            two = jnp.where(half, 0.0, q).astype(bf16)
            for i in range(per):
                part = slice(i * block, (i + 1) * block)
                q_ref[p, c * per + i] = jnp.concatenate([one[part], two[part]], axis=0)
        return 0

    lax.fori_loop(0, tokens // step, project, 0)

    scale = math.log2(math.e) / math.sqrt(HD)
    for p in range(plan.pairs):
        cols = slice(p * LANES, (p + 1) * LANES)
        for g in range(groups):
            starts = [pl.multiple_of(lists_ref[g, j] * block, block) for j in range(chosen)]
            keys = jnp.concatenate([k_ref[pl.ds(s, block), cols] for s in starts], axis=0)
            values = jnp.concatenate([v_ref[pl.ds(s, block), cols] for s in starts], axis=0)
            score = lax.dot_general(
                q_ref[p, g], keys, (((1,), (1,)), ((), ())), preferred_element_type=f32
            )
            e = jnp.exp2(score * scale)
            weight = (e * (1.0 / jnp.sum(e, axis=-1, keepdims=True))).astype(bf16)
            both = jnp.dot(weight, values, preferred_element_type=f32)
            a_ref[g * block : (g + 1) * block, cols] = halves(
                (block, LANES), both[:block], both[block:]
            )


def attend(plan, lists, x, v, weights):
    every, width = x.shape
    groups, chosen = lists.shape
    tokens = every // plan.merge
    block = tokens // groups
    cols = weights[0].shape[1]
    part = pl.BlockSpec((tokens, plan.pairs * LANES), lambda s, _: (s, 0))
    return pl.pallas_call(
        functools.partial(attend_kernel, plan),
        grid_spec=pltpu.PrefetchScalarGridSpec(
            num_scalar_prefetch=1,
            grid=(plan.merge,),
            in_specs=[pl.BlockSpec((tokens, width), lambda s, _: (s, 0)), part]
            + [pl.BlockSpec(w.shape, lambda s, _: (0, 0)) for w in weights],
            out_specs=(part, part),
            scratch_shapes=[
                pltpu.VMEM((width, cols), bf16),
                pltpu.VMEM((plan.pairs, groups, 2 * block, LANES), bf16),
                pltpu.VMEM((tokens, plan.pairs * LANES), bf16),
            ],
        ),
        out_shape=(
            jax.ShapeDtypeStruct((every, plan.pairs * LANES), f32),
            jax.ShapeDtypeStruct((every, plan.pairs * LANES), bf16),
        ),
        compiler_params=params(),
        cost_estimate=cost(
            4 * every * width * cols,
            2 * (every * width + width * cols + 4 * every * plan.pairs * LANES),
            2 * plan.pairs * every * chosen * block,
        ),
        name="attend",
    )(lists, x, v, *weights)


def mix_kernel(plan, groups, decay_ref, a_ref, c_ref, s_ref, u_ref, back_ref, *refs):
    out_refs, mixed = refs[:-1], refs[-1]
    tokens = back_ref.shape[0]
    block = tokens // groups
    width = plan.pairs * LANES
    scale = 1.0 / (N * math.sqrt(block))
    core = plan.core()
    for p in range(plan.pairs):
        cols = slice(p * LANES, (p + 1) * LANES)
        for g in range(groups):
            items = slice((p * groups + g) * N, (p * groups + g + 1) * N)
            state = s_ref[items, :].astype(f32)
            for t in range(plan.merge):
                slot = core if t == 0 else 1 - core
                decay = decay_row(plan, decay_ref, plan.chip() * plan.merge + t, p, g, groups)
                state = decay * state + u_ref[slot, items, :]
                half = first_half((N, LANES))
                wide = jnp.concatenate(
                    [jnp.where(half, state, 0.0), jnp.where(half, 0.0, state)], axis=0
                ).astype(bf16)
                rows = pl.ds(pl.multiple_of(slot * tokens + g * block, block), block)
                read = jnp.dot(c_ref[rows, cols], wide, preferred_element_type=f32)
                mixed[slot, g * block : (g + 1) * block, cols] = (
                    a_ref[rows, cols] + read * scale
                ).astype(bf16)
    local = out_refs[0].shape[0]
    for s in range(plan.merge):
        for k in range(plan.peers):
            out_refs[s * plan.peers + k][...] = jnp.dot(
                back_ref[k * local : (k + 1) * local, :], mixed[s], preferred_element_type=f32
            ).astype(bf16)


def mix(plan, decays, attended, readers, state, updates, back, groups):
    tokens = back.shape[0]
    width = attended.shape[1]
    out = jax.ShapeDtypeStruct((tokens // plan.peers, width), bf16)
    vmem = pl.BlockSpec(memory_space=pltpu.VMEM)
    return pl.pallas_call(
        functools.partial(mix_kernel, plan, groups),
        in_specs=[pl.BlockSpec(memory_space=pltpu.SMEM)] + [vmem] * 5,
        out_shape=(out,) * (plan.merge * plan.peers),
        scratch_shapes=[pltpu.VMEM((plan.merge, tokens, width), bf16)],
        compiler_params=params(),
        cost_estimate=cost(4 * tokens * tokens * width, 2 * tokens * tokens + 16 * tokens * width),
        name="mix",
    )(decays, attended, readers, state, updates, back)


def out_kernel(plan, w_ref, *refs):
    part_refs, out_ref = refs[:-1], refs[-1]
    depth = part_refs[0].shape[1]
    core, me = plan.core(), lax.axis_index("head")
    total = None
    for s in range(plan.merge):
        for k in range(plan.peers):
            owner = lax.rem(me - k + plan.peers, plan.peers) * plan.merge
            owner = owner + (core if s == 0 else 1 - core)
            rows = pl.ds(pl.multiple_of(owner * depth, depth), depth)
            term = jnp.dot(
                part_refs[s * plan.peers + k][...], w_ref[rows, :], preferred_element_type=f32
            )
            total = term if total is None else total + term
    out_ref[...] = total.astype(bf16)


def project_out(plan, w, parts):
    local = parts[0].shape[0]
    width = w.shape[1]
    return pl.pallas_call(
        functools.partial(out_kernel, plan),
        out_shape=jax.ShapeDtypeStruct((local, width), bf16),
        compiler_params=params(),
        cost_estimate=cost(2 * local * w.size, 2 * (w.size + 2 * local * width)),
        name="project_out",
    )(w, *parts)


def body(frames_in, in_weight, out_weight, block_ids, block_lists, decays):
    local_tokens = frames_in.shape[1]
    heads_here = decays.shape[1]
    groups = block_lists.shape[0]
    me = lax.axis_index("head")
    plan = Plan(lax.axis_size("tm"), lax.axis_size("head"), heads_here)

    weights = [in_weight] + [plan.swap(in_weight)] * (plan.merge - 1)
    early, late = reorder(plan, weights)

    own = frames_in[0]
    chunks = 2 if local_tokens >= 512 else 1
    arriving = [
        plan.to_peer(chunk, plan.peers - k, False)
        for k in range(1, plan.peers)
        for chunk in jnp.split(own, chunks)
    ]
    owns = [own]
    if plan.merge == 2:
        owns.append(plan.swap(own))
        arriving = arriving + [plan.swap(chunk) for chunk in arriving]

    w_early, gate = plan.gather(early)
    if gate is not None:
        late, _ = lax.optimization_barrier((late, gate))
    w_late, _ = plan.gather(late)

    ids = jnp.roll(block_ids, -me * local_tokens)
    all_decays = lax.all_gather(decays[0], "tm", axis=0).reshape(-1)
    ids, all_decays = lax.optimization_barrier((ids, all_decays))
    part, rest, back = order(plan, ids, owns, groups)
    x, v, updates, total = project_updates(
        plan, all_decays, part, rest, arriving, w_early, groups
    )

    def exchange(blocks):
        return lax.all_to_all(
            blocks, "tm", split_axis=0, concat_axis=0, tiled=True,
            axis_index_groups=plan.groups(),
        )

    rows = total.shape[0] // plan.chips
    arrived = exchange(total.reshape(plan.chips, rows, LANES))
    states = scan_states(plan, all_decays, arrived, groups)
    state = exchange(states).reshape(total.shape)

    attended, readers = attend(plan, block_lists, x, v, w_late)
    mixed = mix(plan, all_decays, attended, readers, state, updates, back, groups)
    features = [
        mixed[0] if s == 0 and k == 0 else plan.to_peer(mixed[s * plan.peers + k], k, s == 1)
        for s in range(plan.merge)
        for k in range(plan.peers)
    ]
    return project_out(plan, out_weight, features)[None]


def solution(mesh):
    return jax.shard_map(
        body,
        mesh=mesh,
        in_specs=(P("tm", "head", None), P("tm", "head"), P(), P(), P(), P("tm", "head", None)),
        out_specs=P("tm", "head", None),
        check_vma=False,
    )
```

```python
import functools
import math

import jax
import jax.numpy as jnp
from jax import lax
from jax.experimental import pallas as pl
from jax.experimental.pallas import tpu as pltpu
from jax.sharding import PartitionSpec as P

HD = 64
N = 64
LANES = 2 * HD
PIECES = 5
EARLY = (2, 3)
LATE = (0, 1, 4)

epsilon = 1e-06

f32 = jnp.float32
bf16 = jnp.bfloat16


def params(mib=60):
    return pltpu.CompilerParams(vmem_limit_bytes=mib << 20)


def cost(flops, nbytes, transcendentals=0):
    return pl.CostEstimate(
        flops=int(flops), bytes_accessed=int(nbytes), transcendentals=int(transcendentals)
    )


def first_half(shape):
    return lax.broadcasted_iota(jnp.int32, shape, len(shape) - 1) < HD


class Plan:
    def __init__(self, frames, peers, heads_here):
        self.merge = 2 if frames % 2 == 0 and heads_here % 4 == 0 else 1
        self.frames, self.peers = frames, peers
        self.heads = heads_here // self.merge
        self.pairs = self.heads // 2
        self.chips = frames // self.merge

    def core(self):
        return lax.rem(lax.axis_index("tm"), self.merge)

    def chip(self):
        return lax.div(lax.axis_index("tm"), self.merge)

    def swap(self, block):
        return lax.ppermute(block, "tm", [(t, t ^ 1) for t in range(self.frames)])

    def to_peer(self, block, k, other):
        if not other:
            pairs = [(j, (j + k) % self.peers) for j in range(self.peers)]
            return lax.ppermute(block, "head", pairs)
        if k == 0:
            return self.swap(block)
        pairs = [
            (t * self.peers + j, (t ^ 1) * self.peers + (j + k) % self.peers)
            for t in range(self.frames)
            for j in range(self.peers)
        ]
        return lax.ppermute(block, ("tm", "head"), pairs)

    def groups(self):
        if self.merge == 1:
            return None
        return [[j * self.merge + c for j in range(self.chips)] for c in range(self.merge)]

    def decay(self, refs, slot, pair, g):
        head = self.core() * self.heads + 2 * pair
        return halves((1, LANES), refs[slot][head, g], refs[slot][head + 1, g])

    def last_decay(self, refs, pair, g):
        if self.merge == 1:
            return self.decay(refs, 0, pair, g)
        one, two = (self.decay(refs, slot, pair, g) for slot in range(2))
        return jnp.where(self.core() == 0, two, one)


def halves(shape, one, two):
    return jnp.where(first_half(shape), one, two)


def reorder_kernel(plan, *refs):
    w_refs, out_ref = refs[:-1], refs[-1]
    rows = w_refs[0].shape[0]
    width = plan.heads * PIECES * HD
    first = plan.core() == 0

    def chosen(ref, at):
        one = ref[:, at : at + HD]
        if plan.merge == 1:
            return one
        return jnp.where(first, one, ref[:, width + at : width + at + HD])

    to = 0
    for kinds in (EARLY, LATE):
        for p in range(plan.pairs):
            for i in kinds:
                blocks = []
                for ref in w_refs:
                    one, two = (chosen(ref, ((2 * p + h) * PIECES + i) * HD) for h in range(2))
                    blocks.append(jnp.concatenate([one, two], axis=1))
                for s, block in enumerate(blocks):
                    if plan.merge == 2:
                        block = jnp.where(first, block, blocks[1 - s])
                    out_ref[s * rows : (s + 1) * rows, to : to + LANES] = block
                to += LANES


def reorder(plan, weights):
    rows = weights[0].shape[0]
    return pl.pallas_call(
        functools.partial(reorder_kernel, plan),
        out_shape=jax.ShapeDtypeStruct((plan.merge * rows, plan.heads * PIECES * HD), bf16),
        compiler_params=params(),
        cost_estimate=cost(0, 4 * weights[0].size),
        name="reorder",
    )(*weights)


def normalise(part, out, at):
    step = min(128, part.shape[0])

    def norm(c, _):
        start = pl.multiple_of(c * step, step)
        wide = part[pl.ds(start, step), :].astype(f32)
        scale = lax.rsqrt(jnp.mean(wide * wide, axis=-1, keepdims=True) + epsilon)
        out[pl.ds(at + start, step), :] = (wide * scale).astype(bf16)
        return 0

    lax.fori_loop(0, part.shape[0] // step, norm, 0)


def order_kernel(plan, groups, ids_row_ref, ids_col_ref, *refs):
    own_refs = refs[: plan.merge]
    x_ref, rest_ref, back_ref, normed = refs[plan.merge :]
    local = own_refs[0].shape[0]
    tokens = back_ref.shape[0]
    block = tokens // groups
    step = 128
    for s, own in enumerate(own_refs):
        normalise(own, normed, s * local)

    label = lax.broadcasted_iota(jnp.int32, (groups, tokens), 0)
    held = label == ids_row_ref[...]
    held_bf = jnp.where(held, 1.0, 0.0).astype(bf16)
    counts = []
    for c in range(tokens // 256):
        before = lax.broadcasted_iota(jnp.int32, (tokens, 256), 0) < (
            lax.broadcasted_iota(jnp.int32, (tokens, 256), 1) + c * 256
        )
        counts.append(
            jnp.dot(held_bf, jnp.where(before, 1.0, 0.0).astype(bf16), preferred_element_type=f32)
        )
    count = jnp.concatenate(counts, axis=1)
    rank_row = jnp.sum(
        jnp.where(held, count + (label * block).astype(f32), 0.0), axis=0, keepdims=True
    ).astype(jnp.int32)

    def place(c, _):
        at = pl.multiple_of(c * step, step)
        pick = (lax.broadcasted_iota(jnp.int32, (step, tokens), 0) + at) == rank_row
        pick = jnp.where(pick, 1.0, 0.0).astype(bf16)
        rest_ref[pl.ds(at, step), :] = pick[:, local:]
        for s in range(plan.merge):
            x_ref[pl.ds(s * tokens + at, step), :] = jnp.dot(
                pick[:, :local], normed[s * local : (s + 1) * local], preferred_element_type=f32
            ).astype(bf16)
        return 0

    lax.fori_loop(0, tokens // step, place, 0)

    lane = lax.broadcasted_iota(jnp.int32, (tokens, 128), 1)
    held_col = jnp.where(lane == ids_col_ref[...], 1.0, 0.0).astype(bf16)

    def place_back(c, _):
        at = pl.multiple_of(c * step, step)
        before = lax.broadcasted_iota(jnp.int32, (step, tokens), 1) < (
            lax.broadcasted_iota(jnp.int32, (step, tokens), 0) + at
        )
        count = jnp.dot(
            jnp.where(before, 1.0, 0.0).astype(bf16), held_col, preferred_element_type=f32
        )
        lane = lax.broadcasted_iota(jnp.int32, (step, 128), 1)
        mine = lane == ids_col_ref[pl.ds(at, step), :]
        rank = jnp.sum(
            jnp.where(mine, count + (lane * block).astype(f32), 0.0), axis=1, keepdims=True
        ).astype(jnp.int32)
        pick = lax.broadcasted_iota(jnp.int32, (step, tokens), 1) == rank
        back_ref[pl.ds(at, step), :] = jnp.where(pick, 1.0, 0.0).astype(bf16)
        return 0

    lax.fori_loop(0, tokens // step, place_back, 0)


def order(plan, ids, owns, groups):
    tokens = ids.shape[0]
    local, width = owns[0].shape
    return pl.pallas_call(
        functools.partial(order_kernel, plan, groups),
        out_shape=(
            jax.ShapeDtypeStruct((plan.merge * tokens, width), bf16),
            jax.ShapeDtypeStruct((tokens, tokens - local), bf16),
            jax.ShapeDtypeStruct((tokens, tokens), bf16),
        ),
        scratch_shapes=[pltpu.VMEM((plan.merge * local, width), bf16)],
        compiler_params=params(),
        cost_estimate=cost(2 * tokens * tokens * width, 6 * tokens * width),
        name="order",
    )(ids.reshape(1, tokens), ids.reshape(tokens, 1), *owns)


def update_kernel(plan, groups, parts, *refs):
    decay_refs, refs = refs[: plan.merge], refs[plan.merge :]
    part_ref, rest_ref, w_ref, refs = refs[0], refs[1], refs[2], refs[3:]
    frame_refs, refs = refs[: plan.merge * parts], refs[plan.merge * parts :]
    x_ref, v_ref, u_ref, total_ref, normed, kept = refs
    step = x_ref.shape[0]
    block = kept.shape[0] // (groups * plan.pairs)
    here = step // block
    slot, chunk = pl.program_id(0), pl.program_id(1)

    for s in range(plan.merge):

        @pl.when((slot == s) & (chunk == 0))
        def _(s=s):
            at = 0
            for ref in frame_refs[s * parts : (s + 1) * parts]:
                normalise(ref, normed, at)
                at += ref.shape[0]

    more = jnp.dot(rest_ref[...], normed[...], preferred_element_type=f32)
    x_ref[...] = part_ref[...] + more.astype(bf16)
    both = jnp.dot(
        x_ref[...], w_ref[:, : 2 * plan.pairs * LANES], preferred_element_type=f32
    ).astype(bf16)
    for p in range(plan.pairs):
        v = both[:, 2 * p * LANES : (2 * p + 1) * LANES]
        b = both[:, (2 * p + 1) * LANES : (2 * p + 2) * LANES]
        v_ref[:, p * LANES : (p + 1) * LANES] = v
        for i in range(0, here, 2):
            rows = slice(i * block, (i + 2) * block)
            turned = b[rows].astype(f32).T
            half = lax.broadcasted_iota(jnp.int32, turned.shape, 1) < block
            wide = jnp.concatenate(
                [jnp.where(half, turned, 0.0), jnp.where(half, 0.0, turned)], axis=0
            ).astype(bf16)
            outer = jnp.dot(wide, v[rows], preferred_element_type=f32)
            for n in range(2):
                m = outer[n * 2 * N : (n + 1) * 2 * N]
                at = ((i + n) * plan.pairs + p) * N
                u_ref[0, at : at + N, :] = halves((N, LANES), m[:N], m[N:])

    many = u_ref.shape[1]
    there = pl.ds(pl.multiple_of(chunk * many, many), many)
    if plan.merge == 2:

        @pl.when(slot == 0)
        def _():
            kept[there, :] = u_ref[0]

    @pl.when(slot == plan.merge - 1)
    def _():
        peers = total_ref.shape[0]
        share = many // peers
        items = max(1, share // N)
        first = plan.core() == 0
        for d in range(peers):
            for i in range(items):
                row = d * share + i * N
                size = min(N, share)
                item = row // N
                p, g = item % plan.pairs, chunk * here + item // plan.pairs
                last = plan.last_decay(decay_refs, p, g)
                total = u_ref[0, row : row + size, :]
                product = last
                if plan.merge == 2:
                    before = kept[pl.ds(chunk * many + row, size), :]
                    total = jnp.where(first, last, 1.0) * before + jnp.where(first, 1.0, last) * total
                    product = plan.decay(decay_refs, 0, p, g) * plan.decay(decay_refs, 1, p, g)
                total_ref[d, i * size : (i + 1) * size, :] = total.astype(bf16)
                for n in range(3):
                    piece = product.astype(bf16)
                    at = share + n * items + i
                    total_ref[d, at : at + 1, :] = piece
                    product = product - piece.astype(f32)


def share_rows(share):
    return share + 16 * -(-3 * max(1, share // N) // 16)


def project_updates(plan, decays, part, rest, frames, w, groups):
    tokens, width = rest.shape[0], part.shape[1]
    chunks = 4
    step = tokens // chunks
    rows = plan.pairs * groups * N
    every = plan.merge * tokens
    share = rows // plan.chips
    whole = lambda a: pl.BlockSpec(a.shape, lambda s, c: (0,) * a.ndim)
    last = plan.merge - 1
    return pl.pallas_call(
        functools.partial(update_kernel, plan, groups, len(frames) // plan.merge),
        grid=(plan.merge, chunks),
        in_specs=[pl.BlockSpec(memory_space=pltpu.SMEM)] * plan.merge
        + [
            pl.BlockSpec((step, width), lambda s, c: (s * chunks + c, 0)),
            pl.BlockSpec((step, rest.shape[1]), lambda s, c: (c, 0)),
            whole(w),
        ]
        + [whole(f) for f in frames],
        out_specs=(
            pl.BlockSpec((step, width), lambda s, c: (s * chunks + c, 0)),
            pl.BlockSpec((step, plan.pairs * LANES), lambda s, c: (s * chunks + c, 0)),
            pl.BlockSpec((1, rows // chunks, LANES), lambda s, c: (s, c, 0)),
            pl.BlockSpec(
                (plan.chips // chunks, share_rows(share), LANES),
                lambda s, c: (jnp.where(s == last, c, 0), 0, 0),
            ),
        ),
        out_shape=(
            jax.ShapeDtypeStruct((every, width), bf16),
            jax.ShapeDtypeStruct((every, plan.pairs * LANES), bf16),
            jax.ShapeDtypeStruct((plan.merge, rows, LANES), f32),
            jax.ShapeDtypeStruct((plan.chips, share_rows(share), LANES), bf16),
        ),
        scratch_shapes=[
            pltpu.VMEM((rest.shape[1], width), bf16),
            pltpu.VMEM((rows, LANES), f32),
        ],
        compiler_params=params(),
        cost_estimate=cost(
            2 * every * width * (2 * plan.pairs * LANES + rest.shape[1]), 6 * every * width
        ),
        name="project_updates",
    )(*decays, part, rest, w, *frames)


def scan_kernel(plan, u_ref, s_ref):
    share = s_ref.shape[1]
    size = min(share, N)
    items = share // size
    for i in range(items):
        at = slice(i * size, (i + 1) * size)
        state = jnp.zeros((size, LANES), f32)
        for j in range(plan.chips):
            s_ref[j, at, :] = state.astype(bf16)
            decay = jnp.zeros((1, LANES), f32)
            for n in range(3):
                row = share + n * items + i
                decay = decay + u_ref[j, row : row + 1, :].astype(f32)
            state = decay * state + u_ref[j, at, :].astype(f32)


def scan_states(plan, update, share):
    return pl.pallas_call(
        functools.partial(scan_kernel, plan),
        out_shape=jax.ShapeDtypeStruct((plan.chips, share, LANES), bf16),
        compiler_params=params(24),
        cost_estimate=cost(2 * update.size, 4 * update.size),
        name="scan_states",
    )(update)


def attend_kernel(plan, slot, *refs):
    lists_ref, refs = refs[0], refs[1:]
    decay_refs, refs = refs[: plan.merge], refs[plan.merge :]
    x_ref, v_ref, w_ref, u_ref, a_ref, c_ref, q_ref, k_ref = refs
    tokens = x_ref.shape[0]
    groups, chosen = lists_ref.shape
    block = tokens // groups
    step = 256
    per = step // block
    late = 2 * plan.pairs * LANES

    def project(c, _):
        at = pl.multiple_of(c * step, step)
        rows = pl.ds(at, step)
        every = jnp.dot(x_ref[rows, :], w_ref[:, late:], preferred_element_type=f32).astype(bf16)
        half = first_half((step, LANES))

        def head_norm(wide):
            square = wide * wide
            one = jnp.sum(jnp.where(half, square, 0.0), axis=-1, keepdims=True)
            two = jnp.sum(jnp.where(half, 0.0, square), axis=-1, keepdims=True)
            return wide * lax.rsqrt(jnp.where(half, one, two) * (1.0 / HD) + epsilon)

        for p in range(plan.pairs):
            cols = slice(p * LANES, (p + 1) * LANES)
            q, k, reader = (
                every[:, (3 * p + i) * LANES : (3 * p + i + 1) * LANES] for i in range(3)
            )
            c_ref[rows, cols] = reader
            k_ref[rows, cols] = head_norm(k.astype(f32)).astype(bf16)
            q = head_norm(q.astype(f32))
            one = jnp.where(half, q, 0.0).astype(bf16)
            two = jnp.where(half, 0.0, q).astype(bf16)
            for i in range(per):
                part = slice(i * block, (i + 1) * block)
                q_ref[p, c * per + i] = jnp.concatenate([one[part], two[part]], axis=0)
        return 0

    lax.fori_loop(0, tokens // step, project, 0)

    scale = math.log2(math.e) / math.sqrt(HD)
    for p in range(plan.pairs):
        cols = slice(p * LANES, (p + 1) * LANES)
        for g in range(groups):
            rows = slice(g * block, (g + 1) * block)
            starts = [pl.multiple_of(lists_ref[g, j] * block, block) for j in range(chosen)]
            keys = jnp.concatenate([k_ref[pl.ds(s, block), cols] for s in starts], axis=0)
            values = jnp.concatenate([v_ref[pl.ds(s, block), cols] for s in starts], axis=0)
            score = lax.dot_general(
                q_ref[p, g], keys, (((1,), (1,)), ((), ())), preferred_element_type=f32
            )
            e = jnp.exp2(score * scale)
            weight = (e * (1.0 / jnp.sum(e, axis=-1, keepdims=True))).astype(bf16)
            both = jnp.dot(weight, values, preferred_element_type=f32)
            attended = halves((block, LANES), both[:block], both[block:])
            items = slice((g * plan.pairs + p) * N, (g * plan.pairs + p + 1) * N)
            state = u_ref[slot, items, :]
            if plan.merge == 2:
                last = plan.last_decay(decay_refs, p, g)
                state = state + jnp.where(plan.core() == slot, 0.0, last) * u_ref[1 - slot, items, :]
            a_ref[rows, cols] = attended + read_out(c_ref[rows, cols], state, block)


def read_out(readers, state, block):
    half = first_half(state.shape)
    wide = jnp.concatenate([jnp.where(half, state, 0.0), jnp.where(half, 0.0, state)], axis=0)
    return jnp.dot(readers, wide.astype(bf16), preferred_element_type=f32) * (
        1.0 / (N * math.sqrt(block))
    )


def attend(plan, slot, lists, decays, x, v, w, updates):
    every, width = x.shape
    groups, chosen = lists.shape
    tokens = every // plan.merge
    block = tokens // groups
    cols = plan.pairs * LANES
    part = pl.BlockSpec((tokens, cols), lambda i: (0, 0))
    return pl.pallas_call(
        functools.partial(attend_kernel, plan, slot),
        grid=(1,),
        in_specs=[pl.BlockSpec(memory_space=pltpu.SMEM)] * (1 + plan.merge)
        + [
            pl.BlockSpec((tokens, width), lambda i: (slot, 0)),
            pl.BlockSpec((tokens, cols), lambda i: (slot, 0)),
            pl.BlockSpec(w.shape, lambda i: (0, 0)),
            pl.BlockSpec(updates.shape, lambda i: (0, 0, 0)),
        ],
        out_specs=(part, part),
        scratch_shapes=[
            pltpu.VMEM((plan.pairs, groups, 2 * block, LANES), bf16),
            pltpu.VMEM((tokens, cols), bf16),
        ],
        out_shape=(
            jax.ShapeDtypeStruct((tokens, cols), f32),
            jax.ShapeDtypeStruct((tokens, cols), bf16),
        ),
        compiler_params=params(),
        cost_estimate=cost(
            6 * tokens * width * 3 * cols,
            4 * (tokens * width + w.size + updates.size),
            2 * plan.pairs * tokens * chosen * block,
        ),
        name="attend",
    )(lists, *decays, x, v, w, updates)


def mix_kernel(plan, groups, *refs):
    decay_refs, refs = refs[: plan.merge], refs[plan.merge :]
    a_refs, refs = refs[: plan.merge], refs[plan.merge :]
    c_refs, refs = refs[: plan.merge], refs[plan.merge :]
    s_ref, back_ref, out_refs, mixed = refs[0], refs[1], refs[2:-1], refs[-1]
    tokens = back_ref.shape[0]
    block = tokens // groups
    first = plan.core() == 0
    for p in range(plan.pairs):
        cols = slice(p * LANES, (p + 1) * LANES)
        for g in range(groups):
            rows = slice(g * block, (g + 1) * block)
            at = (g * plan.pairs + p) * N
            readers = jnp.concatenate([c[rows, cols] for c in c_refs], axis=0)
            read = read_out(readers, s_ref[at : at + N, :].astype(f32), block)
            decays = [plan.decay(decay_refs, s, p, g) for s in range(plan.merge)]
            if plan.merge == 2:
                both = decays[0] * decays[1]
                decays = [jnp.where(first, decays[0], both), jnp.where(first, both, decays[1])]
            for s in range(plan.merge):
                mixed[s, rows, cols] = (
                    a_refs[s][rows, cols] + decays[s] * read[s * block : (s + 1) * block]
                ).astype(bf16)
    local = out_refs[0].shape[0]
    for s in range(plan.merge):
        for k in range(plan.peers):
            out_refs[s * plan.peers + k][...] = jnp.dot(
                back_ref[k * local : (k + 1) * local, :], mixed[s], preferred_element_type=f32
            ).astype(bf16)


def mix(plan, decays, attended, readers, state, back, groups):
    tokens = back.shape[0]
    width = attended[0].shape[1]
    out = jax.ShapeDtypeStruct((tokens // plan.peers, width), bf16)
    vmem = pl.BlockSpec(memory_space=pltpu.VMEM)
    return pl.pallas_call(
        functools.partial(mix_kernel, plan, groups),
        in_specs=[pl.BlockSpec(memory_space=pltpu.SMEM)] * plan.merge
        + [vmem] * (2 * plan.merge + 2),
        out_shape=(out,) * (plan.merge * plan.peers),
        scratch_shapes=[pltpu.VMEM((plan.merge, tokens, width), bf16)],
        compiler_params=params(24),
        cost_estimate=cost(4 * tokens * tokens * width, 2 * tokens * tokens + 16 * tokens * width),
        name="mix",
    )(*decays, *attended, *readers, state, back)


def out_kernel(plan, w_ref, *refs):
    part_refs, out_ref = refs[:-1], refs[-1]
    depth = part_refs[0].shape[1]
    core, me = plan.core(), lax.axis_index("head")
    total = None
    for s in range(plan.merge):
        for k in range(plan.peers):
            owner = lax.rem(me - k + plan.peers, plan.peers) * plan.merge
            owner = owner + (core if s == 0 else 1 - core)
            rows = pl.ds(pl.multiple_of(owner * depth, depth), depth)
            term = jnp.dot(
                part_refs[s * plan.peers + k][...], w_ref[rows, :], preferred_element_type=f32
            )
            total = term if total is None else total + term
    out_ref[...] = total.astype(bf16)


def project_out(plan, w, parts):
    local = parts[0].shape[0]
    width = w.shape[1]
    return pl.pallas_call(
        functools.partial(out_kernel, plan),
        out_shape=jax.ShapeDtypeStruct((local, width), bf16),
        compiler_params=params(24),
        cost_estimate=cost(2 * local * w.size, 2 * (w.size + 2 * local * width)),
        name="project_out",
    )(w, *parts)


def body(frames_in, in_weight, out_weight, block_ids, block_lists, decays):
    local_tokens = frames_in.shape[1]
    heads_here = decays.shape[1]
    groups = block_lists.shape[0]
    me = lax.axis_index("head")
    plan = Plan(lax.axis_size("tm"), lax.axis_size("head"), heads_here)

    weights = [in_weight] + [plan.swap(in_weight)] * (plan.merge - 1)
    w = lax.all_gather(
        reorder(plan, weights), "tm", axis=0, tiled=True, axis_index_groups=plan.groups()
    )
    rates = [decays[0]] + [plan.swap(decays[0])] * (plan.merge - 1)

    own = frames_in[0]
    chunks = 2 if local_tokens >= 512 else 1
    arriving = [
        plan.to_peer(chunk, plan.peers - k, False)
        for k in range(1, plan.peers)
        for chunk in jnp.split(own, chunks)
    ]
    owns = [own]
    if plan.merge == 2:
        owns.append(plan.swap(own))
        arriving = arriving + [plan.swap(chunk) for chunk in arriving]

    ids = jnp.roll(block_ids, -me * local_tokens)
    part, rest, back = order(plan, ids, owns, groups)
    x, v, updates, total = project_updates(plan, rates, part, rest, arriving, w, groups)

    def exchange(blocks):
        return lax.all_to_all(
            blocks, "tm", split_axis=0, concat_axis=0, tiled=True,
            axis_index_groups=plan.groups(),
        )

    share = updates.shape[1] // plan.chips
    arrived = exchange(total)
    attended = [attend(plan, 0, block_lists, rates, x, v, w, updates)]
    arrived, attended = lax.optimization_barrier((arrived, attended))
    states = scan_states(plan, arrived, share)
    if plan.merge == 2:
        x, states = lax.optimization_barrier((x, states))
        attended.append(attend(plan, 1, block_lists, rates, x, v, w, updates))
    state = exchange(states).reshape(-1, LANES)

    bases, readers = ([a[i] for a in attended] for i in range(2))
    mixed = mix(plan, rates, bases, readers, state, back, groups)
    features = [
        mixed[0] if s == 0 and k == 0 else plan.to_peer(mixed[s * plan.peers + k], k, s == 1)
        for s in range(plan.merge)
        for k in range(plan.peers)
    ]
    return project_out(plan, out_weight, features)[None]


def solution(mesh):
    return jax.shard_map(
        body,
        mesh=mesh,
        in_specs=(P("tm", "head", None), P("tm", "head"), P(), P(), P(), P("tm", "head", None)),
        out_specs=P("tm", "head", None),
        check_vma=False,
    )
```

```python
import functools
import math

import jax
import jax.numpy as jnp
from jax import lax
from jax.experimental import pallas as pl
from jax.experimental.pallas import tpu as pltpu
from jax.sharding import PartitionSpec as P

HD = 64
N = 64
LANES = 2 * HD
PIECES = 5
EARLY = (2, 3)
LATE = (0, 1, 4)

epsilon = 1e-06

f32 = jnp.float32
bf16 = jnp.bfloat16


def params(mib=60):
    return pltpu.CompilerParams(vmem_limit_bytes=mib << 20)


def cost(flops, nbytes, transcendentals=0):
    return pl.CostEstimate(
        flops=int(flops), bytes_accessed=int(nbytes), transcendentals=int(transcendentals)
    )


def first_half(shape):
    return lax.broadcasted_iota(jnp.int32, shape, len(shape) - 1) < HD


class Plan:
    def __init__(self, frames, peers, heads_here):
        self.merge = 2 if frames % 2 == 0 and heads_here % 4 == 0 else 1
        self.frames, self.peers = frames, peers
        self.heads = heads_here // self.merge
        self.pairs = self.heads // 2
        self.chips = frames // self.merge
        self.across = 2 if self.chips % 2 == 0 else 1
        self.along = self.chips // self.across
        self.ringed = self.across == 2 and self.along <= 8

    def core(self):
        return lax.rem(lax.axis_index("tm"), self.merge)

    def chip(self):
        return lax.div(lax.axis_index("tm"), self.merge)

    def swap(self, block):
        return lax.ppermute(block, "tm", [(t, t ^ 1) for t in range(self.frames)])

    def round(self, block):
        a, b, c = self.along, self.across, self.merge
        pairs = [(t, (t + b * c) % (a * b * c)) for t in range(self.frames)]
        return lax.ppermute(block, "tm", pairs)

    def cross(self, block):
        c = self.merge
        pairs = [(t, (t // c ^ 1) * c + t % c) for t in range(self.frames)]
        return lax.ppermute(block, "tm", pairs)

    def assemble(self, refs, out, cols):
        rows = refs[0].shape[0]
        if len(refs) == 1:
            out[...] = refs[0][:, cols]
            return
        a, b = lax.div(self.chip(), self.across), lax.rem(self.chip(), self.across)
        for i, ref in enumerate(refs):
            k, flip = i // 2, i % 2
            there = lax.rem(a - k + self.along, self.along) * self.across
            at = (there + (1 - b if flip else b)) * rows
            out[pl.ds(pl.multiple_of(at, rows), rows), :] = ref[:, cols]

    def to_peer(self, block, k, other):
        if not other:
            pairs = [(j, (j + k) % self.peers) for j in range(self.peers)]
            return lax.ppermute(block, "head", pairs)
        if k == 0:
            return self.swap(block)
        pairs = [
            (t * self.peers + j, (t ^ 1) * self.peers + (j + k) % self.peers)
            for t in range(self.frames)
            for j in range(self.peers)
        ]
        return lax.ppermute(block, ("tm", "head"), pairs)

    def groups(self):
        if self.merge == 1:
            return None
        return [[j * self.merge + c for j in range(self.chips)] for c in range(self.merge)]

    def decay(self, refs, slot, pair, g):
        head = self.core() * self.heads + 2 * pair
        return halves((1, LANES), refs[slot][head, g], refs[slot][head + 1, g])

    def last_decay(self, refs, pair, g):
        if self.merge == 1:
            return self.decay(refs, 0, pair, g)
        one, two = (self.decay(refs, slot, pair, g) for slot in range(2))
        return jnp.where(self.core() == 0, two, one)


def halves(shape, one, two):
    return jnp.where(first_half(shape), one, two)


def reorder_kernel(plan, *refs):
    w_refs, out_ref = refs[:-1], refs[-1]
    rows = w_refs[0].shape[0]
    width = plan.heads * PIECES * HD
    first = plan.core() == 0

    def chosen(ref, at):
        one = ref[:, at : at + HD]
        if plan.merge == 1:
            return one
        return jnp.where(first, one, ref[:, width + at : width + at + HD])

    to = 0
    for kinds in (EARLY, LATE):
        for p in range(plan.pairs):
            for i in kinds:
                blocks = []
                for ref in w_refs:
                    one, two = (chosen(ref, ((2 * p + h) * PIECES + i) * HD) for h in range(2))
                    blocks.append(jnp.concatenate([one, two], axis=1))
                for s, block in enumerate(blocks):
                    if plan.merge == 2:
                        block = jnp.where(first, block, blocks[1 - s])
                    out_ref[s * rows : (s + 1) * rows, to : to + LANES] = block
                to += LANES


def reorder(plan, weights):
    rows = weights[0].shape[0]
    return pl.pallas_call(
        functools.partial(reorder_kernel, plan),
        out_shape=jax.ShapeDtypeStruct((plan.merge * rows, plan.heads * PIECES * HD), bf16),
        compiler_params=params(),
        cost_estimate=cost(0, 4 * weights[0].size),
        name="reorder",
    )(*weights)


def normalise(part, out, at):
    step = min(128, part.shape[0])

    def norm(c, _):
        start = pl.multiple_of(c * step, step)
        wide = part[pl.ds(start, step), :].astype(f32)
        scale = lax.rsqrt(jnp.mean(wide * wide, axis=-1, keepdims=True) + epsilon)
        out[pl.ds(at + start, step), :] = (wide * scale).astype(bf16)
        return 0

    lax.fori_loop(0, part.shape[0] // step, norm, 0)


def pick_kernel(groups, ids_ref, own_ref, rest_ref):
    tokens = ids_ref.shape[1]
    local = own_ref.shape[1]
    block = tokens // groups
    step = 128
    label = lax.broadcasted_iota(jnp.int32, (groups, tokens), 0)
    held = label == ids_ref[...]
    held_bf = jnp.where(held, 1.0, 0.0).astype(bf16)
    counts = []
    for c in range(tokens // 256):
        before = lax.broadcasted_iota(jnp.int32, (tokens, 256), 0) < (
            lax.broadcasted_iota(jnp.int32, (tokens, 256), 1) + c * 256
        )
        counts.append(
            jnp.dot(held_bf, jnp.where(before, 1.0, 0.0).astype(bf16), preferred_element_type=f32)
        )
    count = jnp.concatenate(counts, axis=1)
    rank = jnp.sum(
        jnp.where(held, count + (label * block).astype(f32), 0.0), axis=0, keepdims=True
    ).astype(jnp.int32)

    def place(c, _):
        at = pl.multiple_of(c * step, step)
        pick = (lax.broadcasted_iota(jnp.int32, (step, tokens), 0) + at) == rank
        pick = jnp.where(pick, 1.0, 0.0).astype(bf16)
        own_ref[pl.ds(at, step), :] = pick[:, :local]
        rest_ref[pl.ds(at, step), :] = pick[:, local:]
        return 0

    lax.fori_loop(0, tokens // step, place, 0)


def pick_tokens(ids, local, groups):
    tokens = ids.shape[0]
    return pl.pallas_call(
        functools.partial(pick_kernel, groups),
        out_shape=(
            jax.ShapeDtypeStruct((tokens, local), bf16),
            jax.ShapeDtypeStruct((tokens, tokens - local), bf16),
        ),
        compiler_params=params(),
        cost_estimate=cost(32 * tokens * tokens, 2 * tokens * tokens),
        name="pick_tokens",
    )(ids.reshape(1, tokens))


def back_kernel(groups, ids_ref, back_ref):
    tokens = back_ref.shape[0]
    block = tokens // groups
    step = 128
    lane = lax.broadcasted_iota(jnp.int32, (tokens, 128), 1)
    held = jnp.where(lane == ids_ref[...], 1.0, 0.0).astype(bf16)

    def place(c, _):
        at = pl.multiple_of(c * step, step)
        before = lax.broadcasted_iota(jnp.int32, (step, tokens), 1) < (
            lax.broadcasted_iota(jnp.int32, (step, tokens), 0) + at
        )
        count = jnp.dot(
            jnp.where(before, 1.0, 0.0).astype(bf16), held, preferred_element_type=f32
        )
        lane = lax.broadcasted_iota(jnp.int32, (step, 128), 1)
        mine = lane == ids_ref[pl.ds(at, step), :]
        rank = jnp.sum(
            jnp.where(mine, count + (lane * block).astype(f32), 0.0), axis=1, keepdims=True
        ).astype(jnp.int32)
        pick = lax.broadcasted_iota(jnp.int32, (step, tokens), 1) == rank
        back_ref[pl.ds(at, step), :] = jnp.where(pick, 1.0, 0.0).astype(bf16)
        return 0

    lax.fori_loop(0, tokens // step, place, 0)


def back_tokens(ids, groups):
    tokens = ids.shape[0]
    return pl.pallas_call(
        functools.partial(back_kernel, groups),
        out_shape=jax.ShapeDtypeStruct((tokens, tokens), bf16),
        compiler_params=params(),
        cost_estimate=cost(256 * tokens * tokens, 2 * tokens * tokens),
        name="back_tokens",
    )(ids.reshape(tokens, 1))


def place_kernel(merge, parts, *refs):
    pick_ref, refs = refs[0], refs[1:]
    frame_refs, refs = refs[: merge * parts], refs[merge * parts :]
    base_refs, (x_ref, normed) = refs[:-2], refs[-2:]
    slot, chunk = pl.program_id(0), pl.program_id(1)
    for s in range(merge):

        @pl.when((slot == s) & (chunk == 0))
        def _(s=s):
            at = 0
            for ref in frame_refs[s * parts : (s + 1) * parts]:
                normalise(ref, normed, at)
                at += ref.shape[0]

    placed = jnp.dot(pick_ref[...], normed[...], preferred_element_type=f32).astype(bf16)
    for base in base_refs:
        placed = base[...] + placed
    x_ref[...] = placed


def place_tokens(plan, pick, frames, base):
    tokens, count = pick.shape
    width = frames[0].shape[1]
    chunks = 4
    step = tokens // chunks
    rows = pl.BlockSpec((step, width), lambda s, c: (s * chunks + c, 0))
    return pl.pallas_call(
        functools.partial(place_kernel, plan.merge, len(frames) // plan.merge),
        grid=(plan.merge, chunks),
        in_specs=[pl.BlockSpec((step, count), lambda s, c: (c, 0))]
        + [pl.BlockSpec(f.shape, lambda s, c: (0, 0)) for f in frames]
        + [rows] * len(base),
        out_specs=rows,
        out_shape=jax.ShapeDtypeStruct((plan.merge * tokens, width), bf16),
        scratch_shapes=[pltpu.VMEM((count, width), bf16)],
        compiler_params=params(),
        cost_estimate=cost(4 * plan.merge * tokens * count * width, 6 * tokens * width),
        name="place_tokens",
    )(pick, *frames, *base)


def update_kernel(plan, groups, *refs):
    decay_refs, refs = refs[: plan.merge], refs[plan.merge :]
    x_ref, w_refs = refs[0], refs[1:-5]
    v_ref, u_ref, total_ref, w_scr, kept = refs[-5:]
    step = x_ref.shape[0]
    block = kept.shape[0] // (groups * plan.pairs)
    here = step // block
    slot, chunk = pl.program_id(0), pl.program_id(1)

    @pl.when((slot == 0) & (chunk == 0))
    def _():
        plan.assemble(w_refs, w_scr, slice(0, w_scr.shape[1]))

    both = jnp.dot(x_ref[...], w_scr[...], preferred_element_type=f32).astype(bf16)
    for p in range(plan.pairs):
        v = both[:, 2 * p * LANES : (2 * p + 1) * LANES]
        b = both[:, (2 * p + 1) * LANES : (2 * p + 2) * LANES]
        v_ref[:, p * LANES : (p + 1) * LANES] = v
        for i in range(0, here, 2):
            rows = slice(i * block, (i + 2) * block)
            turned = b[rows].astype(f32).T
            half = lax.broadcasted_iota(jnp.int32, turned.shape, 1) < block
            wide = jnp.concatenate(
                [jnp.where(half, turned, 0.0), jnp.where(half, 0.0, turned)], axis=0
            ).astype(bf16)
            outer = jnp.dot(wide, v[rows], preferred_element_type=f32)
            for n in range(2):
                m = outer[n * 2 * N : (n + 1) * 2 * N]
                at = ((i + n) * plan.pairs + p) * N
                u_ref[0, at : at + N, :] = halves((N, LANES), m[:N], m[N:])

    many = u_ref.shape[1]
    there = pl.ds(pl.multiple_of(chunk * many, many), many)
    if plan.merge == 2:

        @pl.when(slot == 0)
        def _():
            kept[there, :] = u_ref[0]

    @pl.when(slot == plan.merge - 1)
    def _():
        peers = total_ref.shape[0]
        share = many // peers
        items = max(1, share // N)
        first = plan.core() == 0
        for d in range(peers):
            for i in range(items):
                row = d * share + i * N
                size = min(N, share)
                item = row // N
                p, g = item % plan.pairs, chunk * here + item // plan.pairs
                last = plan.last_decay(decay_refs, p, g)
                total = u_ref[0, row : row + size, :]
                product = last
                if plan.merge == 2:
                    before = kept[pl.ds(chunk * many + row, size), :]
                    total = jnp.where(first, last, 1.0) * before + jnp.where(first, 1.0, last) * total
                    product = plan.decay(decay_refs, 0, p, g) * plan.decay(decay_refs, 1, p, g)
                total_ref[d, i * size : (i + 1) * size, :] = total.astype(bf16)
                for n in range(3):
                    piece = product.astype(bf16)
                    at = share + n * items + i
                    total_ref[d, at : at + 1, :] = piece
                    product = product - piece.astype(f32)


def share_rows(share):
    return share + 16 * -(-3 * max(1, share // N) // 16)


def project_updates(plan, decays, x, weights, groups):
    every, width = x.shape
    tokens = every // plan.merge
    chunks = 4
    step = tokens // chunks
    cols = plan.pairs * LANES
    rows = plan.pairs * groups * N
    share = rows // plan.chips
    last = plan.merge - 1
    return pl.pallas_call(
        functools.partial(update_kernel, plan, groups),
        grid=(plan.merge, chunks),
        in_specs=[pl.BlockSpec(memory_space=pltpu.SMEM)] * plan.merge
        + [pl.BlockSpec((step, width), lambda s, c: (s * chunks + c, 0))]
        + [pl.BlockSpec((w.shape[0], 2 * cols), lambda s, c: (0, 0)) for w in weights],
        out_specs=(
            pl.BlockSpec((step, cols), lambda s, c: (s * chunks + c, 0)),
            pl.BlockSpec((1, rows // chunks, LANES), lambda s, c: (s, c, 0)),
            pl.BlockSpec(
                (plan.chips // chunks, share_rows(share), LANES),
                lambda s, c: (jnp.where(s == last, c, 0), 0, 0),
            ),
        ),
        out_shape=(
            jax.ShapeDtypeStruct((every, cols), bf16),
            jax.ShapeDtypeStruct((plan.merge, rows, LANES), f32),
            jax.ShapeDtypeStruct((plan.chips, share_rows(share), LANES), bf16),
        ),
        scratch_shapes=[pltpu.VMEM((width, 2 * cols), bf16), pltpu.VMEM((rows, LANES), f32)],
        compiler_params=params(),
        cost_estimate=cost(4 * every * width * 2 * cols, 4 * every * width),
        name="project_updates",
    )(*decays, x, *weights)


def scan_kernel(plan, u_ref, s_ref):
    share = s_ref.shape[1]
    size = min(share, N)
    items = share // size
    for i in range(items):
        at = slice(i * size, (i + 1) * size)
        state = jnp.zeros((size, LANES), f32)
        for j in range(plan.chips):
            s_ref[j, at, :] = state.astype(bf16)
            decay = jnp.zeros((1, LANES), f32)
            for n in range(3):
                row = share + n * items + i
                decay = decay + u_ref[j, row : row + 1, :].astype(f32)
            state = decay * state + u_ref[j, at, :].astype(f32)


def scan_states(plan, update, share):
    return pl.pallas_call(
        functools.partial(scan_kernel, plan),
        out_shape=jax.ShapeDtypeStruct((plan.chips, share, LANES), bf16),
        compiler_params=params(24),
        cost_estimate=cost(2 * update.size, 4 * update.size),
        name="scan_states",
    )(update)


def attend_kernel(plan, slot, chunks, *refs):
    lists_ref, refs = refs[0], refs[1:]
    decay_refs, refs = refs[: plan.merge], refs[plan.merge :]
    x_ref, v_ref, u_ref, w_refs = refs[0], refs[1], refs[2], refs[3:-6]
    a_ref, c_out_ref, w_scr, q_ref, k_ref, c_ref = refs[-6:]
    tokens = v_ref.shape[0]
    groups, chosen = lists_ref.shape
    block = tokens // groups
    step = x_ref.shape[0]
    per = step // block
    early = 2 * plan.pairs * LANES
    i = pl.program_id(0)

    @pl.when(i == 0)
    def _():
        plan.assemble(w_refs, w_scr, slice(early, early + w_scr.shape[1]))

    @pl.when(i < chunks)
    def _():
        rows = pl.ds(pl.multiple_of(i * step, step), step)
        every = jnp.dot(x_ref[...], w_scr[...], preferred_element_type=f32).astype(bf16)
        half = first_half((step, LANES))

        def head_norm(wide):
            square = wide * wide
            one = jnp.sum(jnp.where(half, square, 0.0), axis=-1, keepdims=True)
            two = jnp.sum(jnp.where(half, 0.0, square), axis=-1, keepdims=True)
            return wide * lax.rsqrt(jnp.where(half, one, two) * (1.0 / HD) + epsilon)

        for p in range(plan.pairs):
            cols = slice(p * LANES, (p + 1) * LANES)
            q, k, reader = (
                every[:, (3 * p + j) * LANES : (3 * p + j + 1) * LANES] for j in range(3)
            )
            c_ref[rows, cols] = reader
            c_out_ref[:, cols] = reader
            k_ref[rows, cols] = head_norm(k.astype(f32)).astype(bf16)
            q = head_norm(q.astype(f32))
            one = jnp.where(half, q, 0.0).astype(bf16)
            two = jnp.where(half, 0.0, q).astype(bf16)
            for j in range(per):
                part = slice(j * block, (j + 1) * block)
                q_ref[p, i * per + j] = jnp.concatenate([one[part], two[part]], axis=0)

    scale = math.log2(math.e) / math.sqrt(HD)

    @pl.when(i >= chunks)
    def _():
        for n in range(per):
            g = (i - chunks) * per + n
            starts = [pl.multiple_of(lists_ref[g, j] * block, block) for j in range(chosen)]
            for p in range(plan.pairs):
                cols = slice(p * LANES, (p + 1) * LANES)
                keys = jnp.concatenate([k_ref[pl.ds(s, block), cols] for s in starts], axis=0)
                values = jnp.concatenate([v_ref[pl.ds(s, block), cols] for s in starts], axis=0)
                score = lax.dot_general(
                    q_ref[p, g], keys, (((1,), (1,)), ((), ())), preferred_element_type=f32
                )
                e = jnp.exp2(score * scale)
                weight = (e * (1.0 / jnp.sum(e, axis=-1, keepdims=True))).astype(bf16)
                both = jnp.dot(weight, values, preferred_element_type=f32)
                attended = halves((block, LANES), both[:block], both[block:])
                items = slice((n * plan.pairs + p) * N, (n * plan.pairs + p + 1) * N)
                state = u_ref[slot, items, :]
                if plan.merge == 2:
                    last = plan.last_decay(decay_refs, p, g)
                    last = jnp.where(plan.core() == slot, 0.0, last)
                    state = state + last * u_ref[1 - slot, items, :]
                readers = c_ref[pl.ds(pl.multiple_of(g * block, block), block), cols]
                a_ref[n * block : (n + 1) * block, cols] = attended + read_out(
                    readers, state, block
                )


def attend(plan, slot, lists, decays, x, v, weights, updates):
    every, width = x.shape
    groups, chosen = lists.shape
    tokens = every // plan.merge
    block = tokens // groups
    cols = plan.pairs * LANES
    chunks = 4
    step = tokens // chunks
    first = lambda i: jnp.minimum(i, chunks - 1)
    then = lambda i: jnp.maximum(i - chunks, 0)
    return pl.pallas_call(
        functools.partial(attend_kernel, plan, slot, chunks),
        grid=(2 * chunks,),
        in_specs=[pl.BlockSpec(memory_space=pltpu.SMEM)] * (1 + plan.merge)
        + [
            pl.BlockSpec((step, width), lambda i: (slot * chunks + first(i), 0)),
            pl.BlockSpec((tokens, cols), lambda i: (slot, 0)),
            pl.BlockSpec(
                (plan.merge, updates.shape[1] // chunks, LANES), lambda i: (0, then(i), 0)
            ),
        ]
        + [pl.BlockSpec(w.shape, lambda i: (0, 0)) for w in weights],
        out_specs=(
            pl.BlockSpec((step, cols), lambda i: (then(i), 0)),
            pl.BlockSpec((step, cols), lambda i: (first(i), 0)),
        ),
        scratch_shapes=[
            pltpu.VMEM((width, 3 * cols), bf16),
            pltpu.VMEM((plan.pairs, groups, 2 * block, LANES), bf16),
            pltpu.VMEM((tokens, cols), bf16),
            pltpu.VMEM((tokens, cols), bf16),
        ],
        out_shape=(
            jax.ShapeDtypeStruct((tokens, cols), f32),
            jax.ShapeDtypeStruct((tokens, cols), bf16),
        ),
        compiler_params=params(),
        cost_estimate=cost(
            6 * tokens * width * 3 * cols,
            4 * (tokens * width + 5 * width * cols + updates.size),
            2 * plan.pairs * tokens * chosen * block,
        ),
        name="attend",
    )(lists, *decays, x, v, updates, *weights)


def read_out(readers, state, block):
    half = first_half(state.shape)
    wide = jnp.concatenate([jnp.where(half, state, 0.0), jnp.where(half, 0.0, state)], axis=0)
    return jnp.dot(readers, wide.astype(bf16), preferred_element_type=f32) * (
        1.0 / (N * math.sqrt(block))
    )


def mix_kernel(plan, chunks, per, *refs):
    decay_refs, refs = refs[: plan.merge], refs[plan.merge :]
    a_refs, refs = refs[: plan.merge], refs[plan.merge :]
    c_refs, refs = refs[: plan.merge], refs[plan.merge :]
    s_ref, back_ref, out_refs, mixed = refs[0], refs[1], refs[2:-1], refs[-1]
    step, cols_here = a_refs[0].shape
    here = s_ref.shape[0] // (plan.pairs * N)
    block = step // here
    first = plan.core() == 0
    i = pl.program_id(0)

    @pl.when(i < chunks)
    def _():
        for n in range(here):
            g = i * here + n
            rows = slice(n * block, (n + 1) * block)
            to = pl.ds(pl.multiple_of(i * step + n * block, block), block)
            for p in range(plan.pairs):
                cols = slice(p * LANES, (p + 1) * LANES)
                at = (n * plan.pairs + p) * N
                readers = jnp.concatenate([c[rows, cols] for c in c_refs], axis=0)
                read = read_out(readers, s_ref[at : at + N, :].astype(f32), block)
                decays = [plan.decay(decay_refs, s, p, g) for s in range(plan.merge)]
                if plan.merge == 2:
                    both = decays[0] * decays[1]
                    decays = [jnp.where(first, decays[0], both), jnp.where(first, both, decays[1])]
                for s in range(plan.merge):
                    there = slice(s * cols_here + p * LANES, s * cols_here + (p + 1) * LANES)
                    mixed[to, there] = (
                        a_refs[s][rows, cols] + decays[s] * read[s * block : (s + 1) * block]
                    ).astype(bf16)

    @pl.when(i >= chunks)
    def _():
        placed = jnp.dot(back_ref[...], mixed[...], preferred_element_type=f32).astype(bf16)
        for k in range(plan.peers):

            @pl.when(lax.div(i - chunks, per) == k)
            def _(k=k):
                for s in range(plan.merge):
                    out_refs[s * plan.peers + k][...] = placed[
                        :, s * cols_here : (s + 1) * cols_here
                    ]


def mix(plan, decays, attended, readers, state, back):
    tokens = back.shape[0]
    width = attended[0].shape[1]
    local = tokens // plan.peers
    chunks = 4
    step = tokens // chunks
    size = min(256, local)
    per = local // size
    first = lambda i: (jnp.minimum(i, chunks - 1), 0)
    return pl.pallas_call(
        functools.partial(mix_kernel, plan, chunks, per),
        grid=(chunks + tokens // size,),
        in_specs=[pl.BlockSpec(memory_space=pltpu.SMEM)] * plan.merge
        + [pl.BlockSpec((step, width), first)] * (2 * plan.merge)
        + [
            pl.BlockSpec((state.shape[0] // chunks, LANES), first),
            pl.BlockSpec((size, tokens), lambda i: (jnp.maximum(i - chunks, 0), 0)),
        ],
        out_specs=tuple(
            pl.BlockSpec(
                (size, width), lambda i, k=k: (jnp.clip(i - chunks - k * per, 0, per - 1), 0)
            )
            for s in range(plan.merge)
            for k in range(plan.peers)
        ),
        out_shape=(jax.ShapeDtypeStruct((local, width), bf16),) * (plan.merge * plan.peers),
        scratch_shapes=[pltpu.VMEM((tokens, plan.merge * width), bf16)],
        compiler_params=params(),
        cost_estimate=cost(4 * tokens * tokens * width, 2 * tokens * tokens + 16 * tokens * width),
        name="mix",
    )(*decays, *attended, *readers, state, back)


def out_kernel(plan, w_ref, *refs):
    part_refs, out_ref = refs[:-1], refs[-1]
    depth = part_refs[0].shape[1]
    core, me = plan.core(), lax.axis_index("head")
    total = None
    for s in range(plan.merge):
        for k in range(plan.peers):
            owner = lax.rem(me - k + plan.peers, plan.peers) * plan.merge
            owner = owner + (core if s == 0 else 1 - core)
            rows = pl.ds(pl.multiple_of(owner * depth, depth), depth)
            term = jnp.dot(
                part_refs[s * plan.peers + k][...], w_ref[rows, :], preferred_element_type=f32
            )
            total = term if total is None else total + term
    out_ref[...] = total.astype(bf16)


def project_out(plan, w, parts):
    local = parts[0].shape[0]
    width = w.shape[1]
    return pl.pallas_call(
        functools.partial(out_kernel, plan),
        out_shape=jax.ShapeDtypeStruct((local, width), bf16),
        compiler_params=params(24),
        cost_estimate=cost(2 * local * w.size, 2 * (w.size + 2 * local * width)),
        name="project_out",
    )(w, *parts)


def body(frames_in, in_weight, out_weight, block_ids, block_lists, decays):
    local_tokens = frames_in.shape[1]
    heads_here = decays.shape[1]
    groups = block_lists.shape[0]
    me = lax.axis_index("head")
    plan = Plan(lax.axis_size("tm"), lax.axis_size("head"), heads_here)

    own = frames_in[0]
    chunks = 2 if local_tokens >= 512 else 1
    arriving = [
        plan.to_peer(chunk, plan.peers - k, False)
        for k in range(1, plan.peers)
        for chunk in jnp.split(own, chunks)
    ]
    owns = [own] + [plan.swap(own)] * (plan.merge - 1)
    rates = [decays[0]] + [plan.swap(decays[0])] * (plan.merge - 1)
    block = reorder(plan, [in_weight] + [plan.swap(in_weight)] * (plan.merge - 1))

    ids = jnp.roll(block_ids, -me * local_tokens)
    pick, rest = pick_tokens(ids, local_tokens, groups)
    part = place_tokens(plan, pick, owns, [])
    back = back_tokens(ids, groups)
    if plan.ringed:
        weights, beside = [], [pick, part, back]
        for k in range(plan.along):
            crossed = plan.cross(block)
            weights += [block, crossed]
            if k < plan.along - 1:
                block = plan.round(block)
                block, crossed, beside[:1] = lax.optimization_barrier((block, crossed, beside[:1]))
                weights[-1] = crossed
                beside = beside[1:]
                n = k - (plan.along - 1 - len(arriving))
                if 0 <= n < len(arriving):
                    arriving[n], block = lax.optimization_barrier((arriving[n], block))
    else:
        weights = [
            lax.all_gather(block, "tm", axis=0, tiled=True, axis_index_groups=plan.groups())
        ]
    if plan.merge == 2:
        arriving = arriving + [plan.swap(chunk) for chunk in arriving]
    x = place_tokens(plan, rest, arriving, [part])
    v, updates, total = project_updates(plan, rates, x, weights, groups)

    def exchange(blocks):
        return lax.all_to_all(
            blocks, "tm", split_axis=0, concat_axis=0, tiled=True,
            axis_index_groups=plan.groups(),
        )

    share = updates.shape[1] // plan.chips
    arrived = exchange(total)
    attended = [attend(plan, 0, block_lists, rates, x, v, weights, updates)]
    arrived, attended = lax.optimization_barrier((arrived, attended))
    states = scan_states(plan, arrived, share)
    if plan.merge == 2:
        x, states = lax.optimization_barrier((x, states))
        attended.append(attend(plan, 1, block_lists, rates, x, v, weights, updates))
    state = exchange(states).reshape(-1, LANES)

    bases, readers = ([a[i] for a in attended] for i in range(2))
    mixed = mix(plan, rates, bases, readers, state, back)
    features = [
        mixed[0] if s == 0 and k == 0 else plan.to_peer(mixed[s * plan.peers + k], k, s == 1)
        for s in range(plan.merge)
        for k in range(plan.peers)
    ]
    return project_out(plan, out_weight, features)[None]


def solution(mesh):
    return jax.shard_map(
        body,
        mesh=mesh,
        in_specs=(P("tm", "head", None), P("tm", "head"), P(), P(), P(), P("tm", "head", None)),
        out_specs=P("tm", "head", None),
        check_vma=False,
    )
```

```python
import functools
import math

import jax
import jax.numpy as jnp
from jax import lax
from jax.experimental import pallas as pl
from jax.experimental.pallas import tpu as pltpu
from jax.sharding import PartitionSpec as P

HD = 64
N = 64
LANES = 2 * HD
PIECES = 5
EARLY = (2, 3)
LATE = (0, 1, 4)

epsilon = 1e-06

f32 = jnp.float32
bf16 = jnp.bfloat16


def params(mib=60):
    return pltpu.CompilerParams(vmem_limit_bytes=mib << 20)


def cost(flops, nbytes, transcendentals=0):
    return pl.CostEstimate(
        flops=int(flops), bytes_accessed=int(nbytes), transcendentals=int(transcendentals)
    )


def first_half(shape):
    return lax.broadcasted_iota(jnp.int32, shape, len(shape) - 1) < HD


class Plan:
    def __init__(self, frames, peers, heads_here):
        self.merge = 2 if frames % 2 == 0 and heads_here % 4 == 0 else 1
        self.frames, self.peers = frames, peers
        self.heads = heads_here // self.merge
        self.pairs = self.heads // 2
        self.chips = frames // self.merge
        self.across = 2 if self.chips % 2 == 0 else 1
        self.along = self.chips // self.across
        self.ringed = self.across == 2 and self.along <= 8

    def core(self):
        return lax.rem(lax.axis_index("tm"), self.merge)

    def chip(self):
        return lax.div(lax.axis_index("tm"), self.merge)

    def swap(self, block):
        return lax.ppermute(block, "tm", [(t, t ^ 1) for t in range(self.frames)])

    def round(self, block):
        a, b, c = self.along, self.across, self.merge
        pairs = [(t, (t + b * c) % (a * b * c)) for t in range(self.frames)]
        return lax.ppermute(block, "tm", pairs)

    def cross(self, block):
        c = self.merge
        pairs = [(t, (t // c ^ 1) * c + t % c) for t in range(self.frames)]
        return lax.ppermute(block, "tm", pairs)

    def gather(self, copies, refs, out, cols):
        if len(refs) == 1:
            return [copies.start(refs[0].at[:, cols], out)]
        rows = refs[0].shape[0]
        a, b = lax.div(self.chip(), self.across), lax.rem(self.chip(), self.across)
        made = []
        for i, ref in enumerate(refs):
            k, flip = i // 2, i % 2
            there = lax.rem(a - k + self.along, self.along) * self.across
            at = pl.multiple_of((there + (1 - b if flip else b)) * rows, rows)
            made.append(copies.start(ref.at[:, cols], out.at[pl.ds(at, rows), :]))
        return made

    def to_peer(self, block, k, other):
        if not other:
            pairs = [(j, (j + k) % self.peers) for j in range(self.peers)]
            return lax.ppermute(block, "head", pairs)
        if k == 0:
            return self.swap(block)
        pairs = [
            (t * self.peers + j, (t ^ 1) * self.peers + (j + k) % self.peers)
            for t in range(self.frames)
            for j in range(self.peers)
        ]
        return lax.ppermute(block, ("tm", "head"), pairs)

    def groups(self):
        if self.merge == 1:
            return None
        return [[j * self.merge + c for j in range(self.chips)] for c in range(self.merge)]

    def decay(self, refs, slot, pair, g):
        head = self.core() * self.heads + 2 * pair
        return halves((1, LANES), refs[slot][head, g], refs[slot][head + 1, g])

    def last_decay(self, refs, pair, g):
        if self.merge == 1:
            return self.decay(refs, 0, pair, g)
        one, two = (self.decay(refs, slot, pair, g) for slot in range(2))
        return jnp.where(self.core() == 0, two, one)


class Copies:
    room = 48

    def __init__(self, sems):
        self.sems, self.made = sems, []

    def start(self, src, dst):
        copy = pltpu.make_async_copy(src, dst, self.sems.at[len(self.made)])
        copy.start()
        self.made.append(copy)
        return copy

    @staticmethod
    def scratch():
        return pltpu.SemaphoreType.DMA((Copies.room,))


def finish(copies):
    for copy in copies:
        copy.wait()


def halves(shape, one, two):
    return jnp.where(first_half(shape), one, two)


def reorder_kernel(plan, *refs):
    w_refs, out_ref = refs[:-1], refs[-1]
    rows = w_refs[0].shape[0]
    width = plan.heads * PIECES * HD
    first = plan.core() == 0

    def chosen(ref, at):
        one = ref[:, at : at + HD]
        if plan.merge == 1:
            return one
        return jnp.where(first, one, ref[:, width + at : width + at + HD])

    to = 0
    for kinds in (EARLY, LATE):
        for p in range(plan.pairs):
            for i in kinds:
                blocks = []
                for ref in w_refs:
                    one, two = (chosen(ref, ((2 * p + h) * PIECES + i) * HD) for h in range(2))
                    blocks.append(jnp.concatenate([one, two], axis=1))
                for s, block in enumerate(blocks):
                    if plan.merge == 2:
                        block = jnp.where(first, block, blocks[1 - s])
                    out_ref[s * rows : (s + 1) * rows, to : to + LANES] = block
                to += LANES


def reorder(plan, weights):
    rows = weights[0].shape[0]
    return pl.pallas_call(
        functools.partial(reorder_kernel, plan),
        out_shape=jax.ShapeDtypeStruct((plan.merge * rows, plan.heads * PIECES * HD), bf16),
        compiler_params=params(),
        cost_estimate=cost(0, 4 * weights[0].size),
        name="reorder",
    )(*weights)


def normalise(part, out, at):
    step = min(128, part.shape[0])

    def norm(c, _):
        start = pl.multiple_of(c * step, step)
        wide = part[pl.ds(start, step), :].astype(f32)
        scale = lax.rsqrt(jnp.mean(wide * wide, axis=-1, keepdims=True) + epsilon)
        out[pl.ds(at + start, step), :] = (wide * scale).astype(bf16)
        return 0

    lax.fori_loop(0, part.shape[0] // step, norm, 0)


def pick_kernel(groups, ids_ref, own_ref, rest_ref):
    tokens = ids_ref.shape[1]
    local = own_ref.shape[1]
    block = tokens // groups
    step = 128
    label = lax.broadcasted_iota(jnp.int32, (groups, tokens), 0)
    held = label == ids_ref[...]
    held_bf = jnp.where(held, 1.0, 0.0).astype(bf16)
    counts = []
    for c in range(tokens // 256):
        before = lax.broadcasted_iota(jnp.int32, (tokens, 256), 0) < (
            lax.broadcasted_iota(jnp.int32, (tokens, 256), 1) + c * 256
        )
        counts.append(
            jnp.dot(held_bf, jnp.where(before, 1.0, 0.0).astype(bf16), preferred_element_type=f32)
        )
    count = jnp.concatenate(counts, axis=1)
    rank = jnp.sum(
        jnp.where(held, count + (label * block).astype(f32), 0.0), axis=0, keepdims=True
    ).astype(jnp.int32)

    def place(c, _):
        at = pl.multiple_of(c * step, step)
        pick = (lax.broadcasted_iota(jnp.int32, (step, tokens), 0) + at) == rank
        pick = jnp.where(pick, 1.0, 0.0).astype(bf16)
        own_ref[pl.ds(at, step), :] = pick[:, :local]
        rest_ref[pl.ds(at, step), :] = pick[:, local:]
        return 0

    lax.fori_loop(0, tokens // step, place, 0)


def pick_tokens(ids, local, groups):
    tokens = ids.shape[0]
    return pl.pallas_call(
        functools.partial(pick_kernel, groups),
        out_shape=(
            jax.ShapeDtypeStruct((tokens, local), bf16),
            jax.ShapeDtypeStruct((tokens, tokens - local), bf16),
        ),
        compiler_params=params(),
        cost_estimate=cost(32 * tokens * tokens, 2 * tokens * tokens),
        name="pick_tokens",
    )(ids.reshape(1, tokens))


def back_kernel(groups, ids_ref, back_ref):
    tokens = back_ref.shape[0]
    block = tokens // groups
    step = 128
    lane = lax.broadcasted_iota(jnp.int32, (tokens, 128), 1)
    held = jnp.where(lane == ids_ref[...], 1.0, 0.0).astype(bf16)

    def place(c, _):
        at = pl.multiple_of(c * step, step)
        before = lax.broadcasted_iota(jnp.int32, (step, tokens), 1) < (
            lax.broadcasted_iota(jnp.int32, (step, tokens), 0) + at
        )
        count = jnp.dot(
            jnp.where(before, 1.0, 0.0).astype(bf16), held, preferred_element_type=f32
        )
        lane = lax.broadcasted_iota(jnp.int32, (step, 128), 1)
        mine = lane == ids_ref[pl.ds(at, step), :]
        rank = jnp.sum(
            jnp.where(mine, count + (lane * block).astype(f32), 0.0), axis=1, keepdims=True
        ).astype(jnp.int32)
        pick = lax.broadcasted_iota(jnp.int32, (step, tokens), 1) == rank
        back_ref[pl.ds(at, step), :] = jnp.where(pick, 1.0, 0.0).astype(bf16)
        return 0

    lax.fori_loop(0, tokens // step, place, 0)


def back_tokens(ids, groups):
    tokens = ids.shape[0]
    return pl.pallas_call(
        functools.partial(back_kernel, groups),
        out_shape=jax.ShapeDtypeStruct((tokens, tokens), bf16),
        compiler_params=params(),
        cost_estimate=cost(256 * tokens * tokens, 2 * tokens * tokens),
        name="back_tokens",
    )(ids.reshape(tokens, 1))


def place_kernel(merge, *refs):
    pick_ref, frame_refs = refs[0], refs[1 : 1 + merge]
    x_ref, pick, raw, normed, x, sems = refs[1 + merge :]
    copies = Copies(sems)
    local = raw.shape[1]
    tokens = pick.shape[0]
    step = 256
    arriving = [copies.start(ref, raw.at[s]) for s, ref in enumerate(frame_refs)]
    picking = copies.start(pick_ref, pick)
    leaving = []
    for s in range(merge):
        arriving[s].wait()
        normalise(raw.at[s], normed, 0)
        if s == 0:
            picking.wait()
        for at in range(0, tokens, step):
            there = slice(s * tokens + at, s * tokens + at + step)
            x[there, :] = jnp.dot(
                pick[at : at + step, :], normed[...], preferred_element_type=f32
            ).astype(bf16)
            leaving.append(copies.start(x.at[there], x_ref.at[there]))
    finish(leaving)


def place_tokens(plan, pick, frames):
    tokens, count = pick.shape
    width = frames[0].shape[1]
    every = plan.merge * tokens
    any_space = pl.BlockSpec(memory_space=pl.ANY)
    return pl.pallas_call(
        functools.partial(place_kernel, plan.merge),
        in_specs=[any_space] * (1 + len(frames)),
        out_specs=any_space,
        out_shape=jax.ShapeDtypeStruct((every, width), bf16),
        scratch_shapes=[
            pltpu.VMEM((tokens, count), bf16),
            pltpu.VMEM((plan.merge, count, width), bf16),
            pltpu.VMEM((count, width), bf16),
            pltpu.VMEM((every, width), bf16),
            Copies.scratch(),
        ],
        compiler_params=params(),
        cost_estimate=cost(4 * every * count * width, 6 * tokens * width),
        name="place_tokens",
    )(pick, *frames)


def update_kernel(plan, groups, parts, *refs):
    decay_refs, refs = refs[: plan.merge], refs[plan.merge :]
    part_ref, rest_ref, refs = refs[0], refs[1], refs[2:]
    frame_refs, refs = refs[: plan.merge * parts], refs[plan.merge * parts :]
    w_refs, refs = refs[:-13], refs[-13:]
    x_out, v_out, u_out, total_ref, rest, raw, normed, w, x, v, b, u, sems = refs
    copies = Copies(sems)
    tokens = rest.shape[0]
    block = tokens // groups
    step = 256
    here = step // block
    many = here * plan.pairs * N

    arriving = []
    for s in range(plan.merge):
        at = 0
        for ref in frame_refs[s * parts : (s + 1) * parts]:
            size = ref.shape[0]
            arriving.append(copies.start(ref, raw.at[s, at : at + size, :]))
            at += size
    picking = [copies.start(rest_ref, rest), copies.start(part_ref, x)]
    weights = plan.gather(copies, w_refs, w, slice(0, w.shape[1]))

    leaving = []
    for s in range(plan.merge):
        finish(arriving[s * parts : (s + 1) * parts])
        normalise(raw.at[s], normed, 0)
        if s == 0:
            finish(picking)
        for at in range(0, tokens, step):
            there = slice(s * tokens + at, s * tokens + at + step)
            more = jnp.dot(rest[at : at + step, :], normed[...], preferred_element_type=f32)
            x[there, :] = x[there, :] + more.astype(bf16)
            leaving.append(copies.start(x.at[there], x_out.at[there]))
    finish(weights)

    def project(c, _):
        at = pl.ds(pl.multiple_of(c * step, step), step)
        both = jnp.dot(x[at, :], w[...], preferred_element_type=f32).astype(bf16)
        for p in range(plan.pairs):
            cols = slice(p * LANES, (p + 1) * LANES)
            v[at, cols] = both[:, 2 * p * LANES : (2 * p + 1) * LANES]
            b[at, cols] = both[:, (2 * p + 1) * LANES : (2 * p + 2) * LANES]
        return 0

    lax.fori_loop(0, plan.merge * tokens // step, project, 0)
    leaving.append(copies.start(v, v_out))

    for s in range(plan.merge):
        for p in range(plan.pairs):
            cols = slice(p * LANES, (p + 1) * LANES)
            for g in range(0, groups, 2):
                rows = slice(s * tokens + g * block, s * tokens + (g + 2) * block)
                turned = b[rows, cols].astype(f32).T
                half = lax.broadcasted_iota(jnp.int32, turned.shape, 1) < block
                wide = jnp.concatenate(
                    [jnp.where(half, turned, 0.0), jnp.where(half, 0.0, turned)], axis=0
                ).astype(bf16)
                outer = jnp.dot(wide, v[rows, cols], preferred_element_type=f32)
                for n in range(2):
                    m = outer[n * 2 * N : (n + 1) * 2 * N]
                    at = ((g + n) * plan.pairs + p) * N
                    u[s, at : at + N, :] = halves((N, LANES), m[:N], m[N:])
        leaving.append(copies.start(u.at[s], u_out.at[s]))

    peers = total_ref.shape[0]
    share = u.shape[1] // peers
    items = max(1, share // N)
    size = min(N, share)
    first = plan.core() == 0
    for d in range(peers):
        for i in range(items):
            row = d * share + i * N
            p, g = row // N % plan.pairs, row // N // plan.pairs
            last = plan.last_decay(decay_refs, p, g)
            total = u[plan.merge - 1, row : row + size, :]
            product = last
            if plan.merge == 2:
                before = u[0, row : row + size, :]
                total = jnp.where(first, last, 1.0) * before + jnp.where(first, 1.0, last) * total
                product = plan.decay(decay_refs, 0, p, g) * plan.decay(decay_refs, 1, p, g)
            total_ref[d, i * size : (i + 1) * size, :] = total.astype(bf16)
            for n in range(3):
                piece = product.astype(bf16)
                at = share + n * items + i
                total_ref[d, at : at + 1, :] = piece
                product = product - piece.astype(f32)
    finish(leaving)


def share_rows(share):
    return share + 16 * -(-3 * max(1, share // N) // 16)


def project_updates(plan, decays, part, rest, frames, weights, groups):
    every, width = part.shape
    tokens, count = rest.shape
    cols = plan.pairs * LANES
    rows = plan.pairs * groups * N
    share = rows // plan.chips
    any_space = pl.BlockSpec(memory_space=pl.ANY)
    return pl.pallas_call(
        functools.partial(update_kernel, plan, groups, len(frames) // plan.merge),
        in_specs=[pl.BlockSpec(memory_space=pltpu.SMEM)] * plan.merge
        + [any_space] * (2 + len(frames) + len(weights)),
        out_specs=(any_space,) * 3 + (pl.BlockSpec(memory_space=pltpu.VMEM),),
        out_shape=(
            jax.ShapeDtypeStruct((every, width), bf16),
            jax.ShapeDtypeStruct((every, cols), bf16),
            jax.ShapeDtypeStruct((plan.merge, rows, LANES), f32),
            jax.ShapeDtypeStruct((plan.chips, share_rows(share), LANES), bf16),
        ),
        scratch_shapes=[
            pltpu.VMEM((tokens, count), bf16),
            pltpu.VMEM((plan.merge, count, width), bf16),
            pltpu.VMEM((count, width), bf16),
            pltpu.VMEM((width, 2 * cols), bf16),
            pltpu.VMEM((every, width), bf16),
            pltpu.VMEM((every, cols), bf16),
            pltpu.VMEM((every, cols), bf16),
            pltpu.VMEM((plan.merge, rows, LANES), f32),
            Copies.scratch(),
        ],
        compiler_params=params(),
        cost_estimate=cost(4 * every * width * (2 * cols + count), 6 * every * width),
        name="project_updates",
    )(*decays, part, rest, *frames, *weights)


def scan_kernel(plan, u_ref, s_ref):
    share = s_ref.shape[1]
    size = min(share, N)
    items = share // size
    for i in range(items):
        at = slice(i * size, (i + 1) * size)
        state = jnp.zeros((size, LANES), f32)
        for j in range(plan.chips):
            s_ref[j, at, :] = state.astype(bf16)
            decay = jnp.zeros((1, LANES), f32)
            for n in range(3):
                row = share + n * items + i
                decay = decay + u_ref[j, row : row + 1, :].astype(f32)
            state = decay * state + u_ref[j, at, :].astype(f32)


def scan_states(plan, update, share):
    return pl.pallas_call(
        functools.partial(scan_kernel, plan),
        out_shape=jax.ShapeDtypeStruct((plan.chips, share, LANES), bf16),
        compiler_params=params(24),
        cost_estimate=cost(2 * update.size, 4 * update.size),
        name="scan_states",
    )(update)


def attend_kernel(plan, slot, *refs):
    lists_ref, refs = refs[0], refs[1:]
    decay_refs, refs = refs[: plan.merge], refs[plan.merge :]
    x_in, v_in, u_in, w_refs, refs = refs[0], refs[1], refs[2], refs[3:-11], refs[-11:]
    a_out, c_out, x, v, u, w, q_ref, k_ref, a, c_ref, sems = refs
    copies = Copies(sems)
    tokens = x.shape[0]
    groups, chosen = lists_ref.shape
    block = tokens // groups
    step = 256
    per = step // block
    early = 2 * plan.pairs * LANES
    mine = slice(slot * tokens, (slot + 1) * tokens)

    weights = plan.gather(copies, w_refs, w, slice(early, early + w.shape[1]))
    arriving = []
    for at in range(0, tokens, step):
        from_ = slice(slot * tokens + at, slot * tokens + at + step)
        arriving.append(copies.start(x_in.at[from_], x.at[at : at + step]))
    later = [copies.start(v_in.at[mine], v), copies.start(u_in, u)]

    half = first_half((step, LANES))

    def head_norm(wide):
        square = wide * wide
        one = jnp.sum(jnp.where(half, square, 0.0), axis=-1, keepdims=True)
        two = jnp.sum(jnp.where(half, 0.0, square), axis=-1, keepdims=True)
        return wide * lax.rsqrt(jnp.where(half, one, two) * (1.0 / HD) + epsilon)

    finish(weights)
    for at in range(0, tokens, step):
        arriving[at // step].wait()
        rows = slice(at, at + step)
        every = jnp.dot(x[rows, :], w[...], preferred_element_type=f32).astype(bf16)
        for p in range(plan.pairs):
            cols = slice(p * LANES, (p + 1) * LANES)
            q, k, reader = (
                every[:, (3 * p + i) * LANES : (3 * p + i + 1) * LANES] for i in range(3)
            )
            c_ref[rows, cols] = reader
            k_ref[rows, cols] = head_norm(k.astype(f32)).astype(bf16)
            q = head_norm(q.astype(f32))
            one = jnp.where(half, q, 0.0).astype(bf16)
            two = jnp.where(half, 0.0, q).astype(bf16)
            for i in range(per):
                part = slice(i * block, (i + 1) * block)
                q_ref[p, at // block + i] = jnp.concatenate([one[part], two[part]], axis=0)
    leaving = [copies.start(c_ref, c_out)]
    finish(later)

    scale = math.log2(math.e) / math.sqrt(HD)
    for g in range(groups):
        rows = slice(g * block, (g + 1) * block)
        starts = [pl.multiple_of(lists_ref[g, j] * block, block) for j in range(chosen)]
        for p in range(plan.pairs):
            cols = slice(p * LANES, (p + 1) * LANES)
            keys = jnp.concatenate([k_ref[pl.ds(s, block), cols] for s in starts], axis=0)
            values = jnp.concatenate([v[pl.ds(s, block), cols] for s in starts], axis=0)
            score = lax.dot_general(
                q_ref[p, g], keys, (((1,), (1,)), ((), ())), preferred_element_type=f32
            )
            e = jnp.exp2(score * scale)
            weight = (e * (1.0 / jnp.sum(e, axis=-1, keepdims=True))).astype(bf16)
            both = jnp.dot(weight, values, preferred_element_type=f32)
            attended = halves((block, LANES), both[:block], both[block:])
            items = slice((g * plan.pairs + p) * N, (g * plan.pairs + p + 1) * N)
            state = u[slot, items, :]
            if plan.merge == 2:
                last = plan.last_decay(decay_refs, p, g)
                last = jnp.where(plan.core() == slot, 0.0, last)
                state = state + last * u[1 - slot, items, :]
            a[rows, cols] = attended + read_out(c_ref[rows, cols], state, block)
        if (g + 1) % per == 0:
            done = slice((g + 1 - per) * block, (g + 1) * block)
            leaving.append(copies.start(a.at[done], a_out.at[done]))
    finish(leaving)


def attend(plan, slot, lists, decays, x, v, weights, updates):
    every, width = x.shape
    groups, chosen = lists.shape
    tokens = every // plan.merge
    block = tokens // groups
    cols = plan.pairs * LANES
    any_space = pl.BlockSpec(memory_space=pl.ANY)
    return pl.pallas_call(
        functools.partial(attend_kernel, plan, slot),
        in_specs=[pl.BlockSpec(memory_space=pltpu.SMEM)] * (1 + plan.merge)
        + [any_space] * (3 + len(weights)),
        out_specs=(any_space,) * 2,
        scratch_shapes=[
            pltpu.VMEM((tokens, width), bf16),
            pltpu.VMEM((tokens, cols), bf16),
            pltpu.VMEM(updates.shape, f32),
            pltpu.VMEM((width, 3 * cols), bf16),
            pltpu.VMEM((plan.pairs, groups, 2 * block, LANES), bf16),
            pltpu.VMEM((tokens, cols), bf16),
            pltpu.VMEM((tokens, cols), f32),
            pltpu.VMEM((tokens, cols), bf16),
            Copies.scratch(),
        ],
        out_shape=(
            jax.ShapeDtypeStruct((tokens, cols), f32),
            jax.ShapeDtypeStruct((tokens, cols), bf16),
        ),
        compiler_params=params(),
        cost_estimate=cost(
            6 * tokens * width * 3 * cols,
            4 * (tokens * width + 5 * width * cols + updates.size),
            2 * plan.pairs * tokens * chosen * block,
        ),
        name="attend",
    )(lists, *decays, x, v, updates, *weights)


def read_out(readers, state, block):
    half = first_half(state.shape)
    wide = jnp.concatenate([jnp.where(half, state, 0.0), jnp.where(half, 0.0, state)], axis=0)
    return jnp.dot(readers, wide.astype(bf16), preferred_element_type=f32) * (
        1.0 / (N * math.sqrt(block))
    )


def mix_kernel(plan, groups, *refs):
    decay_refs, refs = refs[: plan.merge], refs[plan.merge :]
    a_ins, refs = refs[: plan.merge], refs[plan.merge :]
    c_ins, refs = refs[: plan.merge], refs[plan.merge :]
    s_in, back_in, refs = refs[0], refs[1], refs[2:]
    out_refs, (a, c, state, back, mixed, sems) = refs[:-6], refs[-6:]
    copies = Copies(sems)
    tokens = back.shape[0]
    block = tokens // groups
    width = a.shape[2]
    here = groups // 4
    step = here * block
    many = here * plan.pairs * N
    first = plan.core() == 0

    arriving = []
    for i in range(4):
        rows = slice(i * step, (i + 1) * step)
        items = slice(i * many, (i + 1) * many)
        arriving.append([copies.start(s_in.at[items], state.at[items])])
        for s in range(plan.merge):
            arriving[-1] += [
                copies.start(a_ins[s].at[rows], a.at[s, rows, :]),
                copies.start(c_ins[s].at[rows], c.at[s, rows, :]),
            ]
    local = tokens // plan.peers
    turning = [
        copies.start(back_in.at[k * local : (k + 1) * local], back.at[k * local : (k + 1) * local])
        for k in range(plan.peers)
    ]

    for g in range(groups):
        if g % here == 0:
            finish(arriving[g // here])
        rows = slice(g * block, (g + 1) * block)
        for p in range(plan.pairs):
            cols = slice(p * LANES, (p + 1) * LANES)
            at = (g * plan.pairs + p) * N
            readers = jnp.concatenate([c[s, rows, cols] for s in range(plan.merge)], axis=0)
            read = read_out(readers, state[at : at + N, :].astype(f32), block)
            decays = [plan.decay(decay_refs, s, p, g) for s in range(plan.merge)]
            if plan.merge == 2:
                both = decays[0] * decays[1]
                decays = [jnp.where(first, decays[0], both), jnp.where(first, both, decays[1])]
            for s in range(plan.merge):
                there = slice(s * width + p * LANES, s * width + (p + 1) * LANES)
                mixed[rows, there] = (
                    a[s, rows, cols] + decays[s] * read[s * block : (s + 1) * block]
                ).astype(bf16)

    for k in range(plan.peers):
        turning[k].wait()
        placed = jnp.dot(
            back[k * local : (k + 1) * local, :], mixed[...], preferred_element_type=f32
        ).astype(bf16)
        for s in range(plan.merge):
            out_refs[s * plan.peers + k][...] = placed[:, s * width : (s + 1) * width]


def mix(plan, decays, attended, readers, state, back, groups):
    tokens = back.shape[0]
    width = attended[0].shape[1]
    local = tokens // plan.peers
    count = plan.merge * plan.peers
    any_space = pl.BlockSpec(memory_space=pl.ANY)
    return pl.pallas_call(
        functools.partial(mix_kernel, plan, groups),
        in_specs=[pl.BlockSpec(memory_space=pltpu.SMEM)] * plan.merge
        + [any_space] * (2 * plan.merge + 2),
        out_specs=(pl.BlockSpec(memory_space=pltpu.VMEM),) * count,
        out_shape=(jax.ShapeDtypeStruct((local, width), bf16),) * count,
        scratch_shapes=[
            pltpu.VMEM((plan.merge, tokens, width), f32),
            pltpu.VMEM((plan.merge, tokens, width), bf16),
            pltpu.VMEM(state.shape, bf16),
            pltpu.VMEM((tokens, tokens), bf16),
            pltpu.VMEM((tokens, plan.merge * width), bf16),
            Copies.scratch(),
        ],
        compiler_params=params(),
        cost_estimate=cost(4 * tokens * tokens * width, 2 * tokens * tokens + 16 * tokens * width),
        name="mix",
    )(*decays, *attended, *readers, state, back)


def out_kernel(plan, w_ref, *refs):
    part_refs, out_ref = refs[:-1], refs[-1]
    depth = part_refs[0].shape[1]
    core, me = plan.core(), lax.axis_index("head")
    total = None
    for s in range(plan.merge):
        for k in range(plan.peers):
            owner = lax.rem(me - k + plan.peers, plan.peers) * plan.merge
            owner = owner + (core if s == 0 else 1 - core)
            rows = pl.ds(pl.multiple_of(owner * depth, depth), depth)
            term = jnp.dot(
                part_refs[s * plan.peers + k][...], w_ref[rows, :], preferred_element_type=f32
            )
            total = term if total is None else total + term
    out_ref[...] = total.astype(bf16)


def project_out(plan, w, parts):
    local = parts[0].shape[0]
    width = w.shape[1]
    return pl.pallas_call(
        functools.partial(out_kernel, plan),
        out_shape=jax.ShapeDtypeStruct((local, width), bf16),
        compiler_params=params(24),
        cost_estimate=cost(2 * local * w.size, 2 * (w.size + 2 * local * width)),
        name="project_out",
    )(w, *parts)


def body(frames_in, in_weight, out_weight, block_ids, block_lists, decays):
    local_tokens = frames_in.shape[1]
    heads_here = decays.shape[1]
    groups = block_lists.shape[0]
    me = lax.axis_index("head")
    plan = Plan(lax.axis_size("tm"), lax.axis_size("head"), heads_here)

    own = frames_in[0]
    arriving = [plan.to_peer(own, plan.peers - k, False) for k in range(1, plan.peers)]
    owns = [own] + [plan.swap(own)] * (plan.merge - 1)
    rates = [decays[0]] + [plan.swap(decays[0])] * (plan.merge - 1)
    block = reorder(plan, [in_weight] + [plan.swap(in_weight)] * (plan.merge - 1))

    ids = jnp.roll(block_ids, -me * local_tokens)
    pick, rest = pick_tokens(ids, local_tokens, groups)
    part = place_tokens(plan, pick, owns)
    if plan.ringed:
        weights, beside = [], [pick, part]
        for k in range(plan.along):
            crossed = plan.cross(block)
            weights += [block, crossed]
            if k < plan.along - 1:
                block = plan.round(block)
                block, crossed, beside[:1] = lax.optimization_barrier((block, crossed, beside[:1]))
                weights[-1] = crossed
                beside = beside[1:]
                n = k - (plan.along - 1 - len(arriving))
                if 0 <= n < len(arriving):
                    arriving[n], block = lax.optimization_barrier((arriving[n], block))
    else:
        weights = [
            lax.all_gather(block, "tm", axis=0, tiled=True, axis_index_groups=plan.groups())
        ]
    if plan.merge == 2:
        arriving = arriving + [plan.swap(chunk) for chunk in arriving]
    x, v, updates, total = project_updates(plan, rates, part, rest, arriving, weights, groups)

    def exchange(blocks):
        return lax.all_to_all(
            blocks, "tm", split_axis=0, concat_axis=0, tiled=True,
            axis_index_groups=plan.groups(),
        )

    share = updates.shape[1] // plan.chips
    arrived = exchange(total)
    attended = [attend(plan, 0, block_lists, rates, x, v, weights, updates)]
    arrived, attended = lax.optimization_barrier((arrived, attended))
    states = scan_states(plan, arrived, share)
    x, states = lax.optimization_barrier((x, states))
    if plan.merge == 2:
        attended.append(attend(plan, 1, block_lists, rates, x, v, weights, updates))
    state = exchange(states).reshape(-1, LANES)
    ids, attended = lax.optimization_barrier((ids, attended))
    back = back_tokens(ids, groups)

    bases, readers = ([a[i] for a in attended] for i in range(2))
    mixed = mix(plan, rates, bases, readers, state, back, groups)
    features = [
        mixed[0] if s == 0 and k == 0 else plan.to_peer(mixed[s * plan.peers + k], k, s == 1)
        for s in range(plan.merge)
        for k in range(plan.peers)
    ]
    return project_out(plan, out_weight, features)[None]


def solution(mesh):
    return jax.shard_map(
        body,
        mesh=mesh,
        in_specs=(P("tm", "head", None), P("tm", "head"), P(), P(), P(), P("tm", "head", None)),
        out_specs=P("tm", "head", None),
        check_vma=False,
    )
```

```python
import functools
import math

import jax
import jax.numpy as jnp
from jax import lax
from jax.experimental import pallas as pl
from jax.experimental.pallas import tpu as pltpu
from jax.sharding import PartitionSpec as P

HD = 64
N = 64
LANES = 2 * HD
PIECES = 5
EARLY = (2, 3)
LATE = (0, 1, 4)

epsilon = 1e-06

vmem = pl.BlockSpec(memory_space=pltpu.VMEM)
smem = pl.BlockSpec(memory_space=pltpu.SMEM)
hbm = pl.BlockSpec(memory_space=pltpu.HBM)

f32 = jnp.float32
bf16 = jnp.bfloat16


def params(mib=28):
    return pltpu.CompilerParams(vmem_limit_bytes=mib << 20)


def cost(flops, nbytes, transcendentals=0):
    return pl.CostEstimate(
        flops=int(flops), bytes_accessed=int(nbytes), transcendentals=int(transcendentals)
    )


def first_half(shape):
    return lax.broadcasted_iota(jnp.int32, shape, len(shape) - 1) < HD


class Plan:
    def __init__(self, frames, peers, heads_here):
        self.merge = 2 if frames % 2 == 0 and heads_here % 4 == 0 else 1
        self.frames, self.peers = frames, peers
        self.heads = heads_here // self.merge
        self.pairs = self.heads // 2
        self.chips = frames // self.merge
        self.across = 2 if self.chips % 2 == 0 else 1
        self.along = self.chips // self.across
        self.ringed = self.across == 2 and self.along <= 8

    def core(self):
        return lax.rem(lax.axis_index("tm"), self.merge)

    def chip(self):
        return lax.div(lax.axis_index("tm"), self.merge)

    def swap(self, block):
        return lax.ppermute(block, "tm", [(t, t ^ 1) for t in range(self.frames)])

    def round(self, block):
        a, b, c = self.along, self.across, self.merge
        pairs = [(t, (t + b * c) % (a * b * c)) for t in range(self.frames)]
        return lax.ppermute(block, "tm", pairs)

    def cross(self, block):
        c = self.merge
        pairs = [(t, (t // c ^ 1) * c + t % c) for t in range(self.frames)]
        return lax.ppermute(block, "tm", pairs)

    def places(self, refs):
        if len(refs) == 1:
            return [(refs[0], slice(None))]
        rows = refs[0].shape[0]
        a, b = lax.div(self.chip(), self.across), lax.rem(self.chip(), self.across)
        made = []
        for i, ref in enumerate(refs):
            k, flip = i // 2, i % 2
            there = lax.rem(a - k + self.along, self.along) * self.across
            at = pl.multiple_of((there + (1 - b if flip else b)) * rows, rows)
            made.append((ref, pl.ds(at, rows)))
        return made

    def to_peer(self, block, k, other):
        if not other:
            pairs = [(j, (j + k) % self.peers) for j in range(self.peers)]
            return lax.ppermute(block, "head", pairs)
        if k == 0:
            return self.swap(block)
        pairs = [
            (t * self.peers + j, (t ^ 1) * self.peers + (j + k) % self.peers)
            for t in range(self.frames)
            for j in range(self.peers)
        ]
        return lax.ppermute(block, ("tm", "head"), pairs)

    def groups(self):
        if self.merge == 1:
            return None
        return [[j * self.merge + c for j in range(self.chips)] for c in range(self.merge)]

    def decay(self, refs, slot, pair, g):
        head = self.core() * self.heads + 2 * pair
        return halves((1, LANES), refs[slot][head, g], refs[slot][head + 1, g])

    def last_decay(self, refs, pair, g):
        if self.merge == 1:
            return self.decay(refs, 0, pair, g)
        one, two = (self.decay(refs, slot, pair, g) for slot in range(2))
        return jnp.where(self.core() == 0, two, one)


class Copies:
    room = 48

    def __init__(self, sems):
        self.sems, self.made = sems, []

    def start(self, src, dst):
        copy = pltpu.make_async_copy(src, dst, self.sems.at[len(self.made)])
        copy.start()
        self.made.append(copy)
        return copy

    @staticmethod
    def scratch():
        return pltpu.SemaphoreType.DMA((Copies.room,))


def finish(copies):
    for copy in copies:
        copy.wait()


def halves(shape, one, two):
    return jnp.where(first_half(shape), one, two)


def reorder_kernel(plan, *refs):
    w_refs, out_refs = refs[:-2], refs[-2:]
    rows = w_refs[0].shape[0]
    width = plan.heads * PIECES * HD
    first = plan.core() == 0

    def chosen(ref, at):
        one = ref[:, at : at + HD]
        if plan.merge == 1:
            return one
        return jnp.where(first, one, ref[:, width + at : width + at + HD])

    early = [(p, i) for i in EARLY for p in range(plan.pairs)]
    late = [(p, i) for p in range(plan.pairs) for i in LATE]
    for out_ref, order in zip(out_refs, (early, late)):
        for n, (p, i) in enumerate(order):
            blocks = []
            for ref in w_refs:
                one, two = (chosen(ref, ((2 * p + h) * PIECES + i) * HD) for h in range(2))
                blocks.append(jnp.concatenate([one, two], axis=1))
            for s, block in enumerate(blocks):
                if plan.merge == 2:
                    block = jnp.where(first, block, blocks[1 - s])
                out_ref[s * rows : (s + 1) * rows, n * LANES : (n + 1) * LANES] = block


def reorder(plan, weights):
    rows = weights[0].shape[0]
    return pl.pallas_call(
        functools.partial(reorder_kernel, plan),
        out_shape=tuple(
            jax.ShapeDtypeStruct((plan.merge * rows, plan.heads * len(kinds) * HD), bf16)
            for kinds in (EARLY, LATE)
        ),
        compiler_params=params(),
        cost_estimate=cost(0, 4 * weights[0].size),
        name="reorder",
    )(*weights)


def normalise(part, out, at):
    step = min(128, part.shape[0])

    def norm(c, _):
        start = pl.multiple_of(c * step, step)
        wide = part[pl.ds(start, step), :].astype(f32)
        scale = lax.rsqrt(jnp.mean(wide * wide, axis=-1, keepdims=True) + epsilon)
        out[pl.ds(at + start, step), :] = (wide * scale).astype(bf16)
        return 0

    lax.fori_loop(0, part.shape[0] // step, norm, 0)


def pick_kernel(groups, ids_ref, own_ref, rest_ref):
    tokens = ids_ref.shape[1]
    local = own_ref.shape[1]
    block = tokens // groups
    step = 128
    label = lax.broadcasted_iota(jnp.int32, (groups, tokens), 0)
    held = label == ids_ref[...]
    held_bf = jnp.where(held, 1.0, 0.0).astype(bf16)
    counts = []
    for c in range(tokens // 256):
        before = lax.broadcasted_iota(jnp.int32, (tokens, 256), 0) < (
            lax.broadcasted_iota(jnp.int32, (tokens, 256), 1) + c * 256
        )
        counts.append(
            jnp.dot(held_bf, jnp.where(before, 1.0, 0.0).astype(bf16), preferred_element_type=f32)
        )
    count = jnp.concatenate(counts, axis=1)
    rank = jnp.sum(
        jnp.where(held, count + (label * block).astype(f32), 0.0), axis=0, keepdims=True
    ).astype(jnp.int32)

    def place(c, _):
        at = pl.multiple_of(c * step, step)
        pick = (lax.broadcasted_iota(jnp.int32, (step, tokens), 0) + at) == rank
        pick = jnp.where(pick, 1.0, 0.0).astype(bf16)
        own_ref[pl.ds(at, step), :] = pick[:, :local]
        rest_ref[pl.ds(at, step), :] = pick[:, local:]
        return 0

    lax.fori_loop(0, tokens // step, place, 0)


def pick_tokens(ids, local, groups):
    tokens = ids.shape[0]
    return pl.pallas_call(
        functools.partial(pick_kernel, groups),
        out_shape=(
            jax.ShapeDtypeStruct((tokens, local), bf16),
            jax.ShapeDtypeStruct((tokens, tokens - local), bf16),
        ),
        compiler_params=params(),
        cost_estimate=cost(32 * tokens * tokens, 2 * tokens * tokens),
        name="pick_tokens",
    )(ids.reshape(1, tokens))


def back_kernel(groups, ids_ref, back_ref):
    tokens = back_ref.shape[0]
    block = tokens // groups
    step = 128
    lane = lax.broadcasted_iota(jnp.int32, (tokens, 128), 1)
    held = jnp.where(lane == ids_ref[...], 1.0, 0.0).astype(bf16)

    def place(c, _):
        at = pl.multiple_of(c * step, step)
        before = lax.broadcasted_iota(jnp.int32, (step, tokens), 1) < (
            lax.broadcasted_iota(jnp.int32, (step, tokens), 0) + at
        )
        count = jnp.dot(
            jnp.where(before, 1.0, 0.0).astype(bf16), held, preferred_element_type=f32
        )
        lane = lax.broadcasted_iota(jnp.int32, (step, 128), 1)
        mine = lane == ids_ref[pl.ds(at, step), :]
        rank = jnp.sum(
            jnp.where(mine, count + (lane * block).astype(f32), 0.0), axis=1, keepdims=True
        ).astype(jnp.int32)
        pick = lax.broadcasted_iota(jnp.int32, (step, tokens), 1) == rank
        back_ref[pl.ds(at, step), :] = jnp.where(pick, 1.0, 0.0).astype(bf16)
        return 0

    lax.fori_loop(0, tokens // step, place, 0)


def back_tokens(ids, groups):
    tokens = ids.shape[0]
    return pl.pallas_call(
        functools.partial(back_kernel, groups),
        out_shape=jax.ShapeDtypeStruct((tokens, tokens), bf16),
        compiler_params=params(),
        cost_estimate=cost(256 * tokens * tokens, 2 * tokens * tokens),
        name="back_tokens",
    )(ids.reshape(tokens, 1))


def place_kernel(merge, pick_ref, *refs):
    frame_refs, x_ref, normed = refs[:merge], refs[-2], refs[-1]
    tokens = pick_ref.shape[0]
    step = 256
    for s in range(merge):
        normalise(frame_refs[s], normed.at[s], 0)
        for at in range(0, tokens, step):
            x_ref[s * tokens + at : s * tokens + at + step, :] = jnp.dot(
                pick_ref[at : at + step, :], normed[s], preferred_element_type=f32
            ).astype(bf16)


def place_tokens(plan, pick, frames):
    tokens, count = pick.shape
    width = frames[0].shape[1]
    every = plan.merge * tokens
    return pl.pallas_call(
        functools.partial(place_kernel, plan.merge),
        out_shape=jax.ShapeDtypeStruct((every, width), bf16),
        scratch_shapes=[pltpu.VMEM((plan.merge, count, width), bf16)],
        compiler_params=params(),
        cost_estimate=cost(4 * every * count * width, 6 * tokens * width),
        name="place_tokens",
    )(pick, *frames)


def update_kernel(plan, groups, parts, *refs):
    decay_refs, refs = refs[: plan.merge], refs[plan.merge :]
    part_ref, rest_ref, refs = refs[0], refs[1], refs[2:]
    frame_refs, refs = refs[: plan.merge * parts], refs[plan.merge * parts :]
    w_refs, refs = refs[:-13], refs[-13:]
    x_out, v_out, u_out, total_ref, rest, raw, normed, w, turned, x, v, u, sems = refs
    copies = Copies(sems)
    tokens = rest.shape[0]
    block = tokens // groups
    step = 256
    here = step // block
    cols = plan.pairs * LANES

    weights = []
    for ref, rows in plan.places(w_refs):
        weights.append(copies.start(ref.at[:, cols:], turned.at[rows]))
        weights.append(copies.start(ref.at[:, :cols], w.at[rows]))
    arriving, picking = [], [copies.start(rest_ref, rest)]
    for s in range(plan.merge):
        at = 0
        for ref in frame_refs[s * parts : (s + 1) * parts]:
            size = ref.shape[0]
            arriving.append(copies.start(ref, raw.at[s, at : at + size, :]))
            at += size
        mine = slice(s * tokens, (s + 1) * tokens)
        picking.append(copies.start(part_ref.at[mine], x.at[mine]))

    finish(weights)
    maps = jnp.concatenate(
        [
            turned[at : at + LANES, :].astype(f32).T.astype(bf16)
            for at in range(0, turned.shape[0], LANES)
        ],
        axis=1,
    )
    lane = lax.div(lax.broadcasted_iota(jnp.int32, (LANES, step), 1), block)

    leaving = []
    for s in range(plan.merge):
        finish(arriving[s * parts : (s + 1) * parts])
        normalise(raw.at[s], normed, 0)
        if s == 0:
            finish(picking)
        for at in range(0, tokens, step):
            there = slice(s * tokens + at, s * tokens + at + step)
            more = jnp.dot(rest[at : at + step, :], normed[...], preferred_element_type=f32)
            placed = x[there, :] + more.astype(bf16)
            x[there, :] = placed
            leaving.append(copies.start(x.at[there], x_out.at[there]))
            values = jnp.dot(placed, w[...], preferred_element_type=f32).astype(bf16)
            v[there, :] = values
            b = lax.dot_general(
                maps, placed, (((1,), (1,)), ((), ())), preferred_element_type=f32
            )
            for p in range(plan.pairs):
                mine = b[p * LANES : (p + 1) * LANES]
                wide = jnp.concatenate(
                    [jnp.where(lane == i, mine, 0.0).astype(bf16) for i in range(here)], axis=0
                )
                outer = jnp.dot(
                    wide, values[:, p * LANES : (p + 1) * LANES], preferred_element_type=f32
                )
                for i in range(here):
                    m = outer[i * 2 * N : (i + 1) * 2 * N]
                    row = ((at // block + i) * plan.pairs + p) * N
                    u[s, row : row + N, :] = halves((N, LANES), m[:N], m[N:])
        mine = slice(s * tokens, (s + 1) * tokens)
        leaving.append(copies.start(v.at[mine], v_out.at[mine]))
        leaving.append(copies.start(u.at[s], u_out.at[s]))

    peers = total_ref.shape[0]
    share = u.shape[1] // peers
    items = max(1, share // N)
    size = min(N, share)
    first = plan.core() == 0
    for d in range(peers):
        for i in range(items):
            row = d * share + i * N
            p, g = row // N % plan.pairs, row // N // plan.pairs
            last = plan.last_decay(decay_refs, p, g)
            total = u[plan.merge - 1, row : row + size, :]
            product = last
            if plan.merge == 2:
                before = u[0, row : row + size, :]
                total = jnp.where(first, last, 1.0) * before + jnp.where(first, 1.0, last) * total
                product = plan.decay(decay_refs, 0, p, g) * plan.decay(decay_refs, 1, p, g)
            total_ref[d, i * size : (i + 1) * size, :] = total.astype(bf16)
            for n in range(3):
                piece = product.astype(bf16)
                at = share + n * items + i
                total_ref[d, at : at + 1, :] = piece
                product = product - piece.astype(f32)
    finish(leaving)


def share_rows(share):
    return share + 16 * -(-3 * max(1, share // N) // 16)


def project_updates(plan, decays, part, rest, frames, weights, groups):
    every, width = part.shape
    tokens, count = rest.shape
    cols = plan.pairs * LANES
    rows = plan.pairs * groups * N
    share = rows // plan.chips
    return pl.pallas_call(
        functools.partial(update_kernel, plan, groups, len(frames) // plan.merge),
        in_specs=[smem] * plan.merge + [hbm] * (2 + len(frames) + len(weights)),
        out_specs=(hbm,) * 3 + (vmem,),
        out_shape=(
            jax.ShapeDtypeStruct((every, width), bf16),
            jax.ShapeDtypeStruct((every, cols), bf16),
            jax.ShapeDtypeStruct((plan.merge, rows, LANES), f32),
            jax.ShapeDtypeStruct((plan.chips, share_rows(share), LANES), bf16),
        ),
        scratch_shapes=[
            pltpu.VMEM((tokens, count), bf16),
            pltpu.VMEM((plan.merge, count, width), bf16),
            pltpu.VMEM((count, width), bf16),
            pltpu.VMEM((width, cols), bf16),
            pltpu.VMEM((width, cols), bf16),
            pltpu.VMEM((every, width), bf16),
            pltpu.VMEM((every, cols), bf16),
            pltpu.VMEM((plan.merge, rows, LANES), f32),
            Copies.scratch(),
        ],
        compiler_params=params(60),
        cost_estimate=cost(4 * every * width * (2 * cols + count), 6 * every * width),
        name="project_updates",
    )(*decays, part, rest, *frames, *weights)


def scan_kernel(plan, u_ref, s_ref):
    share = s_ref.shape[1]
    size = min(share, N)
    items = share // size
    for i in range(items):
        at = slice(i * size, (i + 1) * size)
        state = jnp.zeros((size, LANES), f32)
        for j in range(plan.chips):
            s_ref[j, at, :] = state.astype(bf16)
            decay = jnp.zeros((1, LANES), f32)
            for n in range(3):
                row = share + n * items + i
                decay = decay + u_ref[j, row : row + 1, :].astype(f32)
            state = decay * state + u_ref[j, at, :].astype(f32)


def scan_states(plan, update, share):
    return pl.pallas_call(
        functools.partial(scan_kernel, plan),
        out_shape=jax.ShapeDtypeStruct((plan.chips, share, LANES), bf16),
        compiler_params=params(24),
        cost_estimate=cost(2 * update.size, 4 * update.size),
        name="scan_states",
    )(update)


def attend_kernel(plan, slot, *refs):
    lists_ref, refs = refs[0], refs[1:]
    decay_refs, refs = refs[: plan.merge], refs[plan.merge :]
    x_in, v_in, u_in, w_refs, refs = refs[0], refs[1], refs[2], refs[3:-13], refs[-13:]
    a_out, c_out, x, v, u, w, q_ref, k_ref, wide_v, e_ref, a, c_ref, sems = refs
    copies = Copies(sems)
    tokens = x.shape[0]
    groups, chosen = lists_ref.shape
    block = tokens // groups
    step = 256
    per = step // block
    mine = slice(slot * tokens, (slot + 1) * tokens)

    weights = [copies.start(ref, w.at[rows]) for ref, rows in plan.places(w_refs)]
    arriving = []
    for at in range(0, tokens, step):
        from_ = slice(slot * tokens + at, slot * tokens + at + step)
        arriving.append(copies.start(x_in.at[from_], x.at[at : at + step]))
    later = [copies.start(v_in.at[mine], v), copies.start(u_in, u)]

    same = lax.div(lax.broadcasted_iota(jnp.int32, (2 * LANES, 2 * LANES), 0), HD) == lax.div(
        lax.broadcasted_iota(jnp.int32, (2 * LANES, 2 * LANES), 1), HD
    )
    same = jnp.where(same, 1.0, 0.0).astype(bf16)

    def head_norm(values):
        square = values * values
        high = square.astype(bf16)
        low = (square - high.astype(f32)).astype(bf16)
        total = jnp.dot(high, same, preferred_element_type=f32)
        total = total + jnp.dot(low, same, preferred_element_type=f32)
        return values * lax.rsqrt(total * (1.0 / HD) + epsilon)

    half = first_half((step, LANES))
    finish(weights)
    for at in range(0, tokens, step):
        arriving[at // step].wait()
        rows = slice(at, at + step)
        every = jnp.dot(x[rows, :], w[...], preferred_element_type=f32).astype(bf16)
        for p in range(plan.pairs):
            cols = slice(p * LANES, (p + 1) * LANES)
            first = 3 * p * LANES
            c_ref[rows, cols] = every[:, first + 2 * LANES : first + 3 * LANES]
            both = head_norm(every[:, first : first + 2 * LANES].astype(f32))
            k_ref[p, rows, :] = both[:, LANES:].astype(bf16)
            q = both[:, :LANES]
            one = jnp.where(half, q, 0.0).astype(bf16)
            two = jnp.where(half, 0.0, q).astype(bf16)
            for i in range(per):
                part = slice(i * block, (i + 1) * block)
                q_ref[p, at // block + i] = jnp.concatenate([one[part], two[part]], axis=0)
    leaving = [copies.start(c_ref, c_out)]
    finish(later)
    for p in range(plan.pairs):
        wide_v[p, :, :LANES] = v[:, p * LANES : (p + 1) * LANES]
        wide_v[p, :, LANES:] = jnp.ones((tokens, LANES), bf16)

    scale = math.log2(math.e) / math.sqrt(HD)
    starts = [
        [pl.multiple_of(lists_ref[g, j] * block, block) for j in range(chosen)]
        for g in range(groups)
    ]
    for g in range(groups):
        for p in range(plan.pairs):
            keys = jnp.concatenate([k_ref[p, pl.ds(s, block), :] for s in starts[g]], axis=0)
            score = lax.dot_general(
                q_ref[p, g], keys, (((1,), (1,)), ((), ())), preferred_element_type=f32
            )
            e_ref[p, g] = jnp.exp2(score * scale).astype(bf16)
    for g in range(groups):
        rows = slice(g * block, (g + 1) * block)
        for p in range(plan.pairs):
            cols = slice(p * LANES, (p + 1) * LANES)
            values = jnp.concatenate([wide_v[p, pl.ds(s, block), :] for s in starts[g]], axis=0)
            both = jnp.dot(e_ref[p, g], values, preferred_element_type=f32)
            both = both[:, :LANES] / both[:, LANES:]
            a[rows, cols] = halves((block, LANES), both[:block], both[block:])
    for g in range(groups):
        rows = slice(g * block, (g + 1) * block)
        for p in range(plan.pairs):
            cols = slice(p * LANES, (p + 1) * LANES)
            items = slice((g * plan.pairs + p) * N, (g * plan.pairs + p + 1) * N)
            state = u[slot, items, :]
            if plan.merge == 2:
                last = plan.last_decay(decay_refs, p, g)
                last = jnp.where(plan.core() == slot, 0.0, last)
                state = state + last * u[1 - slot, items, :]
            a[rows, cols] = a[rows, cols] + read_out(c_ref[rows, cols], state, block)
        if (g + 1) % per == 0:
            done = slice((g + 1 - per) * block, (g + 1) * block)
            leaving.append(copies.start(a.at[done], a_out.at[done]))
    finish(leaving)


def attend(plan, slot, lists, decays, x, v, weights, updates):
    every, width = x.shape
    groups, chosen = lists.shape
    tokens = every // plan.merge
    block = tokens // groups
    cols = plan.pairs * LANES
    return pl.pallas_call(
        functools.partial(attend_kernel, plan, slot),
        in_specs=[smem] * (1 + plan.merge) + [hbm] * (3 + len(weights)),
        out_specs=(hbm,) * 2,
        scratch_shapes=[
            pltpu.VMEM((tokens, width), bf16),
            pltpu.VMEM((tokens, cols), bf16),
            pltpu.VMEM(updates.shape, f32),
            pltpu.VMEM((width, 3 * cols), bf16),
            pltpu.VMEM((plan.pairs, groups, 2 * block, LANES), bf16),
            pltpu.VMEM((plan.pairs, tokens, LANES), bf16),
            pltpu.VMEM((plan.pairs, tokens, 2 * LANES), bf16),
            pltpu.VMEM((plan.pairs, groups, 2 * block, chosen * block), bf16),
            pltpu.VMEM((tokens, cols), f32),
            pltpu.VMEM((tokens, cols), bf16),
            Copies.scratch(),
        ],
        out_shape=(
            jax.ShapeDtypeStruct((tokens, cols), f32),
            jax.ShapeDtypeStruct((tokens, cols), bf16),
        ),
        compiler_params=params(60),
        cost_estimate=cost(
            6 * tokens * width * 3 * cols,
            4 * (tokens * width + 5 * width * cols + updates.size),
            2 * plan.pairs * tokens * chosen * block,
        ),
        name="attend",
    )(lists, *decays, x, v, updates, *weights)


def read_out(readers, state, block):
    half = first_half(state.shape)
    wide = jnp.concatenate([jnp.where(half, state, 0.0), jnp.where(half, 0.0, state)], axis=0)
    return jnp.dot(readers, wide.astype(bf16), preferred_element_type=f32) * (
        1.0 / (N * math.sqrt(block))
    )


def mix_kernel(plan, groups, *refs):
    decay_refs, refs = refs[: plan.merge], refs[plan.merge :]
    a_refs, refs = refs[: plan.merge], refs[plan.merge :]
    c_refs, refs = refs[: plan.merge], refs[plan.merge :]
    s_ref, back_ref, out_refs, mixed = refs[0], refs[1], refs[2:-1], refs[-1]
    tokens = back_ref.shape[0]
    block = tokens // groups
    width = a_refs[0].shape[1]
    first = plan.core() == 0
    for g in range(groups):
        rows = slice(g * block, (g + 1) * block)
        for p in range(plan.pairs):
            cols = slice(p * LANES, (p + 1) * LANES)
            at = (g * plan.pairs + p) * N
            readers = jnp.concatenate([c[rows, cols] for c in c_refs], axis=0)
            read = read_out(readers, s_ref[at : at + N, :].astype(f32), block)
            decays = [plan.decay(decay_refs, s, p, g) for s in range(plan.merge)]
            if plan.merge == 2:
                both = decays[0] * decays[1]
                decays = [jnp.where(first, decays[0], both), jnp.where(first, both, decays[1])]
            for s in range(plan.merge):
                there = slice(s * width + p * LANES, s * width + (p + 1) * LANES)
                mixed[rows, there] = (
                    a_refs[s][rows, cols] + decays[s] * read[s * block : (s + 1) * block]
                ).astype(bf16)
    local = tokens // plan.peers
    for k in range(plan.peers):
        placed = jnp.dot(
            back_ref[k * local : (k + 1) * local, :], mixed[...], preferred_element_type=f32
        ).astype(bf16)
        for s in range(plan.merge):
            out_refs[s * plan.peers + k][...] = placed[:, s * width : (s + 1) * width]


def mix(plan, decays, attended, readers, state, back, groups):
    tokens = back.shape[0]
    width = attended[0].shape[1]
    count = plan.merge * plan.peers
    return pl.pallas_call(
        functools.partial(mix_kernel, plan, groups),
        in_specs=[smem] * plan.merge + [vmem] * (2 * plan.merge + 2),
        out_shape=(jax.ShapeDtypeStruct((tokens // plan.peers, width), bf16),) * count,
        scratch_shapes=[pltpu.VMEM((tokens, plan.merge * width), bf16)],
        compiler_params=params(24),
        cost_estimate=cost(4 * tokens * tokens * width, 2 * tokens * tokens + 16 * tokens * width),
        name="mix",
    )(*decays, *attended, *readers, state, back)


def out_kernel(plan, w_ref, *refs):
    part_refs, out_ref = refs[:-1], refs[-1]
    depth = part_refs[0].shape[1]
    core, me = plan.core(), lax.axis_index("head")
    total = None
    for s in range(plan.merge):
        for k in range(plan.peers):
            owner = lax.rem(me - k + plan.peers, plan.peers) * plan.merge
            owner = owner + (core if s == 0 else 1 - core)
            rows = pl.ds(pl.multiple_of(owner * depth, depth), depth)
            term = jnp.dot(
                part_refs[s * plan.peers + k][...], w_ref[rows, :], preferred_element_type=f32
            )
            total = term if total is None else total + term
    out_ref[...] = total.astype(bf16)


def project_out(plan, w, parts):
    local = parts[0].shape[0]
    width = w.shape[1]
    return pl.pallas_call(
        functools.partial(out_kernel, plan),
        out_shape=jax.ShapeDtypeStruct((local, width), bf16),
        compiler_params=params(24),
        cost_estimate=cost(2 * local * w.size, 2 * (w.size + 2 * local * width)),
        name="project_out",
    )(w, *parts)


def body(frames_in, in_weight, out_weight, block_ids, block_lists, decays):
    local_tokens = frames_in.shape[1]
    heads_here = decays.shape[1]
    groups = block_lists.shape[0]
    me = lax.axis_index("head")
    plan = Plan(lax.axis_size("tm"), lax.axis_size("head"), heads_here)

    own = frames_in[0]
    arriving = [plan.to_peer(own, plan.peers - k, False) for k in range(1, plan.peers)]
    owns = [own] + [plan.swap(own)] * (plan.merge - 1)
    rates = [decays[0]] + [plan.swap(decays[0])] * (plan.merge - 1)
    blocks = reorder(plan, [in_weight] + [plan.swap(in_weight)] * (plan.merge - 1))

    ids = jnp.roll(block_ids, -me * local_tokens)
    ids, rates = lax.optimization_barrier((ids, rates))
    pick, rest = pick_tokens(ids, local_tokens, groups)
    part = place_tokens(plan, pick, owns)
    if plan.ringed:
        def step(block, with_):
            return lax.optimization_barrier((plan.round(block), plan.cross(block), with_))[:2]

        def late_step(tie):
            late[-1], _ = lax.optimization_barrier((late[-1], tie))
            if len(late) < plan.along:
                passed, crossed = step(late[-1], [])
                late.append(passed)
            else:
                crossed = plan.cross(late[-1])
            late_crossed.append(crossed)

        early, early_crossed, late, late_crossed = [blocks[0]], [], [blocks[1]], []
        beside = [pick, part]
        for k in range(plan.along - 1):
            passed, crossed = step(early[-1], beside[k : k + 1])
            early.append(passed)
            early_crossed.append(crossed)
        early_crossed.append(plan.cross(early[-1]))
        late_step(early[min(1, plan.along - 1)])
        arriving, _ = lax.optimization_barrier((arriving, (early_crossed[-1], late[-1])))
        if plan.along > 1:
            late_step(early[min(2, plan.along - 1)])
        early = [b for pair in zip(early, early_crossed) for b in pair]
    else:
        early, late = (
            [lax.all_gather(b, "tm", axis=0, tiled=True, axis_index_groups=plan.groups())]
            for b in blocks
        )
    if plan.merge == 2:
        arriving = arriving + [plan.swap(chunk) for chunk in arriving]
    x, v, updates, total = project_updates(plan, rates, part, rest, arriving, early, groups)
    if plan.ringed:
        while len(late_crossed) < plan.along:
            late_step(total)
        late = [b for pair in zip(late, late_crossed) for b in pair]

    def exchange(blocks):
        return lax.all_to_all(
            blocks, "tm", split_axis=0, concat_axis=0, tiled=True,
            axis_index_groups=plan.groups(),
        )

    share = updates.shape[1] // plan.chips
    arrived = exchange(total)
    attended = [attend(plan, 0, block_lists, rates, x, v, late, updates)]
    arrived, attended = lax.optimization_barrier((arrived, attended))
    states = scan_states(plan, arrived, share)
    x, states = lax.optimization_barrier((x, states))
    if plan.merge == 2:
        attended.append(attend(plan, 1, block_lists, rates, x, v, late, updates))
    state = exchange(states).reshape(-1, LANES)
    ids, attended = lax.optimization_barrier((ids, attended))
    back = back_tokens(ids, groups)

    bases, readers = ([a[i] for a in attended] for i in range(2))
    mixed = mix(plan, rates, bases, readers, state, back, groups)
    features = [
        mixed[0] if s == 0 and k == 0 else plan.to_peer(mixed[s * plan.peers + k], k, s == 1)
        for s in range(plan.merge)
        for k in range(plan.peers)
    ]
    return project_out(plan, out_weight, features)[None]


def solution(mesh):
    return jax.shard_map(
        body,
        mesh=mesh,
        in_specs=(P("tm", "head", None), P("tm", "head"), P(), P(), P(), P("tm", "head", None)),
        out_specs=P("tm", "head", None),
        check_vma=False,
    )
```

```python
import functools
import math

import jax
import jax.numpy as jnp
from jax import lax
from jax.experimental import pallas as pl
from jax.experimental.pallas import tpu as pltpu
from jax.sharding import PartitionSpec as P

HD = 64
N = 64
LANES = 2 * HD
PIECES = 5
EARLY = (2, 3)
LATE = (0, 1, 4)

epsilon = 1e-06

vmem = pl.BlockSpec(memory_space=pltpu.VMEM)
smem = pl.BlockSpec(memory_space=pltpu.SMEM)

f32 = jnp.float32
bf16 = jnp.bfloat16


def params(mib=16):
    return pltpu.CompilerParams(vmem_limit_bytes=mib << 20)


def cost(flops, nbytes, transcendentals=0):
    return pl.CostEstimate(
        flops=int(flops), bytes_accessed=int(nbytes), transcendentals=int(transcendentals)
    )


def first_half(shape):
    return lax.broadcasted_iota(jnp.int32, shape, len(shape) - 1) < HD


class Plan:
    def __init__(self, frames, peers, heads_here):
        self.merge = 2 if frames % 2 == 0 and heads_here % 4 == 0 else 1
        self.frames, self.peers = frames, peers
        self.heads = heads_here // self.merge
        self.pairs = self.heads // 2
        self.chips = frames // self.merge
        self.across = 2 if self.chips % 2 == 0 else 1
        self.along = self.chips // self.across
        self.ringed = self.across == 2 and self.along <= 8

    def core(self):
        return lax.rem(lax.axis_index("tm"), self.merge)

    def chip(self):
        return lax.div(lax.axis_index("tm"), self.merge)

    def swap(self, block):
        return lax.ppermute(block, "tm", [(t, t ^ 1) for t in range(self.frames)])

    def round(self, block):
        a, b, c = self.along, self.across, self.merge
        pairs = [(t, (t + b * c) % (a * b * c)) for t in range(self.frames)]
        return lax.ppermute(block, "tm", pairs)

    def cross(self, block):
        c = self.merge
        pairs = [(t, (t // c ^ 1) * c + t % c) for t in range(self.frames)]
        return lax.ppermute(block, "tm", pairs)

    def places(self, refs):
        if len(refs) == 1:
            return [(refs[0], slice(None))]
        rows = refs[0].shape[0]
        a, b = lax.div(self.chip(), self.across), lax.rem(self.chip(), self.across)
        made = []
        for i, ref in enumerate(refs):
            k, flip = i // 2, i % 2
            there = lax.rem(a - k + self.along, self.along) * self.across
            at = pl.multiple_of((there + (1 - b if flip else b)) * rows, rows)
            made.append((ref, pl.ds(at, rows)))
        return made

    def to_peer(self, block, k, other):
        if not other:
            pairs = [(j, (j + k) % self.peers) for j in range(self.peers)]
            return lax.ppermute(block, "head", pairs)
        if k == 0:
            return self.swap(block)
        pairs = [
            (t * self.peers + j, (t ^ 1) * self.peers + (j + k) % self.peers)
            for t in range(self.frames)
            for j in range(self.peers)
        ]
        return lax.ppermute(block, ("tm", "head"), pairs)

    def groups(self):
        if self.merge == 1:
            return None
        return [[j * self.merge + c for j in range(self.chips)] for c in range(self.merge)]

    def decay(self, refs, slot, pair, g):
        head = self.core() * self.heads + 2 * pair
        return halves((1, LANES), refs[slot][head, g], refs[slot][head + 1, g])

    def last_decay(self, refs, pair, g):
        if self.merge == 1:
            return self.decay(refs, 0, pair, g)
        one, two = (self.decay(refs, slot, pair, g) for slot in range(2))
        return jnp.where(self.core() == 0, two, one)


def halves(shape, one, two):
    return jnp.where(first_half(shape), one, two)


def reorder_kernel(plan, *refs):
    w_refs, out_refs = refs[:-2], refs[-2:]
    rows = w_refs[0].shape[0]
    width = plan.heads * PIECES * HD
    first = plan.core() == 0

    def chosen(ref, at):
        one = ref[:, at : at + HD]
        if plan.merge == 1:
            return one
        return jnp.where(first, one, ref[:, width + at : width + at + HD])

    early = [(p, i) for i in EARLY for p in range(plan.pairs)]
    late = [(p, i) for p in range(plan.pairs) for i in LATE]
    for out_ref, order in zip(out_refs, (early, late)):
        for n, (p, i) in enumerate(order):
            blocks = []
            for ref in w_refs:
                one, two = (chosen(ref, ((2 * p + h) * PIECES + i) * HD) for h in range(2))
                blocks.append(jnp.concatenate([one, two], axis=1))
            for s, block in enumerate(blocks):
                if plan.merge == 2:
                    block = jnp.where(first, block, blocks[1 - s])
                out_ref[s * rows : (s + 1) * rows, n * LANES : (n + 1) * LANES] = block


def reorder(plan, weights):
    rows = weights[0].shape[0]
    return pl.pallas_call(
        functools.partial(reorder_kernel, plan),
        out_shape=tuple(
            jax.ShapeDtypeStruct((plan.merge * rows, plan.heads * len(kinds) * HD), bf16)
            for kinds in (EARLY, LATE)
        ),
        compiler_params=params(),
        cost_estimate=cost(0, 4 * weights[0].size),
        name="reorder",
    )(*weights)


def normalise(part, out, at):
    step = min(128, part.shape[0])

    def norm(c, _):
        start = pl.multiple_of(c * step, step)
        wide = part[pl.ds(start, step), :].astype(f32)
        scale = lax.rsqrt(jnp.mean(wide * wide, axis=-1, keepdims=True) + epsilon)
        out[pl.ds(at + start, step), :] = (wide * scale).astype(bf16)
        return 0

    lax.fori_loop(0, part.shape[0] // step, norm, 0)


def pick_kernel(groups, ids_ref, own_ref, rest_ref):
    tokens = ids_ref.shape[1]
    local = own_ref.shape[1]
    block = tokens // groups
    step = 128
    label = lax.broadcasted_iota(jnp.int32, (groups, tokens), 0)
    held = label == ids_ref[...]
    held_bf = jnp.where(held, 1.0, 0.0).astype(bf16)
    counts = []
    for c in range(tokens // 256):
        before = lax.broadcasted_iota(jnp.int32, (tokens, 256), 0) < (
            lax.broadcasted_iota(jnp.int32, (tokens, 256), 1) + c * 256
        )
        counts.append(
            jnp.dot(held_bf, jnp.where(before, 1.0, 0.0).astype(bf16), preferred_element_type=f32)
        )
    count = jnp.concatenate(counts, axis=1)
    rank = jnp.sum(
        jnp.where(held, count + (label * block).astype(f32), 0.0), axis=0, keepdims=True
    ).astype(jnp.int32)

    def place(c, _):
        at = pl.multiple_of(c * step, step)
        pick = (lax.broadcasted_iota(jnp.int32, (step, tokens), 0) + at) == rank
        pick = jnp.where(pick, 1.0, 0.0).astype(bf16)
        own_ref[pl.ds(at, step), :] = pick[:, :local]
        rest_ref[pl.ds(at, step), :] = pick[:, local:]
        return 0

    lax.fori_loop(0, tokens // step, place, 0)


def pick_tokens(ids, local, groups):
    tokens = ids.shape[0]
    return pl.pallas_call(
        functools.partial(pick_kernel, groups),
        out_shape=(
            jax.ShapeDtypeStruct((tokens, local), bf16),
            jax.ShapeDtypeStruct((tokens, tokens - local), bf16),
        ),
        compiler_params=params(),
        cost_estimate=cost(32 * tokens * tokens, 2 * tokens * tokens),
        name="pick_tokens",
    )(ids.reshape(1, tokens))


def back_kernel(groups, ids_ref, back_ref):
    tokens = back_ref.shape[0]
    block = tokens // groups
    step = 128
    lane = lax.broadcasted_iota(jnp.int32, (tokens, 128), 1)
    held = jnp.where(lane == ids_ref[...], 1.0, 0.0).astype(bf16)

    def place(c, _):
        at = pl.multiple_of(c * step, step)
        before = lax.broadcasted_iota(jnp.int32, (step, tokens), 1) < (
            lax.broadcasted_iota(jnp.int32, (step, tokens), 0) + at
        )
        count = jnp.dot(
            jnp.where(before, 1.0, 0.0).astype(bf16), held, preferred_element_type=f32
        )
        lane = lax.broadcasted_iota(jnp.int32, (step, 128), 1)
        mine = lane == ids_ref[pl.ds(at, step), :]
        rank = jnp.sum(
            jnp.where(mine, count + (lane * block).astype(f32), 0.0), axis=1, keepdims=True
        ).astype(jnp.int32)
        pick = lax.broadcasted_iota(jnp.int32, (step, tokens), 1) == rank
        back_ref[pl.ds(at, step), :] = jnp.where(pick, 1.0, 0.0).astype(bf16)
        return 0

    lax.fori_loop(0, tokens // step, place, 0)


def back_tokens(ids, groups):
    tokens = ids.shape[0]
    return pl.pallas_call(
        functools.partial(back_kernel, groups),
        out_shape=jax.ShapeDtypeStruct((tokens, tokens), bf16),
        compiler_params=params(),
        cost_estimate=cost(256 * tokens * tokens, 2 * tokens * tokens),
        name="back_tokens",
    )(ids.reshape(tokens, 1))


def place_kernel(merge, pick_ref, *refs):
    frame_refs, x_ref, normed = refs[:merge], refs[-2], refs[-1]
    tokens = pick_ref.shape[0]
    step = 256
    for s in range(merge):
        normalise(frame_refs[s], normed.at[s], 0)
        for at in range(0, tokens, step):
            x_ref[s * tokens + at : s * tokens + at + step, :] = jnp.dot(
                pick_ref[at : at + step, :], normed[s], preferred_element_type=f32
            ).astype(bf16)


def place_tokens(plan, pick, frames):
    tokens, count = pick.shape
    width = frames[0].shape[1]
    every = plan.merge * tokens
    return pl.pallas_call(
        functools.partial(place_kernel, plan.merge),
        out_shape=jax.ShapeDtypeStruct((every, width), bf16),
        scratch_shapes=[pltpu.VMEM((plan.merge, count, width), bf16)],
        compiler_params=params(),
        cost_estimate=cost(4 * every * count * width, 6 * tokens * width),
        name="place_tokens",
    )(pick, *frames)


def update_kernel(plan, groups, parts, *refs):
    decay_refs, refs = refs[: plan.merge], refs[plan.merge :]
    part_ref, rest_ref, refs = refs[0], refs[1], refs[2:]
    frame_refs, refs = refs[: plan.merge * parts], refs[plan.merge * parts :]
    w_refs, refs = refs[:-7], refs[-7:]
    x_ref, v_ref, u_ref, total_ref, normed, w, turned = refs
    tokens = rest_ref.shape[0]
    block = tokens // groups
    step = 256
    here = step // block
    cols = plan.pairs * LANES

    for ref, rows in plan.places(w_refs):
        w[rows, :] = ref[:, :cols]
        turned[rows, :] = ref[:, cols:]
    maps = jnp.concatenate(
        [
            turned[at : at + LANES, :].astype(f32).T.astype(bf16)
            for at in range(0, turned.shape[0], LANES)
        ],
        axis=1,
    )
    lane = lax.div(lax.broadcasted_iota(jnp.int32, (LANES, step), 1), block)

    for s in range(plan.merge):
        at = 0
        for ref in frame_refs[s * parts : (s + 1) * parts]:
            normalise(ref, normed.at[s], at)
            at += ref.shape[0]
        for at in range(0, tokens, step):
            there = slice(s * tokens + at, s * tokens + at + step)
            more = jnp.dot(rest_ref[at : at + step, :], normed[s], preferred_element_type=f32)
            placed = part_ref[there, :] + more.astype(bf16)
            x_ref[there, :] = placed
            values = jnp.dot(placed, w[...], preferred_element_type=f32).astype(bf16)
            v_ref[there, :] = values
            b = lax.dot_general(
                maps, placed, (((1,), (1,)), ((), ())), preferred_element_type=f32
            )
            for p in range(plan.pairs):
                mine = b[p * LANES : (p + 1) * LANES]
                wide = jnp.concatenate(
                    [jnp.where(lane == i, mine, 0.0).astype(bf16) for i in range(here)], axis=0
                )
                outer = jnp.dot(
                    wide, values[:, p * LANES : (p + 1) * LANES], preferred_element_type=f32
                )
                for i in range(here):
                    m = outer[i * 2 * N : (i + 1) * 2 * N]
                    row = ((at // block + i) * plan.pairs + p) * N
                    u_ref[s, row : row + N, :] = halves((N, LANES), m[:N], m[N:])

    peers = total_ref.shape[0]
    share = u_ref.shape[1] // peers
    items = max(1, share // N)
    size = min(N, share)
    first = plan.core() == 0
    for d in range(peers):
        for i in range(items):
            row = d * share + i * N
            p, g = row // N % plan.pairs, row // N // plan.pairs
            last = plan.last_decay(decay_refs, p, g)
            total = u_ref[plan.merge - 1, row : row + size, :]
            product = last
            if plan.merge == 2:
                before = u_ref[0, row : row + size, :]
                total = jnp.where(first, last, 1.0) * before + jnp.where(first, 1.0, last) * total
                product = plan.decay(decay_refs, 0, p, g) * plan.decay(decay_refs, 1, p, g)
            total_ref[d, i * size : (i + 1) * size, :] = total.astype(bf16)
            for n in range(3):
                piece = product.astype(bf16)
                at = share + n * items + i
                total_ref[d, at : at + 1, :] = piece
                product = product - piece.astype(f32)


def share_rows(share):
    return share + 16 * -(-3 * max(1, share // N) // 16)


def project_updates(plan, decays, part, rest, frames, weights, groups):
    every, width = part.shape
    tokens, count = rest.shape
    cols = plan.pairs * LANES
    rows = plan.pairs * groups * N
    share = rows // plan.chips
    return pl.pallas_call(
        functools.partial(update_kernel, plan, groups, len(frames) // plan.merge),
        in_specs=[smem] * plan.merge + [vmem] * (2 + len(frames) + len(weights)),
        out_shape=(
            jax.ShapeDtypeStruct((every, width), bf16),
            jax.ShapeDtypeStruct((every, cols), bf16),
            jax.ShapeDtypeStruct((plan.merge, rows, LANES), f32),
            jax.ShapeDtypeStruct((plan.chips, share_rows(share), LANES), bf16),
        ),
        scratch_shapes=[
            pltpu.VMEM((plan.merge, count, width), bf16),
            pltpu.VMEM((width, cols), bf16),
            pltpu.VMEM((width, cols), bf16),
        ],
        compiler_params=params(),
        cost_estimate=cost(4 * every * width * (2 * cols + count), 6 * every * width),
        name="project_updates",
    )(*decays, part, rest, *frames, *weights)


def scan_kernel(plan, u_ref, s_ref):
    share = s_ref.shape[1]
    size = min(share, N)
    items = share // size
    for i in range(items):
        at = slice(i * size, (i + 1) * size)
        state = jnp.zeros((size, LANES), f32)
        for j in range(plan.chips):
            s_ref[j, at, :] = state.astype(bf16)
            decay = jnp.zeros((1, LANES), f32)
            for n in range(3):
                row = share + n * items + i
                decay = decay + u_ref[j, row : row + 1, :].astype(f32)
            state = decay * state + u_ref[j, at, :].astype(f32)


def scan_states(plan, update, share):
    return pl.pallas_call(
        functools.partial(scan_kernel, plan),
        out_shape=jax.ShapeDtypeStruct((plan.chips, share, LANES), bf16),
        compiler_params=params(),
        cost_estimate=cost(2 * update.size, 4 * update.size),
        name="scan_states",
    )(update)


def attend_kernel(plan, slot, *refs):
    lists_ref, refs = refs[0], refs[1:]
    decay_refs, refs = refs[: plan.merge], refs[plan.merge :]
    x_ref, v_ref, u_ref, w_refs, refs = refs[0], refs[1], refs[2], refs[3:-7], refs[-7:]
    a, c_ref, w, q_ref, k_ref, wide_v, e_ref = refs
    tokens = a.shape[0]
    groups, chosen = lists_ref.shape
    block = tokens // groups
    step = 256
    per = step // block
    first_row = slot * tokens
    for ref, rows in plan.places(w_refs):
        w[rows, :] = ref[...]

    same = lax.div(lax.broadcasted_iota(jnp.int32, (2 * LANES, 2 * LANES), 0), HD) == lax.div(
        lax.broadcasted_iota(jnp.int32, (2 * LANES, 2 * LANES), 1), HD
    )
    same = jnp.where(same, 1.0, 0.0).astype(bf16)

    def head_norm(values):
        square = values * values
        high = square.astype(bf16)
        low = (square - high.astype(f32)).astype(bf16)
        total = jnp.dot(high, same, preferred_element_type=f32)
        total = total + jnp.dot(low, same, preferred_element_type=f32)
        return values * lax.rsqrt(total * (1.0 / HD) + epsilon)

    half = first_half((step, LANES))
    for at in range(0, tokens, step):
        rows = slice(at, at + step)
        mine = slice(first_row + at, first_row + at + step)
        every = jnp.dot(x_ref[mine, :], w[...], preferred_element_type=f32).astype(bf16)
        for p in range(plan.pairs):
            cols = slice(p * LANES, (p + 1) * LANES)
            first = 3 * p * LANES
            c_ref[rows, cols] = every[:, first + 2 * LANES : first + 3 * LANES]
            both = head_norm(every[:, first : first + 2 * LANES].astype(f32))
            k_ref[p, rows, :] = both[:, LANES:].astype(bf16)
            q = both[:, :LANES]
            one = jnp.where(half, q, 0.0).astype(bf16)
            two = jnp.where(half, 0.0, q).astype(bf16)
            for i in range(per):
                part = slice(i * block, (i + 1) * block)
                q_ref[p, at // block + i] = jnp.concatenate([one[part], two[part]], axis=0)
    for p in range(plan.pairs):
        wide_v[p, :, :LANES] = v_ref[first_row : first_row + tokens, p * LANES : (p + 1) * LANES]
        wide_v[p, :, LANES:] = jnp.ones((tokens, LANES), bf16)

    scale = math.log2(math.e) / math.sqrt(HD)
    starts = [
        [pl.multiple_of(lists_ref[g, j] * block, block) for j in range(chosen)]
        for g in range(groups)
    ]
    for g in range(groups):
        for p in range(plan.pairs):
            keys = jnp.concatenate([k_ref[p, pl.ds(s, block), :] for s in starts[g]], axis=0)
            score = lax.dot_general(
                q_ref[p, g], keys, (((1,), (1,)), ((), ())), preferred_element_type=f32
            )
            e_ref[p, g] = jnp.exp2(score * scale).astype(bf16)
    for g in range(groups):
        rows = slice(g * block, (g + 1) * block)
        for p in range(plan.pairs):
            cols = slice(p * LANES, (p + 1) * LANES)
            values = jnp.concatenate([wide_v[p, pl.ds(s, block), :] for s in starts[g]], axis=0)
            both = jnp.dot(e_ref[p, g], values, preferred_element_type=f32)
            both = both[:, :LANES] / both[:, LANES:]
            a[rows, cols] = halves((block, LANES), both[:block], both[block:])
    for g in range(groups):
        rows = slice(g * block, (g + 1) * block)
        for p in range(plan.pairs):
            cols = slice(p * LANES, (p + 1) * LANES)
            items = slice((g * plan.pairs + p) * N, (g * plan.pairs + p + 1) * N)
            state = u_ref[slot, items, :]
            if plan.merge == 2:
                last = plan.last_decay(decay_refs, p, g)
                last = jnp.where(plan.core() == slot, 0.0, last)
                state = state + last * u_ref[1 - slot, items, :]
            a[rows, cols] = a[rows, cols] + read_out(c_ref[rows, cols], state, block)


def attend(plan, slot, lists, decays, x, v, weights, updates):
    every, width = x.shape
    groups, chosen = lists.shape
    tokens = every // plan.merge
    block = tokens // groups
    cols = plan.pairs * LANES
    return pl.pallas_call(
        functools.partial(attend_kernel, plan, slot),
        in_specs=[smem] * (1 + plan.merge) + [vmem] * (3 + len(weights)),
        scratch_shapes=[
            pltpu.VMEM((width, 3 * cols), bf16),
            pltpu.VMEM((plan.pairs, groups, 2 * block, LANES), bf16),
            pltpu.VMEM((plan.pairs, tokens, LANES), bf16),
            pltpu.VMEM((plan.pairs, tokens, 2 * LANES), bf16),
            pltpu.VMEM((plan.pairs, groups, 2 * block, chosen * block), bf16),
        ],
        out_shape=(
            jax.ShapeDtypeStruct((tokens, cols), f32),
            jax.ShapeDtypeStruct((tokens, cols), bf16),
        ),
        compiler_params=params(),
        cost_estimate=cost(
            6 * tokens * width * 3 * cols,
            4 * (tokens * width + 5 * width * cols + updates.size),
            2 * plan.pairs * tokens * chosen * block,
        ),
        name="attend",
    )(lists, *decays, x, v, updates, *weights)


def read_out(readers, state, block):
    half = first_half(state.shape)
    wide = jnp.concatenate([jnp.where(half, state, 0.0), jnp.where(half, 0.0, state)], axis=0)
    return jnp.dot(readers, wide.astype(bf16), preferred_element_type=f32) * (
        1.0 / (N * math.sqrt(block))
    )


def mix_kernel(plan, groups, *refs):
    decay_refs, refs = refs[: plan.merge], refs[plan.merge :]
    a_refs, refs = refs[: plan.merge], refs[plan.merge :]
    c_refs, refs = refs[: plan.merge], refs[plan.merge :]
    s_ref, back_ref, out_refs, mixed = refs[0], refs[1], refs[2:-1], refs[-1]
    tokens = back_ref.shape[0]
    block = tokens // groups
    width = a_refs[0].shape[1]
    first = plan.core() == 0
    for g in range(groups):
        rows = slice(g * block, (g + 1) * block)
        for p in range(plan.pairs):
            cols = slice(p * LANES, (p + 1) * LANES)
            at = (g * plan.pairs + p) * N
            readers = jnp.concatenate([c[rows, cols] for c in c_refs], axis=0)
            read = read_out(readers, s_ref[at : at + N, :].astype(f32), block)
            decays = [plan.decay(decay_refs, s, p, g) for s in range(plan.merge)]
            if plan.merge == 2:
                both = decays[0] * decays[1]
                decays = [jnp.where(first, decays[0], both), jnp.where(first, both, decays[1])]
            for s in range(plan.merge):
                there = slice(s * width + p * LANES, s * width + (p + 1) * LANES)
                mixed[rows, there] = (
                    a_refs[s][rows, cols] + decays[s] * read[s * block : (s + 1) * block]
                ).astype(bf16)
    local = tokens // plan.peers
    for k in range(plan.peers):
        placed = jnp.dot(
            back_ref[k * local : (k + 1) * local, :], mixed[...], preferred_element_type=f32
        ).astype(bf16)
        for s in range(plan.merge):
            out_refs[s * plan.peers + k][...] = placed[:, s * width : (s + 1) * width]


def mix(plan, decays, attended, readers, state, back, groups):
    tokens = back.shape[0]
    width = attended[0].shape[1]
    count = plan.merge * plan.peers
    return pl.pallas_call(
        functools.partial(mix_kernel, plan, groups),
        in_specs=[smem] * plan.merge + [vmem] * (2 * plan.merge + 2),
        out_shape=(jax.ShapeDtypeStruct((tokens // plan.peers, width), bf16),) * count,
        scratch_shapes=[pltpu.VMEM((tokens, plan.merge * width), bf16)],
        compiler_params=params(),
        cost_estimate=cost(4 * tokens * tokens * width, 2 * tokens * tokens + 16 * tokens * width),
        name="mix",
    )(*decays, *attended, *readers, state, back)


def out_kernel(plan, w_ref, *refs):
    part_refs, out_ref = refs[:-1], refs[-1]
    depth = part_refs[0].shape[1]
    core, me = plan.core(), lax.axis_index("head")
    total = None
    for s in range(plan.merge):
        for k in range(plan.peers):
            owner = lax.rem(me - k + plan.peers, plan.peers) * plan.merge
            owner = owner + (core if s == 0 else 1 - core)
            rows = pl.ds(pl.multiple_of(owner * depth, depth), depth)
            term = jnp.dot(
                part_refs[s * plan.peers + k][...], w_ref[rows, :], preferred_element_type=f32
            )
            total = term if total is None else total + term
    out_ref[...] = total.astype(bf16)


def project_out(plan, w, parts):
    local = parts[0].shape[0]
    width = w.shape[1]
    return pl.pallas_call(
        functools.partial(out_kernel, plan),
        out_shape=jax.ShapeDtypeStruct((local, width), bf16),
        compiler_params=params(),
        cost_estimate=cost(2 * local * w.size, 2 * (w.size + 2 * local * width)),
        name="project_out",
    )(w, *parts)


def body(frames_in, in_weight, out_weight, block_ids, block_lists, decays):
    local_tokens = frames_in.shape[1]
    heads_here = decays.shape[1]
    groups = block_lists.shape[0]
    me = lax.axis_index("head")
    plan = Plan(lax.axis_size("tm"), lax.axis_size("head"), heads_here)

    own = frames_in[0]
    arriving = [plan.to_peer(own, plan.peers - k, False) for k in range(1, plan.peers)]
    owns = [own] + [plan.swap(own)] * (plan.merge - 1)
    rates = [decays[0]] + [plan.swap(decays[0])] * (plan.merge - 1)
    blocks = reorder(plan, [in_weight] + [plan.swap(in_weight)] * (plan.merge - 1))

    ids = jnp.roll(block_ids, -me * local_tokens)
    ids, rates = lax.optimization_barrier((ids, rates))
    pick, rest = pick_tokens(ids, local_tokens, groups)
    if plan.ringed:
        def step(block, with_):
            return lax.optimization_barrier((plan.round(block), plan.cross(block), with_))[:2]

        early, late, crossed = [blocks[0]], [blocks[1]], [[], []]
        part = None
        for k in range(plan.along - 1):
            passed, across = step(late[-1], [])
            late.append(passed)
            crossed[1].append(across)
            if part is None:
                pick, _ = lax.optimization_barrier((pick, passed))
                part = place_tokens(plan, pick, owns)
            beside = [[pick], [part], [late[-1]]][min(k, 2)]
            passed, across = step(early[-1], beside)
            early.append(passed)
            crossed[0].append(across)
        crossed[0].append(plan.cross(early[-1]))
        crossed[1].append(plan.cross(late[-1]))
        arriving, _ = lax.optimization_barrier((arriving, crossed[0][-1]))
        rest, _ = lax.optimization_barrier((rest, late[-1]))
        early, late = (
            [b for pair in zip(blocks, across) for b in pair]
            for blocks, across in zip((early, late), crossed)
        )
        if part is None:
            part = place_tokens(plan, pick, owns)
    else:
        part = place_tokens(plan, pick, owns)
        early, late = (
            [lax.all_gather(b, "tm", axis=0, tiled=True, axis_index_groups=plan.groups())]
            for b in blocks
        )
    if plan.merge == 2:
        arriving = arriving + [plan.swap(chunk) for chunk in arriving]
    x, v, updates, total = project_updates(plan, rates, part, rest, arriving, early, groups)
    def exchange(blocks):
        return lax.all_to_all(
            blocks, "tm", split_axis=0, concat_axis=0, tiled=True,
            axis_index_groups=plan.groups(),
        )

    share = updates.shape[1] // plan.chips
    arrived = exchange(total)
    attended = [attend(plan, 0, block_lists, rates, x, v, late, updates)]
    arrived, attended = lax.optimization_barrier((arrived, attended))
    states = scan_states(plan, arrived, share)
    x, states = lax.optimization_barrier((x, states))
    if plan.merge == 2:
        attended.append(attend(plan, 1, block_lists, rates, x, v, late, updates))
    state = exchange(states).reshape(-1, LANES)
    ids, attended = lax.optimization_barrier((ids, attended))
    back = back_tokens(ids, groups)

    bases, readers = ([a[i] for a in attended] for i in range(2))
    mixed = mix(plan, rates, bases, readers, state, back, groups)
    features = [
        mixed[0] if s == 0 and k == 0 else plan.to_peer(mixed[s * plan.peers + k], k, s == 1)
        for s in range(plan.merge)
        for k in range(plan.peers)
    ]
    return project_out(plan, out_weight, features)[None]


def solution(mesh):
    return jax.shard_map(
        body,
        mesh=mesh,
        in_specs=(P("tm", "head", None), P("tm", "head"), P(), P(), P(), P("tm", "head", None)),
        out_specs=P("tm", "head", None),
        check_vma=False,
    )
```

```python
import functools
import math

import jax
import jax.numpy as jnp
from jax import lax
from jax.experimental import pallas as pl
from jax.experimental.pallas import tpu as pltpu
from jax.sharding import PartitionSpec as P

HD = 64
N = 64
LANES = 2 * HD
PIECES = 5
EARLY = (2, 3)
LATE = (0, 1, 4)

epsilon = 1e-06

vmem = pl.BlockSpec(memory_space=pltpu.VMEM)
smem = pl.BlockSpec(memory_space=pltpu.SMEM)

hbm = pl.BlockSpec(memory_space=pltpu.HBM)

f32 = jnp.float32
bf16 = jnp.bfloat16


def params(mib=16):
    return pltpu.CompilerParams(vmem_limit_bytes=mib << 20)


def cost(flops, nbytes, transcendentals=0):
    return pl.CostEstimate(
        flops=int(flops), bytes_accessed=int(nbytes), transcendentals=int(transcendentals)
    )


def first_half(shape):
    return lax.broadcasted_iota(jnp.int32, shape, len(shape) - 1) < HD


class Plan:
    def __init__(self, frames, peers, heads_here):
        self.merge = 2 if frames % 2 == 0 and heads_here % 4 == 0 else 1
        self.frames, self.peers = frames, peers
        self.heads = heads_here // self.merge
        self.pairs = self.heads // 2
        self.chips = frames // self.merge
        self.across = 2 if self.chips % 2 == 0 else 1
        self.along = self.chips // self.across
        self.ringed = self.across == 2 and self.along <= 8

    def core(self):
        return lax.rem(lax.axis_index("tm"), self.merge)

    def chip(self):
        return lax.div(lax.axis_index("tm"), self.merge)

    def swap(self, block):
        return lax.ppermute(block, "tm", [(t, t ^ 1) for t in range(self.frames)])

    def round(self, block):
        a, b, c = self.along, self.across, self.merge
        pairs = [(t, (t + b * c) % (a * b * c)) for t in range(self.frames)]
        return lax.ppermute(block, "tm", pairs)

    def cross(self, block):
        c = self.merge
        pairs = [(t, (t // c ^ 1) * c + t % c) for t in range(self.frames)]
        return lax.ppermute(block, "tm", pairs)

    def places(self, refs):
        if len(refs) == 1:
            return [(refs[0], slice(None))]
        rows = refs[0].shape[0]
        a, b = lax.div(self.chip(), self.across), lax.rem(self.chip(), self.across)
        made = []
        for i, ref in enumerate(refs):
            k, flip = i // 2, i % 2
            there = lax.rem(a - k + self.along, self.along) * self.across
            at = pl.multiple_of((there + (1 - b if flip else b)) * rows, rows)
            made.append((ref, pl.ds(at, rows)))
        return made

    def to_peer(self, block, k, other):
        if not other:
            pairs = [(j, (j + k) % self.peers) for j in range(self.peers)]
            return lax.ppermute(block, "head", pairs)
        if k == 0:
            return self.swap(block)
        pairs = [
            (t * self.peers + j, (t ^ 1) * self.peers + (j + k) % self.peers)
            for t in range(self.frames)
            for j in range(self.peers)
        ]
        return lax.ppermute(block, ("tm", "head"), pairs)

    def groups(self):
        if self.merge == 1:
            return None
        return [[j * self.merge + c for j in range(self.chips)] for c in range(self.merge)]

    def decay(self, refs, slot, pair, g):
        head = self.core() * self.heads + 2 * pair
        return halves((1, LANES), refs[slot][head, g], refs[slot][head + 1, g])

    def last_decay(self, refs, pair, g):
        if self.merge == 1:
            return self.decay(refs, 0, pair, g)
        one, two = (self.decay(refs, slot, pair, g) for slot in range(2))
        return jnp.where(self.core() == 0, two, one)


class Copies:
    room = 48

    def __init__(self, sems):
        self.sems, self.count = sems, 0

    def start(self, src, dst):
        copy = pltpu.make_async_copy(src, dst, self.sems.at[self.count])
        copy.start()
        self.count += 1
        return copy

    @staticmethod
    def scratch():
        return pltpu.SemaphoreType.DMA((Copies.room,))


def finish(copies):
    for copy in copies:
        copy.wait()


def halves(shape, one, two):
    return jnp.where(first_half(shape), one, two)


def reorder_kernel(plan, *refs):
    w_refs, out_refs = refs[:-2], refs[-2:]
    rows = w_refs[0].shape[0]
    width = plan.heads * PIECES * HD
    first = plan.core() == 0

    def chosen(ref, at):
        one = ref[:, at : at + HD]
        if plan.merge == 1:
            return one
        return jnp.where(first, one, ref[:, width + at : width + at + HD])

    early = [(p, i) for i in EARLY for p in range(plan.pairs)]
    late = [(p, i) for p in range(plan.pairs) for i in LATE]
    for out_ref, order in zip(out_refs, (early, late)):
        for n, (p, i) in enumerate(order):
            blocks = []
            for ref in w_refs:
                one, two = (chosen(ref, ((2 * p + h) * PIECES + i) * HD) for h in range(2))
                blocks.append(jnp.concatenate([one, two], axis=1))
            for s, block in enumerate(blocks):
                if plan.merge == 2:
                    block = jnp.where(first, block, blocks[1 - s])
                out_ref[s * rows : (s + 1) * rows, n * LANES : (n + 1) * LANES] = block


def reorder(plan, weights):
    rows = weights[0].shape[0]
    return pl.pallas_call(
        functools.partial(reorder_kernel, plan),
        out_shape=tuple(
            jax.ShapeDtypeStruct((plan.merge * rows, plan.heads * len(kinds) * HD), bf16)
            for kinds in (EARLY, LATE)
        ),
        compiler_params=params(),
        cost_estimate=cost(0, 4 * weights[0].size),
        name="reorder",
    )(*weights)


def normalise(part, out, at):
    step = min(128, part.shape[0])

    def norm(c, _):
        start = pl.multiple_of(c * step, step)
        wide = part[pl.ds(start, step), :].astype(f32)
        scale = lax.rsqrt(jnp.mean(wide * wide, axis=-1, keepdims=True) + epsilon)
        out[pl.ds(at + start, step), :] = (wide * scale).astype(bf16)
        return 0

    lax.fori_loop(0, part.shape[0] // step, norm, 0)


def rank_kernel(groups, ids_ref, row_ref, col_ref):
    tokens = ids_ref.shape[1]
    block = tokens // groups
    label = lax.broadcasted_iota(jnp.int32, (groups, tokens), 0)
    held = label == ids_ref[...]
    held_bf = jnp.where(held, 1.0, 0.0).astype(bf16)
    counts = []
    for c in range(tokens // 256):
        before = lax.broadcasted_iota(jnp.int32, (tokens, 256), 0) < (
            lax.broadcasted_iota(jnp.int32, (tokens, 256), 1) + c * 256
        )
        counts.append(
            jnp.dot(held_bf, jnp.where(before, 1.0, 0.0).astype(bf16), preferred_element_type=f32)
        )
    count = jnp.concatenate(counts, axis=1)
    rank = jnp.sum(
        jnp.where(held, count + (label * block).astype(f32), 0.0), axis=0, keepdims=True
    )
    row_ref[...] = rank
    for at in range(0, tokens, LANES):
        wide = jnp.broadcast_to(rank[:, at : at + LANES], (LANES, LANES))
        col_ref[at : at + LANES, :] = wide.T


def rank_tokens(ids, groups):
    tokens = ids.shape[0]
    return pl.pallas_call(
        functools.partial(rank_kernel, groups),
        out_shape=(
            jax.ShapeDtypeStruct((1, tokens), f32),
            jax.ShapeDtypeStruct((tokens, LANES), f32),
        ),
        compiler_params=params(),
        cost_estimate=cost(0, 4 * tokens),
        name="rank_tokens",
    )(ids.reshape(1, tokens))


def picks(rank, at, rows):
    places = lax.broadcasted_iota(jnp.int32, (rows, rank.shape[1]), 0) + at
    return jnp.where(places.astype(f32) == rank, 1.0, 0.0).astype(bf16)


def place_kernel(merge, rank_ref, *refs):
    frame_refs, x_ref, normed = refs[:merge], refs[-2], refs[-1]
    tokens = rank_ref.shape[1]
    local = frame_refs[0].shape[0]
    step = 256
    for s in range(merge):
        normalise(frame_refs[s], normed.at[s], 0)
    for at in range(0, tokens, step):
        pick = picks(rank_ref[:, :local], at, step)
        for s in range(merge):
            x_ref[s * tokens + at : s * tokens + at + step, :] = jnp.dot(
                pick, normed[s], preferred_element_type=f32
            ).astype(bf16)


def place_tokens(plan, rank, frames):
    tokens = rank.shape[1]
    local, width = frames[0].shape
    return pl.pallas_call(
        functools.partial(place_kernel, plan.merge),
        out_shape=jax.ShapeDtypeStruct((plan.merge * tokens, width), bf16),
        scratch_shapes=[pltpu.VMEM((plan.merge, local, width), bf16)],
        compiler_params=params(),
        cost_estimate=cost(0, 4 * tokens),
        name="place_tokens",
    )(rank, *frames)


def update_kernel(plan, groups, parts, *refs):
    decay_refs, refs = refs[: plan.merge], refs[plan.merge :]
    rank_ref, part_ref, refs = refs[0], refs[1], refs[2:]
    frame_refs, refs = refs[: plan.merge * parts], refs[plan.merge * parts :]
    w_refs, refs = refs[:-13], refs[-13:]
    x_out, v_out, local_out, total_ref, raw, normed, w, turned, x, v, u, left, sems = refs
    copies = Copies(sems)
    tokens = rank_ref.shape[1]
    count = raw.shape[1]
    block = tokens // groups
    step = 256
    here = step // block
    cols = plan.pairs * LANES

    arriving, partly, weights = [], [], []
    for s in range(plan.merge):
        at = 0
        for ref in frame_refs[s * parts : (s + 1) * parts]:
            size = ref.shape[0]
            arriving.append(copies.start(ref, raw.at[s, at : at + size, :]))
            at += size
        if s == 0:
            for ref, rows in plan.places(w_refs):
                weights.append(copies.start(ref.at[:, cols:], turned.at[rows]))
                weights.append(copies.start(ref.at[:, :cols], w.at[rows]))
        for at in range(s * tokens, (s + 1) * tokens, step):
            there = slice(at, at + step)
            partly.append(copies.start(part_ref.at[there], x.at[there]))

    lane = lax.div(lax.broadcasted_iota(jnp.int32, (LANES, step), 1), block)
    leaving = []
    for s in range(plan.merge):
        finish(arriving[s * parts : (s + 1) * parts])
        normalise(raw.at[s], normed, 0)
        if s == 0:
            finish(weights)
            maps = jnp.concatenate(
                [
                    turned[at : at + LANES, :].astype(f32).T.astype(bf16)
                    for at in range(0, turned.shape[0], LANES)
                ],
                axis=1,
            )
        for at in range(0, tokens, step):
            there = slice(s * tokens + at, s * tokens + at + step)
            pick = picks(rank_ref[:, tokens - count :], at, step)
            more = jnp.dot(pick, normed[...], preferred_element_type=f32)
            partly[there.start // step].wait()
            placed = x[there, :] + more.astype(bf16)
            x[there, :] = placed
            leaving.append(copies.start(x.at[there], x_out.at[there]))
            values = jnp.dot(placed, w[...], preferred_element_type=f32).astype(bf16)
            v[there, :] = values
            b = lax.dot_general(
                maps, placed, (((1,), (1,)), ((), ())), preferred_element_type=f32
            )
            for p in range(plan.pairs):
                mine = b[p * LANES : (p + 1) * LANES]
                wide = jnp.concatenate(
                    [jnp.where(lane == i, mine, 0.0).astype(bf16) for i in range(here)], axis=0
                )
                outer = jnp.dot(
                    wide, values[:, p * LANES : (p + 1) * LANES], preferred_element_type=f32
                )
                for i in range(here):
                    m = outer[i * 2 * N : (i + 1) * 2 * N]
                    row = ((at // block + i) * plan.pairs + p) * N
                    u[s, row : row + N, :] = halves((N, LANES), m[:N], m[N:])
        mine = slice(s * tokens, (s + 1) * tokens)
        leaving.append(copies.start(v.at[mine], v_out.at[mine]))

    peers = total_ref.shape[0]
    share = u.shape[1] // peers
    items = max(1, share // N)
    size = min(N, share)
    first = plan.core() == 0
    for d in range(peers):
        for i in range(items):
            row = d * share + i * N
            rows = slice(row, row + size)
            p, g = row // N % plan.pairs, row // N // plan.pairs
            product = last = plan.last_decay(decay_refs, p, g)
            if plan.merge == 2:
                one, two = u[0, rows, :], u[1, rows, :]
                one, two = (
                    one + jnp.where(first, 0.0, last) * two,
                    two + jnp.where(first, last, 0.0) * one,
                )
                left[0, rows, :] = one.astype(bf16)
                left[1, rows, :] = two.astype(bf16)
                total = jnp.where(first, two, one)
                product = plan.decay(decay_refs, 0, p, g) * plan.decay(decay_refs, 1, p, g)
            else:
                total = u[0, rows, :]
                left[0, rows, :] = total.astype(bf16)
            total_ref[d, i * size : (i + 1) * size, :] = total.astype(bf16)
            for n in range(3):
                piece = product.astype(bf16)
                at = share + n * items + i
                total_ref[d, at : at + 1, :] = piece
                product = product - piece.astype(f32)
    leaving.append(copies.start(left, local_out))
    finish(leaving)


def share_rows(share):
    return share + 16 * -(-3 * max(1, share // N) // 16)


def project_updates(plan, decays, rank, part, frames, weights, groups):
    every, width = part.shape
    tokens = rank.shape[1]
    count = frames[0].shape[0] * len(frames) // plan.merge
    cols = plan.pairs * LANES
    rows = plan.pairs * groups * N
    share = rows // plan.chips
    return pl.pallas_call(
        functools.partial(update_kernel, plan, groups, len(frames) // plan.merge),
        in_specs=[smem] * plan.merge + [vmem] + [hbm] * (1 + len(frames) + len(weights)),
        out_specs=(hbm,) * 3 + (vmem,),
        out_shape=(
            jax.ShapeDtypeStruct((every, width), bf16),
            jax.ShapeDtypeStruct((every, cols), bf16),
            jax.ShapeDtypeStruct((plan.merge, rows, LANES), bf16),
            jax.ShapeDtypeStruct((plan.chips, share_rows(share), LANES), bf16),
        ),
        scratch_shapes=[
            pltpu.VMEM((plan.merge, count, width), bf16),
            pltpu.VMEM((count, width), bf16),
            pltpu.VMEM((width, cols), bf16),
            pltpu.VMEM((width, cols), bf16),
            pltpu.VMEM((every, width), bf16),
            pltpu.VMEM((every, cols), bf16),
            pltpu.VMEM((plan.merge, rows, LANES), f32),
            pltpu.VMEM((plan.merge, rows, LANES), bf16),
            Copies.scratch(),
        ],
        compiler_params=params(60),
        cost_estimate=cost(4 * every * width * (2 * cols + count), 6 * every * width),
        name="project_updates",
    )(*decays, rank, part, *frames, *weights)


def scan_kernel(plan, u_ref, s_ref):
    share = s_ref.shape[1]
    size = min(share, N)
    items = share // size
    for i in range(items):
        at = slice(i * size, (i + 1) * size)
        state = jnp.zeros((size, LANES), f32)
        for j in range(plan.chips):
            s_ref[j, at, :] = state.astype(bf16)
            decay = jnp.zeros((1, LANES), f32)
            for n in range(3):
                row = share + n * items + i
                decay = decay + u_ref[j, row : row + 1, :].astype(f32)
            state = decay * state + u_ref[j, at, :].astype(f32)


def scan_states(plan, update, share):
    return pl.pallas_call(
        functools.partial(scan_kernel, plan),
        out_shape=jax.ShapeDtypeStruct((plan.chips, share, LANES), bf16),
        compiler_params=params(),
        cost_estimate=cost(2 * update.size, 4 * update.size),
        name="scan_states",
    )(update)


def attend_kernel(plan, slot, *refs):
    lists_ref, x_in, v_in, local_in, refs = refs[0], refs[1], refs[2], refs[3], refs[4:]
    w_refs, refs = refs[:-13], refs[-13:]
    a_out, c_out, x, v, local, w, q_ref, k_ref, wide_v, e_ref, a, c_ref, sems = refs
    copies = Copies(sems)
    tokens = x.shape[0]
    groups, chosen = lists_ref.shape
    block = tokens // groups
    step = 256
    per = step // block

    weights = [copies.start(ref, w.at[rows]) for ref, rows in plan.places(w_refs)]
    arriving = []
    for at in range(0, tokens, step):
        from_ = slice(slot * tokens + at, slot * tokens + at + step)
        arriving.append(copies.start(x_in.at[from_], x.at[at : at + step]))
    mine = slice(slot * tokens, (slot + 1) * tokens)
    later = [copies.start(v_in.at[mine], v), copies.start(local_in.at[slot], local)]

    same = lax.div(lax.broadcasted_iota(jnp.int32, (2 * LANES, 2 * LANES), 0), HD) == lax.div(
        lax.broadcasted_iota(jnp.int32, (2 * LANES, 2 * LANES), 1), HD
    )
    same = jnp.where(same, 1.0, 0.0).astype(bf16)

    def head_norm(values):
        square = values * values
        high = square.astype(bf16)
        low = (square - high.astype(f32)).astype(bf16)
        total = jnp.dot(high, same, preferred_element_type=f32)
        total = total + jnp.dot(low, same, preferred_element_type=f32)
        return values * lax.rsqrt(total * (1.0 / HD) + epsilon)

    half = first_half((step, LANES))
    finish(weights)
    for at in range(0, tokens, step):
        rows = slice(at, at + step)
        arriving[at // step].wait()
        every = jnp.dot(x[rows, :], w[...], preferred_element_type=f32).astype(bf16)
        for p in range(plan.pairs):
            cols = slice(p * LANES, (p + 1) * LANES)
            first = 3 * p * LANES
            c_ref[rows, cols] = every[:, first + 2 * LANES : first + 3 * LANES]
            both = head_norm(every[:, first : first + 2 * LANES].astype(f32))
            k_ref[p, rows, :] = both[:, LANES:].astype(bf16)
            q = both[:, :LANES]
            one = jnp.where(half, q, 0.0).astype(bf16)
            two = jnp.where(half, 0.0, q).astype(bf16)
            for i in range(per):
                part = slice(i * block, (i + 1) * block)
                q_ref[p, at // block + i] = jnp.concatenate([one[part], two[part]], axis=0)
    leaving = [copies.start(c_ref, c_out)]
    finish(later)
    for p in range(plan.pairs):
        wide_v[p, :, :LANES] = v[:, p * LANES : (p + 1) * LANES]
        wide_v[p, :, LANES:] = jnp.ones((tokens, LANES), bf16)

    scale = math.log2(math.e) / math.sqrt(HD)
    starts = [
        [pl.multiple_of(lists_ref[g, j] * block, block) for j in range(chosen)]
        for g in range(groups)
    ]
    for g in range(groups):
        for p in range(plan.pairs):
            keys = jnp.concatenate([k_ref[p, pl.ds(s, block), :] for s in starts[g]], axis=0)
            score = lax.dot_general(
                q_ref[p, g], keys, (((1,), (1,)), ((), ())), preferred_element_type=f32
            )
            e_ref[p, g] = jnp.exp2(score * scale).astype(bf16)
    for g in range(groups):
        rows = slice(g * block, (g + 1) * block)
        for p in range(plan.pairs):
            cols = slice(p * LANES, (p + 1) * LANES)
            values = jnp.concatenate([wide_v[p, pl.ds(s, block), :] for s in starts[g]], axis=0)
            both = jnp.dot(e_ref[p, g], values, preferred_element_type=f32)
            both = both[:, :LANES] / both[:, LANES:]
            a[rows, cols] = halves((block, LANES), both[:block], both[block:])
    for g in range(groups):
        rows = slice(g * block, (g + 1) * block)
        for p in range(plan.pairs):
            cols = slice(p * LANES, (p + 1) * LANES)
            items = slice((g * plan.pairs + p) * N, (g * plan.pairs + p + 1) * N)
            a[rows, cols] = a[rows, cols] + read_out(
                c_ref[rows, cols], local[items, :].astype(f32), block
            )
        if (g + 1) % per == 0:
            done = slice((g + 1 - per) * block, (g + 1) * block)
            leaving.append(copies.start(a.at[done], a_out.at[done]))
    finish(leaving)


def attend(plan, slot, lists, x, v, weights, local):
    every, width = x.shape
    groups, chosen = lists.shape
    tokens = every // plan.merge
    block = tokens // groups
    cols = plan.pairs * LANES
    return pl.pallas_call(
        functools.partial(attend_kernel, plan, slot),
        in_specs=[smem] + [hbm] * (3 + len(weights)),
        out_specs=(hbm,) * 2,
        scratch_shapes=[
            pltpu.VMEM((tokens, width), bf16),
            pltpu.VMEM((tokens, cols), bf16),
            pltpu.VMEM(local.shape[1:], bf16),
            pltpu.VMEM((width, 3 * cols), bf16),
            pltpu.VMEM((plan.pairs, groups, 2 * block, LANES), bf16),
            pltpu.VMEM((plan.pairs, tokens, LANES), bf16),
            pltpu.VMEM((plan.pairs, tokens, 2 * LANES), bf16),
            pltpu.VMEM((plan.pairs, groups, 2 * block, chosen * block), bf16),
            pltpu.VMEM((tokens, cols), f32),
            pltpu.VMEM((tokens, cols), bf16),
            Copies.scratch(),
        ],
        out_shape=(
            jax.ShapeDtypeStruct((tokens, cols), f32),
            jax.ShapeDtypeStruct((tokens, cols), bf16),
        ),
        compiler_params=params(60),
        cost_estimate=cost(
            6 * tokens * width * 3 * cols,
            4 * (tokens * width + 5 * width * cols + local.size),
            2 * plan.pairs * tokens * chosen * block,
        ),
        name="attend",
    )(lists, x, v, local, *weights)


def read_out(readers, state, block):
    half = first_half(state.shape)
    wide = jnp.concatenate([jnp.where(half, state, 0.0), jnp.where(half, 0.0, state)], axis=0)
    return jnp.dot(readers, wide.astype(bf16), preferred_element_type=f32) * (
        1.0 / (N * math.sqrt(block))
    )


def mix_kernel(plan, groups, *refs):
    decay_refs, refs = refs[: plan.merge], refs[plan.merge :]
    a_ins, refs = refs[: plan.merge], refs[plan.merge :]
    c_ins, refs = refs[: plan.merge], refs[plan.merge :]
    s_in, rank_in, refs = refs[0], refs[1], refs[2:]
    out_refs, (a, c, state, rank, mixed, sems) = refs[:-6], refs[-6:]
    copies = Copies(sems)
    tokens = rank.shape[0]
    block = tokens // groups
    width = a.shape[2]
    here = groups // 4
    many = here * plan.pairs * N
    first = plan.core() == 0

    arriving = []
    for i in range(4):
        rows = slice(i * here * block, (i + 1) * here * block)
        items = slice(i * many, (i + 1) * many)
        arriving.append([copies.start(s_in.at[items], state.at[items])])
        for s in range(plan.merge):
            arriving[-1] += [
                copies.start(c_ins[s].at[rows], c.at[s, rows, :]),
                copies.start(a_ins[s].at[rows], a.at[s, rows, :]),
            ]
    ranking = copies.start(rank_in, rank)

    for g in range(groups):
        if g % here == 0:
            finish(arriving[g // here])
        rows = slice(g * block, (g + 1) * block)
        for p in range(plan.pairs):
            cols = slice(p * LANES, (p + 1) * LANES)
            at = (g * plan.pairs + p) * N
            readers = jnp.concatenate([c[s, rows, cols] for s in range(plan.merge)], axis=0)
            read = read_out(readers, state[at : at + N, :].astype(f32), block)
            decays = [plan.decay(decay_refs, s, p, g) for s in range(plan.merge)]
            if plan.merge == 2:
                both = decays[0] * decays[1]
                decays = [jnp.where(first, decays[0], both), jnp.where(first, both, decays[1])]
            for s in range(plan.merge):
                there = slice(s * width + p * LANES, s * width + (p + 1) * LANES)
                mixed[rows, there] = (
                    a[s, rows, cols] + decays[s] * read[s * block : (s + 1) * block]
                ).astype(bf16)

    ranking.wait()
    local = tokens // plan.peers
    step = min(256, local)
    for at in range(0, tokens, step):
        place = rank[at : at + step, :]
        pick = jnp.concatenate(
            [
                jnp.where(
                    (lax.broadcasted_iota(jnp.int32, place.shape, 1) + t).astype(f32) == place,
                    1.0,
                    0.0,
                ).astype(bf16)
                for t in range(0, tokens, LANES)
            ],
            axis=1,
        )
        placed = jnp.dot(pick, mixed[...], preferred_element_type=f32).astype(bf16)
        k, to = at // local, at % local
        for s in range(plan.merge):
            out_refs[s * plan.peers + k][to : to + step, :] = placed[
                :, s * width : (s + 1) * width
            ]


def mix(plan, decays, attended, readers, state, rank, groups):
    tokens = rank.shape[0]
    width = attended[0].shape[1]
    count = plan.merge * plan.peers
    return pl.pallas_call(
        functools.partial(mix_kernel, plan, groups),
        in_specs=[smem] * plan.merge + [hbm] * (2 * plan.merge + 2),
        out_specs=(vmem,) * count,
        out_shape=(jax.ShapeDtypeStruct((tokens // plan.peers, width), bf16),) * count,
        scratch_shapes=[
            pltpu.VMEM((plan.merge, tokens, width), f32),
            pltpu.VMEM((plan.merge, tokens, width), bf16),
            pltpu.VMEM(state.shape, bf16),
            pltpu.VMEM(rank.shape, f32),
            pltpu.VMEM((tokens, plan.merge * width), bf16),
            Copies.scratch(),
        ],
        compiler_params=params(56),
        cost_estimate=cost(4 * tokens * tokens * width, 2 * tokens * tokens + 16 * tokens * width),
        name="mix",
    )(*decays, *attended, *readers, state, rank)


def out_kernel(plan, w_ref, *refs):
    part_refs, out_ref = refs[:-1], refs[-1]
    depth = part_refs[0].shape[1]
    core, me = plan.core(), lax.axis_index("head")
    total = None
    for s in range(plan.merge):
        for k in range(plan.peers):
            owner = lax.rem(me - k + plan.peers, plan.peers) * plan.merge
            owner = owner + (core if s == 0 else 1 - core)
            rows = pl.ds(pl.multiple_of(owner * depth, depth), depth)
            term = jnp.dot(
                part_refs[s * plan.peers + k][...], w_ref[rows, :], preferred_element_type=f32
            )
            total = term if total is None else total + term
    out_ref[...] = total.astype(bf16)


def project_out(plan, w, parts):
    local = parts[0].shape[0]
    width = w.shape[1]
    return pl.pallas_call(
        functools.partial(out_kernel, plan),
        out_shape=jax.ShapeDtypeStruct((local, width), bf16),
        compiler_params=params(),
        cost_estimate=cost(2 * local * w.size, 2 * (w.size + 2 * local * width)),
        name="project_out",
    )(w, *parts)


def body(frames_in, in_weight, out_weight, block_ids, block_lists, decays):
    local_tokens = frames_in.shape[1]
    heads_here = decays.shape[1]
    groups = block_lists.shape[0]
    me = lax.axis_index("head")
    plan = Plan(lax.axis_size("tm"), lax.axis_size("head"), heads_here)

    own = frames_in[0]
    arriving = [plan.to_peer(own, plan.peers - k, False) for k in range(1, plan.peers)]
    owns = [own] + [plan.swap(own)] * (plan.merge - 1)
    rates = [decays[0]] + [plan.swap(decays[0])] * (plan.merge - 1)
    blocks = reorder(plan, [in_weight] + [plan.swap(in_weight)] * (plan.merge - 1))

    ids = jnp.roll(block_ids, -me * local_tokens)
    if plan.ringed:
        def step(block, with_):
            return lax.optimization_barrier((plan.round(block), plan.cross(block), with_))[:2]

        early, late, crossed = [blocks[0]], [blocks[1]], [[], []]
        rank = part = None
        for k in range(plan.along - 1):
            passed, across = step(early[-1], [[], [], late[-1:]][min(k, 2)] + [part] * (k == 1))
            early.append(passed)
            crossed[0].append(across)
            if k == 0:
                ids, rates, _ = lax.optimization_barrier((ids, rates, early[-1]))
                rank, places = rank_tokens(ids, groups)
            passed, across = step(late[-1], [])
            late.append(passed)
            crossed[1].append(across)
            if k == 0:
                rank, _ = lax.optimization_barrier((rank, late[-1]))
                part = place_tokens(plan, rank, owns)
        crossed[0].append(plan.cross(early[-1]))
        arriving, _ = lax.optimization_barrier((arriving, crossed[0][-1]))
        early = [b for pair in zip(early, crossed[0]) for b in pair]
    else:
        rank = part = None
        early, late = (
            [lax.all_gather(b, "tm", axis=0, tiled=True, axis_index_groups=plan.groups())]
            for b in blocks
        )
    if part is None:
        rank, places = rank_tokens(ids, groups)
        part = place_tokens(plan, rank, owns)
    if plan.merge == 2:
        arriving = arriving + [plan.swap(chunk) for chunk in arriving]
    x, v, local, total = project_updates(plan, rates, rank, part, arriving, early, groups)
    if plan.ringed:
        late[-1], _ = lax.optimization_barrier((late[-1], total))
        crossed[1].append(plan.cross(late[-1]))
        late = [b for pair in zip(late, crossed[1]) for b in pair]

    def exchange(blocks):
        return lax.all_to_all(
            blocks, "tm", split_axis=0, concat_axis=0, tiled=True,
            axis_index_groups=plan.groups(),
        )

    share = local.shape[1] // plan.chips
    arrived = exchange(total)
    attended = [attend(plan, 0, block_lists, x, v, late, local)]
    arrived, attended = lax.optimization_barrier((arrived, attended))
    states = scan_states(plan, arrived, share)
    x, states = lax.optimization_barrier((x, states))
    if plan.merge == 2:
        attended.append(attend(plan, 1, block_lists, x, v, late, local))
    state = exchange(states).reshape(-1, LANES)

    bases, readers = ([a[i] for a in attended] for i in range(2))
    mixed = mix(plan, rates, bases, readers, state, places, groups)
    features = [
        mixed[0] if s == 0 and k == 0 else plan.to_peer(mixed[s * plan.peers + k], k, s == 1)
        for s in range(plan.merge)
        for k in range(plan.peers)
    ]
    return project_out(plan, out_weight, features)[None]


def solution(mesh):
    return jax.shard_map(
        body,
        mesh=mesh,
        in_specs=(P("tm", "head", None), P("tm", "head"), P(), P(), P(), P("tm", "head", None)),
        out_specs=P("tm", "head", None),
        check_vma=False,
    )
```

```python
import functools
import math

import jax
import jax.numpy as jnp
from jax import lax
from jax.experimental import pallas as pl
from jax.experimental.pallas import tpu as pltpu
from jax.sharding import PartitionSpec as P

HD = 64
N = 64
LANES = 2 * HD
PIECES = 5
EARLY = (2, 3)
LATE = (0, 1, 4)

epsilon = 1e-06

vmem = pl.BlockSpec(memory_space=pltpu.VMEM)
smem = pl.BlockSpec(memory_space=pltpu.SMEM)

hbm = pl.BlockSpec(memory_space=pltpu.HBM)

f32 = jnp.float32
bf16 = jnp.bfloat16


def params(mib=16):
    return pltpu.CompilerParams(vmem_limit_bytes=mib << 20)


def cost(flops, nbytes, transcendentals=0):
    return pl.CostEstimate(
        flops=int(flops), bytes_accessed=int(nbytes), transcendentals=int(transcendentals)
    )


def first_half(shape):
    return lax.broadcasted_iota(jnp.int32, shape, len(shape) - 1) < HD


class Plan:
    def __init__(self, frames, peers, heads_here):
        self.merge = 2 if frames % 2 == 0 and heads_here % 4 == 0 else 1
        self.frames, self.peers = frames, peers
        self.heads = heads_here // self.merge
        self.pairs = self.heads // 2
        self.chips = frames // self.merge
        self.across = 2 if self.chips % 2 == 0 else 1
        self.along = self.chips // self.across
        self.ringed = self.across == 2 and 2 <= self.along <= 8

    def core(self):
        return lax.rem(lax.axis_index("tm"), self.merge)

    def chip(self):
        return lax.div(lax.axis_index("tm"), self.merge)

    def swap(self, block):
        return lax.ppermute(block, "tm", [(t, t ^ 1) for t in range(self.frames)])

    def round(self, block):
        a, b, c = self.along, self.across, self.merge
        pairs = [(t, (t + b * c) % (a * b * c)) for t in range(self.frames)]
        return lax.ppermute(block, "tm", pairs)

    def cross(self, block):
        c = self.merge
        pairs = [(t, (t // c ^ 1) * c + t % c) for t in range(self.frames)]
        return lax.ppermute(block, "tm", pairs)

    def places(self, refs):
        if len(refs) == 1:
            return [(refs[0], slice(None))]
        rows = refs[0].shape[0]
        a, b = lax.div(self.chip(), self.across), lax.rem(self.chip(), self.across)
        n = self.along
        made = []
        for i, ref in enumerate(refs):
            k, flip = (i, 0) if i < n else (min(i - n, n - 1), 1)
            there = lax.rem(a - k + n, n) * self.across
            at = (there + (1 - b if flip else b)) * rows
            at = at + (rows // 2 if i == 2 * n else 0)
            made.append((ref, pl.ds(pl.multiple_of(at, rows // 2), ref.shape[0])))
        return made

    def to_peer(self, block, k, other):
        if not other:
            pairs = [(j, (j + k) % self.peers) for j in range(self.peers)]
            return lax.ppermute(block, "head", pairs)
        if k == 0:
            return self.swap(block)
        pairs = [
            (t * self.peers + j, (t ^ 1) * self.peers + (j + k) % self.peers)
            for t in range(self.frames)
            for j in range(self.peers)
        ]
        return lax.ppermute(block, ("tm", "head"), pairs)

    def groups(self):
        if self.merge == 1:
            return None
        return [[j * self.merge + c for j in range(self.chips)] for c in range(self.merge)]

    def decay(self, refs, slot, pair, g):
        head = self.core() * self.heads + 2 * pair
        return halves((1, LANES), refs[slot][head, g], refs[slot][head + 1, g])

    def last_decay(self, refs, pair, g):
        if self.merge == 1:
            return self.decay(refs, 0, pair, g)
        one, two = (self.decay(refs, slot, pair, g) for slot in range(2))
        return jnp.where(self.core() == 0, two, one)


class Copies:
    room = 48

    def __init__(self, sems):
        self.sems, self.count = sems, 0

    def start(self, src, dst):
        copy = pltpu.make_async_copy(src, dst, self.sems.at[self.count])
        copy.start()
        self.count += 1
        return copy

    @staticmethod
    def scratch():
        return pltpu.SemaphoreType.DMA((Copies.room,))


def finish(copies):
    for copy in copies:
        copy.wait()


def halves(shape, one, two):
    return jnp.where(first_half(shape), one, two)


def reorder_kernel(plan, *refs):
    w_refs, out_ref = refs[:-1], refs[-1]
    rows = w_refs[0].shape[0]
    width = plan.heads * PIECES * HD
    first = plan.core() == 0

    def chosen(ref, at):
        one = ref[:, at : at + HD]
        if plan.merge == 1:
            return one
        return jnp.where(first, one, ref[:, width + at : width + at + HD])

    order = [(p, i) for i in EARLY for p in range(plan.pairs)]
    order += [(p, i) for p in range(plan.pairs) for i in LATE]
    for n, (p, i) in enumerate(order):
        blocks = []
        for ref in w_refs:
            one, two = (chosen(ref, ((2 * p + h) * PIECES + i) * HD) for h in range(2))
            blocks.append(jnp.concatenate([one, two], axis=1))
        for s, block in enumerate(blocks):
            if plan.merge == 2:
                block = jnp.where(first, block, blocks[1 - s])
            out_ref[s * rows : (s + 1) * rows, n * LANES : (n + 1) * LANES] = block


def reorder(plan, weights):
    rows = weights[0].shape[0]
    return pl.pallas_call(
        functools.partial(reorder_kernel, plan),
        out_shape=jax.ShapeDtypeStruct((plan.merge * rows, plan.heads * PIECES * HD), bf16),
        compiler_params=params(),
        cost_estimate=cost(0, 4 * weights[0].size),
        name="reorder",
    )(*weights)


def normalise(part, out, at):
    step = min(128, part.shape[0])

    def norm(c, _):
        start = pl.multiple_of(c * step, step)
        wide = part[pl.ds(start, step), :].astype(f32)
        scale = lax.rsqrt(jnp.mean(wide * wide, axis=-1, keepdims=True) + epsilon)
        out[pl.ds(at + start, step), :] = (wide * scale).astype(bf16)
        return 0

    lax.fori_loop(0, part.shape[0] // step, norm, 0)


def rank_kernel(groups, ids_ref, row_ref, col_ref):
    tokens = ids_ref.shape[1]
    block = tokens // groups
    label = lax.broadcasted_iota(jnp.int32, (groups, tokens), 0)
    held = label == ids_ref[...]
    held_bf = jnp.where(held, 1.0, 0.0).astype(bf16)
    counts = []
    for c in range(tokens // 256):
        before = lax.broadcasted_iota(jnp.int32, (tokens, 256), 0) < (
            lax.broadcasted_iota(jnp.int32, (tokens, 256), 1) + c * 256
        )
        counts.append(
            jnp.dot(held_bf, jnp.where(before, 1.0, 0.0).astype(bf16), preferred_element_type=f32)
        )
    count = jnp.concatenate(counts, axis=1)
    rank = jnp.sum(
        jnp.where(held, count + (label * block).astype(f32), 0.0), axis=0, keepdims=True
    )
    row_ref[...] = rank
    for at in range(0, tokens, LANES):
        wide = jnp.broadcast_to(rank[:, at : at + LANES], (LANES, LANES))
        col_ref[at : at + LANES, :] = wide.T


def rank_tokens(ids, groups):
    tokens = ids.shape[0]
    return pl.pallas_call(
        functools.partial(rank_kernel, groups),
        out_shape=(
            jax.ShapeDtypeStruct((1, tokens), f32),
            jax.ShapeDtypeStruct((tokens, LANES), f32),
        ),
        compiler_params=params(),
        cost_estimate=cost(0, 4 * tokens),
        name="rank_tokens",
    )(ids.reshape(1, tokens))


def picks(rank, at, rows):
    places = lax.broadcasted_iota(jnp.int32, (rows, rank.shape[1]), 0) + at
    return jnp.where(places.astype(f32) == rank, 1.0, 0.0).astype(bf16)


def place_kernel(merge, parts, start, rank_ref, *refs):
    frame_refs, refs = refs[: merge * parts], refs[merge * parts :]
    base_refs, (x_ref, normed) = refs[:-2], refs[-2:]
    tokens = rank_ref.shape[1]
    count = normed.shape[1]
    step = 256
    for s in range(merge):
        at = 0
        for ref in frame_refs[s * parts : (s + 1) * parts]:
            normalise(ref, normed.at[s], at)
            at += ref.shape[0]
    for at in range(0, tokens, step):
        pick = picks(rank_ref[:, start : start + count], at, step)
        for s in range(merge):
            there = slice(s * tokens + at, s * tokens + at + step)
            placed = jnp.dot(pick, normed[s], preferred_element_type=f32).astype(bf16)
            for base in base_refs:
                placed = base[there, :] + placed
            x_ref[there, :] = placed


def place_tokens(plan, rank, start, frames, base):
    tokens = rank.shape[1]
    width = frames[0].shape[1]
    parts = len(frames) // plan.merge
    count = parts * frames[0].shape[0]
    return pl.pallas_call(
        functools.partial(place_kernel, plan.merge, parts, start),
        out_shape=jax.ShapeDtypeStruct((plan.merge * tokens, width), bf16),
        scratch_shapes=[pltpu.VMEM((plan.merge, count, width), bf16)],
        compiler_params=params(),
        cost_estimate=cost(0, 4 * tokens),
        name="place_tokens",
    )(rank, *frames, *base)


def update_kernel(plan, groups, *refs):
    decay_refs, x_in, refs = refs[: plan.merge], refs[plan.merge], refs[plan.merge + 1 :]
    w_refs, refs = refs[:-10], refs[-10:]
    v_out, local_out, total_ref, w, turned, x, v, u, left, sems = refs
    copies = Copies(sems)
    every = x.shape[0]
    tokens = every // plan.merge
    block = tokens // groups
    step = 256
    here = step // block
    cols = plan.pairs * LANES

    weights, arriving = [], []
    for ref, rows in plan.places(w_refs):
        weights.append(copies.start(ref.at[:, cols : 2 * cols], turned.at[rows]))
        weights.append(copies.start(ref.at[:, :cols], w.at[rows]))
    for at in range(0, every, step):
        arriving.append(copies.start(x_in.at[at : at + step], x.at[at : at + step]))

    finish(weights)
    maps = jnp.concatenate(
        [
            turned[at : at + LANES, :].astype(f32).T.astype(bf16)
            for at in range(0, turned.shape[0], LANES)
        ],
        axis=1,
    )
    lane = lax.div(lax.broadcasted_iota(jnp.int32, (LANES, step), 1), block)
    leaving = []
    for at in range(0, every, step):
        there = slice(at, at + step)
        arriving[at // step].wait()
        values = jnp.dot(x[there, :], w[...], preferred_element_type=f32).astype(bf16)
        v[there, :] = values
        leaving.append(copies.start(v.at[there], v_out.at[there]))
        b = lax.dot_general(
            maps, x[there, :], (((1,), (1,)), ((), ())), preferred_element_type=f32
        )
        for p in range(plan.pairs):
            mine = b[p * LANES : (p + 1) * LANES]
            wide = jnp.concatenate(
                [jnp.where(lane == i, mine, 0.0).astype(bf16) for i in range(here)], axis=0
            )
            outer = jnp.dot(
                wide, values[:, p * LANES : (p + 1) * LANES], preferred_element_type=f32
            )
            for i in range(here):
                m = outer[i * 2 * N : (i + 1) * 2 * N]
                row = ((at % tokens // block + i) * plan.pairs + p) * N
                u[at // tokens, row : row + N, :] = halves((N, LANES), m[:N], m[N:])

    peers = total_ref.shape[0]
    share = u.shape[1] // peers
    items = max(1, share // N)
    size = min(N, share)
    first = plan.core() == 0
    for d in range(peers):
        for i in range(items):
            row = d * share + i * N
            rows = slice(row, row + size)
            p, g = row // N % plan.pairs, row // N // plan.pairs
            product = last = plan.last_decay(decay_refs, p, g)
            if plan.merge == 2:
                one, two = u[0, rows, :], u[1, rows, :]
                one, two = (
                    one + jnp.where(first, 0.0, last) * two,
                    two + jnp.where(first, last, 0.0) * one,
                )
                left[0, rows, :] = one.astype(bf16)
                left[1, rows, :] = two.astype(bf16)
                total = jnp.where(first, two, one)
                product = plan.decay(decay_refs, 0, p, g) * plan.decay(decay_refs, 1, p, g)
            else:
                total = u[0, rows, :]
                left[0, rows, :] = total.astype(bf16)
            total_ref[d, i * size : (i + 1) * size, :] = total.astype(bf16)
            for n in range(3):
                piece = product.astype(bf16)
                at = share + n * items + i
                total_ref[d, at : at + 1, :] = piece
                product = product - piece.astype(f32)
    leaving.append(copies.start(left, local_out))
    finish(leaving)


def share_rows(share):
    return share + 16 * -(-3 * max(1, share // N) // 16)


def project_updates(plan, decays, x, weights, groups):
    every, width = x.shape
    cols = plan.pairs * LANES
    rows = plan.pairs * groups * N
    share = rows // plan.chips
    return pl.pallas_call(
        functools.partial(update_kernel, plan, groups),
        in_specs=[smem] * plan.merge + [hbm] * (1 + len(weights)),
        out_specs=(hbm,) * 2 + (vmem,),
        out_shape=(
            jax.ShapeDtypeStruct((every, cols), bf16),
            jax.ShapeDtypeStruct((plan.merge, rows, LANES), bf16),
            jax.ShapeDtypeStruct((plan.chips, share_rows(share), LANES), bf16),
        ),
        scratch_shapes=[
            pltpu.VMEM((width, cols), bf16),
            pltpu.VMEM((width, cols), bf16),
            pltpu.VMEM((every, width), bf16),
            pltpu.VMEM((every, cols), bf16),
            pltpu.VMEM((plan.merge, rows, LANES), f32),
            pltpu.VMEM((plan.merge, rows, LANES), bf16),
            Copies.scratch(),
        ],
        compiler_params=params(60),
        cost_estimate=cost(4 * every * width * 2 * cols, 6 * every * width),
        name="project_updates",
    )(*decays, x, *weights)


def scan_kernel(plan, u_ref, s_ref):
    share = s_ref.shape[1]
    size = min(share, N)
    items = share // size
    for i in range(items):
        at = slice(i * size, (i + 1) * size)
        state = jnp.zeros((size, LANES), f32)
        for j in range(plan.chips):
            s_ref[j, at, :] = state.astype(bf16)
            decay = jnp.zeros((1, LANES), f32)
            for n in range(3):
                row = share + n * items + i
                decay = decay + u_ref[j, row : row + 1, :].astype(f32)
            state = decay * state + u_ref[j, at, :].astype(f32)


def scan_states(plan, update, share):
    return pl.pallas_call(
        functools.partial(scan_kernel, plan),
        out_shape=jax.ShapeDtypeStruct((plan.chips, share, LANES), bf16),
        compiler_params=params(),
        cost_estimate=cost(2 * update.size, 4 * update.size),
        name="scan_states",
    )(update)


def attend_kernel(plan, slot, *refs):
    lists_ref, x_in, v_in, local_in, refs = refs[0], refs[1], refs[2], refs[3], refs[4:]
    w_refs, refs = refs[:-13], refs[-13:]
    a_out, c_out, x, v, local, w, q_ref, k_ref, wide_v, e_ref, a, c_ref, sems = refs
    copies = Copies(sems)
    tokens = x.shape[0]
    groups, chosen = lists_ref.shape
    block = tokens // groups
    step = 256
    per = step // block

    early = 2 * plan.pairs * LANES
    weights = [
        copies.start(ref.at[:, early : early + w.shape[1]], w.at[rows])
        for ref, rows in plan.places(w_refs)
    ]
    arriving = []
    for at in range(0, tokens, step):
        from_ = slice(slot * tokens + at, slot * tokens + at + step)
        arriving.append(copies.start(x_in.at[from_], x.at[at : at + step]))
    mine = slice(slot * tokens, (slot + 1) * tokens)
    later = [copies.start(v_in.at[mine], v), copies.start(local_in.at[slot], local)]

    same = lax.div(lax.broadcasted_iota(jnp.int32, (2 * LANES, 2 * LANES), 0), HD) == lax.div(
        lax.broadcasted_iota(jnp.int32, (2 * LANES, 2 * LANES), 1), HD
    )
    same = jnp.where(same, 1.0, 0.0).astype(bf16)

    def head_norm(values):
        square = values * values
        high = square.astype(bf16)
        low = (square - high.astype(f32)).astype(bf16)
        total = jnp.dot(high, same, preferred_element_type=f32)
        total = total + jnp.dot(low, same, preferred_element_type=f32)
        return values * lax.rsqrt(total * (1.0 / HD) + epsilon)

    half = first_half((step, LANES))
    finish(weights)
    for at in range(0, tokens, step):
        rows = slice(at, at + step)
        arriving[at // step].wait()
        every = jnp.dot(x[rows, :], w[...], preferred_element_type=f32).astype(bf16)
        for p in range(plan.pairs):
            cols = slice(p * LANES, (p + 1) * LANES)
            first = 3 * p * LANES
            c_ref[rows, cols] = every[:, first + 2 * LANES : first + 3 * LANES]
            both = head_norm(every[:, first : first + 2 * LANES].astype(f32))
            k_ref[p, rows, :] = both[:, LANES:].astype(bf16)
            q = both[:, :LANES]
            one = jnp.where(half, q, 0.0).astype(bf16)
            two = jnp.where(half, 0.0, q).astype(bf16)
            for i in range(per):
                part = slice(i * block, (i + 1) * block)
                q_ref[p, at // block + i] = jnp.concatenate([one[part], two[part]], axis=0)
    leaving = [copies.start(c_ref, c_out)]
    finish(later)
    for p in range(plan.pairs):
        wide_v[p, :, :LANES] = v[:, p * LANES : (p + 1) * LANES]
        wide_v[p, :, LANES:] = jnp.ones((tokens, LANES), bf16)

    scale = math.log2(math.e) / math.sqrt(HD)
    starts = [
        [pl.multiple_of(lists_ref[g, j] * block, block) for j in range(chosen)]
        for g in range(groups)
    ]
    for g in range(groups):
        for p in range(plan.pairs):
            keys = jnp.concatenate([k_ref[p, pl.ds(s, block), :] for s in starts[g]], axis=0)
            score = lax.dot_general(
                q_ref[p, g], keys, (((1,), (1,)), ((), ())), preferred_element_type=f32
            )
            e_ref[p, g] = jnp.exp2(score * scale).astype(bf16)
    for g in range(groups):
        rows = slice(g * block, (g + 1) * block)
        for p in range(plan.pairs):
            cols = slice(p * LANES, (p + 1) * LANES)
            values = jnp.concatenate([wide_v[p, pl.ds(s, block), :] for s in starts[g]], axis=0)
            both = jnp.dot(e_ref[p, g], values, preferred_element_type=f32)
            both = both[:, :LANES] / both[:, LANES:]
            a[rows, cols] = halves((block, LANES), both[:block], both[block:])
    for g in range(groups):
        rows = slice(g * block, (g + 1) * block)
        for p in range(plan.pairs):
            cols = slice(p * LANES, (p + 1) * LANES)
            items = slice((g * plan.pairs + p) * N, (g * plan.pairs + p + 1) * N)
            a[rows, cols] = a[rows, cols] + read_out(
                c_ref[rows, cols], local[items, :].astype(f32), block
            )
        if (g + 1) % per == 0:
            done = slice((g + 1 - per) * block, (g + 1) * block)
            leaving.append(copies.start(a.at[done], a_out.at[done]))
    finish(leaving)


def attend(plan, slot, lists, x, v, weights, local):
    every, width = x.shape
    groups, chosen = lists.shape
    tokens = every // plan.merge
    block = tokens // groups
    cols = plan.pairs * LANES
    return pl.pallas_call(
        functools.partial(attend_kernel, plan, slot),
        in_specs=[smem] + [hbm] * (3 + len(weights)),
        out_specs=(hbm,) * 2,
        scratch_shapes=[
            pltpu.VMEM((tokens, width), bf16),
            pltpu.VMEM((tokens, cols), bf16),
            pltpu.VMEM(local.shape[1:], bf16),
            pltpu.VMEM((width, 3 * cols), bf16),
            pltpu.VMEM((plan.pairs, groups, 2 * block, LANES), bf16),
            pltpu.VMEM((plan.pairs, tokens, LANES), bf16),
            pltpu.VMEM((plan.pairs, tokens, 2 * LANES), bf16),
            pltpu.VMEM((plan.pairs, groups, 2 * block, chosen * block), bf16),
            pltpu.VMEM((tokens, cols), f32),
            pltpu.VMEM((tokens, cols), bf16),
            Copies.scratch(),
        ],
        out_shape=(
            jax.ShapeDtypeStruct((tokens, cols), f32),
            jax.ShapeDtypeStruct((tokens, cols), bf16),
        ),
        compiler_params=params(60),
        cost_estimate=cost(
            6 * tokens * width * 3 * cols,
            4 * (tokens * width + 5 * width * cols + local.size),
            2 * plan.pairs * tokens * chosen * block,
        ),
        name="attend",
    )(lists, x, v, local, *weights)


def read_out(readers, state, block):
    half = first_half(state.shape)
    wide = jnp.concatenate([jnp.where(half, state, 0.0), jnp.where(half, 0.0, state)], axis=0)
    return jnp.dot(readers, wide.astype(bf16), preferred_element_type=f32) * (
        1.0 / (N * math.sqrt(block))
    )


def mix_kernel(plan, groups, *refs):
    decay_refs, refs = refs[: plan.merge], refs[plan.merge :]
    a_ins, refs = refs[: plan.merge], refs[plan.merge :]
    c_ins, refs = refs[: plan.merge], refs[plan.merge :]
    s_in, rank_in, refs = refs[0], refs[1], refs[2:]
    out_refs, (a, c, state, rank, mixed, sems) = refs[:-6], refs[-6:]
    copies = Copies(sems)
    tokens = rank.shape[0]
    block = tokens // groups
    width = a.shape[2]
    here = groups // 4
    many = here * plan.pairs * N
    first = plan.core() == 0

    arriving = []
    for i in range(4):
        rows = slice(i * here * block, (i + 1) * here * block)
        items = slice(i * many, (i + 1) * many)
        arriving.append([copies.start(s_in.at[items], state.at[items])])
        for s in range(plan.merge):
            arriving[-1] += [
                copies.start(c_ins[s].at[rows], c.at[s, rows, :]),
                copies.start(a_ins[s].at[rows], a.at[s, rows, :]),
            ]
    ranking = copies.start(rank_in, rank)

    for g in range(groups):
        if g % here == 0:
            finish(arriving[g // here])
        rows = slice(g * block, (g + 1) * block)
        for p in range(plan.pairs):
            cols = slice(p * LANES, (p + 1) * LANES)
            at = (g * plan.pairs + p) * N
            readers = jnp.concatenate([c[s, rows, cols] for s in range(plan.merge)], axis=0)
            read = read_out(readers, state[at : at + N, :].astype(f32), block)
            decays = [plan.decay(decay_refs, s, p, g) for s in range(plan.merge)]
            if plan.merge == 2:
                both = decays[0] * decays[1]
                decays = [jnp.where(first, decays[0], both), jnp.where(first, both, decays[1])]
            for s in range(plan.merge):
                there = slice(s * width + p * LANES, s * width + (p + 1) * LANES)
                mixed[rows, there] = (
                    a[s, rows, cols] + decays[s] * read[s * block : (s + 1) * block]
                ).astype(bf16)

    ranking.wait()
    local = tokens // plan.peers
    step = min(256, local)
    for at in range(0, tokens, step):
        place = rank[at : at + step, :]
        pick = jnp.concatenate(
            [
                jnp.where(
                    (lax.broadcasted_iota(jnp.int32, place.shape, 1) + t).astype(f32) == place,
                    1.0,
                    0.0,
                ).astype(bf16)
                for t in range(0, tokens, LANES)
            ],
            axis=1,
        )
        placed = jnp.dot(pick, mixed[...], preferred_element_type=f32).astype(bf16)
        k, to = at // local, at % local
        for s in range(plan.merge):
            out_refs[s * plan.peers + k][to : to + step, :] = placed[
                :, s * width : (s + 1) * width
            ]


def mix(plan, decays, attended, readers, state, rank, groups):
    tokens = rank.shape[0]
    width = attended[0].shape[1]
    count = plan.merge * plan.peers
    return pl.pallas_call(
        functools.partial(mix_kernel, plan, groups),
        in_specs=[smem] * plan.merge + [hbm] * (2 * plan.merge + 2),
        out_specs=(vmem,) * count,
        out_shape=(jax.ShapeDtypeStruct((tokens // plan.peers, width), bf16),) * count,
        scratch_shapes=[
            pltpu.VMEM((plan.merge, tokens, width), f32),
            pltpu.VMEM((plan.merge, tokens, width), bf16),
            pltpu.VMEM(state.shape, bf16),
            pltpu.VMEM(rank.shape, f32),
            pltpu.VMEM((tokens, plan.merge * width), bf16),
            Copies.scratch(),
        ],
        compiler_params=params(56),
        cost_estimate=cost(4 * tokens * tokens * width, 2 * tokens * tokens + 16 * tokens * width),
        name="mix",
    )(*decays, *attended, *readers, state, rank)


def out_kernel(plan, w_ref, *refs):
    part_refs, out_ref = refs[:-1], refs[-1]
    depth = part_refs[0].shape[1]
    core, me = plan.core(), lax.axis_index("head")
    total = None
    for s in range(plan.merge):
        for k in range(plan.peers):
            owner = lax.rem(me - k + plan.peers, plan.peers) * plan.merge
            owner = owner + (core if s == 0 else 1 - core)
            rows = pl.ds(pl.multiple_of(owner * depth, depth), depth)
            term = jnp.dot(
                part_refs[s * plan.peers + k][...], w_ref[rows, :], preferred_element_type=f32
            )
            total = term if total is None else total + term
    out_ref[...] = total.astype(bf16)


def project_out(plan, w, parts):
    local = parts[0].shape[0]
    width = w.shape[1]
    return pl.pallas_call(
        functools.partial(out_kernel, plan),
        out_shape=jax.ShapeDtypeStruct((local, width), bf16),
        compiler_params=params(),
        cost_estimate=cost(2 * local * w.size, 2 * (w.size + 2 * local * width)),
        name="project_out",
    )(w, *parts)


def body(frames_in, in_weight, out_weight, block_ids, block_lists, decays):
    local_tokens = frames_in.shape[1]
    heads_here = decays.shape[1]
    groups = block_lists.shape[0]
    me = lax.axis_index("head")
    plan = Plan(lax.axis_size("tm"), lax.axis_size("head"), heads_here)

    own = frames_in[0]
    arriving = [plan.to_peer(own, plan.peers - k, False) for k in range(1, plan.peers)]
    owns = [own] + [plan.swap(own)] * (plan.merge - 1)
    rates = [decays[0]] + [plan.swap(decays[0])] * (plan.merge - 1)
    block = reorder(plan, [in_weight] + [plan.swap(in_weight)] * (plan.merge - 1))
    ids = jnp.roll(block_ids, -me * local_tokens)
    ids, rates = lax.optimization_barrier((ids, rates))
    rank, places = rank_tokens(ids, groups)
    part = place_tokens(plan, rank, 0, owns, [])

    def fill(arriving):
        if plan.merge == 2:
            arriving = arriving + [plan.swap(tokens) for tokens in arriving]
        return place_tokens(plan, rank, local_tokens, arriving, [part])

    if plan.ringed:
        blocks, crossed = [block], []
        half = block.shape[0] // 2
        for k in range(plan.along - 1):
            with_ = part if k == 0 else ()
            if k == plan.along - 2:
                arriving, _ = lax.optimization_barrier((arriving, blocks[-1]))
                x = with_ = fill(arriving)
            passed, across, with_ = lax.optimization_barrier(
                (plan.round(blocks[-1]), plan.cross(blocks[-1]), with_)
            )
            blocks.append(passed)
            crossed.append(across)
        last = [plan.cross(blocks[-1][:half]), plan.round(crossed[-1][half:])]
        weights = blocks + crossed + last
    else:
        weights = [
            lax.all_gather(block, "tm", axis=0, tiled=True, axis_index_groups=plan.groups())
        ]
        x = fill(arriving)
    v, local, total = project_updates(plan, rates, x, weights, groups)

    def exchange(blocks):
        return lax.all_to_all(
            blocks, "tm", split_axis=0, concat_axis=0, tiled=True,
            axis_index_groups=plan.groups(),
        )

    share = local.shape[1] // plan.chips
    arrived = exchange(total)
    attended = [attend(plan, 0, block_lists, x, v, weights, local)]
    arrived, attended = lax.optimization_barrier((arrived, attended))
    states = scan_states(plan, arrived, share)
    x, states = lax.optimization_barrier((x, states))
    if plan.merge == 2:
        attended.append(attend(plan, 1, block_lists, x, v, weights, local))
    state = exchange(states).reshape(-1, LANES)

    bases, readers = ([a[i] for a in attended] for i in range(2))
    mixed = mix(plan, rates, bases, readers, state, places, groups)
    features = [
        mixed[0] if s == 0 and k == 0 else plan.to_peer(mixed[s * plan.peers + k], k, s == 1)
        for s in range(plan.merge)
        for k in range(plan.peers)
    ]
    return project_out(plan, out_weight, features)[None]


def solution(mesh):
    return jax.shard_map(
        body,
        mesh=mesh,
        in_specs=(P("tm", "head", None), P("tm", "head"), P(), P(), P(), P("tm", "head", None)),
        out_specs=P("tm", "head", None),
        check_vma=False,
    )
```

```python
import functools
import math

import jax
import jax.numpy as jnp
from jax import lax
from jax.experimental import pallas as pl
from jax.experimental.pallas import tpu as pltpu
from jax.sharding import PartitionSpec as P

HD = 64
N = 64
LANES = 2 * HD
PIECES = 5
EARLY = (2, 3)
LATE = (0, 1, 4)

epsilon = 1e-06

vmem = pl.BlockSpec(memory_space=pltpu.VMEM)
smem = pl.BlockSpec(memory_space=pltpu.SMEM)

hbm = pl.BlockSpec(memory_space=pltpu.HBM)

f32 = jnp.float32
bf16 = jnp.bfloat16


def params(mib=16):
    return pltpu.CompilerParams(vmem_limit_bytes=mib << 20)


def cost(flops, nbytes, transcendentals=0):
    return pl.CostEstimate(
        flops=int(flops), bytes_accessed=int(nbytes), transcendentals=int(transcendentals)
    )


def first_half(shape):
    return lax.broadcasted_iota(jnp.int32, shape, len(shape) - 1) < HD


class Plan:
    def __init__(self, frames, peers, heads_here, width):
        self.merge = 2 if frames % 2 == 0 and heads_here % 4 == 0 else 1
        self.frames, self.peers = frames, peers
        self.heads = heads_here // self.merge
        self.pairs = self.heads // 2
        self.chips = frames // self.merge
        self.across = 2 if self.chips % 2 == 0 else 1
        self.along = self.chips // self.across
        self.ringed = self.across == 2 and 2 <= self.along <= 8 and width % (self.chips * LANES) == 0

    def core(self):
        return lax.rem(lax.axis_index("tm"), self.merge)

    def chip(self):
        return lax.div(lax.axis_index("tm"), self.merge)

    def swap(self, block):
        return lax.ppermute(block, "tm", [(t, t ^ 1) for t in range(self.frames)])

    def round(self, block):
        a, b, c = self.along, self.across, self.merge
        pairs = [(t, (t + b * c) % (a * b * c)) for t in range(self.frames)]
        return lax.ppermute(block, "tm", pairs)

    def cross(self, block):
        c = self.merge
        pairs = [(t, (t // c ^ 1) * c + t % c) for t in range(self.frames)]
        return lax.ppermute(block, "tm", pairs)

    def last_chip(self):
        a, b = lax.div(self.chip(), self.across), lax.rem(self.chip(), self.across)
        return lax.rem(a + 1, self.along) * self.across + (self.across - 1 - b)

    def places(self, refs):
        if len(refs) == 1:
            return [(refs[0], slice(None))]
        rows = refs[0].shape[0]
        a, b = lax.div(self.chip(), self.across), lax.rem(self.chip(), self.across)
        n = self.along
        made = []
        for i, ref in enumerate(refs):
            k, flip = (i, 0) if i < n else (min(i - n, n - 1), 1)
            there = lax.rem(a - k + n, n) * self.across
            at = (there + (1 - b if flip else b)) * rows
            at = at + (rows // 2 if i == 2 * n else 0)
            made.append((ref, pl.ds(pl.multiple_of(at, rows // 2), ref.shape[0])))
        return made

    def to_peer(self, block, k, other):
        if not other:
            pairs = [(j, (j + k) % self.peers) for j in range(self.peers)]
            return lax.ppermute(block, "head", pairs)
        if k == 0:
            return self.swap(block)
        pairs = [
            (t * self.peers + j, (t ^ 1) * self.peers + (j + k) % self.peers)
            for t in range(self.frames)
            for j in range(self.peers)
        ]
        return lax.ppermute(block, ("tm", "head"), pairs)

    def groups(self):
        if self.merge == 1:
            return None
        return [[j * self.merge + c for j in range(self.chips)] for c in range(self.merge)]

    def decay(self, refs, slot, pair, g):
        head = self.core() * self.heads + 2 * pair
        return halves((1, LANES), refs[slot][head, g], refs[slot][head + 1, g])

    def last_decay(self, refs, pair, g):
        if self.merge == 1:
            return self.decay(refs, 0, pair, g)
        one, two = (self.decay(refs, slot, pair, g) for slot in range(2))
        return jnp.where(self.core() == 0, two, one)


class Copies:
    room = 48

    def __init__(self, sems):
        self.sems, self.count = sems, 0

    def start(self, src, dst):
        copy = pltpu.make_async_copy(src, dst, self.sems.at[self.count])
        copy.start()
        self.count += 1
        return copy

    @staticmethod
    def scratch():
        return pltpu.SemaphoreType.DMA((Copies.room,))


def finish(copies):
    for copy in copies:
        copy.wait()


def halves(shape, one, two):
    return jnp.where(first_half(shape), one, two)


def reorder_kernel(plan, *refs):
    w_refs, out_ref = refs[:-1], refs[-1]
    rows = w_refs[0].shape[0]
    width = plan.heads * PIECES * HD
    first = plan.core() == 0

    def chosen(ref, at):
        one = ref[:, at : at + HD]
        if plan.merge == 1:
            return one
        return jnp.where(first, one, ref[:, width + at : width + at + HD])

    order = [(p, i) for i in EARLY for p in range(plan.pairs)]
    order += [(p, i) for p in range(plan.pairs) for i in LATE]
    for n, (p, i) in enumerate(order):
        blocks = []
        for ref in w_refs:
            one, two = (chosen(ref, ((2 * p + h) * PIECES + i) * HD) for h in range(2))
            blocks.append(jnp.concatenate([one, two], axis=1))
        for s, block in enumerate(blocks):
            if plan.merge == 2:
                block = jnp.where(first, block, blocks[1 - s])
            out_ref[s * rows : (s + 1) * rows, n * LANES : (n + 1) * LANES] = block


def reorder(plan, weights):
    rows = weights[0].shape[0]
    return pl.pallas_call(
        functools.partial(reorder_kernel, plan),
        out_shape=jax.ShapeDtypeStruct((plan.merge * rows, plan.heads * PIECES * HD), bf16),
        compiler_params=params(),
        cost_estimate=cost(0, 4 * weights[0].size),
        name="reorder",
    )(*weights)


def normalise(part, out, at):
    step = min(128, part.shape[0])

    def norm(c, _):
        start = pl.multiple_of(c * step, step)
        wide = part[pl.ds(start, step), :].astype(f32)
        scale = lax.rsqrt(jnp.mean(wide * wide, axis=-1, keepdims=True) + epsilon)
        out[pl.ds(at + start, step), :] = (wide * scale).astype(bf16)
        return 0

    lax.fori_loop(0, part.shape[0] // step, norm, 0)


def rank_kernel(groups, ids_ref, row_ref, col_ref):
    tokens = ids_ref.shape[1]
    block = tokens // groups
    label = lax.broadcasted_iota(jnp.int32, (groups, tokens), 0)
    held = label == ids_ref[...]
    held_bf = jnp.where(held, 1.0, 0.0).astype(bf16)
    counts = []
    for c in range(tokens // 256):
        before = lax.broadcasted_iota(jnp.int32, (tokens, 256), 0) < (
            lax.broadcasted_iota(jnp.int32, (tokens, 256), 1) + c * 256
        )
        counts.append(
            jnp.dot(held_bf, jnp.where(before, 1.0, 0.0).astype(bf16), preferred_element_type=f32)
        )
    count = jnp.concatenate(counts, axis=1)
    rank = jnp.sum(
        jnp.where(held, count + (label * block).astype(f32), 0.0), axis=0, keepdims=True
    )
    row_ref[...] = rank
    for at in range(0, tokens, LANES):
        wide = jnp.broadcast_to(rank[:, at : at + LANES], (LANES, LANES))
        col_ref[at : at + LANES, :] = wide.T


def rank_tokens(ids, groups):
    tokens = ids.shape[0]
    return pl.pallas_call(
        functools.partial(rank_kernel, groups),
        out_shape=(
            jax.ShapeDtypeStruct((1, tokens), f32),
            jax.ShapeDtypeStruct((tokens, LANES), f32),
        ),
        compiler_params=params(),
        cost_estimate=cost(0, 4 * tokens),
        name="rank_tokens",
    )(ids.reshape(1, tokens))


def picks(rank, at, rows):
    places = lax.broadcasted_iota(jnp.int32, (rows, rank.shape[1]), 0) + at
    return jnp.where(places.astype(f32) == rank, 1.0, 0.0).astype(bf16)


def place_kernel(merge, parts, start, rank_ref, *refs):
    frame_refs, refs = refs[: merge * parts], refs[merge * parts :]
    base_refs, (x_ref, normed) = refs[:-2], refs[-2:]
    tokens = rank_ref.shape[1]
    count = normed.shape[1]
    step = 256
    for s in range(merge):
        at = 0
        for ref in frame_refs[s * parts : (s + 1) * parts]:
            normalise(ref, normed.at[s], at)
            at += ref.shape[0]
    for at in range(0, tokens, step):
        pick = picks(rank_ref[:, start : start + count], at, step)
        for s in range(merge):
            there = slice(s * tokens + at, s * tokens + at + step)
            placed = jnp.dot(pick, normed[s], preferred_element_type=f32).astype(bf16)
            for base in base_refs:
                placed = base[there, :] + placed
            x_ref[there, :] = placed


def place_tokens(plan, rank, start, frames, base):
    tokens = rank.shape[1]
    width = frames[0].shape[1]
    parts = len(frames) // plan.merge
    count = parts * frames[0].shape[0]
    return pl.pallas_call(
        functools.partial(place_kernel, plan.merge, parts, start),
        out_shape=jax.ShapeDtypeStruct((plan.merge * tokens, width), bf16),
        scratch_shapes=[pltpu.VMEM((plan.merge, count, width), bf16)],
        compiler_params=params(),
        cost_estimate=cost(0, 4 * tokens),
        name="place_tokens",
    )(rank, *frames, *base)


def project_kernel(plan, x_ref, *refs):
    w_refs, (v_ref, b_ref, rest_ref, w, turned) = refs[:-5], refs[-5:]
    every = x_ref.shape[0]
    step = 256
    cols = plan.pairs * LANES
    if len(w_refs) > 1:
        w[...] = jnp.zeros_like(w)
        turned[...] = jnp.zeros_like(turned)
    for ref, rows in plan.places(w_refs):
        w[rows, :] = ref[:, :cols]
        turned[rows, :] = ref[:, cols : 2 * cols]
    maps = jnp.concatenate(
        [
            turned[at : at + LANES, :].astype(f32).T.astype(bf16)
            for at in range(0, turned.shape[0], LANES)
        ],
        axis=1,
    )
    for at in range(0, every, step):
        x = x_ref[at : at + step, :]
        v_ref[at : at + step, :] = jnp.dot(x, w[...], preferred_element_type=f32)
        b_ref[:, at : at + step] = lax.dot_general(
            maps, x, (((1,), (1,)), ((), ())), preferred_element_type=f32
        )
    count = rest_ref.shape[1]
    there = plan.last_chip() * count
    for at in range(0, every, step):
        rest = x_ref[at : at + step, :count]
        for c in range(count, x_ref.shape[1], count):
            rest = jnp.where(there == c, x_ref[at : at + step, c : c + count], rest)
        rest_ref[at : at + step, :] = rest


def project(plan, x, weights):
    every, width = x.shape
    cols = plan.pairs * LANES
    count = max(LANES, width // plan.chips)
    return pl.pallas_call(
        functools.partial(project_kernel, plan),
        out_shape=(
            jax.ShapeDtypeStruct((every, cols), f32),
            jax.ShapeDtypeStruct((cols, every), f32),
            jax.ShapeDtypeStruct((every, count), bf16),
        ),
        scratch_shapes=[pltpu.VMEM((width, cols), bf16), pltpu.VMEM((width, cols), bf16)],
        compiler_params=params(),
        cost_estimate=cost(0, 4 * width),
        name="project",
    )(x, *weights)


def update_kernel(plan, groups, *refs):
    decay_refs, refs = refs[: plan.merge], refs[plan.merge :]
    v_ref, b_ref, x_ref, last_refs, (left, total_ref, u) = (
        refs[0], refs[1], refs[2], refs[3:-3], refs[-3:]
    )
    every = v_ref.shape[0]
    tokens = every // plan.merge
    block = tokens // groups
    step = 256
    here = step // block
    cols = plan.pairs * LANES
    if last_refs:
        w = jnp.concatenate([ref[:, : 2 * cols] for ref in last_refs], axis=0)
        maps = w[:, cols:].astype(f32).T.astype(bf16)
        w = w[:, :cols]

    lane = lax.div(lax.broadcasted_iota(jnp.int32, (LANES, step), 1), block)
    for at in range(0, every, step):
        there = slice(at, at + step)
        values, b = v_ref[there, :], b_ref[:, there]
        if last_refs:
            x = x_ref[there, :]
            values = values + jnp.dot(x, w, preferred_element_type=f32)
            b = b + lax.dot_general(
                maps, x, (((1,), (1,)), ((), ())), preferred_element_type=f32
            )
        values = values.astype(bf16)
        for p in range(plan.pairs):
            mine = b[p * LANES : (p + 1) * LANES]
            wide = jnp.concatenate(
                [jnp.where(lane == i, mine, 0.0).astype(bf16) for i in range(here)], axis=0
            )
            outer = jnp.dot(
                wide, values[:, p * LANES : (p + 1) * LANES], preferred_element_type=f32
            )
            for i in range(here):
                m = outer[i * 2 * N : (i + 1) * 2 * N]
                row = ((at % tokens // block + i) * plan.pairs + p) * N
                u[at // tokens, row : row + N, :] = halves((N, LANES), m[:N], m[N:])

    peers = total_ref.shape[0]
    share = u.shape[1] // peers
    items = max(1, share // N)
    size = min(N, share)
    first = plan.core() == 0
    for d in range(peers):
        for i in range(items):
            row = d * share + i * N
            rows = slice(row, row + size)
            p, g = row // N % plan.pairs, row // N // plan.pairs
            product = last = plan.last_decay(decay_refs, p, g)
            if plan.merge == 2:
                one, two = u[0, rows, :], u[1, rows, :]
                one, two = (
                    one + jnp.where(first, 0.0, last) * two,
                    two + jnp.where(first, last, 0.0) * one,
                )
                left[0, rows, :] = one.astype(bf16)
                left[1, rows, :] = two.astype(bf16)
                total = jnp.where(first, two, one)
                product = plan.decay(decay_refs, 0, p, g) * plan.decay(decay_refs, 1, p, g)
            else:
                total = u[0, rows, :]
                left[0, rows, :] = total.astype(bf16)
            total_ref[d, i * size : (i + 1) * size, :] = total.astype(bf16)
            for n in range(3):
                piece = product.astype(bf16)
                at = share + n * items + i
                total_ref[d, at : at + 1, :] = piece
                product = product - piece.astype(f32)


def share_rows(share):
    return share + 16 * -(-3 * max(1, share // N) // 16)


def block_updates(plan, decays, v, b, x, last, groups):
    every, cols = v.shape
    rows = plan.pairs * groups * N
    share = rows // plan.chips
    return pl.pallas_call(
        functools.partial(update_kernel, plan, groups),
        in_specs=[smem] * plan.merge + [vmem] * (3 + len(last)),
        out_shape=(
            jax.ShapeDtypeStruct((plan.merge, rows, LANES), bf16),
            jax.ShapeDtypeStruct((plan.chips, share_rows(share), LANES), bf16),
        ),
        scratch_shapes=[pltpu.VMEM((plan.merge, rows, LANES), f32)],
        compiler_params=params(),
        cost_estimate=cost(4 * every * 256 * 2 * cols, 6 * every * cols),
        name="block_updates",
    )(*decays, v, b, x, *last)


def scan_kernel(plan, u_ref, s_ref):
    share = s_ref.shape[1]
    size = min(share, N)
    items = share // size
    for i in range(items):
        at = slice(i * size, (i + 1) * size)
        state = jnp.zeros((size, LANES), f32)
        for j in range(plan.chips):
            s_ref[j, at, :] = state.astype(bf16)
            decay = jnp.zeros((1, LANES), f32)
            for n in range(3):
                row = share + n * items + i
                decay = decay + u_ref[j, row : row + 1, :].astype(f32)
            state = decay * state + u_ref[j, at, :].astype(f32)


def scan_states(plan, update, share):
    return pl.pallas_call(
        functools.partial(scan_kernel, plan),
        out_shape=jax.ShapeDtypeStruct((plan.chips, share, LANES), bf16),
        compiler_params=params(),
        cost_estimate=cost(2 * update.size, 4 * update.size),
        name="scan_states",
    )(update)


def attend_kernel(plan, slot, *refs):
    lists_ref, x_in, local_in, refs = refs[0], refs[1], refs[2], refs[3:]
    w_refs, refs = refs[:-12], refs[-12:]
    a_out, c_out, x, local, w, q_ref, k_ref, wide_v, e_ref, a, c_ref, sems = refs
    copies = Copies(sems)
    tokens = x.shape[0]
    groups, chosen = lists_ref.shape
    block = tokens // groups
    step = 256
    per = step // block
    wide = plan.pairs * LANES

    weights = []
    for ref, rows in plan.places(w_refs):
        weights.append(copies.start(ref.at[:, :wide], w.at[rows, :wide]))
        weights.append(copies.start(ref.at[:, 2 * wide :], w.at[rows, wide:]))
    arriving = []
    for at in range(0, tokens, step):
        from_ = slice(slot * tokens + at, slot * tokens + at + step)
        arriving.append(copies.start(x_in.at[from_], x.at[at : at + step]))
    later = copies.start(local_in.at[slot], local)

    same = lax.div(lax.broadcasted_iota(jnp.int32, (2 * LANES, 2 * LANES), 0), HD) == lax.div(
        lax.broadcasted_iota(jnp.int32, (2 * LANES, 2 * LANES), 1), HD
    )
    same = jnp.where(same, 1.0, 0.0).astype(bf16)

    def head_norm(values):
        square = values * values
        high = square.astype(bf16)
        low = (square - high.astype(f32)).astype(bf16)
        total = jnp.dot(high, same, preferred_element_type=f32)
        total = total + jnp.dot(low, same, preferred_element_type=f32)
        return values * lax.rsqrt(total * (1.0 / HD) + epsilon)

    half = first_half((step, LANES))
    finish(weights)
    for at in range(0, tokens, step):
        rows = slice(at, at + step)
        arriving[at // step].wait()
        every = jnp.dot(x[rows, :], w[...], preferred_element_type=f32).astype(bf16)
        for p in range(plan.pairs):
            cols = slice(p * LANES, (p + 1) * LANES)
            wide_v[p, rows, :LANES] = every[:, cols]
            first = wide + 3 * p * LANES
            c_ref[rows, cols] = every[:, first + 2 * LANES : first + 3 * LANES]
            both = head_norm(every[:, first : first + 2 * LANES].astype(f32))
            k_ref[p, rows, :] = both[:, LANES:].astype(bf16)
            q = both[:, :LANES]
            one = jnp.where(half, q, 0.0).astype(bf16)
            two = jnp.where(half, 0.0, q).astype(bf16)
            for i in range(per):
                part = slice(i * block, (i + 1) * block)
                q_ref[p, at // block + i] = jnp.concatenate([one[part], two[part]], axis=0)
    leaving = [copies.start(c_ref, c_out)]
    later.wait()
    for p in range(plan.pairs):
        wide_v[p, :, LANES:] = jnp.ones((tokens, LANES), bf16)

    scale = math.log2(math.e) / math.sqrt(HD)
    starts = [
        [pl.multiple_of(lists_ref[g, j] * block, block) for j in range(chosen)]
        for g in range(groups)
    ]
    for g in range(groups):
        for p in range(plan.pairs):
            keys = jnp.concatenate([k_ref[p, pl.ds(s, block), :] for s in starts[g]], axis=0)
            score = lax.dot_general(
                q_ref[p, g], keys, (((1,), (1,)), ((), ())), preferred_element_type=f32
            )
            e_ref[p, g] = jnp.exp2(score * scale).astype(bf16)
    for g in range(groups):
        rows = slice(g * block, (g + 1) * block)
        for p in range(plan.pairs):
            cols = slice(p * LANES, (p + 1) * LANES)
            values = jnp.concatenate([wide_v[p, pl.ds(s, block), :] for s in starts[g]], axis=0)
            both = jnp.dot(e_ref[p, g], values, preferred_element_type=f32)
            both = both[:, :LANES] / both[:, LANES:]
            a[rows, cols] = halves((block, LANES), both[:block], both[block:])
    for g in range(groups):
        rows = slice(g * block, (g + 1) * block)
        for p in range(plan.pairs):
            cols = slice(p * LANES, (p + 1) * LANES)
            items = slice((g * plan.pairs + p) * N, (g * plan.pairs + p + 1) * N)
            a[rows, cols] = a[rows, cols] + read_out(
                c_ref[rows, cols], local[items, :].astype(f32), block
            )
        if (g + 1) % per == 0:
            done = slice((g + 1 - per) * block, (g + 1) * block)
            leaving.append(copies.start(a.at[done], a_out.at[done]))
    finish(leaving)


def attend(plan, slot, lists, x, weights, local):
    every, width = x.shape
    groups, chosen = lists.shape
    tokens = every // plan.merge
    block = tokens // groups
    cols = plan.pairs * LANES
    return pl.pallas_call(
        functools.partial(attend_kernel, plan, slot),
        in_specs=[smem] + [hbm] * (2 + len(weights)),
        out_specs=(hbm,) * 2,
        scratch_shapes=[
            pltpu.VMEM((tokens, width), bf16),
            pltpu.VMEM(local.shape[1:], bf16),
            pltpu.VMEM((width, 4 * cols), bf16),
            pltpu.VMEM((plan.pairs, groups, 2 * block, LANES), bf16),
            pltpu.VMEM((plan.pairs, tokens, LANES), bf16),
            pltpu.VMEM((plan.pairs, tokens, 2 * LANES), bf16),
            pltpu.VMEM((plan.pairs, groups, 2 * block, chosen * block), bf16),
            pltpu.VMEM((tokens, cols), f32),
            pltpu.VMEM((tokens, cols), bf16),
            Copies.scratch(),
        ],
        out_shape=(
            jax.ShapeDtypeStruct((tokens, cols), f32),
            jax.ShapeDtypeStruct((tokens, cols), bf16),
        ),
        compiler_params=params(60),
        cost_estimate=cost(
            6 * tokens * width * 3 * cols,
            4 * (tokens * width + 5 * width * cols + local.size),
            2 * plan.pairs * tokens * chosen * block,
        ),
        name="attend",
    )(lists, x, local, *weights)


def read_out(readers, state, block):
    half = first_half(state.shape)
    wide = jnp.concatenate([jnp.where(half, state, 0.0), jnp.where(half, 0.0, state)], axis=0)
    return jnp.dot(readers, wide.astype(bf16), preferred_element_type=f32) * (
        1.0 / (N * math.sqrt(block))
    )


def mix_kernel(plan, groups, *refs):
    decay_refs, refs = refs[: plan.merge], refs[plan.merge :]
    a_ins, refs = refs[: plan.merge], refs[plan.merge :]
    c_ins, refs = refs[: plan.merge], refs[plan.merge :]
    s_in, rank_in, refs = refs[0], refs[1], refs[2:]
    out_refs, (a, c, state, rank, mixed, sems) = refs[:-6], refs[-6:]
    copies = Copies(sems)
    tokens = rank.shape[0]
    block = tokens // groups
    width = a.shape[2]
    here = groups // 4
    many = here * plan.pairs * N
    first = plan.core() == 0

    arriving = []
    for i in range(4):
        rows = slice(i * here * block, (i + 1) * here * block)
        items = slice(i * many, (i + 1) * many)
        arriving.append([copies.start(s_in.at[items], state.at[items])])
        for s in range(plan.merge):
            arriving[-1] += [
                copies.start(c_ins[s].at[rows], c.at[s, rows, :]),
                copies.start(a_ins[s].at[rows], a.at[s, rows, :]),
            ]
    ranking = copies.start(rank_in, rank)

    for g in range(groups):
        if g % here == 0:
            finish(arriving[g // here])
        rows = slice(g * block, (g + 1) * block)
        for p in range(plan.pairs):
            cols = slice(p * LANES, (p + 1) * LANES)
            at = (g * plan.pairs + p) * N
            readers = jnp.concatenate([c[s, rows, cols] for s in range(plan.merge)], axis=0)
            read = read_out(readers, state[at : at + N, :].astype(f32), block)
            decays = [plan.decay(decay_refs, s, p, g) for s in range(plan.merge)]
            if plan.merge == 2:
                both = decays[0] * decays[1]
                decays = [jnp.where(first, decays[0], both), jnp.where(first, both, decays[1])]
            for s in range(plan.merge):
                there = slice(s * width + p * LANES, s * width + (p + 1) * LANES)
                mixed[rows, there] = (
                    a[s, rows, cols] + decays[s] * read[s * block : (s + 1) * block]
                ).astype(bf16)

    ranking.wait()
    local = tokens // plan.peers
    for k in list(range(1, plan.peers)) + [0]:
        placed = back_rows(rank, k * local, mixed, local)
        for s in range(plan.merge):
            out_refs[s * plan.peers + k][...] = placed[:, s * width : (s + 1) * width]


def back_rows(rank, start, mixed, rows):
    tokens = rank.shape[0]
    step = min(256, rows)
    placed = []
    for at in range(start, start + rows, step):
        place = rank[at : at + step, :]
        lane = lax.broadcasted_iota(jnp.int32, place.shape, 1)
        pick = jnp.concatenate(
            [
                jnp.where((lane + t).astype(f32) == place, 1.0, 0.0).astype(bf16)
                for t in range(0, tokens, LANES)
            ],
            axis=1,
        )
        placed.append(jnp.dot(pick, mixed[...], preferred_element_type=f32).astype(bf16))
    return jnp.concatenate(placed, axis=0)


def mix(plan, decays, attended, readers, state, rank, groups):
    tokens = rank.shape[0]
    width = attended[0].shape[1]
    count = plan.merge * plan.peers
    return pl.pallas_call(
        functools.partial(mix_kernel, plan, groups),
        in_specs=[smem] * plan.merge + [hbm] * (2 * plan.merge + 2),
        out_specs=(vmem,) * count,
        out_shape=(jax.ShapeDtypeStruct((tokens // plan.peers, width), bf16),) * count,
        scratch_shapes=[
            pltpu.VMEM((plan.merge, tokens, width), f32),
            pltpu.VMEM((plan.merge, tokens, width), bf16),
            pltpu.VMEM(state.shape, bf16),
            pltpu.VMEM(rank.shape, f32),
            pltpu.VMEM((tokens, plan.merge * width), bf16),
            Copies.scratch(),
        ],
        compiler_params=params(56),
        cost_estimate=cost(4 * tokens * tokens * width, 2 * tokens * tokens + 16 * tokens * width),
        name="mix",
    )(*decays, *attended, *readers, state, rank)


def out_kernel(plan, sources, w_ref, *refs):
    part_refs, base_refs, out_ref = refs[: len(sources)], refs[len(sources) : -1], refs[-1]
    depth = part_refs[0].shape[1]
    core, me = plan.core(), lax.axis_index("head")
    total = base_refs[0][...] if base_refs else 0.0
    for (s, k), part in zip(sources, part_refs):
        owner = lax.rem(me - k + plan.peers, plan.peers) * plan.merge
        owner = owner + (core if s == 0 else 1 - core)
        rows = pl.ds(pl.multiple_of(owner * depth, depth), depth)
        total = total + jnp.dot(part[...], w_ref[rows, :], preferred_element_type=f32)
    out_ref[...] = total.astype(out_ref.dtype)


def project_out(plan, w, parts, base, kind):
    local, width = next(iter(parts.values())).shape[0], w.shape[1]
    return pl.pallas_call(
        functools.partial(out_kernel, plan, list(parts)),
        out_shape=jax.ShapeDtypeStruct((local, width), kind),
        compiler_params=params(),
        cost_estimate=cost(0, 4 * local),
        name="project_out",
    )(w, *parts.values(), *base)


def body(frames_in, in_weight, out_weight, block_ids, block_lists, decays):
    local_tokens = frames_in.shape[1]
    heads_here = decays.shape[1]
    groups = block_lists.shape[0]
    me = lax.axis_index("head")
    plan = Plan(lax.axis_size("tm"), lax.axis_size("head"), heads_here, frames_in.shape[2])

    own = frames_in[0]
    arriving = [plan.to_peer(own, plan.peers - k, False) for k in range(1, plan.peers)]
    owns = [own] + [plan.swap(own)] * (plan.merge - 1)
    rates = [decays[0]] + [plan.swap(decays[0])] * (plan.merge - 1)
    block = reorder(plan, [in_weight] + [plan.swap(in_weight)] * (plan.merge - 1))
    ids = jnp.roll(block_ids, -me * local_tokens)
    ids, rates = lax.optimization_barrier((ids, rates))
    rank, places = rank_tokens(ids, groups)
    part = place_tokens(plan, rank, 0, owns, [])

    def fill(arriving):
        if plan.merge == 2:
            arriving = arriving + [plan.swap(tokens) for tokens in arriving]
        return place_tokens(plan, rank, local_tokens, arriving, [part])

    if plan.ringed:
        blocks, crossed = [block], []
        half = block.shape[0] // 2
        for k in range(plan.along - 1):
            with_ = part if k == 0 else ()
            if k == plan.along - 2:
                arriving, _ = lax.optimization_barrier((arriving, blocks[-1]))
                x = with_ = fill(arriving)
            passed, across, with_ = lax.optimization_barrier(
                (plan.round(blocks[-1]), plan.cross(blocks[-1]), with_)
            )
            blocks.append(passed)
            crossed.append(across)
        last = [plan.cross(blocks[-1][:half]), plan.round(crossed[-1][half:])]
        weights = blocks + crossed + last
    else:
        weights = [
            lax.all_gather(block, "tm", axis=0, tiled=True, axis_index_groups=plan.groups())
        ]
        x = fill(arriving)
    if plan.ringed:
        v, b, x_last = project(plan, x, weights[:-2])
        local, total = block_updates(plan, rates, v, b, x_last, last, groups)
    else:
        v, b, x_last = project(plan, x, weights)
        local, total = block_updates(plan, rates, v, b, x_last, [], groups)

    def exchange(blocks):
        return lax.all_to_all(
            blocks, "tm", split_axis=0, concat_axis=0, tiled=True,
            axis_index_groups=plan.groups(),
        )

    share = local.shape[1] // plan.chips
    arrived = exchange(total)
    attended = [attend(plan, 0, block_lists, x, weights, local)]
    arrived, attended = lax.optimization_barrier((arrived, attended))
    states = scan_states(plan, arrived, share)
    x, states = lax.optimization_barrier((x, states))
    if plan.merge == 2:
        attended.append(attend(plan, 1, block_lists, x, weights, local))
    state = exchange(states).reshape(-1, LANES)

    bases, readers = ([a[i] for a in attended] for i in range(2))
    mixed = mix(plan, rates, bases, readers, state, places, groups)
    moved = {
        (s, k): plan.to_peer(mixed[s * plan.peers + k], k, s == 1)
        for s in range(plan.merge)
        for k in range(1, plan.peers)
    }
    near = {(0, 0): mixed[0]}
    if plan.merge == 2:
        near[1, 0] = plan.swap(mixed[plan.peers])
    result = project_out(plan, out_weight, near, [], f32)
    return project_out(plan, out_weight, moved, [result], bf16)[None]


def solution(mesh):
    return jax.shard_map(
        body,
        mesh=mesh,
        in_specs=(P("tm", "head", None), P("tm", "head"), P(), P(), P(), P("tm", "head", None)),
        out_specs=P("tm", "head", None),
        check_vma=False,
    )
```

```python
import functools
import math

import jax
import jax.numpy as jnp
from jax import lax
from jax.experimental import pallas as pl
from jax.experimental.pallas import tpu as pltpu
from jax.sharding import PartitionSpec as P

HD = 64
N = 64
LANES = 2 * HD
PIECES = 5
EARLY = (2, 3)
LATE = (0, 1, 4)

epsilon = 1e-06

vmem = pl.BlockSpec(memory_space=pltpu.VMEM)
smem = pl.BlockSpec(memory_space=pltpu.SMEM)

hbm = pl.BlockSpec(memory_space=pltpu.HBM)

f32 = jnp.float32
bf16 = jnp.bfloat16


def params(mib=16):
    return pltpu.CompilerParams(vmem_limit_bytes=mib << 20)


def cost(flops, nbytes, transcendentals=0):
    return pl.CostEstimate(
        flops=int(flops), bytes_accessed=int(nbytes), transcendentals=int(transcendentals)
    )


def first_half(shape):
    return lax.broadcasted_iota(jnp.int32, shape, len(shape) - 1) < HD


class Plan:
    def __init__(self, frames, peers, heads_here, width):
        self.merge = 2 if frames % 2 == 0 and heads_here % 4 == 0 else 1
        self.frames, self.peers = frames, peers
        self.heads = heads_here // self.merge
        self.pairs = self.heads // 2
        self.chips = frames // self.merge
        self.across = 2 if self.chips % 2 == 0 else 1
        self.along = self.chips // self.across
        self.ringed = self.across == 2 and 2 <= self.along <= 8 and width % (self.chips * LANES) == 0

    def core(self):
        return lax.rem(lax.axis_index("tm"), self.merge)

    def chip(self):
        return lax.div(lax.axis_index("tm"), self.merge)

    def swap(self, block):
        return lax.ppermute(block, "tm", [(t, t ^ 1) for t in range(self.frames)])

    def round(self, block):
        a, b, c = self.along, self.across, self.merge
        pairs = [(t, (t + b * c) % (a * b * c)) for t in range(self.frames)]
        return lax.ppermute(block, "tm", pairs)

    def cross(self, block):
        c = self.merge
        pairs = [(t, (t // c ^ 1) * c + t % c) for t in range(self.frames)]
        return lax.ppermute(block, "tm", pairs)

    def last_chip(self):
        a, b = lax.div(self.chip(), self.across), lax.rem(self.chip(), self.across)
        return lax.rem(a + 1, self.along) * self.across + (self.across - 1 - b)

    def places(self, refs):
        if len(refs) == 1:
            return [(refs[0], slice(None))]
        rows = refs[0].shape[0]
        a, b = lax.div(self.chip(), self.across), lax.rem(self.chip(), self.across)
        n = self.along
        made = []
        for i, ref in enumerate(refs):
            k, flip = (i, 0) if i < n else (min(i - n, n - 1), 1)
            there = lax.rem(a - k + n, n) * self.across
            at = (there + (1 - b if flip else b)) * rows
            at = at + (rows // 2 if i == 2 * n else 0)
            made.append((ref, pl.ds(pl.multiple_of(at, rows // 2), ref.shape[0])))
        return made

    def to_peer(self, block, k, other):
        if not other:
            pairs = [(j, (j + k) % self.peers) for j in range(self.peers)]
            return lax.ppermute(block, "head", pairs)
        if k == 0:
            return self.swap(block)
        pairs = [
            (t * self.peers + j, (t ^ 1) * self.peers + (j + k) % self.peers)
            for t in range(self.frames)
            for j in range(self.peers)
        ]
        return lax.ppermute(block, ("tm", "head"), pairs)

    def groups(self):
        if self.merge == 1:
            return None
        return [[j * self.merge + c for j in range(self.chips)] for c in range(self.merge)]

    def decay(self, refs, slot, pair, g):
        head = self.core() * self.heads + 2 * pair
        return halves((1, LANES), refs[slot][head, g], refs[slot][head + 1, g])

    def last_decay(self, refs, pair, g):
        if self.merge == 1:
            return self.decay(refs, 0, pair, g)
        one, two = (self.decay(refs, slot, pair, g) for slot in range(2))
        return jnp.where(self.core() == 0, two, one)


class Copies:
    room = 48

    def __init__(self, sems):
        self.sems, self.count = sems, 0

    def start(self, src, dst):
        copy = pltpu.make_async_copy(src, dst, self.sems.at[self.count])
        copy.start()
        self.count += 1
        return copy

    @staticmethod
    def scratch():
        return pltpu.SemaphoreType.DMA((Copies.room,))


def finish(copies):
    for copy in copies:
        copy.wait()


def halves(shape, one, two):
    return jnp.where(first_half(shape), one, two)


def reorder_kernel(plan, *refs):
    w_refs, out_ref = refs[:-1], refs[-1]
    rows = w_refs[0].shape[0]
    width = plan.heads * PIECES * HD
    first = plan.core() == 0

    def chosen(ref, at):
        one = ref[:, at : at + HD]
        if plan.merge == 1:
            return one
        return jnp.where(first, one, ref[:, width + at : width + at + HD])

    order = [(p, i) for i in EARLY for p in range(plan.pairs)]
    order += [(p, i) for p in range(plan.pairs) for i in LATE]
    for n, (p, i) in enumerate(order):
        blocks = []
        for ref in w_refs:
            one, two = (chosen(ref, ((2 * p + h) * PIECES + i) * HD) for h in range(2))
            blocks.append(jnp.concatenate([one, two], axis=1))
        for s, block in enumerate(blocks):
            if plan.merge == 2:
                block = jnp.where(first, block, blocks[1 - s])
            out_ref[s * rows : (s + 1) * rows, n * LANES : (n + 1) * LANES] = block


def reorder(plan, weights):
    rows = weights[0].shape[0]
    return pl.pallas_call(
        functools.partial(reorder_kernel, plan),
        out_shape=jax.ShapeDtypeStruct((plan.merge * rows, plan.heads * PIECES * HD), bf16),
        compiler_params=params(),
        cost_estimate=cost(0, 4 * weights[0].size),
        name="reorder",
    )(*weights)


def normalise(part, out, at):
    step = min(128, part.shape[0])

    def norm(c, _):
        start = pl.multiple_of(c * step, step)
        wide = part[pl.ds(start, step), :].astype(f32)
        scale = lax.rsqrt(jnp.mean(wide * wide, axis=-1, keepdims=True) + epsilon)
        out[pl.ds(at + start, step), :] = (wide * scale).astype(bf16)
        return 0

    lax.fori_loop(0, part.shape[0] // step, norm, 0)


def rank_kernel(groups, ids_ref, row_ref, col_ref):
    tokens = ids_ref.shape[1]
    block = tokens // groups
    label = lax.broadcasted_iota(jnp.int32, (groups, tokens), 0)
    held = label == ids_ref[...]
    held_bf = jnp.where(held, 1.0, 0.0).astype(bf16)
    counts = []
    for c in range(tokens // 256):
        before = lax.broadcasted_iota(jnp.int32, (tokens, 256), 0) < (
            lax.broadcasted_iota(jnp.int32, (tokens, 256), 1) + c * 256
        )
        counts.append(
            jnp.dot(held_bf, jnp.where(before, 1.0, 0.0).astype(bf16), preferred_element_type=f32)
        )
    count = jnp.concatenate(counts, axis=1)
    rank = jnp.sum(
        jnp.where(held, count + (label * block).astype(f32), 0.0), axis=0, keepdims=True
    )
    row_ref[...] = rank
    for at in range(0, tokens, LANES):
        wide = jnp.broadcast_to(rank[:, at : at + LANES], (LANES, LANES))
        col_ref[at : at + LANES, :] = wide.T


def rank_tokens(ids, groups):
    tokens = ids.shape[0]
    return pl.pallas_call(
        functools.partial(rank_kernel, groups),
        out_shape=(
            jax.ShapeDtypeStruct((1, tokens), f32),
            jax.ShapeDtypeStruct((tokens, LANES), f32),
        ),
        compiler_params=params(),
        cost_estimate=cost(0, 4 * tokens),
        name="rank_tokens",
    )(ids.reshape(1, tokens))


def picks(rank, at, rows):
    places = lax.broadcasted_iota(jnp.int32, (rows, rank.shape[1]), 0) + at
    return jnp.where(places.astype(f32) == rank, 1.0, 0.0).astype(bf16)


def place_kernel(merge, parts, start, rank_ref, *refs):
    frame_refs, refs = refs[: merge * parts], refs[merge * parts :]
    base_refs, (x_ref, normed) = refs[:-2], refs[-2:]
    tokens = rank_ref.shape[1]
    count = normed.shape[1]
    step = 256
    for s in range(merge):
        at = 0
        for ref in frame_refs[s * parts : (s + 1) * parts]:
            normalise(ref, normed.at[s], at)
            at += ref.shape[0]
    for at in range(0, tokens, step):
        pick = picks(rank_ref[:, start : start + count], at, step)
        for s in range(merge):
            there = slice(s * tokens + at, s * tokens + at + step)
            placed = jnp.dot(pick, normed[s], preferred_element_type=f32).astype(bf16)
            for base in base_refs:
                placed = base[there, :] + placed
            x_ref[there, :] = placed


def place_tokens(plan, rank, start, frames, base):
    tokens = rank.shape[1]
    width = frames[0].shape[1]
    parts = len(frames) // plan.merge
    count = parts * frames[0].shape[0]
    return pl.pallas_call(
        functools.partial(place_kernel, plan.merge, parts, start),
        out_shape=jax.ShapeDtypeStruct((plan.merge * tokens, width), bf16),
        scratch_shapes=[pltpu.VMEM((plan.merge, count, width), bf16)],
        compiler_params=params(),
        cost_estimate=cost(0, 4 * tokens),
        name="place_tokens",
    )(rank, *frames, *base)


def project_kernel(plan, x_ref, *refs):
    w_refs, (v_ref, b_ref, rest_ref, w, turned) = refs[:-5], refs[-5:]
    every = x_ref.shape[0]
    step = 256
    cols = plan.pairs * LANES
    if len(w_refs) > 1:
        w[...] = jnp.zeros_like(w)
        turned[...] = jnp.zeros_like(turned)
    for ref, rows in plan.places(w_refs):
        w[rows, :] = ref[:, :cols]
        turned[rows, :] = ref[:, cols : 2 * cols]
    maps = jnp.concatenate(
        [
            turned[at : at + LANES, :].astype(f32).T.astype(bf16)
            for at in range(0, turned.shape[0], LANES)
        ],
        axis=1,
    )
    for at in range(0, every, step):
        x = x_ref[at : at + step, :]
        v_ref[at : at + step, :] = jnp.dot(x, w[...], preferred_element_type=f32)
        b_ref[:, at : at + step] = lax.dot_general(
            maps, x, (((1,), (1,)), ((), ())), preferred_element_type=f32
        )
    count = rest_ref.shape[1]
    there = plan.last_chip() * count
    for at in range(0, every, step):
        rest = x_ref[at : at + step, :count]
        for c in range(count, x_ref.shape[1], count):
            rest = jnp.where(there == c, x_ref[at : at + step, c : c + count], rest)
        rest_ref[at : at + step, :] = rest


def project(plan, x, weights):
    every, width = x.shape
    cols = plan.pairs * LANES
    count = max(LANES, width // plan.chips)
    return pl.pallas_call(
        functools.partial(project_kernel, plan),
        out_shape=(
            jax.ShapeDtypeStruct((every, cols), f32),
            jax.ShapeDtypeStruct((cols, every), f32),
            jax.ShapeDtypeStruct((every, count), bf16),
        ),
        scratch_shapes=[pltpu.VMEM((width, cols), bf16), pltpu.VMEM((width, cols), bf16)],
        compiler_params=params(),
        cost_estimate=cost(0, 4 * width),
        name="project",
    )(x, *weights)


def update_kernel(plan, groups, *refs):
    decay_refs, refs = refs[: plan.merge], refs[plan.merge :]
    v_ref, b_ref, x_ref, last_refs, (left, total_ref, u) = (
        refs[0], refs[1], refs[2], refs[3:-3], refs[-3:]
    )
    every = v_ref.shape[0]
    tokens = every // plan.merge
    block = tokens // groups
    step = 256
    here = step // block
    cols = plan.pairs * LANES
    if last_refs:
        w = jnp.concatenate([ref[:, : 2 * cols] for ref in last_refs], axis=0)
        maps = w[:, cols:].astype(f32).T.astype(bf16)
        w = w[:, :cols]

    lane = lax.div(lax.broadcasted_iota(jnp.int32, (LANES, step), 1), block)
    for at in range(0, every, step):
        there = slice(at, at + step)
        values, b = v_ref[there, :], b_ref[:, there]
        if last_refs:
            x = x_ref[there, :]
            values = values + jnp.dot(x, w, preferred_element_type=f32)
            b = b + lax.dot_general(
                maps, x, (((1,), (1,)), ((), ())), preferred_element_type=f32
            )
        values = values.astype(bf16)
        for p in range(plan.pairs):
            mine = b[p * LANES : (p + 1) * LANES]
            wide = jnp.concatenate(
                [jnp.where(lane == i, mine, 0.0).astype(bf16) for i in range(here)], axis=0
            )
            outer = jnp.dot(
                wide, values[:, p * LANES : (p + 1) * LANES], preferred_element_type=f32
            )
            for i in range(here):
                m = outer[i * 2 * N : (i + 1) * 2 * N]
                row = ((at % tokens // block + i) * plan.pairs + p) * N
                u[at // tokens, row : row + N, :] = halves((N, LANES), m[:N], m[N:])

    peers = total_ref.shape[0]
    share = u.shape[1] // peers
    items = max(1, share // N)
    size = min(N, share)
    first = plan.core() == 0
    for d in range(peers):
        for i in range(items):
            row = d * share + i * N
            rows = slice(row, row + size)
            p, g = row // N % plan.pairs, row // N // plan.pairs
            product = last = plan.last_decay(decay_refs, p, g)
            if plan.merge == 2:
                one, two = u[0, rows, :], u[1, rows, :]
                one, two = (
                    one + jnp.where(first, 0.0, last) * two,
                    two + jnp.where(first, last, 0.0) * one,
                )
                left[0, rows, :] = one.astype(bf16)
                left[1, rows, :] = two.astype(bf16)
                total = jnp.where(first, two, one)
                product = plan.decay(decay_refs, 0, p, g) * plan.decay(decay_refs, 1, p, g)
            else:
                total = u[0, rows, :]
                left[0, rows, :] = total.astype(bf16)
            total_ref[d, i * size : (i + 1) * size, :] = total.astype(bf16)
            for n in range(3):
                piece = product.astype(bf16)
                at = share + n * items + i
                total_ref[d, at : at + 1, :] = piece
                product = product - piece.astype(f32)


def share_rows(share):
    return share + 16 * -(-3 * max(1, share // N) // 16)


def block_updates(plan, decays, v, b, x, last, groups):
    every, cols = v.shape
    rows = plan.pairs * groups * N
    share = rows // plan.chips
    return pl.pallas_call(
        functools.partial(update_kernel, plan, groups),
        in_specs=[smem] * plan.merge + [vmem] * (3 + len(last)),
        out_shape=(
            jax.ShapeDtypeStruct((plan.merge, rows, LANES), bf16),
            jax.ShapeDtypeStruct((plan.chips, share_rows(share), LANES), bf16),
        ),
        scratch_shapes=[pltpu.VMEM((plan.merge, rows, LANES), f32)],
        compiler_params=params(),
        cost_estimate=cost(4 * every * 256 * 2 * cols, 6 * every * cols),
        name="block_updates",
    )(*decays, v, b, x, *last)


def scan_kernel(plan, u_ref, *s_refs):
    splits = len(s_refs)
    share = s_refs[0].shape[1] * splits
    size = min(share, N)
    items = share // size
    for i in range(items):
        out_ref, to = s_refs[i % splits], i // splits * size
        state = jnp.zeros((size, LANES), f32)
        for j in range(plan.chips):
            out_ref[j, to : to + size, :] = state.astype(bf16)
            decay = jnp.zeros((1, LANES), f32)
            for n in range(3):
                row = share + n * items + i
                decay = decay + u_ref[j, row : row + 1, :].astype(f32)
            state = decay * state + u_ref[j, i * size : (i + 1) * size, :].astype(f32)


def scan_states(plan, update, share, splits):
    return pl.pallas_call(
        functools.partial(scan_kernel, plan),
        out_shape=(jax.ShapeDtypeStruct((plan.chips, share // splits, LANES), bf16),) * splits,
        compiler_params=params(),
        cost_estimate=cost(2 * update.size, 4 * update.size),
        name="scan_states",
    )(update)


def attend_kernel(plan, groups, *refs):
    lists_ref, x_in, local_in, refs = refs[0], refs[1], refs[2], refs[3:]
    ends = 2 * plan.merge + 10
    w_refs, refs = refs[:-ends], refs[-ends:]
    a_outs, refs = refs[: plan.merge], refs[plan.merge :]
    c_outs, refs = refs[: plan.merge], refs[plan.merge :]
    x, local, w, q_ref, k_ref, wide_v, e_ref, a, c_ref, sems = refs
    copies = Copies(sems)
    tokens = a.shape[1]
    chosen = lists_ref.shape[0] // groups
    block = tokens // groups
    step = 256
    per = step // block
    wide = plan.pairs * LANES

    weights, arriving = [], []
    for ref, rows in plan.places(w_refs):
        weights.append(copies.start(ref.at[:, :wide], w.at[rows, :wide]))
        weights.append(copies.start(ref.at[:, 2 * wide :], w.at[rows, wide:]))
    for at in range(0, plan.merge * tokens, step):
        arriving.append(copies.start(x_in.at[at : at + step], x.at[at : at + step]))
    later = [copies.start(local_in.at[s], local.at[s]) for s in range(plan.merge)]

    same = lax.div(lax.broadcasted_iota(jnp.int32, (2 * LANES, 2 * LANES), 0), HD) == lax.div(
        lax.broadcasted_iota(jnp.int32, (2 * LANES, 2 * LANES), 1), HD
    )
    same = jnp.where(same, 1.0, 0.0).astype(bf16)

    def head_norm(values):
        square = values * values
        high = square.astype(bf16)
        low = (square - high.astype(f32)).astype(bf16)
        total = jnp.dot(high, same, preferred_element_type=f32)
        total = total + jnp.dot(low, same, preferred_element_type=f32)
        return values * lax.rsqrt(total * (1.0 / HD) + epsilon)

    half = first_half((step, LANES))
    scale = math.log2(math.e) / math.sqrt(HD)
    starts = [
        [pl.multiple_of(lists_ref[g * chosen + j] * block, block) for j in range(chosen)]
        for g in range(groups)
    ]
    for p in range(plan.pairs):
        wide_v[p, :, LANES:] = jnp.ones((tokens, LANES), bf16)
    finish(weights)
    leaving = []
    for slot in range(plan.merge):
        for at in range(0, tokens, step):
            rows = slice(at, at + step)
            there = slot * tokens + at
            arriving[there // step].wait()
            every = jnp.dot(
                x[there : there + step, :], w[...], preferred_element_type=f32
            ).astype(bf16)
            for p in range(plan.pairs):
                cols = slice(p * LANES, (p + 1) * LANES)
                wide_v[p, rows, :LANES] = every[:, cols]
                first = wide + 3 * p * LANES
                c_ref[slot, rows, cols] = every[:, first + 2 * LANES : first + 3 * LANES]
                both = head_norm(every[:, first : first + 2 * LANES].astype(f32))
                k_ref[p, rows, :] = both[:, LANES:].astype(bf16)
                q = both[:, :LANES]
                one = jnp.where(half, q, 0.0).astype(bf16)
                two = jnp.where(half, 0.0, q).astype(bf16)
                for i in range(per):
                    part = slice(i * block, (i + 1) * block)
                    q_ref[p, at // block + i] = jnp.concatenate([one[part], two[part]], axis=0)
        leaving.append(copies.start(c_ref.at[slot], c_outs[slot]))
        for g in range(groups):
            for p in range(plan.pairs):
                keys = jnp.concatenate([k_ref[p, pl.ds(s, block), :] for s in starts[g]], axis=0)
                score = lax.dot_general(
                    q_ref[p, g], keys, (((1,), (1,)), ((), ())), preferred_element_type=f32
                )
                e_ref[p, g] = jnp.exp2(score * scale).astype(bf16)
        for g in range(groups):
            rows = slice(g * block, (g + 1) * block)
            for p in range(plan.pairs):
                cols = slice(p * LANES, (p + 1) * LANES)
                values = jnp.concatenate(
                    [wide_v[p, pl.ds(s, block), :] for s in starts[g]], axis=0
                )
                both = jnp.dot(e_ref[p, g], values, preferred_element_type=f32)
                both = both[:, :LANES] / both[:, LANES:]
                a[slot, rows, cols] = halves((block, LANES), both[:block], both[block:])
        later[slot].wait()
        for g in range(groups):
            rows = slice(g * block, (g + 1) * block)
            for p in range(plan.pairs):
                cols = slice(p * LANES, (p + 1) * LANES)
                items = slice((g * plan.pairs + p) * N, (g * plan.pairs + p + 1) * N)
                a[slot, rows, cols] = a[slot, rows, cols] + read_out(
                    c_ref[slot, rows, cols], local[slot, items, :].astype(f32), block
                )
        leaving.append(copies.start(a.at[slot], a_outs[slot]))
    finish(leaving)


def attend(plan, groups, lists, x, weights, local):
    every, width = x.shape
    chosen = lists.shape[0] // groups
    tokens = every // plan.merge
    block = tokens // groups
    cols = plan.pairs * LANES
    return pl.pallas_call(
        functools.partial(attend_kernel, plan, groups),
        in_specs=[smem] + [hbm] * (2 + len(weights)),
        out_specs=(hbm,) * (2 * plan.merge),
        scratch_shapes=[
            pltpu.VMEM((every, width), bf16),
            pltpu.VMEM(local.shape, bf16),
            pltpu.VMEM((width, 4 * cols), bf16),
            pltpu.VMEM((plan.pairs, groups, 2 * block, LANES), bf16),
            pltpu.VMEM((plan.pairs, tokens, LANES), bf16),
            pltpu.VMEM((plan.pairs, tokens, 2 * LANES), bf16),
            pltpu.VMEM((plan.pairs, groups, 2 * block, chosen * block), bf16),
            pltpu.VMEM((plan.merge, tokens, cols), f32),
            pltpu.VMEM((plan.merge, tokens, cols), bf16),
            Copies.scratch(),
        ],
        out_shape=(jax.ShapeDtypeStruct((tokens, cols), f32),) * plan.merge
        + (jax.ShapeDtypeStruct((tokens, cols), bf16),) * plan.merge,
        compiler_params=params(60),
        cost_estimate=cost(
            6 * every * width * 3 * cols,
            4 * (every * width + 5 * width * cols + local.size),
            2 * plan.pairs * every * chosen * block,
        ),
        name="attend",
    )(lists, x, local, *weights)


def read_out(readers, state, block):
    half = first_half(state.shape)
    wide = jnp.concatenate([jnp.where(half, state, 0.0), jnp.where(half, 0.0, state)], axis=0)
    return jnp.dot(readers, wide.astype(bf16), preferred_element_type=f32) * (
        1.0 / (N * math.sqrt(block))
    )


def mix_kernel(plan, groups, pairs, *refs):
    decay_refs, refs = refs[: plan.merge], refs[plan.merge :]
    a_ins, refs = refs[: plan.merge], refs[plan.merge :]
    c_ins, refs = refs[: plan.merge], refs[plan.merge :]
    s_in, rank_in, refs = refs[0], refs[1], refs[2:]
    out_refs, (a, c, state, rank, mixed, sems) = refs[:-6], refs[-6:]
    copies = Copies(sems)
    tokens = rank.shape[0]
    block = tokens // groups
    width = a.shape[2]
    here = groups // 2
    many = here * len(pairs) * N
    first = plan.core() == 0
    cols_in = slice(pairs[0] * LANES, (pairs[-1] + 1) * LANES)

    arriving = []
    for i in range(2):
        rows = slice(i * here * block, (i + 1) * here * block)
        items = slice(i * many, (i + 1) * many)
        arriving.append([copies.start(s_in.at[items], state.at[items])])
        for s in range(plan.merge):
            arriving[-1] += [
                copies.start(c_ins[s].at[rows, cols_in], c.at[s, rows, :]),
                copies.start(a_ins[s].at[rows, cols_in], a.at[s, rows, :]),
            ]
    ranking = copies.start(rank_in, rank)

    for g in range(groups):
        if g % here == 0:
            finish(arriving[g // here])
        rows = slice(g * block, (g + 1) * block)
        for i, p in enumerate(pairs):
            cols = slice(i * LANES, (i + 1) * LANES)
            at = (g * len(pairs) + i) * N
            readers = jnp.concatenate([c[s, rows, cols] for s in range(plan.merge)], axis=0)
            read = read_out(readers, state[at : at + N, :].astype(f32), block)
            decays = [plan.decay(decay_refs, s, p, g) for s in range(plan.merge)]
            if plan.merge == 2:
                both = decays[0] * decays[1]
                decays = [jnp.where(first, decays[0], both), jnp.where(first, both, decays[1])]
            for s in range(plan.merge):
                there = slice(s * width + i * LANES, s * width + (i + 1) * LANES)
                mixed[rows, there] = (
                    a[s, rows, cols] + decays[s] * read[s * block : (s + 1) * block]
                ).astype(bf16)

    ranking.wait()
    local = tokens // plan.peers
    for k in list(range(1, plan.peers)) + [0]:
        placed = back_rows(rank, k * local, mixed, local)
        for s in range(plan.merge):
            out_refs[s * plan.peers + k][...] = placed[:, s * width : (s + 1) * width]


def back_rows(rank, start, mixed, rows):
    tokens = rank.shape[0]
    step = min(256, rows)
    placed = []
    for at in range(start, start + rows, step):
        place = rank[at : at + step, :]
        lane = lax.broadcasted_iota(jnp.int32, place.shape, 1)
        pick = jnp.concatenate(
            [
                jnp.where((lane + t).astype(f32) == place, 1.0, 0.0).astype(bf16)
                for t in range(0, tokens, LANES)
            ],
            axis=1,
        )
        placed.append(jnp.dot(pick, mixed[...], preferred_element_type=f32).astype(bf16))
    return jnp.concatenate(placed, axis=0)


def mix(plan, pairs, decays, attended, readers, state, rank, groups):
    tokens = rank.shape[0]
    width = len(pairs) * LANES
    count = plan.merge * plan.peers
    return pl.pallas_call(
        functools.partial(mix_kernel, plan, groups, pairs),
        in_specs=[smem] * plan.merge + [hbm] * (2 * plan.merge + 2),
        out_specs=(vmem,) * count,
        out_shape=(jax.ShapeDtypeStruct((tokens // plan.peers, width), bf16),) * count,
        scratch_shapes=[
            pltpu.VMEM((plan.merge, tokens, width), f32),
            pltpu.VMEM((plan.merge, tokens, width), bf16),
            pltpu.VMEM(state.shape, bf16),
            pltpu.VMEM(rank.shape, f32),
            pltpu.VMEM((tokens, plan.merge * width), bf16),
            Copies.scratch(),
        ],
        compiler_params=params(60),
        cost_estimate=cost(4 * tokens * tokens * width, 2 * tokens * tokens + 16 * tokens * width),
        name="mix",
    )(*decays, *attended, *readers, state, rank)


def out_kernel(plan, sources, w_ref, *refs):
    part_refs, base_refs, out_ref = refs[: len(sources)], refs[len(sources) : -1], refs[-1]
    depth = plan.pairs * LANES
    core, me = plan.core(), lax.axis_index("head")
    total = base_refs[0][...] if base_refs else 0.0
    for (s, k, at), part in zip(sources, part_refs):
        owner = lax.rem(me - k + plan.peers, plan.peers) * plan.merge
        owner = owner + (core if s == 0 else 1 - core)
        rows = pl.ds(pl.multiple_of(owner * depth + at, LANES), part.shape[1])
        total = total + jnp.dot(part[...], w_ref[rows, :], preferred_element_type=f32)
    out_ref[...] = total.astype(out_ref.dtype)


def project_out(plan, w, parts, base, kind):
    local, width = next(iter(parts.values())).shape[0], w.shape[1]
    return pl.pallas_call(
        functools.partial(out_kernel, plan, list(parts)),
        out_shape=jax.ShapeDtypeStruct((local, width), kind),
        compiler_params=params(),
        cost_estimate=cost(0, 4 * local),
        name="project_out",
    )(w, *parts.values(), *base)


def body(frames_in, in_weight, out_weight, block_ids, block_lists, decays):
    local_tokens = frames_in.shape[1]
    heads_here = decays.shape[1]
    groups = block_lists.shape[0]
    me = lax.axis_index("head")
    plan = Plan(lax.axis_size("tm"), lax.axis_size("head"), heads_here, frames_in.shape[2])

    own = frames_in[0]
    arriving = [plan.to_peer(own, plan.peers - k, False) for k in range(1, plan.peers)]
    owns = [own] + [plan.swap(own)] * (plan.merge - 1)
    rates = [decays[0]] + [plan.swap(decays[0])] * (plan.merge - 1)
    block = reorder(plan, [in_weight] + [plan.swap(in_weight)] * (plan.merge - 1))
    ids = jnp.roll(block_ids, -me * local_tokens)
    ids, rates, lists = lax.optimization_barrier((ids, rates, block_lists.reshape(-1)))
    rank, places = rank_tokens(ids, groups)
    part = place_tokens(plan, rank, 0, owns, [])

    def fill(arriving):
        if plan.merge == 2:
            arriving = arriving + [plan.swap(tokens) for tokens in arriving]
        return place_tokens(plan, rank, local_tokens, arriving, [part])

    if plan.ringed:
        blocks, crossed = [block], []
        half = block.shape[0] // 2
        for k in range(plan.along - 1):
            with_ = part if k == 0 else ()
            if k == plan.along - 2:
                arriving, _ = lax.optimization_barrier((arriving, blocks[-1]))
                x = with_ = fill(arriving)
            passed, across, with_ = lax.optimization_barrier(
                (plan.round(blocks[-1]), plan.cross(blocks[-1]), with_)
            )
            blocks.append(passed)
            crossed.append(across)
        last = [plan.cross(blocks[-1][:half]), plan.round(crossed[-1][half:])]
        weights = blocks + crossed + last
    else:
        weights = [
            lax.all_gather(block, "tm", axis=0, tiled=True, axis_index_groups=plan.groups())
        ]
        x = fill(arriving)
    if plan.ringed:
        v, b, x_last = project(plan, x, weights[:-2])
        local, total = block_updates(plan, rates, v, b, x_last, last, groups)
    else:
        v, b, x_last = project(plan, x, weights)
        local, total = block_updates(plan, rates, v, b, x_last, [], groups)

    def exchange(blocks):
        return lax.all_to_all(
            blocks, "tm", split_axis=0, concat_axis=0, tiled=True,
            axis_index_groups=plan.groups(),
        )

    share = local.shape[1] // plan.chips
    splits = plan.pairs if share % (plan.pairs * N) == 0 else 1
    arrived = exchange(total)
    attended = attend(plan, groups, lists, x, weights, local)
    arrived, attended = lax.optimization_barrier((arrived, attended))
    bases, readers = attended[: plan.merge], attended[plan.merge :]
    states = [exchange(s) for s in scan_states(plan, arrived, share, splits)]

    near, moved = {}, []
    for i, state in enumerate(states):
        pairs = list(range(plan.pairs)) if splits == 1 else [i]
        mixed = mix(
            plan, pairs, rates, bases, readers, state.reshape(-1, LANES), places, groups
        )
        at = pairs[0] * LANES
        moved.append(
            {
                (s, k, at): plan.to_peer(mixed[s * plan.peers + k], k, s == 1)
                for s in range(plan.merge)
                for k in range(1, plan.peers)
            }
        )
        near[0, 0, at] = mixed[0]
        if plan.merge == 2:
            near[1, 0, at] = plan.swap(mixed[plan.peers])
    for parts in moved[:-1]:
        near |= parts
    result = project_out(plan, out_weight, near, [], f32)
    return project_out(plan, out_weight, moved[-1], [result], bf16)[None]


def solution(mesh):
    return jax.shard_map(
        body,
        mesh=mesh,
        in_specs=(P("tm", "head", None), P("tm", "head"), P(), P(), P(), P("tm", "head", None)),
        out_specs=P("tm", "head", None),
        check_vma=False,
    )
```

```python
import functools
import math

import jax
import jax.numpy as jnp
from jax import lax
from jax.experimental import pallas as pl
from jax.experimental.pallas import tpu as pltpu
from jax.sharding import PartitionSpec as P

HD = 64
N = 64
LANES = 2 * HD
PIECES = 5
EARLY = (2, 3)
LATE = (0, 1, 4)

epsilon = 1e-06

vmem = pl.BlockSpec(memory_space=pltpu.VMEM)
smem = pl.BlockSpec(memory_space=pltpu.SMEM)

hbm = pl.BlockSpec(memory_space=pltpu.HBM)

f32 = jnp.float32
bf16 = jnp.bfloat16


def params(mib=16):
    return pltpu.CompilerParams(vmem_limit_bytes=mib << 20)


def cost(flops, nbytes, transcendentals=0):
    return pl.CostEstimate(
        flops=int(flops), bytes_accessed=int(nbytes), transcendentals=int(transcendentals)
    )


def first_half(shape):
    return lax.broadcasted_iota(jnp.int32, shape, len(shape) - 1) < HD


class Plan:
    def __init__(self, frames, peers, heads_here, width):
        self.merge = 2 if frames % 2 == 0 and heads_here % 4 == 0 else 1
        self.frames, self.peers = frames, peers
        self.heads = heads_here // self.merge
        self.pairs = self.heads // 2
        self.chips = frames // self.merge
        self.across = 2 if self.chips % 2 == 0 else 1
        self.along = self.chips // self.across
        self.ringed = self.across == 2 and 2 <= self.along <= 8 and width % (self.chips * LANES) == 0

    def core(self):
        return lax.rem(lax.axis_index("tm"), self.merge)

    def chip(self):
        return lax.div(lax.axis_index("tm"), self.merge)

    def swap(self, block):
        return lax.ppermute(block, "tm", [(t, t ^ 1) for t in range(self.frames)])

    def round(self, block):
        a, b, c = self.along, self.across, self.merge
        pairs = [(t, (t + b * c) % (a * b * c)) for t in range(self.frames)]
        return lax.ppermute(block, "tm", pairs)

    def cross(self, block):
        c = self.merge
        pairs = [(t, (t // c ^ 1) * c + t % c) for t in range(self.frames)]
        return lax.ppermute(block, "tm", pairs)

    def last_chip(self):
        a, b = lax.div(self.chip(), self.across), lax.rem(self.chip(), self.across)
        return lax.rem(a + 1, self.along) * self.across + (self.across - 1 - b)

    def places(self, refs):
        if len(refs) == 1:
            return [(refs[0], slice(None))]
        rows = refs[0].shape[0]
        a, b = lax.div(self.chip(), self.across), lax.rem(self.chip(), self.across)
        n = self.along
        made = []
        for i, ref in enumerate(refs):
            k, flip = (i, 0) if i < n else (min(i - n, n - 1), 1)
            there = lax.rem(a - k + n, n) * self.across
            at = (there + (1 - b if flip else b)) * rows
            at = at + (rows // 2 if i == 2 * n else 0)
            made.append((ref, pl.ds(pl.multiple_of(at, rows // 2), ref.shape[0])))
        return made

    def to_peer(self, block, k, other):
        if not other:
            pairs = [(j, (j + k) % self.peers) for j in range(self.peers)]
            return lax.ppermute(block, "head", pairs)
        if k == 0:
            return self.swap(block)
        pairs = [
            (t * self.peers + j, (t ^ 1) * self.peers + (j + k) % self.peers)
            for t in range(self.frames)
            for j in range(self.peers)
        ]
        return lax.ppermute(block, ("tm", "head"), pairs)

    def groups(self):
        if self.merge == 1:
            return None
        return [[j * self.merge + c for j in range(self.chips)] for c in range(self.merge)]

    def decay(self, refs, slot, pair, g):
        head = self.core() * self.heads + 2 * pair
        return halves((1, LANES), refs[slot][head, g], refs[slot][head + 1, g])

    def last_decay(self, refs, pair, g):
        if self.merge == 1:
            return self.decay(refs, 0, pair, g)
        one, two = (self.decay(refs, slot, pair, g) for slot in range(2))
        return jnp.where(self.core() == 0, two, one)


class Copies:
    room = 48

    def __init__(self, sems):
        self.sems, self.count = sems, 0

    def start(self, src, dst):
        copy = pltpu.make_async_copy(src, dst, self.sems.at[self.count])
        copy.start()
        self.count += 1
        return copy

    @staticmethod
    def scratch():
        return pltpu.SemaphoreType.DMA((Copies.room,))


def finish(copies):
    for copy in copies:
        copy.wait()


def halves(shape, one, two):
    return jnp.where(first_half(shape), one, two)


def reorder_kernel(plan, *refs):
    w_refs, out_ref = refs[:-1], refs[-1]
    rows = w_refs[0].shape[0]
    width = plan.heads * PIECES * HD
    first = plan.core() == 0

    def chosen(ref, at):
        one = ref[:, at : at + HD]
        if plan.merge == 1:
            return one
        return jnp.where(first, one, ref[:, width + at : width + at + HD])

    order = [(p, i) for i in EARLY for p in range(plan.pairs)]
    order += [(p, i) for p in range(plan.pairs) for i in LATE]
    for n, (p, i) in enumerate(order):
        blocks = []
        for ref in w_refs:
            one, two = (chosen(ref, ((2 * p + h) * PIECES + i) * HD) for h in range(2))
            blocks.append(jnp.concatenate([one, two], axis=1))
        for s, block in enumerate(blocks):
            if plan.merge == 2:
                block = jnp.where(first, block, blocks[1 - s])
            out_ref[s * rows : (s + 1) * rows, n * LANES : (n + 1) * LANES] = block


def reorder(plan, weights):
    rows = weights[0].shape[0]
    return pl.pallas_call(
        functools.partial(reorder_kernel, plan),
        out_shape=jax.ShapeDtypeStruct((plan.merge * rows, plan.heads * PIECES * HD), bf16),
        compiler_params=params(),
        cost_estimate=cost(0, 4 * weights[0].size),
        name="reorder",
    )(*weights)


def normalise(part, out, at):
    step = min(128, part.shape[0])

    def norm(c, _):
        start = pl.multiple_of(c * step, step)
        wide = part[pl.ds(start, step), :].astype(f32)
        scale = lax.rsqrt(jnp.mean(wide * wide, axis=-1, keepdims=True) + epsilon)
        out[pl.ds(at + start, step), :] = (wide * scale).astype(bf16)
        return 0

    lax.fori_loop(0, part.shape[0] // step, norm, 0)


def rank_kernel(groups, ids_ref, row_ref):
    tokens = ids_ref.shape[1]
    block = tokens // groups
    label = lax.broadcasted_iota(jnp.int32, (groups, tokens), 0)
    held = label == ids_ref[...]
    held_bf = jnp.where(held, 1.0, 0.0).astype(bf16)
    counts = []
    for c in range(tokens // 256):
        before = lax.broadcasted_iota(jnp.int32, (tokens, 256), 0) < (
            lax.broadcasted_iota(jnp.int32, (tokens, 256), 1) + c * 256
        )
        counts.append(
            jnp.dot(held_bf, jnp.where(before, 1.0, 0.0).astype(bf16), preferred_element_type=f32)
        )
    count = jnp.concatenate(counts, axis=1)
    row_ref[...] = jnp.sum(
        jnp.where(held, count + (label * block).astype(f32), 0.0), axis=0, keepdims=True
    )


def rank_tokens(ids, groups):
    tokens = ids.shape[0]
    return pl.pallas_call(
        functools.partial(rank_kernel, groups),
        out_shape=jax.ShapeDtypeStruct((1, tokens), f32),
        compiler_params=params(),
        cost_estimate=cost(0, 4 * tokens),
        name="rank_tokens",
    )(ids.reshape(1, tokens))


def turn_kernel(row_ref, col_ref):
    for at in range(0, col_ref.shape[0], LANES):
        col_ref[at : at + LANES, :] = jnp.broadcast_to(
            row_ref[:, at : at + LANES], (LANES, LANES)
        ).T


def turn_places(rank):
    return pl.pallas_call(
        turn_kernel,
        out_shape=jax.ShapeDtypeStruct((rank.shape[1], LANES), f32),
        compiler_params=params(),
        cost_estimate=cost(0, 4 * LANES),
        name="turn_places",
    )(rank)


def picks(rank, at, rows):
    places = lax.broadcasted_iota(jnp.int32, (rows, rank.shape[1]), 0) + at
    return jnp.where(places.astype(f32) == rank, 1.0, 0.0).astype(bf16)


def place_kernel(merge, parts, start, rank_ref, *refs):
    frame_refs, refs = refs[: merge * parts], refs[merge * parts :]
    base_refs, (x_ref, normed) = refs[:-2], refs[-2:]
    tokens = rank_ref.shape[1]
    count = normed.shape[1]
    step = 256
    for s in range(merge):
        at = 0
        for ref in frame_refs[s * parts : (s + 1) * parts]:
            normalise(ref, normed.at[s], at)
            at += ref.shape[0]
    for at in range(0, tokens, step):
        pick = picks(rank_ref[:, start : start + count], at, step)
        for s in range(merge):
            there = slice(s * tokens + at, s * tokens + at + step)
            placed = jnp.dot(pick, normed[s], preferred_element_type=f32).astype(bf16)
            for base in base_refs:
                placed = base[there, :] + placed
            x_ref[there, :] = placed


def place_tokens(plan, rank, start, frames, base):
    tokens = rank.shape[1]
    width = frames[0].shape[1]
    parts = len(frames) // plan.merge
    count = parts * frames[0].shape[0]
    return pl.pallas_call(
        functools.partial(place_kernel, plan.merge, parts, start),
        out_shape=jax.ShapeDtypeStruct((plan.merge * tokens, width), bf16),
        scratch_shapes=[pltpu.VMEM((plan.merge, count, width), bf16)],
        compiler_params=params(),
        cost_estimate=cost(0, 4 * tokens),
        name="place_tokens",
    )(rank, *frames, *base)


def project_kernel(plan, x_ref, *refs):
    w_refs, (v_ref, b_ref, rest_ref, w, turned) = refs[:-5], refs[-5:]
    every = x_ref.shape[0]
    step = 256
    cols = plan.pairs * LANES
    if len(w_refs) > 1:
        w[...] = jnp.zeros_like(w)
        turned[...] = jnp.zeros_like(turned)
    for ref, rows in plan.places(w_refs):
        w[rows, :] = ref[:, :cols]
        turned[rows, :] = ref[:, cols : 2 * cols]
    maps = jnp.concatenate(
        [
            turned[at : at + LANES, :].astype(f32).T.astype(bf16)
            for at in range(0, turned.shape[0], LANES)
        ],
        axis=1,
    )
    for at in range(0, every, step):
        x = x_ref[at : at + step, :]
        v_ref[at : at + step, :] = jnp.dot(x, w[...], preferred_element_type=f32)
        b_ref[:, at : at + step] = lax.dot_general(
            maps, x, (((1,), (1,)), ((), ())), preferred_element_type=f32
        )
    count = rest_ref.shape[1]
    there = plan.last_chip() * count
    for at in range(0, every, step):
        rest = x_ref[at : at + step, :count]
        for c in range(count, x_ref.shape[1], count):
            rest = jnp.where(there == c, x_ref[at : at + step, c : c + count], rest)
        rest_ref[at : at + step, :] = rest


def project(plan, x, weights):
    every, width = x.shape
    cols = plan.pairs * LANES
    count = max(LANES, width // plan.chips)
    return pl.pallas_call(
        functools.partial(project_kernel, plan),
        out_shape=(
            jax.ShapeDtypeStruct((every, cols), f32),
            jax.ShapeDtypeStruct((cols, every), f32),
            jax.ShapeDtypeStruct((every, count), bf16),
        ),
        scratch_shapes=[pltpu.VMEM((width, cols), bf16), pltpu.VMEM((width, cols), bf16)],
        compiler_params=params(),
        cost_estimate=cost(0, 4 * width),
        name="project",
    )(x, *weights)


def update_kernel(plan, groups, *refs):
    decay_refs, refs = refs[: plan.merge], refs[plan.merge :]
    v_ref, b_ref, x_ref, last_refs, (left, total_out, total_ref, u, sems) = (
        refs[0], refs[1], refs[2], refs[3:-5], refs[-5:]
    )
    copies = Copies(sems)
    leaving = []
    every = v_ref.shape[0]
    tokens = every // plan.merge
    block = tokens // groups
    step = 256
    here = step // block
    cols = plan.pairs * LANES
    if last_refs:
        w = jnp.concatenate([ref[:, : 2 * cols] for ref in last_refs], axis=0)
        maps = w[:, cols:].astype(f32).T.astype(bf16)
        w = w[:, :cols]

    lane = lax.div(lax.broadcasted_iota(jnp.int32, (LANES, step), 1), block)
    for at in range(0, every, step):
        there = slice(at, at + step)
        values, b = v_ref[there, :], b_ref[:, there]
        if last_refs:
            x = x_ref[there, :]
            values = values + jnp.dot(x, w, preferred_element_type=f32)
            b = b + lax.dot_general(
                maps, x, (((1,), (1,)), ((), ())), preferred_element_type=f32
            )
        values = values.astype(bf16)
        for p in range(plan.pairs):
            mine = b[p * LANES : (p + 1) * LANES]
            wide = jnp.concatenate(
                [jnp.where(lane == i, mine, 0.0).astype(bf16) for i in range(here)], axis=0
            )
            outer = jnp.dot(
                wide, values[:, p * LANES : (p + 1) * LANES], preferred_element_type=f32
            )
            for i in range(here):
                m = outer[i * 2 * N : (i + 1) * 2 * N]
                row = ((at % tokens // block + i) * plan.pairs + p) * N
                u[at // tokens, row : row + N, :] = halves((N, LANES), m[:N], m[N:])

    peers = total_ref.shape[0]
    share = u.shape[1] // peers
    items = max(1, share // N)
    size = min(N, share)
    first = plan.core() == 0
    for d in range(peers):
        for i in range(items):
            row = d * share + i * N
            rows = slice(row, row + size)
            p, g = row // N % plan.pairs, row // N // plan.pairs
            product = last = plan.last_decay(decay_refs, p, g)
            if plan.merge == 2:
                one, two = u[0, rows, :], u[1, rows, :]
                one, two = (
                    one + jnp.where(first, 0.0, last) * two,
                    two + jnp.where(first, last, 0.0) * one,
                )
                left[0, rows, :] = one.astype(bf16)
                left[1, rows, :] = two.astype(bf16)
                total = jnp.where(first, two, one)
                product = plan.decay(decay_refs, 0, p, g) * plan.decay(decay_refs, 1, p, g)
            else:
                total = u[0, rows, :]
                left[0, rows, :] = total.astype(bf16)
            total_ref[d, i * size : (i + 1) * size, :] = total.astype(bf16)
            for n in range(3):
                piece = product.astype(bf16)
                at = share + n * items + i
                total_ref[d, at : at + 1, :] = piece
                product = product - piece.astype(f32)
        if (d + 1) % (peers // 4) == 0:
            done = slice(d + 1 - peers // 4, d + 1)
            leaving.append(copies.start(total_ref.at[done], total_out.at[done]))
    finish(leaving)


def share_rows(share):
    return share + 16 * -(-3 * max(1, share // N) // 16)


def block_updates(plan, decays, v, b, x, last, groups):
    every, cols = v.shape
    rows = plan.pairs * groups * N
    share = rows // plan.chips
    return pl.pallas_call(
        functools.partial(update_kernel, plan, groups),
        in_specs=[smem] * plan.merge + [vmem] * (3 + len(last)),
        out_specs=(vmem, hbm),
        out_shape=(
            jax.ShapeDtypeStruct((plan.merge, rows, LANES), bf16),
            jax.ShapeDtypeStruct((plan.chips, share_rows(share), LANES), bf16),
        ),
        scratch_shapes=[
            pltpu.VMEM((plan.chips, share_rows(share), LANES), bf16),
            pltpu.VMEM((plan.merge, rows, LANES), f32),
            Copies.scratch(),
        ],
        compiler_params=params(),
        cost_estimate=cost(4 * every * 256 * 2 * cols, 6 * every * cols),
        name="block_updates",
    )(*decays, v, b, x, *last)


def scan_kernel(plan, u_ref, s_ref):
    share = s_ref.shape[1]
    size = min(share, N)
    items = share // size
    for i in range(items):
        at = slice(i * size, (i + 1) * size)
        state = jnp.zeros((size, LANES), f32)
        for j in range(plan.chips):
            s_ref[j, at, :] = state.astype(bf16)
            decay = jnp.zeros((1, LANES), f32)
            for n in range(3):
                row = share + n * items + i
                decay = decay + u_ref[j, row : row + 1, :].astype(f32)
            state = decay * state + u_ref[j, at, :].astype(f32)


def scan_states(plan, update, share):
    return pl.pallas_call(
        functools.partial(scan_kernel, plan),
        out_shape=jax.ShapeDtypeStruct((plan.chips, share, LANES), bf16),
        compiler_params=params(),
        cost_estimate=cost(2 * update.size, 4 * update.size),
        name="scan_states",
    )(update)


def attend_kernel(plan, slot, *refs):
    lists_ref, x_in, local_in, refs = refs[0], refs[1], refs[2], refs[3:]
    w_refs, refs = refs[:-12], refs[-12:]
    a_out, c_out, x, local, w, q_ref, k_ref, wide_v, e_ref, a, c_ref, sems = refs
    copies = Copies(sems)
    tokens = x.shape[0]
    groups, chosen = lists_ref.shape
    block = tokens // groups
    step = 256
    per = step // block
    wide = plan.pairs * LANES

    weights = []
    for ref, rows in plan.places(w_refs):
        weights.append(copies.start(ref.at[:, :wide], w.at[rows, :wide]))
        weights.append(copies.start(ref.at[:, 2 * wide :], w.at[rows, wide:]))
    arriving = []
    for at in range(0, tokens, step):
        from_ = slice(slot * tokens + at, slot * tokens + at + step)
        arriving.append(copies.start(x_in.at[from_], x.at[at : at + step]))
    later = copies.start(local_in.at[slot], local)

    same = lax.div(lax.broadcasted_iota(jnp.int32, (2 * LANES, 2 * LANES), 0), HD) == lax.div(
        lax.broadcasted_iota(jnp.int32, (2 * LANES, 2 * LANES), 1), HD
    )
    same = jnp.where(same, 1.0, 0.0).astype(bf16)

    def head_norm(values):
        square = values * values
        high = square.astype(bf16)
        low = (square - high.astype(f32)).astype(bf16)
        total = jnp.dot(high, same, preferred_element_type=f32)
        total = total + jnp.dot(low, same, preferred_element_type=f32)
        return values * lax.rsqrt(total * (1.0 / HD) + epsilon)

    half = first_half((step, LANES))
    finish(weights)
    for at in range(0, tokens, step):
        rows = slice(at, at + step)
        arriving[at // step].wait()
        every = jnp.dot(x[rows, :], w[...], preferred_element_type=f32).astype(bf16)
        for p in range(plan.pairs):
            cols = slice(p * LANES, (p + 1) * LANES)
            wide_v[p, rows, :LANES] = every[:, cols]
            first = wide + 3 * p * LANES
            c_ref[rows, cols] = every[:, first + 2 * LANES : first + 3 * LANES]
            both = head_norm(every[:, first : first + 2 * LANES].astype(f32))
            k_ref[p, rows, :] = both[:, LANES:].astype(bf16)
            q = both[:, :LANES]
            one = jnp.where(half, q, 0.0).astype(bf16)
            two = jnp.where(half, 0.0, q).astype(bf16)
            for i in range(per):
                part = slice(i * block, (i + 1) * block)
                q_ref[p, at // block + i] = jnp.concatenate([one[part], two[part]], axis=0)
    leaving = [copies.start(c_ref, c_out)]
    later.wait()
    for p in range(plan.pairs):
        wide_v[p, :, LANES:] = jnp.ones((tokens, LANES), bf16)

    scale = math.log2(math.e) / math.sqrt(HD)
    starts = [
        [pl.multiple_of(lists_ref[g, j] * block, block) for j in range(chosen)]
        for g in range(groups)
    ]
    for g in range(groups):
        for p in range(plan.pairs):
            keys = jnp.concatenate([k_ref[p, pl.ds(s, block), :] for s in starts[g]], axis=0)
            score = lax.dot_general(
                q_ref[p, g], keys, (((1,), (1,)), ((), ())), preferred_element_type=f32
            )
            e_ref[p, g] = jnp.exp2(score * scale).astype(bf16)
    for g in range(groups):
        rows = slice(g * block, (g + 1) * block)
        for p in range(plan.pairs):
            cols = slice(p * LANES, (p + 1) * LANES)
            values = jnp.concatenate([wide_v[p, pl.ds(s, block), :] for s in starts[g]], axis=0)
            both = jnp.dot(e_ref[p, g], values, preferred_element_type=f32)
            both = both[:, :LANES] / both[:, LANES:]
            a[rows, cols] = halves((block, LANES), both[:block], both[block:])
    for g in range(groups):
        rows = slice(g * block, (g + 1) * block)
        for p in range(plan.pairs):
            cols = slice(p * LANES, (p + 1) * LANES)
            items = slice((g * plan.pairs + p) * N, (g * plan.pairs + p + 1) * N)
            a[rows, cols] = a[rows, cols] + read_out(
                c_ref[rows, cols], local[items, :].astype(f32), block
            )
        if (g + 1) % per == 0:
            done = slice((g + 1 - per) * block, (g + 1) * block)
            leaving.append(copies.start(a.at[done], a_out.at[done]))
    finish(leaving)


def attend(plan, slot, lists, x, weights, local):
    every, width = x.shape
    groups, chosen = lists.shape
    tokens = every // plan.merge
    block = tokens // groups
    cols = plan.pairs * LANES
    return pl.pallas_call(
        functools.partial(attend_kernel, plan, slot),
        in_specs=[smem] + [hbm] * (2 + len(weights)),
        out_specs=(hbm,) * 2,
        scratch_shapes=[
            pltpu.VMEM((tokens, width), bf16),
            pltpu.VMEM(local.shape[1:], bf16),
            pltpu.VMEM((width, 4 * cols), bf16),
            pltpu.VMEM((plan.pairs, groups, 2 * block, LANES), bf16),
            pltpu.VMEM((plan.pairs, tokens, LANES), bf16),
            pltpu.VMEM((plan.pairs, tokens, 2 * LANES), bf16),
            pltpu.VMEM((plan.pairs, groups, 2 * block, chosen * block), bf16),
            pltpu.VMEM((tokens, cols), f32),
            pltpu.VMEM((tokens, cols), bf16),
            Copies.scratch(),
        ],
        out_shape=(
            jax.ShapeDtypeStruct((tokens, cols), f32),
            jax.ShapeDtypeStruct((tokens, cols), bf16),
        ),
        compiler_params=params(60),
        cost_estimate=cost(
            6 * tokens * width * 3 * cols,
            4 * (tokens * width + 5 * width * cols + local.size),
            2 * plan.pairs * tokens * chosen * block,
        ),
        name="attend",
    )(lists, x, local, *weights)


def read_out(readers, state, block):
    half = first_half(state.shape)
    wide = jnp.concatenate([jnp.where(half, state, 0.0), jnp.where(half, 0.0, state)], axis=0)
    return jnp.dot(readers, wide.astype(bf16), preferred_element_type=f32) * (
        1.0 / (N * math.sqrt(block))
    )


def mix_kernel(plan, groups, *refs):
    decay_refs, refs = refs[: plan.merge], refs[plan.merge :]
    a_ins, refs = refs[: plan.merge], refs[plan.merge :]
    c_ins, refs = refs[: plan.merge], refs[plan.merge :]
    s_in, rank_in, refs = refs[0], refs[1], refs[2:]
    out_refs, (a, c, state, rank, mixed, out, sems) = refs[:-7], refs[-7:]
    copies = Copies(sems)
    tokens = rank.shape[0]
    block = tokens // groups
    width = a.shape[2]
    here = groups // 4
    many = here * plan.pairs * N
    first = plan.core() == 0

    arriving = []
    for i in range(4):
        rows = slice(i * here * block, (i + 1) * here * block)
        items = slice(i * many, (i + 1) * many)
        arriving.append([copies.start(s_in.at[items], state.at[items])])
        for s in range(plan.merge):
            arriving[-1] += [
                copies.start(c_ins[s].at[rows], c.at[s, rows, :]),
                copies.start(a_ins[s].at[rows], a.at[s, rows, :]),
            ]
    ranking = copies.start(rank_in, rank)

    for g in range(groups):
        if g % here == 0:
            finish(arriving[g // here])
        rows = slice(g * block, (g + 1) * block)
        for p in range(plan.pairs):
            cols = slice(p * LANES, (p + 1) * LANES)
            at = (g * plan.pairs + p) * N
            readers = jnp.concatenate([c[s, rows, cols] for s in range(plan.merge)], axis=0)
            read = read_out(readers, state[at : at + N, :].astype(f32), block)
            decays = [plan.decay(decay_refs, s, p, g) for s in range(plan.merge)]
            if plan.merge == 2:
                both = decays[0] * decays[1]
                decays = [jnp.where(first, decays[0], both), jnp.where(first, both, decays[1])]
            for s in range(plan.merge):
                there = slice(s * width + p * LANES, s * width + (p + 1) * LANES)
                mixed[rows, there] = (
                    a[s, rows, cols] + decays[s] * read[s * block : (s + 1) * block]
                ).astype(bf16)

    ranking.wait()
    local = tokens // plan.peers
    leaving = []
    for k in list(range(1, plan.peers)) + [0]:
        placed = back_rows(rank, k * local, mixed, local)
        for s in range(plan.merge):
            i = s * plan.peers + k
            out[i] = placed[:, s * width : (s + 1) * width]
            leaving.append(copies.start(out.at[i], out_refs[i]))
    finish(leaving)


def back_rows(rank, start, mixed, rows):
    tokens = rank.shape[0]
    step = min(256, rows)
    placed = []
    for at in range(start, start + rows, step):
        place = rank[at : at + step, :]
        lane = lax.broadcasted_iota(jnp.int32, place.shape, 1)
        pick = jnp.concatenate(
            [
                jnp.where((lane + t).astype(f32) == place, 1.0, 0.0).astype(bf16)
                for t in range(0, tokens, LANES)
            ],
            axis=1,
        )
        placed.append(jnp.dot(pick, mixed[...], preferred_element_type=f32).astype(bf16))
    return jnp.concatenate(placed, axis=0)


def mix(plan, decays, attended, readers, state, rank, groups):
    tokens = rank.shape[0]
    width = attended[0].shape[1]
    count = plan.merge * plan.peers
    return pl.pallas_call(
        functools.partial(mix_kernel, plan, groups),
        in_specs=[smem] * plan.merge + [hbm] * (2 * plan.merge + 2),
        out_specs=(hbm,) * count,
        out_shape=(jax.ShapeDtypeStruct((tokens // plan.peers, width), bf16),) * count,
        scratch_shapes=[
            pltpu.VMEM((plan.merge, tokens, width), f32),
            pltpu.VMEM((plan.merge, tokens, width), bf16),
            pltpu.VMEM(state.shape, bf16),
            pltpu.VMEM(rank.shape, f32),
            pltpu.VMEM((tokens, plan.merge * width), bf16),
            pltpu.VMEM((count, tokens // plan.peers, width), bf16),
            Copies.scratch(),
        ],
        compiler_params=params(60),
        cost_estimate=cost(4 * tokens * tokens * width, 2 * tokens * tokens + 16 * tokens * width),
        name="mix",
    )(*decays, *attended, *readers, state, rank)


def out_kernel(plan, sources, w_ref, *refs):
    part_refs, base_refs, out_ref = refs[: len(sources)], refs[len(sources) : -3], refs[-3]
    kept, sems = refs[-2:]
    copies = Copies(sems)
    depth = part_refs[0].shape[1]
    core, me = plan.core(), lax.axis_index("head")
    owners = []
    for s, k in sources:
        owner = lax.rem(me - k + plan.peers, plan.peers) * plan.merge
        owners.append(owner + (core if s == 0 else 1 - core))
    leaving = []
    step = min(128, out_ref.shape[0])
    for at in range(0, out_ref.shape[0], step):
        there = slice(at, at + step)
        total = base_refs[0][there, :] if base_refs else 0.0
        for owner, part in zip(owners, part_refs):
            rows = pl.ds(pl.multiple_of(owner * depth, depth), depth)
            total = total + jnp.dot(part[there, :], w_ref[rows, :], preferred_element_type=f32)
        if base_refs:
            kept[there, :] = total.astype(out_ref.dtype)
            leaving.append(copies.start(kept.at[there], out_ref.at[there]))
        else:
            out_ref[there, :] = total.astype(out_ref.dtype)
    finish(leaving)


def project_out(plan, w, parts, base, kind):
    local, width = next(iter(parts.values())).shape[0], w.shape[1]
    return pl.pallas_call(
        functools.partial(out_kernel, plan, list(parts)),
        in_specs=[vmem] * (1 + len(parts) + len(base)),
        out_specs=hbm if base else vmem,
        out_shape=jax.ShapeDtypeStruct((local, width), kind),
        scratch_shapes=[pltpu.VMEM((local, width), kind), Copies.scratch()],
        compiler_params=params(),
        cost_estimate=cost(0, 4 * local),
        name="project_out",
    )(w, *parts.values(), *base)


def body(frames_in, in_weight, out_weight, block_ids, block_lists, decays):
    local_tokens = frames_in.shape[1]
    heads_here = decays.shape[1]
    groups = block_lists.shape[0]
    me = lax.axis_index("head")
    plan = Plan(lax.axis_size("tm"), lax.axis_size("head"), heads_here, frames_in.shape[2])

    own = frames_in[0]
    arriving = [plan.to_peer(own, plan.peers - k, False) for k in range(1, plan.peers)]
    owns = [own] + [plan.swap(own)] * (plan.merge - 1)
    rates = [decays[0]] + [plan.swap(decays[0])] * (plan.merge - 1)
    block = reorder(plan, [in_weight] + [plan.swap(in_weight)] * (plan.merge - 1))
    ids = jnp.roll(block_ids, -me * local_tokens)
    ids, rates = lax.optimization_barrier((ids, rates))
    rank = rank_tokens(ids, groups)

    def fill(arriving, part):
        if plan.merge == 2:
            arriving = arriving + [plan.swap(tokens) for tokens in arriving]
        return place_tokens(plan, rank, local_tokens, arriving, [part])

    if plan.ringed:
        blocks, crossed = [block], []
        half = block.shape[0] // 2
        for k in range(plan.along - 1):
            with_ = rank if k == 0 else ()
            if k == min(1, plan.along - 2):
                rank, owns, _ = lax.optimization_barrier((rank, owns, blocks[-1]))
                part = with_ = place_tokens(plan, rank, 0, owns, [])
                places = turn_places(rank)
            if k == plan.along - 2:
                arriving, _ = lax.optimization_barrier((arriving, blocks[-1]))
                x = with_ = fill(arriving, part)
            passed, across, with_ = lax.optimization_barrier(
                (plan.round(blocks[-1]), plan.cross(blocks[-1]), with_)
            )
            blocks.append(passed)
            crossed.append(across)
        last = [plan.cross(blocks[-1][:half]), plan.round(crossed[-1][half:])]
        weights = blocks + crossed + last
    else:
        weights = [
            lax.all_gather(block, "tm", axis=0, tiled=True, axis_index_groups=plan.groups())
        ]
        places = turn_places(rank)
        x = fill(arriving, place_tokens(plan, rank, 0, owns, []))
    if plan.ringed:
        v, b, x_last = project(plan, x, weights[:-2])
        local, total = block_updates(plan, rates, v, b, x_last, last, groups)
    else:
        v, b, x_last = project(plan, x, weights)
        local, total = block_updates(plan, rates, v, b, x_last, [], groups)

    def exchange(blocks):
        return lax.all_to_all(
            blocks, "tm", split_axis=0, concat_axis=0, tiled=True,
            axis_index_groups=plan.groups(),
        )

    share = local.shape[1] // plan.chips
    arrived = exchange(total)
    attended = [attend(plan, 0, block_lists, x, weights, local)]
    arrived, attended = lax.optimization_barrier((arrived, attended))
    states = scan_states(plan, arrived, share)
    x, states = lax.optimization_barrier((x, states))
    if plan.merge == 2:
        attended.append(attend(plan, 1, block_lists, x, weights, local))
    state = exchange(states).reshape(-1, LANES)

    bases, readers = ([a[i] for a in attended] for i in range(2))
    mixed = mix(plan, rates, bases, readers, state, places, groups)
    moved = {
        (s, k): plan.to_peer(mixed[s * plan.peers + k], k, s == 1)
        for s in range(plan.merge)
        for k in range(1, plan.peers)
    }
    near = {(0, 0): mixed[0]}
    if plan.merge == 2:
        near[1, 0] = plan.swap(mixed[plan.peers])
    result = project_out(plan, out_weight, near, [], f32)
    return project_out(plan, out_weight, moved, [result], bf16)[None]


def solution(mesh):
    return jax.shard_map(
        body,
        mesh=mesh,
        in_specs=(P("tm", "head", None), P("tm", "head"), P(), P(), P(), P("tm", "head", None)),
        out_specs=P("tm", "head", None),
        check_vma=False,
    )
```

```python
import functools
import math

import jax
import jax.numpy as jnp
from jax import lax
from jax.experimental import pallas as pl
from jax.experimental.pallas import tpu as pltpu
from jax.sharding import PartitionSpec as P

HD = 64
N = 64
LANES = 2 * HD
PIECES = 5
EARLY = (2, 3)
LATE = (0, 1, 4)

epsilon = 1e-06

vmem = pl.BlockSpec(memory_space=pltpu.VMEM)
smem = pl.BlockSpec(memory_space=pltpu.SMEM)

hbm = pl.BlockSpec(memory_space=pltpu.HBM)

f32 = jnp.float32
bf16 = jnp.bfloat16


def params(mib=16):
    return pltpu.CompilerParams(vmem_limit_bytes=mib << 20)


def cost(flops, nbytes, transcendentals=0):
    return pl.CostEstimate(
        flops=int(flops), bytes_accessed=int(nbytes), transcendentals=int(transcendentals)
    )


def first_half(shape):
    return lax.broadcasted_iota(jnp.int32, shape, len(shape) - 1) < HD


class Plan:
    def __init__(self, frames, peers, heads_here, width):
        self.merge = 2 if frames % 2 == 0 and heads_here % 4 == 0 else 1
        self.frames, self.peers = frames, peers
        self.heads = heads_here // self.merge
        self.pairs = self.heads // 2
        self.chips = frames // self.merge
        self.across = 2 if self.chips % 2 == 0 else 1
        self.along = self.chips // self.across
        self.ringed = self.across == 2 and 2 <= self.along <= 8 and width % (self.chips * LANES) == 0

    def core(self):
        return lax.rem(lax.axis_index("tm"), self.merge)

    def chip(self):
        return lax.div(lax.axis_index("tm"), self.merge)

    def swap(self, block):
        return lax.ppermute(block, "tm", [(t, t ^ 1) for t in range(self.frames)])

    def round(self, block):
        a, b, c = self.along, self.across, self.merge
        pairs = [(t, (t + b * c) % (a * b * c)) for t in range(self.frames)]
        return lax.ppermute(block, "tm", pairs)

    def cross(self, block):
        c = self.merge
        pairs = [(t, (t // c ^ 1) * c + t % c) for t in range(self.frames)]
        return lax.ppermute(block, "tm", pairs)

    def last_chip(self):
        a, b = lax.div(self.chip(), self.across), lax.rem(self.chip(), self.across)
        return lax.rem(a + 1, self.along) * self.across + (self.across - 1 - b)

    def places(self, refs):
        if len(refs) == 1:
            return [(refs[0], slice(None))]
        rows = refs[0].shape[0]
        a, b = lax.div(self.chip(), self.across), lax.rem(self.chip(), self.across)
        n = self.along
        made = []
        for i, ref in enumerate(refs):
            k, flip = (i, 0) if i < n else (min(i - n, n - 1), 1)
            there = lax.rem(a - k + n, n) * self.across
            at = (there + (1 - b if flip else b)) * rows
            at = at + (rows // 2 if i == 2 * n else 0)
            made.append((ref, pl.ds(pl.multiple_of(at, rows // 2), ref.shape[0])))
        return made

    def to_peer(self, block, k, other):
        if not other:
            pairs = [(j, (j + k) % self.peers) for j in range(self.peers)]
            return lax.ppermute(block, "head", pairs)
        if k == 0:
            return self.swap(block)
        pairs = [
            (t * self.peers + j, (t ^ 1) * self.peers + (j + k) % self.peers)
            for t in range(self.frames)
            for j in range(self.peers)
        ]
        return lax.ppermute(block, ("tm", "head"), pairs)

    def groups(self):
        if self.merge == 1:
            return None
        return [[j * self.merge + c for j in range(self.chips)] for c in range(self.merge)]

    def decay(self, refs, slot, pair, g):
        head = self.core() * self.heads + 2 * pair
        return halves((1, LANES), refs[slot][head, g], refs[slot][head + 1, g])

    def last_decay(self, refs, pair, g):
        if self.merge == 1:
            return self.decay(refs, 0, pair, g)
        one, two = (self.decay(refs, slot, pair, g) for slot in range(2))
        return jnp.where(self.core() == 0, two, one)


class Copies:
    room = 48

    def __init__(self, sems):
        self.sems, self.count = sems, 0

    def start(self, src, dst):
        copy = pltpu.make_async_copy(src, dst, self.sems.at[self.count])
        copy.start()
        self.count += 1
        return copy

    @staticmethod
    def scratch():
        return pltpu.SemaphoreType.DMA((Copies.room,))


def finish(copies):
    for copy in copies:
        copy.wait()


def halves(shape, one, two):
    return jnp.where(first_half(shape), one, two)


def reorder_kernel(plan, *refs):
    w_ref, out_ref = refs[0], refs[-1]
    rows = w_ref.shape[0]
    width = plan.heads * PIECES * HD
    first = plan.core() == 0

    def chosen(at):
        one = w_ref[:, at : at + HD]
        if plan.merge == 1:
            return one
        return jnp.where(first, one, w_ref[:, width + at : width + at + HD])

    order = [(p, i) for i in EARLY for p in range(plan.pairs)]
    order += [(p, i) for p in range(plan.pairs) for i in LATE]
    for n, (p, i) in enumerate(order):
        block = jnp.concatenate(
            [chosen(((2 * p + h) * PIECES + i) * HD) for h in range(2)], axis=1
        )
        cols = slice(n * LANES, (n + 1) * LANES)
        if len(refs) == 2:
            out_ref[:, cols] = block
        else:
            mine = refs[1][:, cols]
            out_ref[:rows, cols] = jnp.where(first, mine, block)
            out_ref[rows:, cols] = jnp.where(first, block, mine)


def reorder(plan, w, mine=()):
    rows = w.shape[0] * (1 + len(mine))
    return pl.pallas_call(
        functools.partial(reorder_kernel, plan),
        out_shape=jax.ShapeDtypeStruct((rows, plan.heads * PIECES * HD), bf16),
        compiler_params=params(),
        cost_estimate=cost(0, 4 * rows),
        name="reorder",
    )(w, *mine)


def normalise(part, out, at):
    step = min(128, part.shape[0])

    def norm(c, _):
        start = pl.multiple_of(c * step, step)
        wide = part[pl.ds(start, step), :].astype(f32)
        scale = lax.rsqrt(jnp.mean(wide * wide, axis=-1, keepdims=True) + epsilon)
        out[pl.ds(at + start, step), :] = (wide * scale).astype(bf16)
        return 0

    lax.fori_loop(0, part.shape[0] // step, norm, 0)


def rank_kernel(groups, ids_ref, row_ref):
    tokens = ids_ref.shape[1]
    block = tokens // groups
    label = lax.broadcasted_iota(jnp.int32, (groups, tokens), 0)
    held = label == ids_ref[...]
    held_bf = jnp.where(held, 1.0, 0.0).astype(bf16)
    counts = []
    for c in range(tokens // 256):
        before = lax.broadcasted_iota(jnp.int32, (tokens, 256), 0) < (
            lax.broadcasted_iota(jnp.int32, (tokens, 256), 1) + c * 256
        )
        counts.append(
            jnp.dot(held_bf, jnp.where(before, 1.0, 0.0).astype(bf16), preferred_element_type=f32)
        )
    count = jnp.concatenate(counts, axis=1)
    row_ref[...] = jnp.sum(
        jnp.where(held, count + (label * block).astype(f32), 0.0), axis=0, keepdims=True
    )


def rank_tokens(ids, groups):
    tokens = ids.shape[0]
    return pl.pallas_call(
        functools.partial(rank_kernel, groups),
        out_shape=jax.ShapeDtypeStruct((1, tokens), f32),
        compiler_params=params(),
        cost_estimate=cost(0, 4 * tokens),
        name="rank_tokens",
    )(ids.reshape(1, tokens))


def turn_kernel(row_ref, col_ref):
    for at in range(0, col_ref.shape[0], LANES):
        col_ref[at : at + LANES, :] = jnp.broadcast_to(
            row_ref[:, at : at + LANES], (LANES, LANES)
        ).T


def turn_places(rank):
    return pl.pallas_call(
        turn_kernel,
        out_shape=jax.ShapeDtypeStruct((rank.shape[1], LANES), f32),
        compiler_params=params(),
        cost_estimate=cost(2e10, 4 * LANES),
        name="turn_places",
    )(rank)


def picks(rank, at, rows):
    places = lax.broadcasted_iota(jnp.int32, (rows, rank.shape[1]), 0) + at
    return jnp.where(places.astype(f32) == rank, 1.0, 0.0).astype(bf16)


def place_kernel(merge, parts, start, rank_ref, *refs):
    frame_refs, refs = refs[:parts], refs[parts:]
    base_refs, (x_ref, normed) = refs[:-2], refs[-2:]
    tokens = rank_ref.shape[1]
    count = normed.shape[1]
    step = 256
    at = 0
    for ref in frame_refs:
        normalise(ref, normed.at[at // count], at % count)
        at += ref.shape[0]
    for at in range(0, tokens, step):
        pick = picks(rank_ref[:, start : start + count], at, step)
        for s in range(merge):
            there = slice(s * tokens + at, s * tokens + at + step)
            placed = jnp.dot(pick, normed[s], preferred_element_type=f32).astype(bf16)
            for base in base_refs:
                placed = base[there, :] + placed
            x_ref[there, :] = placed


def place_tokens(plan, rank, start, frames, base):
    tokens = rank.shape[1]
    width = frames[0].shape[1]
    count = sum(f.shape[0] for f in frames) // plan.merge
    return pl.pallas_call(
        functools.partial(place_kernel, plan.merge, len(frames), start),
        out_shape=jax.ShapeDtypeStruct((plan.merge * tokens, width), bf16),
        scratch_shapes=[pltpu.VMEM((plan.merge, count, width), bf16)],
        compiler_params=params(),
        cost_estimate=cost(0, 4 * tokens),
        name="place_tokens",
    )(rank, *frames, *base)


def project_kernel(plan, x_ref, *refs):
    w_refs, (v_ref, b_ref, rest_ref, w, turned) = refs[:-5], refs[-5:]
    every = x_ref.shape[0]
    step = 256
    cols = plan.pairs * LANES
    if len(w_refs) > 1:
        w[...] = jnp.zeros_like(w)
        turned[...] = jnp.zeros_like(turned)
    for ref, rows in plan.places(w_refs):
        w[rows, :] = ref[:, :cols]
        turned[rows, :] = ref[:, cols : 2 * cols]
    maps = jnp.concatenate(
        [
            turned[at : at + LANES, :].astype(f32).T.astype(bf16)
            for at in range(0, turned.shape[0], LANES)
        ],
        axis=1,
    )
    for at in range(0, every, step):
        x = x_ref[at : at + step, :]
        v_ref[at : at + step, :] = jnp.dot(x, w[...], preferred_element_type=f32)
        b_ref[:, at : at + step] = lax.dot_general(
            maps, x, (((1,), (1,)), ((), ())), preferred_element_type=f32
        )
    count = rest_ref.shape[1]
    there = plan.last_chip() * count
    for at in range(0, every, step):
        rest = x_ref[at : at + step, :count]
        for c in range(count, x_ref.shape[1], count):
            rest = jnp.where(there == c, x_ref[at : at + step, c : c + count], rest)
        rest_ref[at : at + step, :] = rest


def project(plan, x, weights):
    every, width = x.shape
    cols = plan.pairs * LANES
    count = max(LANES, width // plan.chips)
    return pl.pallas_call(
        functools.partial(project_kernel, plan),
        out_shape=(
            jax.ShapeDtypeStruct((every, cols), f32),
            jax.ShapeDtypeStruct((cols, every), f32),
            jax.ShapeDtypeStruct((every, count), bf16),
        ),
        scratch_shapes=[pltpu.VMEM((width, cols), bf16), pltpu.VMEM((width, cols), bf16)],
        compiler_params=params(),
        cost_estimate=cost(0, 4 * width),
        name="project",
    )(x, *weights)


def update_kernel(plan, groups, *refs):
    decay_refs, refs = refs[: plan.merge], refs[plan.merge :]
    v_ref, b_ref, x_ref, last_refs, (left, total_out, total_ref, u, sems) = (
        refs[0], refs[1], refs[2], refs[3:-5], refs[-5:]
    )
    copies = Copies(sems)
    leaving = []
    every = v_ref.shape[0]
    tokens = every // plan.merge
    block = tokens // groups
    step = 256
    here = step // block
    cols = plan.pairs * LANES
    if last_refs:
        w = jnp.concatenate([ref[:, : 2 * cols] for ref in last_refs], axis=0)
        maps = w[:, cols:].astype(f32).T.astype(bf16)
        w = w[:, :cols]

    lane = lax.div(lax.broadcasted_iota(jnp.int32, (LANES, step), 1), block)
    for at in range(0, every, step):
        there = slice(at, at + step)
        values, b = v_ref[there, :], b_ref[:, there]
        if last_refs:
            x = x_ref[there, :]
            values = values + jnp.dot(x, w, preferred_element_type=f32)
            b = b + lax.dot_general(
                maps, x, (((1,), (1,)), ((), ())), preferred_element_type=f32
            )
        values = values.astype(bf16)
        for p in range(plan.pairs):
            mine = b[p * LANES : (p + 1) * LANES]
            wide = jnp.concatenate(
                [jnp.where(lane == i, mine, 0.0).astype(bf16) for i in range(here)], axis=0
            )
            outer = jnp.dot(
                wide, values[:, p * LANES : (p + 1) * LANES], preferred_element_type=f32
            )
            for i in range(here):
                m = outer[i * 2 * N : (i + 1) * 2 * N]
                row = ((at % tokens // block + i) * plan.pairs + p) * N
                u[at // tokens, row : row + N, :] = halves((N, LANES), m[:N], m[N:])

    peers = total_ref.shape[0]
    share = u.shape[1] // peers
    items = max(1, share // N)
    size = min(N, share)
    first = plan.core() == 0
    for d in range(peers):
        for i in range(items):
            row = d * share + i * N
            rows = slice(row, row + size)
            p, g = row // N % plan.pairs, row // N // plan.pairs
            product = last = plan.last_decay(decay_refs, p, g)
            if plan.merge == 2:
                one, two = u[0, rows, :], u[1, rows, :]
                one, two = (
                    one + jnp.where(first, 0.0, last) * two,
                    two + jnp.where(first, last, 0.0) * one,
                )
                left[0, rows, :] = one.astype(bf16)
                left[1, rows, :] = two.astype(bf16)
                total = jnp.where(first, two, one)
                product = plan.decay(decay_refs, 0, p, g) * plan.decay(decay_refs, 1, p, g)
            else:
                total = u[0, rows, :]
                left[0, rows, :] = total.astype(bf16)
            total_ref[d, i * size : (i + 1) * size, :] = total.astype(bf16)
            for n in range(3):
                piece = product.astype(bf16)
                at = share + n * items + i
                total_ref[d, at : at + 1, :] = piece
                product = product - piece.astype(f32)
        if (d + 1) % (peers // 4) == 0:
            done = slice(d + 1 - peers // 4, d + 1)
            leaving.append(copies.start(total_ref.at[done], total_out.at[done]))
    finish(leaving)


def share_rows(share):
    return share + 16 * -(-3 * max(1, share // N) // 16)


def block_updates(plan, decays, v, b, x, last, groups):
    every, cols = v.shape
    rows = plan.pairs * groups * N
    share = rows // plan.chips
    return pl.pallas_call(
        functools.partial(update_kernel, plan, groups),
        in_specs=[smem] * plan.merge + [vmem] * (3 + len(last)),
        out_specs=(vmem, hbm),
        out_shape=(
            jax.ShapeDtypeStruct((plan.merge, rows, LANES), bf16),
            jax.ShapeDtypeStruct((plan.chips, share_rows(share), LANES), bf16),
        ),
        scratch_shapes=[
            pltpu.VMEM((plan.chips, share_rows(share), LANES), bf16),
            pltpu.VMEM((plan.merge, rows, LANES), f32),
            Copies.scratch(),
        ],
        compiler_params=params(),
        cost_estimate=cost(4 * every * 256 * 2 * cols, 6 * every * cols),
        name="block_updates",
    )(*decays, v, b, x, *last)


def scan_kernel(plan, u_ref, s_ref):
    share = s_ref.shape[1]
    size = min(share, N)
    items = share // size
    for i in range(items):
        at = slice(i * size, (i + 1) * size)
        state = jnp.zeros((size, LANES), f32)
        for j in range(plan.chips):
            s_ref[j, at, :] = state.astype(bf16)
            decay = jnp.zeros((1, LANES), f32)
            for n in range(3):
                row = share + n * items + i
                decay = decay + u_ref[j, row : row + 1, :].astype(f32)
            state = decay * state + u_ref[j, at, :].astype(f32)


def scan_states(plan, update, share):
    return pl.pallas_call(
        functools.partial(scan_kernel, plan),
        out_shape=jax.ShapeDtypeStruct((plan.chips, share, LANES), bf16),
        compiler_params=params(),
        cost_estimate=cost(2 * update.size, 4 * update.size),
        name="scan_states",
    )(update)


def attend_kernel(plan, slot, *refs):
    lists_ref, x_in, local_in, refs = refs[0], refs[1], refs[2], refs[3:]
    w_refs, refs = refs[:-12], refs[-12:]
    a_out, c_out, x, local, w, q_ref, k_ref, wide_v, e_ref, a, c_ref, sems = refs
    copies = Copies(sems)
    tokens = x.shape[0]
    groups, chosen = lists_ref.shape
    block = tokens // groups
    step = 256
    per = step // block
    wide = plan.pairs * LANES

    weights = []
    for ref, rows in plan.places(w_refs):
        weights.append(copies.start(ref.at[:, :wide], w.at[rows, :wide]))
        weights.append(copies.start(ref.at[:, 2 * wide :], w.at[rows, wide:]))
    arriving = []
    for at in range(0, tokens, step):
        from_ = slice(slot * tokens + at, slot * tokens + at + step)
        arriving.append(copies.start(x_in.at[from_], x.at[at : at + step]))
    later = copies.start(local_in.at[slot], local)

    same = lax.div(lax.broadcasted_iota(jnp.int32, (2 * LANES, 2 * LANES), 0), HD) == lax.div(
        lax.broadcasted_iota(jnp.int32, (2 * LANES, 2 * LANES), 1), HD
    )
    same = jnp.where(same, 1.0, 0.0).astype(bf16)

    def head_norm(values):
        square = values * values
        high = square.astype(bf16)
        low = (square - high.astype(f32)).astype(bf16)
        total = jnp.dot(high, same, preferred_element_type=f32)
        total = total + jnp.dot(low, same, preferred_element_type=f32)
        return values * lax.rsqrt(total * (1.0 / HD) + epsilon)

    half = first_half((step, LANES))
    finish(weights)
    for at in range(0, tokens, step):
        rows = slice(at, at + step)
        arriving[at // step].wait()
        every = jnp.dot(x[rows, :], w[...], preferred_element_type=f32).astype(bf16)
        for p in range(plan.pairs):
            cols = slice(p * LANES, (p + 1) * LANES)
            wide_v[p, rows, :LANES] = every[:, cols]
            first = wide + 3 * p * LANES
            c_ref[rows, cols] = every[:, first + 2 * LANES : first + 3 * LANES]
            both = head_norm(every[:, first : first + 2 * LANES].astype(f32))
            k_ref[p, rows, :] = both[:, LANES:].astype(bf16)
            q = both[:, :LANES]
            one = jnp.where(half, q, 0.0).astype(bf16)
            two = jnp.where(half, 0.0, q).astype(bf16)
            for i in range(per):
                part = slice(i * block, (i + 1) * block)
                q_ref[p, at // block + i] = jnp.concatenate([one[part], two[part]], axis=0)
    leaving = [copies.start(c_ref, c_out)]
    later.wait()
    for p in range(plan.pairs):
        wide_v[p, :, LANES:] = jnp.ones((tokens, LANES), bf16)

    scale = math.log2(math.e) / math.sqrt(HD)
    starts = [
        [pl.multiple_of(lists_ref[g, j] * block, block) for j in range(chosen)]
        for g in range(groups)
    ]
    for g in range(groups):
        for p in range(plan.pairs):
            keys = jnp.concatenate([k_ref[p, pl.ds(s, block), :] for s in starts[g]], axis=0)
            score = lax.dot_general(
                q_ref[p, g], keys, (((1,), (1,)), ((), ())), preferred_element_type=f32
            )
            e_ref[p, g] = jnp.exp2(score * scale).astype(bf16)
    for g in range(groups):
        rows = slice(g * block, (g + 1) * block)
        for p in range(plan.pairs):
            cols = slice(p * LANES, (p + 1) * LANES)
            values = jnp.concatenate([wide_v[p, pl.ds(s, block), :] for s in starts[g]], axis=0)
            both = jnp.dot(e_ref[p, g], values, preferred_element_type=f32)
            both = both[:, :LANES] / both[:, LANES:]
            a[rows, cols] = halves((block, LANES), both[:block], both[block:])
    for g in range(groups):
        rows = slice(g * block, (g + 1) * block)
        for p in range(plan.pairs):
            cols = slice(p * LANES, (p + 1) * LANES)
            items = slice((g * plan.pairs + p) * N, (g * plan.pairs + p + 1) * N)
            a[rows, cols] = a[rows, cols] + read_out(
                c_ref[rows, cols], local[items, :].astype(f32), block
            )
        if (g + 1) % per == 0:
            done = slice((g + 1 - per) * block, (g + 1) * block)
            leaving.append(copies.start(a.at[done], a_out.at[done]))
    finish(leaving)


def attend(plan, slot, lists, x, weights, local):
    every, width = x.shape
    groups, chosen = lists.shape
    tokens = every // plan.merge
    block = tokens // groups
    cols = plan.pairs * LANES
    return pl.pallas_call(
        functools.partial(attend_kernel, plan, slot),
        in_specs=[smem] + [hbm] * (2 + len(weights)),
        out_specs=(hbm,) * 2,
        scratch_shapes=[
            pltpu.VMEM((tokens, width), bf16),
            pltpu.VMEM(local.shape[1:], bf16),
            pltpu.VMEM((width, 4 * cols), bf16),
            pltpu.VMEM((plan.pairs, groups, 2 * block, LANES), bf16),
            pltpu.VMEM((plan.pairs, tokens, LANES), bf16),
            pltpu.VMEM((plan.pairs, tokens, 2 * LANES), bf16),
            pltpu.VMEM((plan.pairs, groups, 2 * block, chosen * block), bf16),
            pltpu.VMEM((tokens, cols), f32),
            pltpu.VMEM((tokens, cols), bf16),
            Copies.scratch(),
        ],
        out_shape=(
            jax.ShapeDtypeStruct((tokens, cols), f32),
            jax.ShapeDtypeStruct((tokens, cols), bf16),
        ),
        compiler_params=params(60 + 3 * slot),
        cost_estimate=cost(
            6 * tokens * width * 3 * cols,
            4 * (tokens * width + 5 * width * cols + local.size),
            2 * plan.pairs * tokens * chosen * block,
        ),
        name="attend",
    )(lists, x, local, *weights)


def read_out(readers, state, block):
    half = first_half(state.shape)
    wide = jnp.concatenate([jnp.where(half, state, 0.0), jnp.where(half, 0.0, state)], axis=0)
    return jnp.dot(readers, wide.astype(bf16), preferred_element_type=f32) * (
        1.0 / (N * math.sqrt(block))
    )


def mix_kernel(plan, groups, *refs):
    decay_refs, refs = refs[: plan.merge], refs[plan.merge :]
    a_ins, refs = refs[: plan.merge], refs[plan.merge :]
    c_ins, refs = refs[: plan.merge], refs[plan.merge :]
    s_in, rank_in, refs = refs[0], refs[1], refs[2:]
    out_refs, (a, c, state, rank, mixed, out, sems) = refs[:-7], refs[-7:]
    copies = Copies(sems)
    tokens = rank.shape[0]
    block = tokens // groups
    width = a.shape[2]
    here = groups // 4
    many = here * plan.pairs * N
    first = plan.core() == 0

    arriving = []
    for i in range(4):
        rows = slice(i * here * block, (i + 1) * here * block)
        items = slice(i * many, (i + 1) * many)
        arriving.append([copies.start(s_in.at[items], state.at[items])])
        for s in range(plan.merge):
            arriving[-1] += [
                copies.start(c_ins[s].at[rows], c.at[s, rows, :]),
                copies.start(a_ins[s].at[rows], a.at[s, rows, :]),
            ]
    ranking = copies.start(rank_in, rank)

    for g in range(groups):
        if g % here == 0:
            finish(arriving[g // here])
        rows = slice(g * block, (g + 1) * block)
        for p in range(plan.pairs):
            cols = slice(p * LANES, (p + 1) * LANES)
            at = (g * plan.pairs + p) * N
            readers = jnp.concatenate([c[s, rows, cols] for s in range(plan.merge)], axis=0)
            read = read_out(readers, state[at : at + N, :].astype(f32), block)
            decays = [plan.decay(decay_refs, s, p, g) for s in range(plan.merge)]
            if plan.merge == 2:
                both = decays[0] * decays[1]
                decays = [jnp.where(first, decays[0], both), jnp.where(first, both, decays[1])]
            for s in range(plan.merge):
                there = slice(s * width + p * LANES, s * width + (p + 1) * LANES)
                mixed[rows, there] = (
                    a[s, rows, cols] + decays[s] * read[s * block : (s + 1) * block]
                ).astype(bf16)

    ranking.wait()
    local = tokens // plan.peers
    leaving = []
    for k in list(range(1, plan.peers)) + [0]:
        placed = back_rows(rank, k * local, mixed, local)
        for s in range(plan.merge):
            i = s * plan.peers + k
            out[i] = placed[:, s * width : (s + 1) * width]
            leaving.append(copies.start(out.at[i], out_refs[i]))
    finish(leaving)


def back_rows(rank, start, mixed, rows):
    tokens = rank.shape[0]
    step = min(256, rows)
    placed = []
    for at in range(start, start + rows, step):
        place = rank[at : at + step, :]
        lane = lax.broadcasted_iota(jnp.int32, place.shape, 1)
        pick = jnp.concatenate(
            [
                jnp.where((lane + t).astype(f32) == place, 1.0, 0.0).astype(bf16)
                for t in range(0, tokens, LANES)
            ],
            axis=1,
        )
        placed.append(jnp.dot(pick, mixed[...], preferred_element_type=f32).astype(bf16))
    return jnp.concatenate(placed, axis=0)


def mix(plan, decays, attended, readers, state, rank, groups):
    tokens = rank.shape[0]
    width = attended[0].shape[1]
    count = plan.merge * plan.peers
    return pl.pallas_call(
        functools.partial(mix_kernel, plan, groups),
        in_specs=[smem] * plan.merge + [hbm] * (2 * plan.merge + 2),
        out_specs=(hbm,) * count,
        out_shape=(jax.ShapeDtypeStruct((tokens // plan.peers, width), bf16),) * count,
        scratch_shapes=[
            pltpu.VMEM((plan.merge, tokens, width), f32),
            pltpu.VMEM((plan.merge, tokens, width), bf16),
            pltpu.VMEM(state.shape, bf16),
            pltpu.VMEM(rank.shape, f32),
            pltpu.VMEM((tokens, plan.merge * width), bf16),
            pltpu.VMEM((count, tokens // plan.peers, width), bf16),
            Copies.scratch(),
        ],
        compiler_params=params(60),
        cost_estimate=cost(4 * tokens * tokens * width, 2 * tokens * tokens + 16 * tokens * width),
        name="mix",
    )(*decays, *attended, *readers, state, rank)


def out_kernel(plan, sources, w_ref, *refs):
    part_refs, base_refs, out_ref = refs[: len(sources)], refs[len(sources) : -3], refs[-3]
    kept, sems = refs[-2:]
    copies = Copies(sems)
    depth = part_refs[0].shape[1]
    core, me = plan.core(), lax.axis_index("head")
    owners = []
    for s, k in sources:
        owner = lax.rem(me - k + plan.peers, plan.peers) * plan.merge
        owners.append(owner + (core if s == 0 else 1 - core))
    leaving = []
    step = min(128, out_ref.shape[0])
    for at in range(0, out_ref.shape[0], step):
        there = slice(at, at + step)
        total = base_refs[0][there, :] if base_refs else 0.0
        for owner, part in zip(owners, part_refs):
            rows = pl.ds(pl.multiple_of(owner * depth, depth), depth)
            total = total + jnp.dot(part[there, :], w_ref[rows, :], preferred_element_type=f32)
        if base_refs:
            kept[there, :] = total.astype(out_ref.dtype)
            leaving.append(copies.start(kept.at[there], out_ref.at[there]))
        else:
            out_ref[there, :] = total.astype(out_ref.dtype)
    finish(leaving)


def project_out(plan, w, parts, base, kind):
    local, width = next(iter(parts.values())).shape[0], w.shape[1]
    return pl.pallas_call(
        functools.partial(out_kernel, plan, list(parts)),
        in_specs=[vmem] * (1 + len(parts) + len(base)),
        out_specs=hbm if base else vmem,
        out_shape=jax.ShapeDtypeStruct((local, width), kind),
        scratch_shapes=[pltpu.VMEM((local, width), kind), Copies.scratch()],
        compiler_params=params(),
        cost_estimate=cost(0, 4 * local),
        name="project_out",
    )(w, *parts.values(), *base)


def body(frames_in, in_weight, out_weight, block_ids, block_lists, decays):
    local_tokens = frames_in.shape[1]
    heads_here = decays.shape[1]
    groups = block_lists.shape[0]
    me = lax.axis_index("head")
    plan = Plan(lax.axis_size("tm"), lax.axis_size("head"), heads_here, frames_in.shape[2])

    own = frames_in[0]
    arriving = [plan.to_peer(own, plan.peers - k, False) for k in range(1, plan.peers)]
    owns = [own] + [plan.swap(own)] * (plan.merge - 1)
    rates = [decays[0]] + [plan.swap(decays[0])] * (plan.merge - 1)
    block = reorder(plan, in_weight)
    if plan.merge == 2:
        block = reorder(plan, plan.swap(in_weight), [block])
    ids = jnp.roll(block_ids, -me * local_tokens)
    ids, rates = lax.optimization_barrier((ids, rates))
    rank = rank_tokens(ids, groups)

    def fill(arriving, part):
        if plan.merge == 2:
            arriving = arriving + [plan.swap(tokens) for tokens in arriving]
        return place_tokens(plan, rank, local_tokens, arriving, [part])

    if plan.ringed:
        blocks, crossed = [block], []
        half = block.shape[0] // 2
        for k in range(plan.along - 1):
            with_ = rank if k == 0 else ()
            if k == min(1, plan.along - 2):
                rank, owns, _ = lax.optimization_barrier((rank, owns, blocks[-1]))
                part = with_ = place_tokens(plan, rank, 0, owns, [])
            if k == plan.along - 2:
                arriving, _ = lax.optimization_barrier((arriving, blocks[-1]))
                x = fill(arriving, part)
            passed, across, with_ = lax.optimization_barrier(
                (plan.round(blocks[-1]), plan.cross(blocks[-1]), with_)
            )
            if k == plan.along - 2:
                rank, passed, across = lax.optimization_barrier((rank, passed, across))
                places, passed, across = lax.optimization_barrier(
                    (turn_places(rank), passed, across)
                )
            blocks.append(passed)
            crossed.append(across)
        last = [plan.cross(blocks[-1][:half]), plan.round(crossed[-1][half:])]
        weights = blocks + crossed + last
    else:
        weights = [
            lax.all_gather(block, "tm", axis=0, tiled=True, axis_index_groups=plan.groups())
        ]
        places = turn_places(rank)
        x = fill(arriving, place_tokens(plan, rank, 0, owns, []))
    if plan.ringed:
        v, b, x_last = project(plan, x, weights[:-2])
        local, total = block_updates(plan, rates, v, b, x_last, last, groups)
    else:
        v, b, x_last = project(plan, x, weights)
        local, total = block_updates(plan, rates, v, b, x_last, [], groups)

    def exchange(blocks):
        return lax.all_to_all(
            blocks, "tm", split_axis=0, concat_axis=0, tiled=True,
            axis_index_groups=plan.groups(),
        )

    share = local.shape[1] // plan.chips
    arrived = exchange(total)
    attended = [attend(plan, 0, block_lists, x, weights, local)]
    arrived, attended = lax.optimization_barrier((arrived, attended))
    states = scan_states(plan, arrived, share)
    x, states = lax.optimization_barrier((x, states))
    if plan.merge == 2:
        attended.append(attend(plan, 1, block_lists, x, weights, local))
    state = exchange(states).reshape(-1, LANES)

    bases, readers = ([a[i] for a in attended] for i in range(2))
    mixed = mix(plan, rates, bases, readers, state, places, groups)
    moved = {
        (s, k): plan.to_peer(mixed[s * plan.peers + k], k, s == 1)
        for s in range(plan.merge)
        for k in range(1, plan.peers)
    }
    near = {(0, 0): mixed[0]}
    if plan.merge == 2:
        near[1, 0] = plan.swap(mixed[plan.peers])
    result = project_out(plan, out_weight, near, [], f32)
    return project_out(plan, out_weight, moved, [result], bf16)[None]


def solution(mesh):
    return jax.shard_map(
        body,
        mesh=mesh,
        in_specs=(P("tm", "head", None), P("tm", "head"), P(), P(), P(), P("tm", "head", None)),
        out_specs=P("tm", "head", None),
        check_vma=False,
    )
```

```python
import functools
import math

import jax
import jax.numpy as jnp
from jax import lax
from jax.experimental import pallas as pl
from jax.experimental.pallas import tpu as pltpu
from jax.sharding import PartitionSpec as P

HD = 64
N = 64
LANES = 2 * HD
PIECES = 5
EARLY = (2, 3)
LATE = (0, 1, 4)

epsilon = 1e-06

vmem = pl.BlockSpec(memory_space=pltpu.VMEM)
smem = pl.BlockSpec(memory_space=pltpu.SMEM)

hbm = pl.BlockSpec(memory_space=pltpu.HBM)

f32 = jnp.float32
bf16 = jnp.bfloat16


def params(mib=16):
    return pltpu.CompilerParams(vmem_limit_bytes=mib << 20)


def cost(flops, nbytes, transcendentals=0):
    return pl.CostEstimate(
        flops=int(flops), bytes_accessed=int(nbytes), transcendentals=int(transcendentals)
    )


def first_half(shape):
    return lax.broadcasted_iota(jnp.int32, shape, len(shape) - 1) < HD


class Plan:
    def __init__(self, frames, peers, heads_here, width):
        self.merge = 2 if frames % 2 == 0 and heads_here % 4 == 0 else 1
        self.frames, self.peers = frames, peers
        self.heads = heads_here // self.merge
        self.pairs = self.heads // 2
        self.chips = frames // self.merge
        self.across = 2 if self.chips % 2 == 0 else 1
        self.along = self.chips // self.across
        self.ringed = self.across == 2 and 2 <= self.along <= 8 and width % (self.chips * LANES) == 0

    def core(self):
        return lax.rem(lax.axis_index("tm"), self.merge)

    def chip(self):
        return lax.div(lax.axis_index("tm"), self.merge)

    def swap(self, block):
        return lax.ppermute(block, "tm", [(t, t ^ 1) for t in range(self.frames)])

    def round(self, block):
        a, b, c = self.along, self.across, self.merge
        pairs = [(t, (t + b * c) % (a * b * c)) for t in range(self.frames)]
        return lax.ppermute(block, "tm", pairs)

    def cross(self, block):
        c = self.merge
        pairs = [(t, (t // c ^ 1) * c + t % c) for t in range(self.frames)]
        return lax.ppermute(block, "tm", pairs)

    def last_chip(self):
        a, b = lax.div(self.chip(), self.across), lax.rem(self.chip(), self.across)
        return lax.rem(a + 1, self.along) * self.across + (self.across - 1 - b)

    def places(self, refs):
        if len(refs) == 1:
            return [(refs[0], slice(None))]
        rows = refs[0].shape[0]
        a, b = lax.div(self.chip(), self.across), lax.rem(self.chip(), self.across)
        n = self.along
        made = []
        for i, ref in enumerate(refs):
            k, flip = (i, 0) if i < n else (min(i - n, n - 1), 1)
            there = lax.rem(a - k + n, n) * self.across
            at = (there + (1 - b if flip else b)) * rows
            at = at + (rows // 2 if i == 2 * n else 0)
            made.append((ref, pl.ds(pl.multiple_of(at, rows // 2), ref.shape[0])))
        return made

    def to_peer(self, block, k, other):
        if not other:
            pairs = [(j, (j + k) % self.peers) for j in range(self.peers)]
            return lax.ppermute(block, "head", pairs)
        if k == 0:
            return self.swap(block)
        pairs = [
            (t * self.peers + j, (t ^ 1) * self.peers + (j + k) % self.peers)
            for t in range(self.frames)
            for j in range(self.peers)
        ]
        return lax.ppermute(block, ("tm", "head"), pairs)

    def groups(self):
        if self.merge == 1:
            return None
        return [[j * self.merge + c for j in range(self.chips)] for c in range(self.merge)]

    def decay(self, refs, slot, pair, g):
        head = self.core() * self.heads + 2 * pair
        return halves((1, LANES), refs[slot][head, g], refs[slot][head + 1, g])

    def last_decay(self, refs, pair, g):
        if self.merge == 1:
            return self.decay(refs, 0, pair, g)
        one, two = (self.decay(refs, slot, pair, g) for slot in range(2))
        return jnp.where(self.core() == 0, two, one)


class Copies:
    room = 48

    def __init__(self, sems):
        self.sems, self.count = sems, 0

    def start(self, src, dst):
        copy = pltpu.make_async_copy(src, dst, self.sems.at[self.count])
        copy.start()
        self.count += 1
        return copy

    @staticmethod
    def scratch():
        return pltpu.SemaphoreType.DMA((Copies.room,))


def finish(copies):
    for copy in copies:
        copy.wait()


def halves(shape, one, two):
    return jnp.where(first_half(shape), one, two)


def reorder_kernel(plan, *refs):
    w_ref, out_ref = refs[0], refs[-1]
    rows = w_ref.shape[0]
    width = plan.heads * PIECES * HD
    first = plan.core() == 0

    def chosen(at):
        one = w_ref[:, at : at + HD]
        if plan.merge == 1:
            return one
        return jnp.where(first, one, w_ref[:, width + at : width + at + HD])

    order = [(p, i) for i in EARLY for p in range(plan.pairs)]
    order += [(p, i) for p in range(plan.pairs) for i in LATE]
    for n, (p, i) in enumerate(order):
        block = jnp.concatenate(
            [chosen(((2 * p + h) * PIECES + i) * HD) for h in range(2)], axis=1
        )
        cols = slice(n * LANES, (n + 1) * LANES)
        if len(refs) == 2:
            out_ref[:, cols] = block
        else:
            mine = refs[1][:, cols]
            out_ref[:rows, cols] = jnp.where(first, mine, block)
            out_ref[rows:, cols] = jnp.where(first, block, mine)


def reorder(plan, w, mine=()):
    rows = w.shape[0] * (1 + len(mine))
    return pl.pallas_call(
        functools.partial(reorder_kernel, plan),
        out_shape=jax.ShapeDtypeStruct((rows, plan.heads * PIECES * HD), bf16),
        compiler_params=params(),
        cost_estimate=cost(0, 4 * rows),
        name="reorder",
    )(w, *mine)


def normalise(part, out, at):
    step = min(128, part.shape[0])

    def norm(c, _):
        start = pl.multiple_of(c * step, step)
        wide = part[pl.ds(start, step), :].astype(f32)
        scale = lax.rsqrt(jnp.mean(wide * wide, axis=-1, keepdims=True) + epsilon)
        out[pl.ds(at + start, step), :] = (wide * scale).astype(bf16)
        return 0

    lax.fori_loop(0, part.shape[0] // step, norm, 0)


def rank_kernel(groups, ids_ref, row_ref):
    tokens = ids_ref.shape[1]
    block = tokens // groups
    label = lax.broadcasted_iota(jnp.int32, (groups, tokens), 0)
    held = label == ids_ref[...]
    held_bf = jnp.where(held, 1.0, 0.0).astype(bf16)
    counts = []
    for c in range(tokens // 256):
        before = lax.broadcasted_iota(jnp.int32, (tokens, 256), 0) < (
            lax.broadcasted_iota(jnp.int32, (tokens, 256), 1) + c * 256
        )
        counts.append(
            jnp.dot(held_bf, jnp.where(before, 1.0, 0.0).astype(bf16), preferred_element_type=f32)
        )
    count = jnp.concatenate(counts, axis=1)
    row_ref[...] = jnp.sum(
        jnp.where(held, count + (label * block).astype(f32), 0.0), axis=0, keepdims=True
    )


def rank_tokens(ids, groups):
    tokens = ids.shape[0]
    return pl.pallas_call(
        functools.partial(rank_kernel, groups),
        out_shape=jax.ShapeDtypeStruct((1, tokens), f32),
        compiler_params=params(),
        cost_estimate=cost(0, 4 * tokens),
        name="rank_tokens",
    )(ids.reshape(1, tokens))


def back_kernel(row_ref, back_ref):
    tokens = back_ref.shape[0]
    lane = lax.broadcasted_iota(jnp.int32, (LANES, LANES), 1)
    for at in range(0, tokens, LANES):
        place = jnp.broadcast_to(row_ref[:, at : at + LANES], (LANES, LANES)).T
        for t in range(0, tokens, LANES):
            back_ref[at : at + LANES, t : t + LANES] = jnp.where(
                (lane + t).astype(f32) == place, 1.0, 0.0
            ).astype(bf16)


def back_tokens(rank):
    return pl.pallas_call(
        back_kernel,
        out_shape=jax.ShapeDtypeStruct((rank.shape[1], rank.shape[1]), bf16),
        compiler_params=params(),
        cost_estimate=cost(2e10, 4 * LANES),
        name="back_tokens",
    )(rank)


def picks(rank, at, rows):
    places = lax.broadcasted_iota(jnp.int32, (rows, rank.shape[1]), 0) + at
    return jnp.where(places.astype(f32) == rank, 1.0, 0.0).astype(bf16)


def place_kernel(merge, parts, start, rank_ref, *refs):
    frame_refs, refs = refs[:parts], refs[parts:]
    base_refs, (x_ref, normed) = refs[:-2], refs[-2:]
    tokens = rank_ref.shape[1]
    count = normed.shape[1]
    step = 256
    at = 0
    for ref in frame_refs:
        normalise(ref, normed.at[at // count], at % count)
        at += ref.shape[0]
    for at in range(0, tokens, step):
        pick = picks(rank_ref[:, start : start + count], at, step)
        for s in range(merge):
            there = slice(s * tokens + at, s * tokens + at + step)
            placed = jnp.dot(pick, normed[s], preferred_element_type=f32).astype(bf16)
            for base in base_refs:
                placed = base[there, :] + placed
            x_ref[there, :] = placed


def place_tokens(plan, rank, start, frames, base):
    tokens = rank.shape[1]
    width = frames[0].shape[1]
    count = sum(f.shape[0] for f in frames) // plan.merge
    return pl.pallas_call(
        functools.partial(place_kernel, plan.merge, len(frames), start),
        out_shape=jax.ShapeDtypeStruct((plan.merge * tokens, width), bf16),
        scratch_shapes=[pltpu.VMEM((plan.merge, count, width), bf16)],
        compiler_params=params(),
        cost_estimate=cost(0, 4 * tokens),
        name="place_tokens",
    )(rank, *frames, *base)


def project_kernel(plan, x_ref, *refs):
    w_refs, (v_ref, b_ref, rest_ref, w, turned) = refs[:-5], refs[-5:]
    every = x_ref.shape[0]
    step = 256
    cols = plan.pairs * LANES
    if len(w_refs) > 1:
        w[...] = jnp.zeros_like(w)
        turned[...] = jnp.zeros_like(turned)
    for ref, rows in plan.places(w_refs):
        w[rows, :] = ref[:, :cols]
        turned[rows, :] = ref[:, cols : 2 * cols]
    maps = jnp.concatenate(
        [
            turned[at : at + LANES, :].astype(f32).T.astype(bf16)
            for at in range(0, turned.shape[0], LANES)
        ],
        axis=1,
    )
    for at in range(0, every, step):
        x = x_ref[at : at + step, :]
        v_ref[at : at + step, :] = jnp.dot(x, w[...], preferred_element_type=f32)
        b_ref[:, at : at + step] = lax.dot_general(
            maps, x, (((1,), (1,)), ((), ())), preferred_element_type=f32
        )
    count = rest_ref.shape[1]
    there = plan.last_chip() * count
    for at in range(0, every, step):
        rest = x_ref[at : at + step, :count]
        for c in range(count, x_ref.shape[1], count):
            rest = jnp.where(there == c, x_ref[at : at + step, c : c + count], rest)
        rest_ref[at : at + step, :] = rest


def project(plan, x, weights):
    every, width = x.shape
    cols = plan.pairs * LANES
    count = max(LANES, width // plan.chips)
    return pl.pallas_call(
        functools.partial(project_kernel, plan),
        out_shape=(
            jax.ShapeDtypeStruct((every, cols), f32),
            jax.ShapeDtypeStruct((cols, every), f32),
            jax.ShapeDtypeStruct((every, count), bf16),
        ),
        scratch_shapes=[pltpu.VMEM((width, cols), bf16), pltpu.VMEM((width, cols), bf16)],
        compiler_params=params(),
        cost_estimate=cost(0, 4 * width),
        name="project",
    )(x, *weights)


def update_kernel(plan, groups, *refs):
    decay_refs, refs = refs[: plan.merge], refs[plan.merge :]
    v_ref, b_ref, x_ref, last_refs, (left_out, total_out, left, total_ref, u, sems) = (
        refs[0], refs[1], refs[2], refs[3:-6], refs[-6:]
    )
    copies = Copies(sems)
    leaving = []
    every = v_ref.shape[0]
    tokens = every // plan.merge
    block = tokens // groups
    step = 256
    here = step // block
    cols = plan.pairs * LANES
    if last_refs:
        w = jnp.concatenate([ref[:, : 2 * cols] for ref in last_refs], axis=0)
        maps = w[:, cols:].astype(f32).T.astype(bf16)
        w = w[:, :cols]

    lane = lax.div(lax.broadcasted_iota(jnp.int32, (LANES, step), 1), block)
    for at in range(0, every, step):
        there = slice(at, at + step)
        values, b = v_ref[there, :], b_ref[:, there]
        if last_refs:
            x = x_ref[there, :]
            values = values + jnp.dot(x, w, preferred_element_type=f32)
            b = b + lax.dot_general(
                maps, x, (((1,), (1,)), ((), ())), preferred_element_type=f32
            )
        values = values.astype(bf16)
        for p in range(plan.pairs):
            mine = b[p * LANES : (p + 1) * LANES]
            wide = jnp.concatenate(
                [jnp.where(lane == i, mine, 0.0).astype(bf16) for i in range(here)], axis=0
            )
            outer = jnp.dot(
                wide, values[:, p * LANES : (p + 1) * LANES], preferred_element_type=f32
            )
            for i in range(here):
                m = outer[i * 2 * N : (i + 1) * 2 * N]
                row = ((at % tokens // block + i) * plan.pairs + p) * N
                u[at // tokens, row : row + N, :] = halves((N, LANES), m[:N], m[N:])

    peers = total_ref.shape[0]
    share = u.shape[1] // peers
    items = max(1, share // N)
    size = min(N, share)
    first = plan.core() == 0
    for d in range(peers):
        for i in range(items):
            row = d * share + i * N
            rows = slice(row, row + size)
            p, g = row // N % plan.pairs, row // N // plan.pairs
            product = last = plan.last_decay(decay_refs, p, g)
            if plan.merge == 2:
                one, two = u[0, rows, :], u[1, rows, :]
                one, two = (
                    one + jnp.where(first, 0.0, last) * two,
                    two + jnp.where(first, last, 0.0) * one,
                )
                left[0, rows, :] = one.astype(bf16)
                left[1, rows, :] = two.astype(bf16)
                total = jnp.where(first, two, one)
                product = plan.decay(decay_refs, 0, p, g) * plan.decay(decay_refs, 1, p, g)
            else:
                total = u[0, rows, :]
                left[0, rows, :] = total.astype(bf16)
            total_ref[d, i * size : (i + 1) * size, :] = total.astype(bf16)
            for n in range(3):
                piece = product.astype(bf16)
                at = share + n * items + i
                total_ref[d, at : at + 1, :] = piece
                product = product - piece.astype(f32)
        if (d + 1) % (peers // 4) == 0:
            done = slice(d + 1 - peers // 4, d + 1)
            leaving.append(copies.start(total_ref.at[done], total_out.at[done]))
            done = slice((d + 1 - peers // 4) * share, (d + 1) * share)
            for s in range(plan.merge):
                leaving.append(copies.start(left.at[s, done], left_out.at[s, done]))
    finish(leaving)


def share_rows(share):
    return share + 16 * -(-3 * max(1, share // N) // 16)


def block_updates(plan, decays, v, b, x, last, groups):
    every, cols = v.shape
    rows = plan.pairs * groups * N
    share = rows // plan.chips
    return pl.pallas_call(
        functools.partial(update_kernel, plan, groups),
        in_specs=[smem] * plan.merge + [vmem] * (3 + len(last)),
        out_specs=(hbm, hbm),
        out_shape=(
            jax.ShapeDtypeStruct((plan.merge, rows, LANES), bf16),
            jax.ShapeDtypeStruct((plan.chips, share_rows(share), LANES), bf16),
        ),
        scratch_shapes=[
            pltpu.VMEM((plan.merge, rows, LANES), bf16),
            pltpu.VMEM((plan.chips, share_rows(share), LANES), bf16),
            pltpu.VMEM((plan.merge, rows, LANES), f32),
            Copies.scratch(),
        ],
        compiler_params=params(),
        cost_estimate=cost(4 * every * 256 * 2 * cols, 6 * every * cols),
        name="block_updates",
    )(*decays, v, b, x, *last)


def scan_kernel(plan, u_ref, s_ref):
    share = s_ref.shape[1]
    size = min(share, N)
    items = share // size
    for i in range(items):
        at = slice(i * size, (i + 1) * size)
        state = jnp.zeros((size, LANES), f32)
        for j in range(plan.chips):
            s_ref[j, at, :] = state.astype(bf16)
            decay = jnp.zeros((1, LANES), f32)
            for n in range(3):
                row = share + n * items + i
                decay = decay + u_ref[j, row : row + 1, :].astype(f32)
            state = decay * state + u_ref[j, at, :].astype(f32)


def scan_states(plan, update, share):
    return pl.pallas_call(
        functools.partial(scan_kernel, plan),
        out_shape=jax.ShapeDtypeStruct((plan.chips, share, LANES), bf16),
        compiler_params=params(),
        cost_estimate=cost(2 * update.size, 4 * update.size),
        name="scan_states",
    )(update)


def attend_kernel(plan, slot, *refs):
    lists_ref, x_in, local_in, refs = refs[0], refs[1], refs[2], refs[3:]
    w_refs, refs = refs[:-12], refs[-12:]
    a_out, c_out, x, local, w, q_ref, k_ref, wide_v, e_ref, a, c_ref, sems = refs
    copies = Copies(sems)
    tokens = x.shape[0]
    groups, chosen = lists_ref.shape
    block = tokens // groups
    step = 256
    per = step // block
    wide = plan.pairs * LANES

    weights = []
    for ref, rows in plan.places(w_refs):
        weights.append(copies.start(ref.at[:, :wide], w.at[rows, :wide]))
        weights.append(copies.start(ref.at[:, 2 * wide :], w.at[rows, wide:]))
    arriving = []
    for at in range(0, tokens, step):
        from_ = slice(slot * tokens + at, slot * tokens + at + step)
        arriving.append(copies.start(x_in.at[from_], x.at[at : at + step]))
    later = copies.start(local_in.at[slot], local)

    same = lax.div(lax.broadcasted_iota(jnp.int32, (2 * LANES, 2 * LANES), 0), HD) == lax.div(
        lax.broadcasted_iota(jnp.int32, (2 * LANES, 2 * LANES), 1), HD
    )
    same = jnp.where(same, 1.0, 0.0).astype(bf16)

    def head_norm(values):
        square = values * values
        high = square.astype(bf16)
        low = (square - high.astype(f32)).astype(bf16)
        total = jnp.dot(high, same, preferred_element_type=f32)
        total = total + jnp.dot(low, same, preferred_element_type=f32)
        return values * lax.rsqrt(total * (1.0 / HD) + epsilon)

    half = first_half((step, LANES))
    finish(weights)
    for at in range(0, tokens, step):
        rows = slice(at, at + step)
        arriving[at // step].wait()
        every = jnp.dot(x[rows, :], w[...], preferred_element_type=f32).astype(bf16)
        for p in range(plan.pairs):
            cols = slice(p * LANES, (p + 1) * LANES)
            wide_v[p, rows, :LANES] = every[:, cols]
            first = wide + 3 * p * LANES
            c_ref[rows, cols] = every[:, first + 2 * LANES : first + 3 * LANES]
            both = head_norm(every[:, first : first + 2 * LANES].astype(f32))
            k_ref[p, rows, :] = both[:, LANES:].astype(bf16)
            q = both[:, :LANES]
            one = jnp.where(half, q, 0.0).astype(bf16)
            two = jnp.where(half, 0.0, q).astype(bf16)
            for i in range(per):
                part = slice(i * block, (i + 1) * block)
                q_ref[p, at // block + i] = jnp.concatenate([one[part], two[part]], axis=0)
    leaving = [copies.start(c_ref, c_out)]
    later.wait()
    for p in range(plan.pairs):
        wide_v[p, :, LANES:] = jnp.ones((tokens, LANES), bf16)

    scale = math.log2(math.e) / math.sqrt(HD)
    starts = [
        [pl.multiple_of(lists_ref[g, j] * block, block) for j in range(chosen)]
        for g in range(groups)
    ]
    for g in range(groups):
        for p in range(plan.pairs):
            keys = jnp.concatenate([k_ref[p, pl.ds(s, block), :] for s in starts[g]], axis=0)
            score = lax.dot_general(
                q_ref[p, g], keys, (((1,), (1,)), ((), ())), preferred_element_type=f32
            )
            e_ref[p, g] = jnp.exp2(score * scale).astype(bf16)
    for g in range(groups):
        rows = slice(g * block, (g + 1) * block)
        for p in range(plan.pairs):
            cols = slice(p * LANES, (p + 1) * LANES)
            values = jnp.concatenate([wide_v[p, pl.ds(s, block), :] for s in starts[g]], axis=0)
            both = jnp.dot(e_ref[p, g], values, preferred_element_type=f32)
            both = both[:, :LANES] / both[:, LANES:]
            a[rows, cols] = halves((block, LANES), both[:block], both[block:])
    for g in range(groups):
        rows = slice(g * block, (g + 1) * block)
        for p in range(plan.pairs):
            cols = slice(p * LANES, (p + 1) * LANES)
            items = slice((g * plan.pairs + p) * N, (g * plan.pairs + p + 1) * N)
            a[rows, cols] = a[rows, cols] + read_out(
                c_ref[rows, cols], local[items, :].astype(f32), block
            )
        if (g + 1) % per == 0:
            done = slice((g + 1 - per) * block, (g + 1) * block)
            leaving.append(copies.start(a.at[done], a_out.at[done]))
    finish(leaving)


def attend(plan, slot, lists, x, weights, local):
    every, width = x.shape
    groups, chosen = lists.shape
    tokens = every // plan.merge
    block = tokens // groups
    cols = plan.pairs * LANES
    return pl.pallas_call(
        functools.partial(attend_kernel, plan, slot),
        in_specs=[smem] + [hbm] * (2 + len(weights)),
        out_specs=(hbm,) * 2,
        scratch_shapes=[
            pltpu.VMEM((tokens, width), bf16),
            pltpu.VMEM(local.shape[1:], bf16),
            pltpu.VMEM((width, 4 * cols), bf16),
            pltpu.VMEM((plan.pairs, groups, 2 * block, LANES), bf16),
            pltpu.VMEM((plan.pairs, tokens, LANES), bf16),
            pltpu.VMEM((plan.pairs, tokens, 2 * LANES), bf16),
            pltpu.VMEM((plan.pairs, groups, 2 * block, chosen * block), bf16),
            pltpu.VMEM((tokens, cols), f32),
            pltpu.VMEM((tokens, cols), bf16),
            Copies.scratch(),
        ],
        out_shape=(
            jax.ShapeDtypeStruct((tokens, cols), f32),
            jax.ShapeDtypeStruct((tokens, cols), bf16),
        ),
        compiler_params=params(60),
        cost_estimate=cost(
            6 * tokens * width * 3 * cols,
            4 * (tokens * width + 5 * width * cols + local.size),
            2 * plan.pairs * tokens * chosen * block,
        ),
        name="attend",
    )(lists, x, local, *weights)


def read_out(readers, state, block):
    half = first_half(state.shape)
    wide = jnp.concatenate([jnp.where(half, state, 0.0), jnp.where(half, 0.0, state)], axis=0)
    return jnp.dot(readers, wide.astype(bf16), preferred_element_type=f32) * (
        1.0 / (N * math.sqrt(block))
    )


def mix_kernel(plan, groups, *refs):
    decay_refs, refs = refs[: plan.merge], refs[plan.merge :]
    a_ins, refs = refs[: plan.merge], refs[plan.merge :]
    c_ins, refs = refs[: plan.merge], refs[plan.merge :]
    s_in, back_in, refs = refs[0], refs[1], refs[2:]
    out_refs, (a, c, state, back, mixed, out, sems) = refs[:-7], refs[-7:]
    copies = Copies(sems)
    tokens = back.shape[0]
    block = tokens // groups
    width = a.shape[2]
    here = groups // 4
    many = here * plan.pairs * N
    first = plan.core() == 0

    arriving = []
    for i in range(4):
        rows = slice(i * here * block, (i + 1) * here * block)
        items = slice(i * many, (i + 1) * many)
        arriving.append([copies.start(s_in.at[items], state.at[items])])
        for s in range(plan.merge):
            arriving[-1] += [
                copies.start(c_ins[s].at[rows], c.at[s, rows, :]),
                copies.start(a_ins[s].at[rows], a.at[s, rows, :]),
            ]
    local = tokens // plan.peers
    order = list(range(1, plan.peers)) + [0]
    turning = []
    for k in order:
        rows = slice(k * local, (k + 1) * local)
        turning.append(copies.start(back_in.at[rows], back.at[rows]))

    for g in range(groups):
        if g % here == 0:
            finish(arriving[g // here])
        rows = slice(g * block, (g + 1) * block)
        for p in range(plan.pairs):
            cols = slice(p * LANES, (p + 1) * LANES)
            at = (g * plan.pairs + p) * N
            readers = jnp.concatenate([c[s, rows, cols] for s in range(plan.merge)], axis=0)
            read = read_out(readers, state[at : at + N, :].astype(f32), block)
            decays = [plan.decay(decay_refs, s, p, g) for s in range(plan.merge)]
            if plan.merge == 2:
                both = decays[0] * decays[1]
                decays = [jnp.where(first, decays[0], both), jnp.where(first, both, decays[1])]
            for s in range(plan.merge):
                there = slice(s * width + p * LANES, s * width + (p + 1) * LANES)
                mixed[rows, there] = (
                    a[s, rows, cols] + decays[s] * read[s * block : (s + 1) * block]
                ).astype(bf16)

    leaving = []
    for k, turned in zip(order, turning):
        turned.wait()
        placed = jnp.dot(
            back[k * local : (k + 1) * local, :], mixed[...], preferred_element_type=f32
        ).astype(bf16)
        for s in range(plan.merge):
            i = s * plan.peers + k
            out[i] = placed[:, s * width : (s + 1) * width]
            leaving.append(copies.start(out.at[i], out_refs[i]))
    finish(leaving)


def mix(plan, decays, attended, readers, state, back, groups):
    tokens = back.shape[0]
    width = attended[0].shape[1]
    count = plan.merge * plan.peers
    return pl.pallas_call(
        functools.partial(mix_kernel, plan, groups),
        in_specs=[smem] * plan.merge + [hbm] * (2 * plan.merge + 2),
        out_specs=(hbm,) * count,
        out_shape=(jax.ShapeDtypeStruct((tokens // plan.peers, width), bf16),) * count,
        scratch_shapes=[
            pltpu.VMEM((plan.merge, tokens, width), f32),
            pltpu.VMEM((plan.merge, tokens, width), bf16),
            pltpu.VMEM(state.shape, bf16),
            pltpu.VMEM(back.shape, bf16),
            pltpu.VMEM((tokens, plan.merge * width), bf16),
            pltpu.VMEM((count, tokens // plan.peers, width), bf16),
            Copies.scratch(),
        ],
        compiler_params=params(52),
        cost_estimate=cost(4 * tokens * tokens * width, 2 * tokens * tokens + 16 * tokens * width),
        name="mix",
    )(*decays, *attended, *readers, state, back)


def out_kernel(plan, sources, w_ref, *refs):
    part_refs, base_refs, out_ref = refs[: len(sources)], refs[len(sources) : -3], refs[-3]
    kept, sems = refs[-2:]
    copies = Copies(sems)
    depth = part_refs[0].shape[1]
    core, me = plan.core(), lax.axis_index("head")
    owners = []
    for s, k in sources:
        owner = lax.rem(me - k + plan.peers, plan.peers) * plan.merge
        owners.append(owner + (core if s == 0 else 1 - core))
    leaving = []
    step = min(128, out_ref.shape[0])
    for at in range(0, out_ref.shape[0], step):
        there = slice(at, at + step)
        total = base_refs[0][there, :] if base_refs else 0.0
        for owner, part in zip(owners, part_refs):
            rows = pl.ds(pl.multiple_of(owner * depth, depth), depth)
            total = total + jnp.dot(part[there, :], w_ref[rows, :], preferred_element_type=f32)
        if base_refs:
            kept[there, :] = total.astype(out_ref.dtype)
            leaving.append(copies.start(kept.at[there], out_ref.at[there]))
        else:
            out_ref[there, :] = total.astype(out_ref.dtype)
    finish(leaving)


def project_out(plan, w, parts, base, kind):
    local, width = next(iter(parts.values())).shape[0], w.shape[1]
    return pl.pallas_call(
        functools.partial(out_kernel, plan, list(parts)),
        in_specs=[vmem] * (1 + len(parts) + len(base)),
        out_specs=hbm if base else vmem,
        out_shape=jax.ShapeDtypeStruct((local, width), kind),
        scratch_shapes=[pltpu.VMEM((local, width), kind), Copies.scratch()],
        compiler_params=params(),
        cost_estimate=cost(0, 4 * local),
        name="project_out",
    )(w, *parts.values(), *base)


def body(frames_in, in_weight, out_weight, block_ids, block_lists, decays):
    local_tokens = frames_in.shape[1]
    heads_here = decays.shape[1]
    groups = block_lists.shape[0]
    me = lax.axis_index("head")
    plan = Plan(lax.axis_size("tm"), lax.axis_size("head"), heads_here, frames_in.shape[2])

    own = frames_in[0]
    arriving = [plan.to_peer(own, plan.peers - k, False) for k in range(1, plan.peers)]
    owns = [own] + [plan.swap(own)] * (plan.merge - 1)
    rates = [decays[0]] + [plan.swap(decays[0])] * (plan.merge - 1)
    block = reorder(plan, in_weight)
    if plan.merge == 2:
        block = reorder(plan, plan.swap(in_weight), [block])
    ids = jnp.roll(block_ids, -me * local_tokens)
    ids, rates = lax.optimization_barrier((ids, rates))
    rank = rank_tokens(ids, groups)

    def fill(arriving, part):
        if plan.merge == 2:
            arriving = arriving + [plan.swap(tokens) for tokens in arriving]
        return place_tokens(plan, rank, local_tokens, arriving, [part])

    if plan.ringed:
        blocks, crossed = [block], []
        half = block.shape[0] // 2
        for k in range(plan.along - 1):
            with_ = rank if k == 0 else ()
            if k == min(1, plan.along - 2):
                rank, owns, _ = lax.optimization_barrier((rank, owns, blocks[-1]))
                part = with_ = place_tokens(plan, rank, 0, owns, [])
            if k == plan.along - 2:
                arriving, _ = lax.optimization_barrier((arriving, blocks[-1]))
                x = fill(arriving, part)
            passed, across, with_ = lax.optimization_barrier(
                (plan.round(blocks[-1]), plan.cross(blocks[-1]), with_)
            )
            if k == plan.along - 2:
                rank, passed, across = lax.optimization_barrier((rank, passed, across))
                places, passed, across = lax.optimization_barrier(
                    (back_tokens(rank), passed, across)
                )
            blocks.append(passed)
            crossed.append(across)
        last = [plan.cross(blocks[-1][:half]), plan.round(crossed[-1][half:])]
        weights = blocks + crossed + last
    else:
        weights = [
            lax.all_gather(block, "tm", axis=0, tiled=True, axis_index_groups=plan.groups())
        ]
        places = back_tokens(rank)
        x = fill(arriving, place_tokens(plan, rank, 0, owns, []))
    if plan.ringed:
        v, b, x_last = project(plan, x, weights[:-2])
        local, total = block_updates(plan, rates, v, b, x_last, last, groups)
    else:
        v, b, x_last = project(plan, x, weights)
        local, total = block_updates(plan, rates, v, b, x_last, [], groups)

    def exchange(blocks):
        return lax.all_to_all(
            blocks, "tm", split_axis=0, concat_axis=0, tiled=True,
            axis_index_groups=plan.groups(),
        )

    share = local.shape[1] // plan.chips
    arrived = exchange(total)
    attended = [attend(plan, 0, block_lists, x, weights, local)]
    arrived, attended = lax.optimization_barrier((arrived, attended))
    states = scan_states(plan, arrived, share)
    x, states = lax.optimization_barrier((x, states))
    if plan.merge == 2:
        attended.append(attend(plan, 1, block_lists, x, weights, local))
    state = exchange(states).reshape(-1, LANES)

    bases, readers = ([a[i] for a in attended] for i in range(2))
    mixed = mix(plan, rates, bases, readers, state, places, groups)
    moved = {
        (s, k): plan.to_peer(mixed[s * plan.peers + k], k, s == 1)
        for s in range(plan.merge)
        for k in range(1, plan.peers)
    }
    near = {(0, 0): mixed[0]}
    if plan.merge == 2:
        near[1, 0] = plan.swap(mixed[plan.peers])
    result = project_out(plan, out_weight, near, [], f32)
    return project_out(plan, out_weight, moved, [result], bf16)[None]


def solution(mesh):
    return jax.shard_map(
        body,
        mesh=mesh,
        in_specs=(P("tm", "head", None), P("tm", "head"), P(), P(), P(), P("tm", "head", None)),
        out_specs=P("tm", "head", None),
        check_vma=False,
    )
```

```python
import functools
import math

import jax
import jax.numpy as jnp
from jax import lax
from jax.experimental import pallas as pl
from jax.experimental.pallas import tpu as pltpu
from jax.sharding import PartitionSpec as P

HD = 64
N = 64
LANES = 2 * HD
PIECES = 5
EARLY = (2, 3)
LATE = (0, 1, 4)

epsilon = 1e-06

vmem = pl.BlockSpec(memory_space=pltpu.VMEM)
smem = pl.BlockSpec(memory_space=pltpu.SMEM)

hbm = pl.BlockSpec(memory_space=pltpu.HBM)

f32 = jnp.float32
bf16 = jnp.bfloat16


def params(mib=16):
    return pltpu.CompilerParams(vmem_limit_bytes=mib << 20)


def cost(flops, nbytes, transcendentals=0):
    return pl.CostEstimate(
        flops=int(flops), bytes_accessed=int(nbytes), transcendentals=int(transcendentals)
    )


def first_half(shape):
    return lax.broadcasted_iota(jnp.int32, shape, len(shape) - 1) < HD


class Plan:
    def __init__(self, frames, peers, heads_here, width):
        self.merge = 2 if frames % 2 == 0 and heads_here % 4 == 0 else 1
        self.frames, self.peers = frames, peers
        self.heads = heads_here // self.merge
        self.pairs = self.heads // 2
        self.chips = frames // self.merge
        self.across = 2 if self.chips % 2 == 0 else 1
        self.along = self.chips // self.across
        self.ringed = self.across == 2 and 2 <= self.along <= 8 and width % (self.chips * LANES) == 0

    def core(self):
        return lax.rem(lax.axis_index("tm"), self.merge)

    def chip(self):
        return lax.div(lax.axis_index("tm"), self.merge)

    def swap(self, block):
        return lax.ppermute(block, "tm", [(t, t ^ 1) for t in range(self.frames)])

    def round(self, block):
        a, b, c = self.along, self.across, self.merge
        pairs = [(t, (t + b * c) % (a * b * c)) for t in range(self.frames)]
        return lax.ppermute(block, "tm", pairs)

    def cross(self, block):
        c = self.merge
        pairs = [(t, (t // c ^ 1) * c + t % c) for t in range(self.frames)]
        return lax.ppermute(block, "tm", pairs)

    def last_chip(self):
        a, b = lax.div(self.chip(), self.across), lax.rem(self.chip(), self.across)
        return lax.rem(a + 1, self.along) * self.across + (self.across - 1 - b)

    def places(self, refs):
        if len(refs) == 1:
            return [(refs[0], slice(None))]
        rows = refs[0].shape[0]
        a, b = lax.div(self.chip(), self.across), lax.rem(self.chip(), self.across)
        n = self.along
        made = []
        for i, ref in enumerate(refs):
            k, flip = (i, 0) if i < n else (min(i - n, n - 1), 1)
            there = lax.rem(a - k + n, n) * self.across
            at = (there + (1 - b if flip else b)) * rows
            at = at + (rows // 2 if i == 2 * n else 0)
            made.append((ref, pl.ds(pl.multiple_of(at, rows // 2), ref.shape[0])))
        return made

    def to_peer(self, block, k, other):
        if not other:
            pairs = [(j, (j + k) % self.peers) for j in range(self.peers)]
            return lax.ppermute(block, "head", pairs)
        if k == 0:
            return self.swap(block)
        pairs = [
            (t * self.peers + j, (t ^ 1) * self.peers + (j + k) % self.peers)
            for t in range(self.frames)
            for j in range(self.peers)
        ]
        return lax.ppermute(block, ("tm", "head"), pairs)

    def groups(self):
        if self.merge == 1:
            return None
        return [[j * self.merge + c for j in range(self.chips)] for c in range(self.merge)]

    def decay(self, refs, slot, pair, g):
        head = self.core() * self.heads + 2 * pair
        return halves((1, LANES), refs[slot][head, g], refs[slot][head + 1, g])


class Copies:
    room = 48

    def __init__(self, sems):
        self.sems, self.count = sems, 0

    def start(self, src, dst):
        copy = pltpu.make_async_copy(src, dst, self.sems.at[self.count])
        copy.start()
        self.count += 1
        return copy

    @staticmethod
    def scratch():
        return pltpu.SemaphoreType.DMA((Copies.room,))


def finish(copies):
    for copy in copies:
        copy.wait()


def halves(shape, one, two):
    return jnp.where(first_half(shape), one, two)


def reorder_kernel(plan, *refs):
    w_ref, out_ref = refs[0], refs[-1]
    rows = w_ref.shape[0]
    width = plan.heads * PIECES * HD
    first = plan.core() == 0

    def chosen(at):
        one = w_ref[:, at : at + HD]
        if plan.merge == 1:
            return one
        return jnp.where(first, one, w_ref[:, width + at : width + at + HD])

    order = [(p, i) for i in EARLY for p in range(plan.pairs)]
    order += [(p, i) for p in range(plan.pairs) for i in LATE]
    for n, (p, i) in enumerate(order):
        block = jnp.concatenate(
            [chosen(((2 * p + h) * PIECES + i) * HD) for h in range(2)], axis=1
        )
        cols = slice(n * LANES, (n + 1) * LANES)
        if len(refs) == 2:
            out_ref[:, cols] = block
        else:
            mine = refs[1][:, cols]
            out_ref[:rows, cols] = jnp.where(first, mine, block)
            out_ref[rows:, cols] = jnp.where(first, block, mine)


def reorder(plan, w, mine=()):
    rows = w.shape[0] * (1 + len(mine))
    return pl.pallas_call(
        functools.partial(reorder_kernel, plan),
        out_shape=jax.ShapeDtypeStruct((rows, plan.heads * PIECES * HD), bf16),
        compiler_params=params(),
        cost_estimate=cost(0, 4 * rows),
        name="reorder",
    )(w, *mine)


def normalise(part, out, at):
    step = min(128, part.shape[0])

    def norm(c, _):
        start = pl.multiple_of(c * step, step)
        wide = part[pl.ds(start, step), :].astype(f32)
        scale = lax.rsqrt(jnp.mean(wide * wide, axis=-1, keepdims=True) + epsilon)
        out[pl.ds(at + start, step), :] = (wide * scale).astype(bf16)
        return 0

    lax.fori_loop(0, part.shape[0] // step, norm, 0)


def rank_kernel(groups, ids_ref, row_ref):
    tokens = ids_ref.shape[1]
    block = tokens // groups
    label = lax.broadcasted_iota(jnp.int32, (groups, tokens), 0)
    held = label == ids_ref[...]
    held_bf = jnp.where(held, 1.0, 0.0).astype(bf16)
    counts = []
    for c in range(tokens // 256):
        before = lax.broadcasted_iota(jnp.int32, (tokens, 256), 0) < (
            lax.broadcasted_iota(jnp.int32, (tokens, 256), 1) + c * 256
        )
        counts.append(
            jnp.dot(held_bf, jnp.where(before, 1.0, 0.0).astype(bf16), preferred_element_type=f32)
        )
    count = jnp.concatenate(counts, axis=1)
    row_ref[...] = jnp.sum(
        jnp.where(held, count + (label * block).astype(f32), 0.0), axis=0, keepdims=True
    )


def rank_tokens(ids, groups):
    tokens = ids.shape[0]
    return pl.pallas_call(
        functools.partial(rank_kernel, groups),
        out_shape=jax.ShapeDtypeStruct((1, tokens), f32),
        compiler_params=params(),
        cost_estimate=cost(0, 4 * tokens),
        name="rank_tokens",
    )(ids.reshape(1, tokens))


def back_kernel(row_ref, back_ref):
    tokens = back_ref.shape[0]
    lane = lax.broadcasted_iota(jnp.int32, (LANES, LANES), 1)
    for at in range(0, tokens, LANES):
        place = jnp.broadcast_to(row_ref[:, at : at + LANES], (LANES, LANES)).T
        for t in range(0, tokens, LANES):
            back_ref[at : at + LANES, t : t + LANES] = jnp.where(
                (lane + t).astype(f32) == place, 1.0, 0.0
            ).astype(bf16)


def back_tokens(rank):
    return pl.pallas_call(
        back_kernel,
        out_shape=jax.ShapeDtypeStruct((rank.shape[1], rank.shape[1]), bf16),
        compiler_params=params(),
        cost_estimate=cost(0, 4 * LANES),
        name="back_tokens",
    )(rank)


def hold(values):
    def kernel(in_ref, out_ref):
        out_ref[...] = in_ref[...]

    return pl.pallas_call(
        kernel,
        out_shape=jax.ShapeDtypeStruct(values.shape, values.dtype),
        compiler_params=params(),
        cost_estimate=cost(2e10, 4 * LANES),
        name="hold",
    )(values)


def picks(rank, at, rows):
    places = lax.broadcasted_iota(jnp.int32, (rows, rank.shape[1]), 0) + at
    return jnp.where(places.astype(f32) == rank, 1.0, 0.0).astype(bf16)


def place_kernel(merge, parts, start, rank_ref, *refs):
    frame_refs, refs = refs[:parts], refs[parts:]
    base_refs, (x_ref, normed) = refs[:-2], refs[-2:]
    tokens = rank_ref.shape[1]
    count = normed.shape[1]
    step = 256
    at = 0
    for ref in frame_refs:
        normalise(ref, normed.at[at // count], at % count)
        at += ref.shape[0]
    for at in range(0, tokens, step):
        pick = picks(rank_ref[:, start : start + count], at, step)
        for s in range(merge):
            there = slice(s * tokens + at, s * tokens + at + step)
            placed = jnp.dot(pick, normed[s], preferred_element_type=f32).astype(bf16)
            for base in base_refs:
                placed = base[there, :] + placed
            x_ref[there, :] = placed


def place_tokens(plan, rank, start, frames, base):
    tokens = rank.shape[1]
    width = frames[0].shape[1]
    count = sum(f.shape[0] for f in frames) // plan.merge
    return pl.pallas_call(
        functools.partial(place_kernel, plan.merge, len(frames), start),
        out_shape=jax.ShapeDtypeStruct((plan.merge * tokens, width), bf16),
        scratch_shapes=[pltpu.VMEM((plan.merge, count, width), bf16)],
        compiler_params=params(),
        cost_estimate=cost(0, 4 * tokens),
        name="place_tokens",
    )(rank, *frames, *base)


def project_kernel(plan, x_ref, *refs):
    w_refs, (v_ref, b_ref, rest_ref, w, turned) = refs[:-5], refs[-5:]
    every = x_ref.shape[0]
    step = 256
    cols = plan.pairs * LANES
    if len(w_refs) > 1:
        w[...] = jnp.zeros_like(w)
        turned[...] = jnp.zeros_like(turned)
    for ref, rows in plan.places(w_refs):
        w[rows, :] = ref[:, :cols]
        turned[rows, :] = ref[:, cols : 2 * cols]
    maps = jnp.concatenate(
        [
            turned[at : at + LANES, :].astype(f32).T.astype(bf16)
            for at in range(0, turned.shape[0], LANES)
        ],
        axis=1,
    )
    for at in range(0, every, step):
        x = x_ref[at : at + step, :]
        v_ref[at : at + step, :] = jnp.dot(x, w[...], preferred_element_type=f32)
        b_ref[:, at : at + step] = lax.dot_general(
            maps, x, (((1,), (1,)), ((), ())), preferred_element_type=f32
        )
    count = rest_ref.shape[1]
    there = plan.last_chip() * count
    for at in range(0, every, step):
        rest = x_ref[at : at + step, :count]
        for c in range(count, x_ref.shape[1], count):
            rest = jnp.where(there == c, x_ref[at : at + step, c : c + count], rest)
        rest_ref[at : at + step, :] = rest


def project(plan, x, weights):
    every, width = x.shape
    cols = plan.pairs * LANES
    count = max(LANES, width // plan.chips)
    return pl.pallas_call(
        functools.partial(project_kernel, plan),
        out_shape=(
            jax.ShapeDtypeStruct((every, cols), f32),
            jax.ShapeDtypeStruct((cols, every), f32),
            jax.ShapeDtypeStruct((every, count), bf16),
        ),
        scratch_shapes=[pltpu.VMEM((width, cols), bf16), pltpu.VMEM((width, cols), bf16)],
        compiler_params=params(),
        cost_estimate=cost(0, 4 * width),
        name="project",
    )(x, *weights)


def update_kernel(plan, groups, decay_ref, *refs):
    v_ref, b_ref, x_ref, last_refs, (left, total_out, total_ref, u, sems) = (
        refs[0], refs[1], refs[2], refs[3:-5], refs[-5:]
    )
    copies = Copies(sems)
    leaving = []
    every = v_ref.shape[0]
    tokens = every // plan.merge
    block = tokens // groups
    step = 256
    here = step // block
    cols = plan.pairs * LANES
    if last_refs:
        w = jnp.concatenate([ref[:, : 2 * cols] for ref in last_refs], axis=0)
        maps = w[:, cols:].astype(f32).T.astype(bf16)
        w = w[:, :cols]

    lane = lax.div(lax.broadcasted_iota(jnp.int32, (LANES, step), 1), block)
    for at in range(0, every, step):
        there = slice(at, at + step)
        values, b = v_ref[there, :], b_ref[:, there]
        if last_refs:
            x = x_ref[there, :]
            values = values + jnp.dot(x, w, preferred_element_type=f32)
            b = b + lax.dot_general(
                maps, x, (((1,), (1,)), ((), ())), preferred_element_type=f32
            )
        values = values.astype(bf16)
        for p in range(plan.pairs):
            mine = b[p * LANES : (p + 1) * LANES]
            wide = jnp.concatenate(
                [jnp.where(lane == i, mine, 0.0).astype(bf16) for i in range(here)], axis=0
            )
            outer = jnp.dot(
                wide, values[:, p * LANES : (p + 1) * LANES], preferred_element_type=f32
            )
            for i in range(here):
                m = outer[i * 2 * N : (i + 1) * 2 * N]
                row = ((at % tokens // block + i) * plan.pairs + p) * N
                u[at // tokens, row : row + N, :] = halves((N, LANES), m[:N], m[N:])

    peers = total_ref.shape[0]
    share = u.shape[1] // peers
    items = max(1, share // N)
    size = min(N, share)
    first = plan.core() == 0
    for d in range(peers):
        for i in range(items):
            row = d * share + i * N
            rows = slice(row, row + size)
            item = slice(row // N, row // N + 1)
            last, product = decay_ref[0, item, :], decay_ref[1, item, :]
            if plan.merge == 2:
                one, two = u[0, rows, :], u[1, rows, :]
                one, two = (
                    one + jnp.where(first, 0.0, last) * two,
                    two + jnp.where(first, last, 0.0) * one,
                )
                left[0, rows, :] = one.astype(bf16)
                left[1, rows, :] = two.astype(bf16)
                total = jnp.where(first, two, one)
            else:
                total = u[0, rows, :]
                left[0, rows, :] = total.astype(bf16)
            total_ref[d, i * size : (i + 1) * size, :] = total.astype(bf16)
            for n in range(3):
                piece = product.astype(bf16)
                at = share + n * items + i
                total_ref[d, at : at + 1, :] = piece
                product = product - piece.astype(f32)
        if (d + 1) % (peers // 4) == 0:
            done = slice(d + 1 - peers // 4, d + 1)
            leaving.append(copies.start(total_ref.at[done], total_out.at[done]))
    finish(leaving)


def share_rows(share):
    return share + 16 * -(-3 * max(1, share // N) // 16)


def block_updates(plan, decays, v, b, x, last, groups):
    every, cols = v.shape
    rows = plan.pairs * groups * N
    share = rows // plan.chips
    return pl.pallas_call(
        functools.partial(update_kernel, plan, groups),
        in_specs=[vmem] * (4 + len(last)),
        out_specs=(vmem, hbm),
        out_shape=(
            jax.ShapeDtypeStruct((plan.merge, rows, LANES), bf16),
            jax.ShapeDtypeStruct((plan.chips, share_rows(share), LANES), bf16),
        ),
        scratch_shapes=[
            pltpu.VMEM((plan.chips, share_rows(share), LANES), bf16),
            pltpu.VMEM((plan.merge, rows, LANES), f32),
            Copies.scratch(),
        ],
        compiler_params=params(),
        cost_estimate=cost(4 * every * 256 * 2 * cols, 6 * every * cols),
        name="block_updates",
    )(decays, v, b, x, *last)


def decay_kernel(plan, groups, *refs):
    rate_refs, out_ref = refs[:-1], refs[-1]
    first = plan.core() == 0
    for g in range(groups):
        for p in range(plan.pairs):
            row = slice(g * plan.pairs + p, g * plan.pairs + p + 1)
            slots = [plan.decay(rate_refs, s, p, g) for s in range(plan.merge)]
            together, last = slots[0], slots[0]
            if plan.merge == 2:
                together = slots[0] * slots[1]
                last = jnp.where(first, slots[1], slots[0])
                slots = [
                    jnp.where(first, slots[0], together),
                    jnp.where(first, together, slots[1]),
                ]
            for i, value in enumerate([last, together] + slots):
                out_ref[i, row, :] = value


def decay_tables(plan, rates, groups):
    return pl.pallas_call(
        functools.partial(decay_kernel, plan, groups),
        in_specs=[smem] * plan.merge,
        out_shape=jax.ShapeDtypeStruct((2 + plan.merge, plan.pairs * groups, LANES), f32),
        compiler_params=params(),
        cost_estimate=cost(0, 4 * LANES),
        name="decay_tables",
    )(*rates)


def scan_kernel(plan, u_ref, s_ref):
    share = s_ref.shape[1]
    size = min(share, N)
    items = share // size
    for i in range(items):
        at = slice(i * size, (i + 1) * size)
        state = jnp.zeros((size, LANES), f32)
        for j in range(plan.chips):
            s_ref[j, at, :] = state.astype(bf16)
            decay = jnp.zeros((1, LANES), f32)
            for n in range(3):
                row = share + n * items + i
                decay = decay + u_ref[j, row : row + 1, :].astype(f32)
            state = decay * state + u_ref[j, at, :].astype(f32)


def scan_states(plan, update, share):
    return pl.pallas_call(
        functools.partial(scan_kernel, plan),
        out_shape=jax.ShapeDtypeStruct((plan.chips, share, LANES), bf16),
        compiler_params=params(),
        cost_estimate=cost(2 * update.size, 4 * update.size),
        name="scan_states",
    )(update)


def attend_kernel(plan, slot, *refs):
    lists_ref, x_in, local_in, refs = refs[0], refs[1], refs[2], refs[3:]
    w_refs, refs = refs[:-12], refs[-12:]
    a_out, c_out, x, local, w, q_ref, k_ref, wide_v, e_ref, a, c_ref, sems = refs
    copies = Copies(sems)
    tokens = x.shape[0]
    groups, chosen = lists_ref.shape
    block = tokens // groups
    step = 256
    per = step // block
    wide = plan.pairs * LANES

    weights = []
    for ref, rows in plan.places(w_refs):
        weights.append(copies.start(ref.at[:, :wide], w.at[rows, :wide]))
        weights.append(copies.start(ref.at[:, 2 * wide :], w.at[rows, wide:]))
    arriving = []
    for at in range(0, tokens, step):
        from_ = slice(slot * tokens + at, slot * tokens + at + step)
        arriving.append(copies.start(x_in.at[from_], x.at[at : at + step]))
    later = copies.start(local_in.at[slot], local)

    same = lax.div(lax.broadcasted_iota(jnp.int32, (2 * LANES, 2 * LANES), 0), HD) == lax.div(
        lax.broadcasted_iota(jnp.int32, (2 * LANES, 2 * LANES), 1), HD
    )
    same = jnp.where(same, 1.0, 0.0).astype(bf16)

    def head_norm(values):
        square = values * values
        high = square.astype(bf16)
        low = (square - high.astype(f32)).astype(bf16)
        total = jnp.dot(high, same, preferred_element_type=f32)
        total = total + jnp.dot(low, same, preferred_element_type=f32)
        return values * lax.rsqrt(total * (1.0 / HD) + epsilon)

    half = first_half((step, LANES))
    finish(weights)
    for at in range(0, tokens, step):
        rows = slice(at, at + step)
        arriving[at // step].wait()
        every = jnp.dot(x[rows, :], w[...], preferred_element_type=f32).astype(bf16)
        for p in range(plan.pairs):
            cols = slice(p * LANES, (p + 1) * LANES)
            wide_v[p, rows, :LANES] = every[:, cols]
            first = wide + 3 * p * LANES
            c_ref[rows, cols] = every[:, first + 2 * LANES : first + 3 * LANES]
            both = head_norm(every[:, first : first + 2 * LANES].astype(f32))
            k_ref[p, rows, :] = both[:, LANES:].astype(bf16)
            q = both[:, :LANES]
            one = jnp.where(half, q, 0.0).astype(bf16)
            two = jnp.where(half, 0.0, q).astype(bf16)
            for i in range(per):
                part = slice(i * block, (i + 1) * block)
                q_ref[p, at // block + i] = jnp.concatenate([one[part], two[part]], axis=0)
    leaving = [copies.start(c_ref, c_out)]
    later.wait()
    for p in range(plan.pairs):
        wide_v[p, :, LANES:] = jnp.ones((tokens, LANES), bf16)

    scale = math.log2(math.e) / math.sqrt(HD)
    starts = [
        [pl.multiple_of(lists_ref[g, j] * block, block) for j in range(chosen)]
        for g in range(groups)
    ]
    for g in range(groups):
        for p in range(plan.pairs):
            keys = jnp.concatenate([k_ref[p, pl.ds(s, block), :] for s in starts[g]], axis=0)
            score = lax.dot_general(
                q_ref[p, g], keys, (((1,), (1,)), ((), ())), preferred_element_type=f32
            )
            e_ref[p, g] = jnp.exp2(score * scale).astype(bf16)
    for g in range(groups):
        rows = slice(g * block, (g + 1) * block)
        for p in range(plan.pairs):
            cols = slice(p * LANES, (p + 1) * LANES)
            values = jnp.concatenate([wide_v[p, pl.ds(s, block), :] for s in starts[g]], axis=0)
            both = jnp.dot(e_ref[p, g], values, preferred_element_type=f32)
            both = both[:, :LANES] / both[:, LANES:]
            a[rows, cols] = halves((block, LANES), both[:block], both[block:])
    for g in range(groups):
        rows = slice(g * block, (g + 1) * block)
        for p in range(plan.pairs):
            cols = slice(p * LANES, (p + 1) * LANES)
            items = slice((g * plan.pairs + p) * N, (g * plan.pairs + p + 1) * N)
            a[rows, cols] = a[rows, cols] + read_out(
                c_ref[rows, cols], local[items, :].astype(f32), block
            )
        if (g + 1) % per == 0:
            done = slice((g + 1 - per) * block, (g + 1) * block)
            leaving.append(copies.start(a.at[done], a_out.at[done]))
    finish(leaving)


def attend(plan, slot, lists, x, weights, local):
    every, width = x.shape
    groups, chosen = lists.shape
    tokens = every // plan.merge
    block = tokens // groups
    cols = plan.pairs * LANES
    return pl.pallas_call(
        functools.partial(attend_kernel, plan, slot),
        in_specs=[smem] + [hbm] * (2 + len(weights)),
        out_specs=(hbm,) * 2,
        scratch_shapes=[
            pltpu.VMEM((tokens, width), bf16),
            pltpu.VMEM(local.shape[1:], bf16),
            pltpu.VMEM((width, 4 * cols), bf16),
            pltpu.VMEM((plan.pairs, groups, 2 * block, LANES), bf16),
            pltpu.VMEM((plan.pairs, tokens, LANES), bf16),
            pltpu.VMEM((plan.pairs, tokens, 2 * LANES), bf16),
            pltpu.VMEM((plan.pairs, groups, 2 * block, chosen * block), bf16),
            pltpu.VMEM((tokens, cols), f32),
            pltpu.VMEM((tokens, cols), bf16),
            Copies.scratch(),
        ],
        out_shape=(
            jax.ShapeDtypeStruct((tokens, cols), f32),
            jax.ShapeDtypeStruct((tokens, cols), bf16),
        ),
        compiler_params=params(60),
        cost_estimate=cost(
            6 * tokens * width * 3 * cols,
            4 * (tokens * width + 5 * width * cols + local.size),
            2 * plan.pairs * tokens * chosen * block,
        ),
        name="attend",
    )(lists, x, local, *weights)


def read_out(readers, state, block):
    half = first_half(state.shape)
    wide = jnp.concatenate([jnp.where(half, state, 0.0), jnp.where(half, 0.0, state)], axis=0)
    return jnp.dot(readers, wide.astype(bf16), preferred_element_type=f32) * (
        1.0 / (N * math.sqrt(block))
    )


def mix_kernel(plan, groups, decay_in, *refs):
    a_ins, refs = refs[: plan.merge], refs[plan.merge :]
    c_ins, refs = refs[: plan.merge], refs[plan.merge :]
    s_in, back_in, refs = refs[0], refs[1], refs[2:]
    out_refs, (decay, a, c, state, back, mixed, out, sems) = refs[:-8], refs[-8:]
    copies = Copies(sems)
    tokens = back.shape[0]
    block = tokens // groups
    width = a.shape[2]
    here = groups // 4
    many = here * plan.pairs * N

    arriving = []
    decaying = copies.start(decay_in, decay)
    for i in range(4):
        rows = slice(i * here * block, (i + 1) * here * block)
        items = slice(i * many, (i + 1) * many)
        arriving.append([copies.start(s_in.at[items], state.at[items])])
        for s in range(plan.merge):
            arriving[-1] += [
                copies.start(c_ins[s].at[rows], c.at[s, rows, :]),
                copies.start(a_ins[s].at[rows], a.at[s, rows, :]),
            ]
    local = tokens // plan.peers
    order = list(range(1, plan.peers)) + [0]
    turning = []
    for k in order:
        rows = slice(k * local, (k + 1) * local)
        turning.append(copies.start(back_in.at[rows], back.at[rows]))

    decaying.wait()
    for g in range(groups):
        if g % here == 0:
            finish(arriving[g // here])
        rows = slice(g * block, (g + 1) * block)
        for p in range(plan.pairs):
            cols = slice(p * LANES, (p + 1) * LANES)
            at = (g * plan.pairs + p) * N
            readers = jnp.concatenate([c[s, rows, cols] for s in range(plan.merge)], axis=0)
            read = read_out(readers, state[at : at + N, :].astype(f32), block)
            item = slice(g * plan.pairs + p, g * plan.pairs + p + 1)
            for s in range(plan.merge):
                there = slice(s * width + p * LANES, s * width + (p + 1) * LANES)
                mixed[rows, there] = (
                    a[s, rows, cols]
                    + decay[2 + s, item, :] * read[s * block : (s + 1) * block]
                ).astype(bf16)

    leaving = []
    for k, turned in zip(order, turning):
        turned.wait()
        placed = jnp.dot(
            back[k * local : (k + 1) * local, :], mixed[...], preferred_element_type=f32
        ).astype(bf16)
        for s in range(plan.merge):
            i = s * plan.peers + k
            out[i] = placed[:, s * width : (s + 1) * width]
            leaving.append(copies.start(out.at[i], out_refs[i]))
    finish(leaving)


def mix(plan, decays, attended, readers, state, back, groups):
    tokens = back.shape[0]
    width = attended[0].shape[1]
    count = plan.merge * plan.peers
    return pl.pallas_call(
        functools.partial(mix_kernel, plan, groups),
        in_specs=[hbm] * (2 * plan.merge + 3),
        out_specs=(hbm,) * count,
        out_shape=(jax.ShapeDtypeStruct((tokens // plan.peers, width), bf16),) * count,
        scratch_shapes=[
            pltpu.VMEM(decays.shape, f32),
            pltpu.VMEM((plan.merge, tokens, width), f32),
            pltpu.VMEM((plan.merge, tokens, width), bf16),
            pltpu.VMEM(state.shape, bf16),
            pltpu.VMEM(back.shape, bf16),
            pltpu.VMEM((tokens, plan.merge * width), bf16),
            pltpu.VMEM((count, tokens // plan.peers, width), bf16),
            Copies.scratch(),
        ],
        compiler_params=params(52),
        cost_estimate=cost(4 * tokens * tokens * width, 2 * tokens * tokens + 16 * tokens * width),
        name="mix",
    )(decays, *attended, *readers, state, back)


def out_kernel(plan, sources, w_ref, *refs):
    part_refs, base_refs, out_ref = refs[: len(sources)], refs[len(sources) : -3], refs[-3]
    kept, sems = refs[-2:]
    copies = Copies(sems)
    depth = part_refs[0].shape[1]
    core, me = plan.core(), lax.axis_index("head")
    owners = []
    for s, k in sources:
        owner = lax.rem(me - k + plan.peers, plan.peers) * plan.merge
        owners.append(owner + (core if s == 0 else 1 - core))
    leaving = []
    step = min(128, out_ref.shape[0])
    for at in range(0, out_ref.shape[0], step):
        there = slice(at, at + step)
        total = base_refs[0][there, :] if base_refs else 0.0
        for owner, part in zip(owners, part_refs):
            rows = pl.ds(pl.multiple_of(owner * depth, depth), depth)
            total = total + jnp.dot(part[there, :], w_ref[rows, :], preferred_element_type=f32)
        if base_refs:
            kept[there, :] = total.astype(out_ref.dtype)
            leaving.append(copies.start(kept.at[there], out_ref.at[there]))
        else:
            out_ref[there, :] = total.astype(out_ref.dtype)
    finish(leaving)


def project_out(plan, w, parts, base, kind):
    local, width = next(iter(parts.values())).shape[0], w.shape[1]
    return pl.pallas_call(
        functools.partial(out_kernel, plan, list(parts)),
        in_specs=[vmem] * (1 + len(parts) + len(base)),
        out_specs=hbm if base else vmem,
        out_shape=jax.ShapeDtypeStruct((local, width), kind),
        scratch_shapes=[pltpu.VMEM((local, width), kind), Copies.scratch()],
        compiler_params=params(),
        cost_estimate=cost(0, 4 * local),
        name="project_out",
    )(w, *parts.values(), *base)


def body(frames_in, in_weight, out_weight, block_ids, block_lists, decays):
    local_tokens = frames_in.shape[1]
    heads_here = decays.shape[1]
    groups = block_lists.shape[0]
    me = lax.axis_index("head")
    plan = Plan(lax.axis_size("tm"), lax.axis_size("head"), heads_here, frames_in.shape[2])

    own = frames_in[0]
    arriving = [plan.to_peer(own, plan.peers - k, False) for k in range(1, plan.peers)]
    owns = [own] + [plan.swap(own)] * (plan.merge - 1)
    rates = [decays[0]] + [plan.swap(decays[0])] * (plan.merge - 1)
    block = reorder(plan, in_weight)
    if plan.merge == 2:
        block = reorder(plan, plan.swap(in_weight), [block])
    ids = jnp.roll(block_ids, -me * local_tokens)
    ids, rates = lax.optimization_barrier((ids, rates))
    tables = decay_tables(plan, rates, groups)
    rank = rank_tokens(ids, groups)

    def fill(arriving, part):
        if plan.merge == 2:
            arriving = arriving + [plan.swap(tokens) for tokens in arriving]
        return place_tokens(plan, rank, local_tokens, arriving, [part])

    if plan.ringed:
        blocks, crossed = [block], []
        half = block.shape[0] // 2
        for k in range(plan.along - 1):
            with_ = ()
            if k == 0:
                places = back_tokens(rank)
                with_ = (places, tables)
            if k == min(1, plan.along - 2):
                rank, owns, _ = lax.optimization_barrier((rank, owns, blocks[-1]))
                part = with_ = place_tokens(plan, rank, 0, owns, [])
            if k == plan.along - 2:
                arriving, _ = lax.optimization_barrier((arriving, blocks[-1]))
                x = fill(arriving, part)
            passed, across, with_ = lax.optimization_barrier(
                (plan.round(blocks[-1]), plan.cross(blocks[-1]), with_)
            )
            if k == plan.along - 2:
                tables, passed, across = lax.optimization_barrier((tables, passed, across))
                tables, passed, across = lax.optimization_barrier(
                    (hold(tables), passed, across)
                )
            blocks.append(passed)
            crossed.append(across)
        last = [plan.cross(blocks[-1][:half]), plan.round(crossed[-1][half:])]
        weights = blocks + crossed + last
    else:
        weights = [
            lax.all_gather(block, "tm", axis=0, tiled=True, axis_index_groups=plan.groups())
        ]
        places = back_tokens(rank)
        x = fill(arriving, place_tokens(plan, rank, 0, owns, []))
    if plan.ringed:
        v, b, x_last = project(plan, x, weights[:-2])
        local, total = block_updates(plan, tables, v, b, x_last, last, groups)
    else:
        v, b, x_last = project(plan, x, weights)
        local, total = block_updates(plan, tables, v, b, x_last, [], groups)

    def exchange(blocks):
        return lax.all_to_all(
            blocks, "tm", split_axis=0, concat_axis=0, tiled=True,
            axis_index_groups=plan.groups(),
        )

    share = local.shape[1] // plan.chips
    arrived = exchange(total)
    attended = [attend(plan, 0, block_lists, x, weights, local)]
    arrived, attended = lax.optimization_barrier((arrived, attended))
    states = scan_states(plan, arrived, share)
    x, states = lax.optimization_barrier((x, states))
    if plan.merge == 2:
        attended.append(attend(plan, 1, block_lists, x, weights, local))
    state = exchange(states).reshape(-1, LANES)

    bases, readers = ([a[i] for a in attended] for i in range(2))
    mixed = mix(plan, tables, bases, readers, state, places, groups)
    moved = {
        (s, k): plan.to_peer(mixed[s * plan.peers + k], k, s == 1)
        for s in range(plan.merge)
        for k in range(1, plan.peers)
    }
    near = {(0, 0): mixed[0]}
    if plan.merge == 2:
        near[1, 0] = plan.swap(mixed[plan.peers])
    result = project_out(plan, out_weight, near, [], f32)
    last = {key: moved.pop(key) for key in list(moved)[-1:]}
    if moved:
        result = project_out(plan, out_weight, moved, [result], f32)
    return project_out(plan, out_weight, last, [result], bf16)[None]


def solution(mesh):
    return jax.shard_map(
        body,
        mesh=mesh,
        in_specs=(P("tm", "head", None), P("tm", "head"), P(), P(), P(), P("tm", "head", None)),
        out_specs=P("tm", "head", None),
        check_vma=False,
    )
```

```python
import functools
import math

import jax
import jax.numpy as jnp
from jax import lax
from jax.experimental import pallas as pl
from jax.experimental.pallas import tpu as pltpu
from jax.sharding import PartitionSpec as P

HD = 64
N = 64
LANES = 2 * HD
PIECES = 5
EARLY = (2, 3)
LATE = (0, 1, 4)

epsilon = 1e-06

vmem = pl.BlockSpec(memory_space=pltpu.VMEM)
smem = pl.BlockSpec(memory_space=pltpu.SMEM)

hbm = pl.BlockSpec(memory_space=pltpu.HBM)

f32 = jnp.float32
bf16 = jnp.bfloat16


def params(mib=16):
    return pltpu.CompilerParams(vmem_limit_bytes=mib << 20)


def cost(flops, nbytes, transcendentals=0):
    return pl.CostEstimate(
        flops=int(flops), bytes_accessed=int(nbytes), transcendentals=int(transcendentals)
    )


def first_half(shape):
    return lax.broadcasted_iota(jnp.int32, shape, len(shape) - 1) < HD


class Plan:
    def __init__(self, frames, peers, heads_here, width):
        self.merge = 2 if frames % 2 == 0 and heads_here % 4 == 0 else 1
        self.frames, self.peers = frames, peers
        self.heads = heads_here // self.merge
        self.pairs = self.heads // 2
        self.chips = frames // self.merge
        self.across = 2 if self.chips % 2 == 0 else 1
        self.along = self.chips // self.across
        self.ringed = self.across == 2 and 2 <= self.along <= 8 and width % (self.chips * LANES) == 0

    def core(self):
        return lax.rem(lax.axis_index("tm"), self.merge)

    def chip(self):
        return lax.div(lax.axis_index("tm"), self.merge)

    def swap(self, block):
        return lax.ppermute(block, "tm", [(t, t ^ 1) for t in range(self.frames)])

    def round(self, block):
        a, b, c = self.along, self.across, self.merge
        pairs = [(t, (t + b * c) % (a * b * c)) for t in range(self.frames)]
        return lax.ppermute(block, "tm", pairs)

    def cross(self, block):
        c = self.merge
        pairs = [(t, (t // c ^ 1) * c + t % c) for t in range(self.frames)]
        return lax.ppermute(block, "tm", pairs)

    def last_chip(self):
        a, b = lax.div(self.chip(), self.across), lax.rem(self.chip(), self.across)
        return lax.rem(a + 1, self.along) * self.across + (self.across - 1 - b)

    def places(self, refs):
        if len(refs) == 1:
            return [(refs[0], slice(None))]
        rows = refs[0].shape[0]
        a, b = lax.div(self.chip(), self.across), lax.rem(self.chip(), self.across)
        n = self.along
        made = []
        for i, ref in enumerate(refs):
            k, flip = (i, 0) if i < n else (min(i - n, n - 1), 1)
            there = lax.rem(a - k + n, n) * self.across
            at = (there + (1 - b if flip else b)) * rows
            at = at + (rows // 2 if i == 2 * n else 0)
            made.append((ref, pl.ds(pl.multiple_of(at, rows // 2), ref.shape[0])))
        return made

    def to_peer(self, block, k, other):
        if not other:
            pairs = [(j, (j + k) % self.peers) for j in range(self.peers)]
            return lax.ppermute(block, "head", pairs)
        if k == 0:
            return self.swap(block)
        pairs = [
            (t * self.peers + j, (t ^ 1) * self.peers + (j + k) % self.peers)
            for t in range(self.frames)
            for j in range(self.peers)
        ]
        return lax.ppermute(block, ("tm", "head"), pairs)

    def groups(self):
        if self.merge == 1:
            return None
        return [[j * self.merge + c for j in range(self.chips)] for c in range(self.merge)]

    def decay(self, refs, slot, pair, g):
        head = self.core() * self.heads + 2 * pair
        return halves((1, LANES), refs[slot][head, g], refs[slot][head + 1, g])


class Copies:
    room = 48

    def __init__(self, sems):
        self.sems, self.count = sems, 0

    def start(self, src, dst):
        copy = pltpu.make_async_copy(src, dst, self.sems.at[self.count])
        copy.start()
        self.count += 1
        return copy

    @staticmethod
    def scratch():
        return pltpu.SemaphoreType.DMA((Copies.room,))


def finish(copies):
    for copy in copies:
        copy.wait()


def halves(shape, one, two):
    return jnp.where(first_half(shape), one, two)


def reorder_kernel(plan, *refs):
    w_ref, out_ref = refs[0], refs[-1]
    rows = w_ref.shape[0]
    width = plan.heads * PIECES * HD
    first = plan.core() == 0

    def chosen(at):
        one = w_ref[:, at : at + HD]
        if plan.merge == 1:
            return one
        return jnp.where(first, one, w_ref[:, width + at : width + at + HD])

    order = [(p, i) for i in EARLY for p in range(plan.pairs)]
    order += [(p, i) for p in range(plan.pairs) for i in LATE]
    for n, (p, i) in enumerate(order):
        block = jnp.concatenate(
            [chosen(((2 * p + h) * PIECES + i) * HD) for h in range(2)], axis=1
        )
        cols = slice(n * LANES, (n + 1) * LANES)
        if len(refs) == 2:
            out_ref[:, cols] = block
        else:
            mine = refs[1][:, cols]
            out_ref[:rows, cols] = jnp.where(first, mine, block)
            out_ref[rows:, cols] = jnp.where(first, block, mine)


def reorder(plan, w, mine=()):
    rows = w.shape[0] * (1 + len(mine))
    return pl.pallas_call(
        functools.partial(reorder_kernel, plan),
        out_shape=jax.ShapeDtypeStruct((rows, plan.heads * PIECES * HD), bf16),
        compiler_params=params(),
        cost_estimate=cost(0, 4 * rows),
        name="reorder",
    )(w, *mine)


def normalise(part, out, at):
    step = min(128, part.shape[0])

    def norm(c, _):
        start = pl.multiple_of(c * step, step)
        wide = part[pl.ds(start, step), :].astype(f32)
        scale = lax.rsqrt(jnp.mean(wide * wide, axis=-1, keepdims=True) + epsilon)
        out[pl.ds(at + start, step), :] = (wide * scale).astype(bf16)
        return 0

    lax.fori_loop(0, part.shape[0] // step, norm, 0)


def rank_kernel(groups, ids_ref, row_ref):
    tokens = ids_ref.shape[1]
    block = tokens // groups
    label = lax.broadcasted_iota(jnp.int32, (groups, tokens), 0)
    held = label == ids_ref[...]
    held_bf = jnp.where(held, 1.0, 0.0).astype(bf16)
    counts = []
    for c in range(tokens // 256):
        before = lax.broadcasted_iota(jnp.int32, (tokens, 256), 0) < (
            lax.broadcasted_iota(jnp.int32, (tokens, 256), 1) + c * 256
        )
        counts.append(
            jnp.dot(held_bf, jnp.where(before, 1.0, 0.0).astype(bf16), preferred_element_type=f32)
        )
    count = jnp.concatenate(counts, axis=1)
    row_ref[...] = jnp.sum(
        jnp.where(held, count + (label * block).astype(f32), 0.0), axis=0, keepdims=True
    )


def rank_tokens(ids, groups):
    tokens = ids.shape[0]
    return pl.pallas_call(
        functools.partial(rank_kernel, groups),
        out_shape=jax.ShapeDtypeStruct((1, tokens), f32),
        compiler_params=params(),
        cost_estimate=cost(0, 4 * tokens),
        name="rank_tokens",
    )(ids.reshape(1, tokens))


def back_kernel(row_ref, back_ref):
    tokens = back_ref.shape[0]
    lane = lax.broadcasted_iota(jnp.int32, (LANES, LANES), 1)
    for at in range(0, tokens, LANES):
        place = jnp.broadcast_to(row_ref[:, at : at + LANES], (LANES, LANES)).T
        for t in range(0, tokens, LANES):
            back_ref[at : at + LANES, t : t + LANES] = jnp.where(
                (lane + t).astype(f32) == place, 1.0, 0.0
            ).astype(bf16)


def back_tokens(rank):
    return pl.pallas_call(
        back_kernel,
        out_shape=jax.ShapeDtypeStruct((rank.shape[1], rank.shape[1]), bf16),
        compiler_params=params(),
        cost_estimate=cost(0, 4 * LANES),
        name="back_tokens",
    )(rank)


def hold(values):
    def kernel(in_ref, out_ref):
        out_ref[...] = in_ref[...]

    return pl.pallas_call(
        kernel,
        out_shape=jax.ShapeDtypeStruct(values.shape, values.dtype),
        compiler_params=params(),
        cost_estimate=cost(2e10, 4 * LANES),
        name="hold",
    )(values)


def picks(rank, at, rows):
    places = lax.broadcasted_iota(jnp.int32, (rows, rank.shape[1]), 0) + at
    return jnp.where(places.astype(f32) == rank, 1.0, 0.0).astype(bf16)


def place_kernel(slots, parts, start, rank_ref, *refs):
    frame_refs, refs = refs[: len(slots) * parts], refs[len(slots) * parts :]
    base_refs, (x_ref, normed) = refs[:-2], refs[-2:]
    tokens = rank_ref.shape[1]
    count = normed.shape[1]
    step = 256
    for i in range(len(slots)):
        at = 0
        for ref in frame_refs[i * parts : (i + 1) * parts]:
            rows = ref.shape[0]
            normalise(ref, normed.at[i], at)
            at += rows
    for at in range(0, tokens, step):
        pick = picks(rank_ref[:, start : start + count], at, step)
        for i, slot in enumerate(slots):
            placed = jnp.dot(pick, normed[i], preferred_element_type=f32).astype(bf16)
            for base in base_refs:
                placed = base[slot * tokens + at : slot * tokens + at + step, :] + placed
            x_ref[i * tokens + at : i * tokens + at + step, :] = placed


def place_tokens(slots, rank, start, frames, base):
    tokens = rank.shape[1]
    width = frames[0].shape[1]
    parts = len(frames) // len(slots)
    count = parts * frames[0].shape[0]
    return pl.pallas_call(
        functools.partial(place_kernel, slots, parts, start),
        out_shape=jax.ShapeDtypeStruct((len(slots) * tokens, width), bf16),
        scratch_shapes=[pltpu.VMEM((len(slots), count, width), bf16)],
        compiler_params=params(),
        cost_estimate=cost(0, 4 * tokens),
        name="place_tokens",
    )(rank, *frames, *base)


def project_kernel(plan, *refs):
    x_refs, refs = refs[: plan.merge], refs[plan.merge :]
    w_refs, (v_ref, b_ref, rest_ref, w, turned) = refs[:-5], refs[-5:]
    tokens, width = x_refs[0].shape
    step = 256
    cols = plan.pairs * LANES
    if len(w_refs) > 1:
        w[...] = jnp.zeros_like(w)
        turned[...] = jnp.zeros_like(turned)
    for ref, rows in plan.places(w_refs):
        w[rows, :] = ref[:, :cols]
        turned[rows, :] = ref[:, cols : 2 * cols]
    maps = jnp.concatenate(
        [
            turned[at : at + LANES, :].astype(f32).T.astype(bf16)
            for at in range(0, turned.shape[0], LANES)
        ],
        axis=1,
    )
    count = rest_ref.shape[1]
    there = plan.last_chip() * count
    for s, x_ref in enumerate(x_refs):
        for at in range(0, tokens, step):
            rows = slice(s * tokens + at, s * tokens + at + step)
            x = x_ref[at : at + step, :]
            v_ref[rows, :] = jnp.dot(x, w[...], preferred_element_type=f32)
            b_ref[:, rows] = lax.dot_general(
                maps, x, (((1,), (1,)), ((), ())), preferred_element_type=f32
            )
            rest = x[:, :count]
            for c in range(count, width, count):
                rest = jnp.where(there == c, x[:, c : c + count], rest)
            rest_ref[rows, :] = rest


def project(plan, x, weights):
    every, width = x[0].shape[0] * plan.merge, x[0].shape[1]
    cols = plan.pairs * LANES
    count = max(LANES, width // plan.chips)
    return pl.pallas_call(
        functools.partial(project_kernel, plan),
        out_shape=(
            jax.ShapeDtypeStruct((every, cols), f32),
            jax.ShapeDtypeStruct((cols, every), f32),
            jax.ShapeDtypeStruct((every, count), bf16),
        ),
        scratch_shapes=[pltpu.VMEM((width, cols), bf16), pltpu.VMEM((width, cols), bf16)],
        compiler_params=params(),
        cost_estimate=cost(0, 4 * width),
        name="project",
    )(*x, *weights)


def update_kernel(plan, groups, decay_ref, *refs):
    v_ref, b_ref, x_ref, last_refs, (left, total_out, total_ref, u, sems) = (
        refs[0], refs[1], refs[2], refs[3:-5], refs[-5:]
    )
    copies = Copies(sems)
    leaving = []
    every = v_ref.shape[0]
    tokens = every // plan.merge
    block = tokens // groups
    step = 256
    here = step // block
    cols = plan.pairs * LANES
    if last_refs:
        w = jnp.concatenate([ref[:, : 2 * cols] for ref in last_refs], axis=0)
        maps = w[:, cols:].astype(f32).T.astype(bf16)
        w = w[:, :cols]

    lane = lax.div(lax.broadcasted_iota(jnp.int32, (LANES, step), 1), block)
    for at in range(0, every, step):
        there = slice(at, at + step)
        values, b = v_ref[there, :], b_ref[:, there]
        if last_refs:
            x = x_ref[there, :]
            values = values + jnp.dot(x, w, preferred_element_type=f32)
            b = b + lax.dot_general(
                maps, x, (((1,), (1,)), ((), ())), preferred_element_type=f32
            )
        values = values.astype(bf16)
        for p in range(plan.pairs):
            mine = b[p * LANES : (p + 1) * LANES]
            wide = jnp.concatenate(
                [jnp.where(lane == i, mine, 0.0).astype(bf16) for i in range(here)], axis=0
            )
            outer = jnp.dot(
                wide, values[:, p * LANES : (p + 1) * LANES], preferred_element_type=f32
            )
            for i in range(here):
                m = outer[i * 2 * N : (i + 1) * 2 * N]
                row = ((at % tokens // block + i) * plan.pairs + p) * N
                u[at // tokens, row : row + N, :] = halves((N, LANES), m[:N], m[N:])

    peers = total_ref.shape[0]
    share = u.shape[1] // peers
    items = max(1, share // N)
    size = min(N, share)
    first = plan.core() == 0
    for d in range(peers):
        for i in range(items):
            row = d * share + i * N
            rows = slice(row, row + size)
            item = slice(row // N, row // N + 1)
            last, product = decay_ref[0, item, :], decay_ref[1, item, :]
            if plan.merge == 2:
                one, two = u[0, rows, :], u[1, rows, :]
                one, two = (
                    one + jnp.where(first, 0.0, last) * two,
                    two + jnp.where(first, last, 0.0) * one,
                )
                left[0, rows, :] = one.astype(bf16)
                left[1, rows, :] = two.astype(bf16)
                total = jnp.where(first, two, one)
            else:
                total = u[0, rows, :]
                left[0, rows, :] = total.astype(bf16)
            total_ref[d, i * size : (i + 1) * size, :] = total.astype(bf16)
            for n in range(3):
                piece = product.astype(bf16)
                at = share + n * items + i
                total_ref[d, at : at + 1, :] = piece
                product = product - piece.astype(f32)
        if (d + 1) % (peers // 4) == 0:
            done = slice(d + 1 - peers // 4, d + 1)
            leaving.append(copies.start(total_ref.at[done], total_out.at[done]))
    finish(leaving)


def share_rows(share):
    return share + 16 * -(-3 * max(1, share // N) // 16)


def block_updates(plan, decays, v, b, x, last, groups):
    every, cols = v.shape
    rows = plan.pairs * groups * N
    share = rows // plan.chips
    return pl.pallas_call(
        functools.partial(update_kernel, plan, groups),
        in_specs=[vmem] * (4 + len(last)),
        out_specs=(vmem, hbm),
        out_shape=(
            jax.ShapeDtypeStruct((plan.merge, rows, LANES), bf16),
            jax.ShapeDtypeStruct((plan.chips, share_rows(share), LANES), bf16),
        ),
        scratch_shapes=[
            pltpu.VMEM((plan.chips, share_rows(share), LANES), bf16),
            pltpu.VMEM((plan.merge, rows, LANES), f32),
            Copies.scratch(),
        ],
        compiler_params=params(),
        cost_estimate=cost(4 * every * 256 * 2 * cols, 6 * every * cols),
        name="block_updates",
    )(decays, v, b, x, *last)


def decay_kernel(plan, groups, *refs):
    rate_refs, out_ref = refs[:-1], refs[-1]
    first = plan.core() == 0
    for g in range(groups):
        for p in range(plan.pairs):
            row = slice(g * plan.pairs + p, g * plan.pairs + p + 1)
            slots = [plan.decay(rate_refs, s, p, g) for s in range(plan.merge)]
            together, last = slots[0], slots[0]
            if plan.merge == 2:
                together = slots[0] * slots[1]
                last = jnp.where(first, slots[1], slots[0])
                slots = [
                    jnp.where(first, slots[0], together),
                    jnp.where(first, together, slots[1]),
                ]
            for i, value in enumerate([last, together] + slots):
                out_ref[i, row, :] = value


def decay_tables(plan, rates, groups):
    return pl.pallas_call(
        functools.partial(decay_kernel, plan, groups),
        in_specs=[smem] * plan.merge,
        out_shape=jax.ShapeDtypeStruct((2 + plan.merge, plan.pairs * groups, LANES), f32),
        compiler_params=params(),
        cost_estimate=cost(0, 4 * LANES),
        name="decay_tables",
    )(*rates)


def scan_kernel(plan, u_ref, s_ref):
    share = s_ref.shape[1]
    size = min(share, N)
    items = share // size
    for i in range(items):
        at = slice(i * size, (i + 1) * size)
        state = jnp.zeros((size, LANES), f32)
        for j in range(plan.chips):
            s_ref[j, at, :] = state.astype(bf16)
            decay = jnp.zeros((1, LANES), f32)
            for n in range(3):
                row = share + n * items + i
                decay = decay + u_ref[j, row : row + 1, :].astype(f32)
            state = decay * state + u_ref[j, at, :].astype(f32)


def scan_states(plan, update, share):
    return pl.pallas_call(
        functools.partial(scan_kernel, plan),
        out_shape=jax.ShapeDtypeStruct((plan.chips, share, LANES), bf16),
        compiler_params=params(),
        cost_estimate=cost(2 * update.size, 4 * update.size),
        name="scan_states",
    )(update)


def attend_kernel(plan, slot, *refs):
    lists_ref, x_in, local_in, refs = refs[0], refs[1], refs[2], refs[3:]
    w_refs, refs = refs[:-12], refs[-12:]
    a_out, c_out, x, local, w, q_ref, k_ref, wide_v, e_ref, a, c_ref, sems = refs
    copies = Copies(sems)
    tokens = x.shape[0]
    groups, chosen = lists_ref.shape
    block = tokens // groups
    step = 256
    per = step // block
    wide = plan.pairs * LANES

    weights = []
    for ref, rows in plan.places(w_refs):
        weights.append(copies.start(ref.at[:, :wide], w.at[rows, :wide]))
        weights.append(copies.start(ref.at[:, 2 * wide :], w.at[rows, wide:]))
    arriving = []
    for at in range(0, tokens, step):
        arriving.append(copies.start(x_in.at[at : at + step], x.at[at : at + step]))
    later = copies.start(local_in.at[slot], local)

    same = lax.div(lax.broadcasted_iota(jnp.int32, (2 * LANES, 2 * LANES), 0), HD) == lax.div(
        lax.broadcasted_iota(jnp.int32, (2 * LANES, 2 * LANES), 1), HD
    )
    same = jnp.where(same, 1.0, 0.0).astype(bf16)

    def head_norm(values):
        square = values * values
        high = square.astype(bf16)
        low = (square - high.astype(f32)).astype(bf16)
        total = jnp.dot(high, same, preferred_element_type=f32)
        total = total + jnp.dot(low, same, preferred_element_type=f32)
        return values * lax.rsqrt(total * (1.0 / HD) + epsilon)

    half = first_half((step, LANES))
    finish(weights)
    for at in range(0, tokens, step):
        rows = slice(at, at + step)
        arriving[at // step].wait()
        every = jnp.dot(x[rows, :], w[...], preferred_element_type=f32).astype(bf16)
        for p in range(plan.pairs):
            cols = slice(p * LANES, (p + 1) * LANES)
            wide_v[p, rows, :LANES] = every[:, cols]
            first = wide + 3 * p * LANES
            c_ref[rows, cols] = every[:, first + 2 * LANES : first + 3 * LANES]
            both = head_norm(every[:, first : first + 2 * LANES].astype(f32))
            k_ref[p, rows, :] = both[:, LANES:].astype(bf16)
            q = both[:, :LANES]
            one = jnp.where(half, q, 0.0).astype(bf16)
            two = jnp.where(half, 0.0, q).astype(bf16)
            for i in range(per):
                part = slice(i * block, (i + 1) * block)
                q_ref[p, at // block + i] = jnp.concatenate([one[part], two[part]], axis=0)
    leaving = [copies.start(c_ref, c_out)]
    later.wait()
    for p in range(plan.pairs):
        wide_v[p, :, LANES:] = jnp.ones((tokens, LANES), bf16)

    scale = math.log2(math.e) / math.sqrt(HD)
    starts = [
        [pl.multiple_of(lists_ref[g, j] * block, block) for j in range(chosen)]
        for g in range(groups)
    ]
    for g in range(groups):
        for p in range(plan.pairs):
            keys = jnp.concatenate([k_ref[p, pl.ds(s, block), :] for s in starts[g]], axis=0)
            score = lax.dot_general(
                q_ref[p, g], keys, (((1,), (1,)), ((), ())), preferred_element_type=f32
            )
            e_ref[p, g] = jnp.exp2(score * scale).astype(bf16)
    for g in range(groups):
        rows = slice(g * block, (g + 1) * block)
        for p in range(plan.pairs):
            cols = slice(p * LANES, (p + 1) * LANES)
            values = jnp.concatenate([wide_v[p, pl.ds(s, block), :] for s in starts[g]], axis=0)
            both = jnp.dot(e_ref[p, g], values, preferred_element_type=f32)
            both = both[:, :LANES] / both[:, LANES:]
            a[rows, cols] = halves((block, LANES), both[:block], both[block:])
    for g in range(groups):
        rows = slice(g * block, (g + 1) * block)
        for p in range(plan.pairs):
            cols = slice(p * LANES, (p + 1) * LANES)
            items = slice((g * plan.pairs + p) * N, (g * plan.pairs + p + 1) * N)
            a[rows, cols] = a[rows, cols] + read_out(
                c_ref[rows, cols], local[items, :].astype(f32), block
            )
        if (g + 1) % per == 0:
            done = slice((g + 1 - per) * block, (g + 1) * block)
            leaving.append(copies.start(a.at[done], a_out.at[done]))
    finish(leaving)


def attend(plan, slot, lists, x, weights, local):
    tokens, width = x.shape
    every = tokens * plan.merge
    groups, chosen = lists.shape
    block = tokens // groups
    cols = plan.pairs * LANES
    return pl.pallas_call(
        functools.partial(attend_kernel, plan, slot),
        in_specs=[smem] + [hbm] * (2 + len(weights)),
        out_specs=(hbm,) * 2,
        scratch_shapes=[
            pltpu.VMEM((tokens, width), bf16),
            pltpu.VMEM(local.shape[1:], bf16),
            pltpu.VMEM((width, 4 * cols), bf16),
            pltpu.VMEM((plan.pairs, groups, 2 * block, LANES), bf16),
            pltpu.VMEM((plan.pairs, tokens, LANES), bf16),
            pltpu.VMEM((plan.pairs, tokens, 2 * LANES), bf16),
            pltpu.VMEM((plan.pairs, groups, 2 * block, chosen * block), bf16),
            pltpu.VMEM((tokens, cols), f32),
            pltpu.VMEM((tokens, cols), bf16),
            Copies.scratch(),
        ],
        out_shape=(
            jax.ShapeDtypeStruct((tokens, cols), f32),
            jax.ShapeDtypeStruct((tokens, cols), bf16),
        ),
        compiler_params=params(60),
        cost_estimate=cost(
            6 * tokens * width * 3 * cols,
            4 * (tokens * width + 5 * width * cols + local.size),
            2 * plan.pairs * tokens * chosen * block,
        ),
        name="attend",
    )(lists, x, local, *weights)


def read_out(readers, state, block):
    half = first_half(state.shape)
    wide = jnp.concatenate([jnp.where(half, state, 0.0), jnp.where(half, 0.0, state)], axis=0)
    return jnp.dot(readers, wide.astype(bf16), preferred_element_type=f32) * (
        1.0 / (N * math.sqrt(block))
    )


def mix_kernel(plan, groups, decay_in, *refs):
    a_ins, refs = refs[: plan.merge], refs[plan.merge :]
    c_ins, refs = refs[: plan.merge], refs[plan.merge :]
    state, back_in, refs = refs[0], refs[1], refs[2:]
    out_refs, (decay, a, c, back, mixed, out, sems) = refs[:-7], refs[-7:]
    copies = Copies(sems)
    tokens = back.shape[0]
    block = tokens // groups
    width = a.shape[2]
    here = groups // 4

    arriving = []
    decaying = copies.start(decay_in, decay)
    for i in range(4):
        rows = slice(i * here * block, (i + 1) * here * block)
        arriving.append([])
        for s in range(plan.merge):
            arriving[-1] += [
                copies.start(c_ins[s].at[rows], c.at[s, rows, :]),
                copies.start(a_ins[s].at[rows], a.at[s, rows, :]),
            ]
    local = tokens // plan.peers
    order = list(range(1, plan.peers)) + [0]
    turning = []
    for k in order:
        rows = slice(k * local, (k + 1) * local)
        turning.append(copies.start(back_in.at[rows], back.at[rows]))

    decaying.wait()
    for g in range(groups):
        if g % here == 0:
            finish(arriving[g // here])
        rows = slice(g * block, (g + 1) * block)
        for p in range(plan.pairs):
            cols = slice(p * LANES, (p + 1) * LANES)
            at = (g * plan.pairs + p) * N
            readers = jnp.concatenate([c[s, rows, cols] for s in range(plan.merge)], axis=0)
            read = read_out(readers, state[at : at + N, :].astype(f32), block)
            item = slice(g * plan.pairs + p, g * plan.pairs + p + 1)
            for s in range(plan.merge):
                there = slice(s * width + p * LANES, s * width + (p + 1) * LANES)
                mixed[rows, there] = (
                    a[s, rows, cols]
                    + decay[2 + s, item, :] * read[s * block : (s + 1) * block]
                ).astype(bf16)

    leaving = []
    for k, turned in zip(order, turning):
        turned.wait()
        placed = jnp.dot(
            back[k * local : (k + 1) * local, :], mixed[...], preferred_element_type=f32
        ).astype(bf16)
        for s in range(plan.merge):
            i = s * plan.peers + k
            out[i] = placed[:, s * width : (s + 1) * width]
            leaving.append(copies.start(out.at[i], out_refs[i]))
    finish(leaving)


def mix(plan, decays, attended, readers, state, back, groups):
    tokens = back.shape[0]
    width = attended[0].shape[1]
    count = plan.merge * plan.peers
    return pl.pallas_call(
        functools.partial(mix_kernel, plan, groups),
        in_specs=[hbm] * (2 * plan.merge + 1) + [vmem, hbm],
        out_specs=(hbm,) * count,
        out_shape=(jax.ShapeDtypeStruct((tokens // plan.peers, width), bf16),) * count,
        scratch_shapes=[
            pltpu.VMEM(decays.shape, f32),
            pltpu.VMEM((plan.merge, tokens, width), f32),
            pltpu.VMEM((plan.merge, tokens, width), bf16),
            pltpu.VMEM(back.shape, bf16),
            pltpu.VMEM((tokens, plan.merge * width), bf16),
            pltpu.VMEM((count, tokens // plan.peers, width), bf16),
            Copies.scratch(),
        ],
        compiler_params=params(52),
        cost_estimate=cost(4 * tokens * tokens * width, 2 * tokens * tokens + 16 * tokens * width),
        name="mix",
    )(decays, *attended, *readers, state, back)


def out_kernel(plan, sources, w_ref, *refs):
    part_refs, base_refs, out_ref = refs[: len(sources)], refs[len(sources) : -3], refs[-3]
    kept, sems = refs[-2:]
    copies = Copies(sems)
    depth = part_refs[0].shape[1]
    core, me = plan.core(), lax.axis_index("head")
    owners = []
    for s, k in sources:
        owner = lax.rem(me - k + plan.peers, plan.peers) * plan.merge
        owners.append(owner + (core if s == 0 else 1 - core))
    leaving = []
    step = min(128, out_ref.shape[0])
    for at in range(0, out_ref.shape[0], step):
        there = slice(at, at + step)
        total = base_refs[0][there, :] if base_refs else 0.0
        for owner, part in zip(owners, part_refs):
            rows = pl.ds(pl.multiple_of(owner * depth, depth), depth)
            total = total + jnp.dot(part[there, :], w_ref[rows, :], preferred_element_type=f32)
        if base_refs:
            kept[there, :] = total.astype(out_ref.dtype)
            leaving.append(copies.start(kept.at[there], out_ref.at[there]))
        else:
            out_ref[there, :] = total.astype(out_ref.dtype)
    finish(leaving)


def project_out(plan, w, parts, base, kind):
    local, width = next(iter(parts.values())).shape[0], w.shape[1]
    return pl.pallas_call(
        functools.partial(out_kernel, plan, list(parts)),
        in_specs=[vmem] * (1 + len(parts) + len(base)),
        out_specs=hbm if base else vmem,
        out_shape=jax.ShapeDtypeStruct((local, width), kind),
        scratch_shapes=[pltpu.VMEM((local, width), kind), Copies.scratch()],
        compiler_params=params(),
        cost_estimate=cost(0, 4 * local),
        name="project_out",
    )(w, *parts.values(), *base)


def body(frames_in, in_weight, out_weight, block_ids, block_lists, decays):
    local_tokens = frames_in.shape[1]
    heads_here = decays.shape[1]
    groups = block_lists.shape[0]
    me = lax.axis_index("head")
    plan = Plan(lax.axis_size("tm"), lax.axis_size("head"), heads_here, frames_in.shape[2])

    own = frames_in[0]
    arriving = [plan.to_peer(own, plan.peers - k, False) for k in range(1, plan.peers)]
    owns = [own] + [plan.swap(own)] * (plan.merge - 1)
    rates = [decays[0]] + [plan.swap(decays[0])] * (plan.merge - 1)
    block = reorder(plan, in_weight)
    if plan.merge == 2:
        block = reorder(plan, plan.swap(in_weight), [block])
    ids = jnp.roll(block_ids, -me * local_tokens)
    ids, rates = lax.optimization_barrier((ids, rates))
    tables = decay_tables(plan, rates, groups)
    rank = rank_tokens(ids, groups)

    def fill(slot, arriving, part):
        if slot == 1:
            arriving = [plan.swap(tokens) for tokens in arriving]
        return place_tokens([slot], rank, local_tokens, arriving, [part])

    if plan.ringed:
        blocks, crossed = [block], []
        half = block.shape[0] // 2
        for k in range(plan.along - 1):
            with_ = ()
            if k == 0:
                places = back_tokens(rank)
                with_ = (places, tables)
            if k == min(1, plan.along - 2):
                rank, owns, _ = lax.optimization_barrier((rank, owns, blocks[-1]))
                part = with_ = place_tokens(list(range(plan.merge)), rank, 0, owns, [])
            if k == plan.along - 2:
                arriving, _ = lax.optimization_barrier((arriving, blocks[-1]))
                x = [fill(s, arriving, part) for s in range(plan.merge)]
            passed, across, with_ = lax.optimization_barrier(
                (plan.round(blocks[-1]), plan.cross(blocks[-1]), with_)
            )
            if k == plan.along - 2:
                tables, passed, across, x[0] = lax.optimization_barrier(
                    (tables, passed, across, x[0])
                )
                tables, passed, across = lax.optimization_barrier(
                    (hold(tables), passed, across)
                )
            blocks.append(passed)
            crossed.append(across)
        last = [plan.cross(blocks[-1][:half]), plan.round(crossed[-1][half:])]
        weights = blocks + crossed + last
    else:
        weights = [
            lax.all_gather(block, "tm", axis=0, tiled=True, axis_index_groups=plan.groups())
        ]
        places = back_tokens(rank)
        part = place_tokens(list(range(plan.merge)), rank, 0, owns, [])
        x = [fill(s, arriving, part) for s in range(plan.merge)]
    if plan.ringed:
        v, b, x_last = project(plan, x, weights[:-2])
        local, total = block_updates(plan, tables, v, b, x_last, last, groups)
    else:
        v, b, x_last = project(plan, x, weights)
        local, total = block_updates(plan, tables, v, b, x_last, [], groups)

    def exchange(blocks):
        return lax.all_to_all(
            blocks, "tm", split_axis=0, concat_axis=0, tiled=True,
            axis_index_groups=plan.groups(),
        )

    share = local.shape[1] // plan.chips
    arrived = exchange(total)
    attended = [attend(plan, 0, block_lists, x[0], weights, local)]
    arrived, attended = lax.optimization_barrier((arrived, attended))
    states = scan_states(plan, arrived, share)
    x, states = lax.optimization_barrier((x, states))
    if plan.merge == 2:
        attended.append(attend(plan, 1, block_lists, x[1], weights, local))
    state = exchange(states).reshape(-1, LANES)

    bases, readers = ([a[i] for a in attended] for i in range(2))
    mixed = mix(plan, tables, bases, readers, state, places, groups)
    moved = {
        (s, k): plan.to_peer(mixed[s * plan.peers + k], k, s == 1)
        for s in range(plan.merge)
        for k in range(1, plan.peers)
    }
    near = {(0, 0): mixed[0]}
    if plan.merge == 2:
        near[1, 0] = plan.swap(mixed[plan.peers])
    result = project_out(plan, out_weight, near, [], f32)
    last = {key: moved.pop(key) for key in list(moved)[-1:]}
    if moved:
        result = project_out(plan, out_weight, moved, [result], f32)
    return project_out(plan, out_weight, last, [result], bf16)[None]


def solution(mesh):
    return jax.shard_map(
        body,
        mesh=mesh,
        in_specs=(P("tm", "head", None), P("tm", "head"), P(), P(), P(), P("tm", "head", None)),
        out_specs=P("tm", "head", None),
        check_vma=False,
    )
```

```python
import functools
import math

import jax
import jax.numpy as jnp
from jax import lax
from jax.experimental import pallas as pl
from jax.experimental.pallas import tpu as pltpu
from jax.sharding import PartitionSpec as P

HD = 64
N = 64
LANES = 2 * HD
PIECES = 5
EARLY = (2, 3)
LATE = (0, 1, 4)

epsilon = 1e-06

vmem = pl.BlockSpec(memory_space=pltpu.VMEM)
smem = pl.BlockSpec(memory_space=pltpu.SMEM)

hbm = pl.BlockSpec(memory_space=pltpu.HBM)

f32 = jnp.float32
bf16 = jnp.bfloat16


def params(mib=16):
    return pltpu.CompilerParams(vmem_limit_bytes=mib << 20)


def cost(flops, nbytes, transcendentals=0):
    return pl.CostEstimate(
        flops=int(flops), bytes_accessed=int(nbytes), transcendentals=int(transcendentals)
    )


def first_half(shape):
    return lax.broadcasted_iota(jnp.int32, shape, len(shape) - 1) < HD


class Plan:
    def __init__(self, frames, peers, heads_here, width):
        self.merge = 2 if frames % 2 == 0 and heads_here % 4 == 0 else 1
        self.frames, self.peers = frames, peers
        self.heads = heads_here // self.merge
        self.pairs = self.heads // 2
        self.chips = frames // self.merge
        self.across = 2 if self.chips % 2 == 0 else 1
        self.along = self.chips // self.across
        self.ringed = self.across == 2 and 2 <= self.along <= 8 and width % (self.chips * LANES) == 0

    def core(self):
        return lax.rem(lax.axis_index("tm"), self.merge)

    def chip(self):
        return lax.div(lax.axis_index("tm"), self.merge)

    def swap(self, block):
        return lax.ppermute(block, "tm", [(t, t ^ 1) for t in range(self.frames)])

    def round(self, block):
        a, b, c = self.along, self.across, self.merge
        pairs = [(t, (t + b * c) % (a * b * c)) for t in range(self.frames)]
        return lax.ppermute(block, "tm", pairs)

    def cross(self, block):
        c = self.merge
        pairs = [(t, (t // c ^ 1) * c + t % c) for t in range(self.frames)]
        return lax.ppermute(block, "tm", pairs)

    def last_chip(self):
        a, b = lax.div(self.chip(), self.across), lax.rem(self.chip(), self.across)
        return lax.rem(a + 1, self.along) * self.across + (self.across - 1 - b)

    def places(self, refs):
        if len(refs) == 1:
            return [(refs[0], slice(None))]
        rows = refs[0].shape[0]
        a, b = lax.div(self.chip(), self.across), lax.rem(self.chip(), self.across)
        n = self.along
        made = []
        for i, ref in enumerate(refs):
            k, flip = (i, 0) if i < n else (min(i - n, n - 1), 1)
            there = lax.rem(a - k + n, n) * self.across
            at = (there + (1 - b if flip else b)) * rows
            at = at + (rows // 2 if i == 2 * n else 0)
            made.append((ref, pl.ds(pl.multiple_of(at, rows // 2), ref.shape[0])))
        return made

    def to_peer(self, block, k, other):
        if not other:
            pairs = [(j, (j + k) % self.peers) for j in range(self.peers)]
            return lax.ppermute(block, "head", pairs)
        if k == 0:
            return self.swap(block)
        pairs = [
            (t * self.peers + j, (t ^ 1) * self.peers + (j + k) % self.peers)
            for t in range(self.frames)
            for j in range(self.peers)
        ]
        return lax.ppermute(block, ("tm", "head"), pairs)

    def groups(self):
        if self.merge == 1:
            return None
        return [[j * self.merge + c for j in range(self.chips)] for c in range(self.merge)]

    def decay(self, refs, slot, pair, g):
        head = self.core() * self.heads + 2 * pair
        return halves((1, LANES), refs[slot][head, g], refs[slot][head + 1, g])


class Copies:
    room = 48

    def __init__(self, sems):
        self.sems, self.count = sems, 0

    def start(self, src, dst):
        copy = pltpu.make_async_copy(src, dst, self.sems.at[self.count])
        copy.start()
        self.count += 1
        return copy

    @staticmethod
    def scratch():
        return pltpu.SemaphoreType.DMA((Copies.room,))


def finish(copies):
    for copy in copies:
        copy.wait()


def halves(shape, one, two):
    return jnp.where(first_half(shape), one, two)


def reorder_kernel(plan, *refs):
    w_ref, out_ref = refs[0], refs[-1]
    rows = w_ref.shape[0]
    width = plan.heads * PIECES * HD
    first = plan.core() == 0

    def chosen(at):
        one = w_ref[:, at : at + HD]
        if plan.merge == 1:
            return one
        return jnp.where(first, one, w_ref[:, width + at : width + at + HD])

    order = [(p, i) for i in EARLY for p in range(plan.pairs)]
    order += [(p, i) for p in range(plan.pairs) for i in LATE]
    for n, (p, i) in enumerate(order):
        block = jnp.concatenate(
            [chosen(((2 * p + h) * PIECES + i) * HD) for h in range(2)], axis=1
        )
        cols = slice(n * LANES, (n + 1) * LANES)
        if len(refs) == 2:
            out_ref[:, cols] = block
        else:
            mine = refs[1][:, cols]
            out_ref[:rows, cols] = jnp.where(first, mine, block)
            out_ref[rows:, cols] = jnp.where(first, block, mine)


def reorder(plan, w, mine=()):
    rows = w.shape[0] * (1 + len(mine))
    return pl.pallas_call(
        functools.partial(reorder_kernel, plan),
        out_shape=jax.ShapeDtypeStruct((rows, plan.heads * PIECES * HD), bf16),
        compiler_params=params(),
        cost_estimate=cost(0, 4 * rows),
        name="reorder",
    )(w, *mine)


def normalise(part, out, at):
    step = min(128, part.shape[0])

    def norm(c, _):
        start = pl.multiple_of(c * step, step)
        wide = part[pl.ds(start, step), :].astype(f32)
        scale = lax.rsqrt(jnp.mean(wide * wide, axis=-1, keepdims=True) + epsilon)
        out[pl.ds(at + start, step), :] = (wide * scale).astype(bf16)
        return 0

    lax.fori_loop(0, part.shape[0] // step, norm, 0)


def rank_kernel(groups, ids_ref, row_ref):
    tokens = ids_ref.shape[1]
    block = tokens // groups
    label = lax.broadcasted_iota(jnp.int32, (groups, tokens), 0)
    held = label == ids_ref[...]
    held_bf = jnp.where(held, 1.0, 0.0).astype(bf16)
    counts = []
    for c in range(tokens // 256):
        before = lax.broadcasted_iota(jnp.int32, (tokens, 256), 0) < (
            lax.broadcasted_iota(jnp.int32, (tokens, 256), 1) + c * 256
        )
        counts.append(
            jnp.dot(held_bf, jnp.where(before, 1.0, 0.0).astype(bf16), preferred_element_type=f32)
        )
    count = jnp.concatenate(counts, axis=1)
    row_ref[...] = jnp.sum(
        jnp.where(held, count + (label * block).astype(f32), 0.0), axis=0, keepdims=True
    )


def rank_tokens(ids, groups):
    tokens = ids.shape[0]
    return pl.pallas_call(
        functools.partial(rank_kernel, groups),
        out_shape=jax.ShapeDtypeStruct((1, tokens), f32),
        compiler_params=params(),
        cost_estimate=cost(0, 4 * tokens),
        name="rank_tokens",
    )(ids.reshape(1, tokens))


def back_kernel(row_ref, back_ref):
    tokens = back_ref.shape[0]
    lane = lax.broadcasted_iota(jnp.int32, (LANES, LANES), 1)
    for at in range(0, tokens, LANES):
        place = jnp.broadcast_to(row_ref[:, at : at + LANES], (LANES, LANES)).T
        for t in range(0, tokens, LANES):
            back_ref[at : at + LANES, t : t + LANES] = jnp.where(
                (lane + t).astype(f32) == place, 1.0, 0.0
            ).astype(bf16)


def back_tokens(rank):
    return pl.pallas_call(
        back_kernel,
        out_shape=jax.ShapeDtypeStruct((rank.shape[1], rank.shape[1]), bf16),
        compiler_params=params(),
        cost_estimate=cost(0, 4 * LANES),
        name="back_tokens",
    )(rank)


def hold(values):
    def kernel(in_ref, out_ref):
        out_ref[...] = in_ref[...]

    return pl.pallas_call(
        kernel,
        out_shape=jax.ShapeDtypeStruct(values.shape, values.dtype),
        compiler_params=params(),
        cost_estimate=cost(2e10, 4 * LANES),
        name="hold",
    )(values)


def picks(rank, at, rows):
    places = lax.broadcasted_iota(jnp.int32, (rows, rank.shape[1]), 0) + at
    return jnp.where(places.astype(f32) == rank, 1.0, 0.0).astype(bf16)


def place_kernel(slots, parts, start, rank_ref, *refs):
    frame_refs, refs = refs[: len(slots) * parts], refs[len(slots) * parts :]
    base_refs, (x_ref, normed) = refs[:-2], refs[-2:]
    tokens = rank_ref.shape[1]
    count = normed.shape[1]
    step = 256
    for i in range(len(slots)):
        at = 0
        for ref in frame_refs[i * parts : (i + 1) * parts]:
            rows = ref.shape[0]
            normalise(ref, normed.at[i], at)
            at += rows
    for at in range(0, tokens, step):
        pick = picks(rank_ref[:, start : start + count], at, step)
        for i, slot in enumerate(slots):
            placed = jnp.dot(pick, normed[i], preferred_element_type=f32).astype(bf16)
            for base in base_refs:
                placed = base[slot * tokens + at : slot * tokens + at + step, :] + placed
            x_ref[i * tokens + at : i * tokens + at + step, :] = placed


def place_tokens(slots, rank, start, frames, base):
    tokens = rank.shape[1]
    width = frames[0].shape[1]
    parts = len(frames) // len(slots)
    count = parts * frames[0].shape[0]
    return pl.pallas_call(
        functools.partial(place_kernel, slots, parts, start),
        out_shape=jax.ShapeDtypeStruct((len(slots) * tokens, width), bf16),
        scratch_shapes=[pltpu.VMEM((len(slots), count, width), bf16)],
        compiler_params=params(),
        cost_estimate=cost(0, 4 * tokens),
        name="place_tokens",
    )(rank, *frames, *base)


def project_kernel(plan, *refs):
    x_refs, refs = refs[: plan.merge], refs[plan.merge :]
    w_refs, (v_ref, b_ref, rest_ref, w, turned) = refs[:-5], refs[-5:]
    tokens, width = x_refs[0].shape
    step = 256
    cols = plan.pairs * LANES
    if len(w_refs) > 1:
        w[...] = jnp.zeros_like(w)
        turned[...] = jnp.zeros_like(turned)
    for ref, rows in plan.places(w_refs):
        w[rows, :] = ref[:, :cols]
        turned[rows, :] = ref[:, cols : 2 * cols]
    maps = jnp.concatenate(
        [
            turned[at : at + LANES, :].astype(f32).T.astype(bf16)
            for at in range(0, turned.shape[0], LANES)
        ],
        axis=1,
    )
    count = rest_ref.shape[1]
    there = plan.last_chip() * count
    for s, x_ref in enumerate(x_refs):
        for at in range(0, tokens, step):
            rows = slice(s * tokens + at, s * tokens + at + step)
            x = x_ref[at : at + step, :]
            v_ref[rows, :] = jnp.dot(x, w[...], preferred_element_type=f32)
            b_ref[:, rows] = lax.dot_general(
                maps, x, (((1,), (1,)), ((), ())), preferred_element_type=f32
            )
    for s, x_ref in enumerate(x_refs):
        for at in range(0, tokens, step):
            here = slice(at, at + step)
            rest = x_ref[here, :count]
            for c in range(count, width, count):
                rest = jnp.where(there == c, x_ref[here, c : c + count], rest)
            rest_ref[s * tokens + at : s * tokens + at + step, :] = rest


def project(plan, x, weights):
    every, width = x[0].shape[0] * plan.merge, x[0].shape[1]
    cols = plan.pairs * LANES
    count = max(LANES, width // plan.chips)
    return pl.pallas_call(
        functools.partial(project_kernel, plan),
        out_shape=(
            jax.ShapeDtypeStruct((every, cols), f32),
            jax.ShapeDtypeStruct((cols, every), f32),
            jax.ShapeDtypeStruct((every, count), bf16),
        ),
        scratch_shapes=[pltpu.VMEM((width, cols), bf16), pltpu.VMEM((width, cols), bf16)],
        compiler_params=params(),
        cost_estimate=cost(0, 4 * width),
        name="project",
    )(*x, *weights)


def update_kernel(plan, groups, decay_ref, *refs):
    v_ref, b_ref, x_ref, last_refs, (left, total_out, total_ref, u, sems) = (
        refs[0], refs[1], refs[2], refs[3:-5], refs[-5:]
    )
    copies = Copies(sems)
    leaving = []
    every = v_ref.shape[0]
    tokens = every // plan.merge
    block = tokens // groups
    step = 256
    here = step // block
    cols = plan.pairs * LANES
    if last_refs:
        w = jnp.concatenate([ref[:, : 2 * cols] for ref in last_refs], axis=0)
        maps = w[:, cols:].astype(f32).T.astype(bf16)
        w = w[:, :cols]

    lane = lax.div(lax.broadcasted_iota(jnp.int32, (LANES, step), 1), block)
    for at in range(0, every, step):
        there = slice(at, at + step)
        values, b = v_ref[there, :], b_ref[:, there]
        if last_refs:
            x = x_ref[there, :]
            values = values + jnp.dot(x, w, preferred_element_type=f32)
            b = b + lax.dot_general(
                maps, x, (((1,), (1,)), ((), ())), preferred_element_type=f32
            )
        values = values.astype(bf16)
        for p in range(plan.pairs):
            mine = b[p * LANES : (p + 1) * LANES]
            wide = jnp.concatenate(
                [jnp.where(lane == i, mine, 0.0).astype(bf16) for i in range(here)], axis=0
            )
            outer = jnp.dot(
                wide, values[:, p * LANES : (p + 1) * LANES], preferred_element_type=f32
            )
            for i in range(here):
                m = outer[i * 2 * N : (i + 1) * 2 * N]
                row = ((at % tokens // block + i) * plan.pairs + p) * N
                u[at // tokens, row : row + N, :] = halves((N, LANES), m[:N], m[N:])

    peers = total_ref.shape[0]
    share = u.shape[1] // peers
    items = max(1, share // N)
    size = min(N, share)
    first = plan.core() == 0
    for d in range(peers):
        for i in range(items):
            row = d * share + i * N
            rows = slice(row, row + size)
            item = slice(row // N, row // N + 1)
            last, product = decay_ref[0, item, :], decay_ref[1, item, :]
            if plan.merge == 2:
                one, two = u[0, rows, :], u[1, rows, :]
                one, two = (
                    one + jnp.where(first, 0.0, last) * two,
                    two + jnp.where(first, last, 0.0) * one,
                )
                left[0, rows, :] = one.astype(bf16)
                left[1, rows, :] = two.astype(bf16)
                total = jnp.where(first, two, one)
            else:
                total = u[0, rows, :]
                left[0, rows, :] = total.astype(bf16)
            total_ref[d, i * size : (i + 1) * size, :] = total.astype(bf16)
            for n in range(3):
                piece = product.astype(bf16)
                at = share + n * items + i
                total_ref[d, at : at + 1, :] = piece
                product = product - piece.astype(f32)
        if (d + 1) % (peers // 4) == 0:
            done = slice(d + 1 - peers // 4, d + 1)
            leaving.append(copies.start(total_ref.at[done], total_out.at[done]))
    finish(leaving)


def share_rows(share):
    return share + 16 * -(-3 * max(1, share // N) // 16)


def block_updates(plan, decays, v, b, x, last, groups):
    every, cols = v.shape
    rows = plan.pairs * groups * N
    share = rows // plan.chips
    return pl.pallas_call(
        functools.partial(update_kernel, plan, groups),
        in_specs=[vmem] * (4 + len(last)),
        out_specs=(vmem, hbm),
        out_shape=(
            jax.ShapeDtypeStruct((plan.merge, rows, LANES), bf16),
            jax.ShapeDtypeStruct((plan.chips, share_rows(share), LANES), bf16),
        ),
        scratch_shapes=[
            pltpu.VMEM((plan.chips, share_rows(share), LANES), bf16),
            pltpu.VMEM((plan.merge, rows, LANES), f32),
            Copies.scratch(),
        ],
        compiler_params=params(),
        cost_estimate=cost(4 * every * 256 * 2 * cols, 6 * every * cols),
        name="block_updates",
    )(decays, v, b, x, *last)


def decay_kernel(plan, groups, *refs):
    rate_refs, out_ref = refs[:-1], refs[-1]
    first = plan.core() == 0
    for g in range(groups):
        for p in range(plan.pairs):
            row = slice(g * plan.pairs + p, g * plan.pairs + p + 1)
            slots = [plan.decay(rate_refs, s, p, g) for s in range(plan.merge)]
            together, last = slots[0], slots[0]
            if plan.merge == 2:
                together = slots[0] * slots[1]
                last = jnp.where(first, slots[1], slots[0])
                slots = [
                    jnp.where(first, slots[0], together),
                    jnp.where(first, together, slots[1]),
                ]
            for i, value in enumerate([last, together] + slots):
                out_ref[i, row, :] = value


def decay_tables(plan, rates, groups):
    return pl.pallas_call(
        functools.partial(decay_kernel, plan, groups),
        in_specs=[smem] * plan.merge,
        out_shape=jax.ShapeDtypeStruct((2 + plan.merge, plan.pairs * groups, LANES), f32),
        compiler_params=params(),
        cost_estimate=cost(0, 4 * LANES),
        name="decay_tables",
    )(*rates)


def scan_kernel(plan, u_ref, s_ref):
    share = s_ref.shape[1]
    size = min(share, N)
    items = share // size
    for i in range(items):
        at = slice(i * size, (i + 1) * size)
        state = jnp.zeros((size, LANES), f32)
        for j in range(plan.chips):
            s_ref[j, at, :] = state.astype(bf16)
            decay = jnp.zeros((1, LANES), f32)
            for n in range(3):
                row = share + n * items + i
                decay = decay + u_ref[j, row : row + 1, :].astype(f32)
            state = decay * state + u_ref[j, at, :].astype(f32)


def scan_states(plan, update, share):
    return pl.pallas_call(
        functools.partial(scan_kernel, plan),
        out_shape=jax.ShapeDtypeStruct((plan.chips, share, LANES), bf16),
        compiler_params=params(),
        cost_estimate=cost(2 * update.size, 4 * update.size),
        name="scan_states",
    )(update)


def attend_kernel(plan, slot, *refs):
    lists_ref, x_in, local_in, refs = refs[0], refs[1], refs[2], refs[3:]
    w_refs, refs = refs[:-12], refs[-12:]
    a_out, c_out, x, local, w, q_ref, k_ref, wide_v, e_ref, a, c_ref, sems = refs
    copies = Copies(sems)
    tokens = x.shape[0]
    groups, chosen = lists_ref.shape
    block = tokens // groups
    step = 256
    per = step // block
    wide = plan.pairs * LANES

    weights = []
    for ref, rows in plan.places(w_refs):
        weights.append(copies.start(ref.at[:, :wide], w.at[rows, :wide]))
        weights.append(copies.start(ref.at[:, 2 * wide :], w.at[rows, wide:]))
    arriving = []
    for at in range(0, tokens, step):
        arriving.append(copies.start(x_in.at[at : at + step], x.at[at : at + step]))
    later = copies.start(local_in.at[slot], local)

    same = lax.div(lax.broadcasted_iota(jnp.int32, (2 * LANES, 2 * LANES), 0), HD) == lax.div(
        lax.broadcasted_iota(jnp.int32, (2 * LANES, 2 * LANES), 1), HD
    )
    same = jnp.where(same, 1.0, 0.0).astype(bf16)

    def head_norm(values):
        square = values * values
        high = square.astype(bf16)
        low = (square - high.astype(f32)).astype(bf16)
        total = jnp.dot(high, same, preferred_element_type=f32)
        total = total + jnp.dot(low, same, preferred_element_type=f32)
        return values * lax.rsqrt(total * (1.0 / HD) + epsilon)

    half = first_half((step, LANES))
    finish(weights)
    for at in range(0, tokens, step):
        rows = slice(at, at + step)
        arriving[at // step].wait()
        every = jnp.dot(x[rows, :], w[...], preferred_element_type=f32).astype(bf16)
        for p in range(plan.pairs):
            cols = slice(p * LANES, (p + 1) * LANES)
            wide_v[p, rows, :LANES] = every[:, cols]
            first = wide + 3 * p * LANES
            c_ref[rows, cols] = every[:, first + 2 * LANES : first + 3 * LANES]
            both = head_norm(every[:, first : first + 2 * LANES].astype(f32))
            k_ref[p, rows, :] = both[:, LANES:].astype(bf16)
            q = both[:, :LANES]
            one = jnp.where(half, q, 0.0).astype(bf16)
            two = jnp.where(half, 0.0, q).astype(bf16)
            for i in range(per):
                part = slice(i * block, (i + 1) * block)
                q_ref[p, at // block + i] = jnp.concatenate([one[part], two[part]], axis=0)
    leaving = [copies.start(c_ref, c_out)]
    later.wait()
    for p in range(plan.pairs):
        wide_v[p, :, LANES:] = jnp.ones((tokens, LANES), bf16)

    scale = math.log2(math.e) / math.sqrt(HD)
    starts = [
        [pl.multiple_of(lists_ref[g, j] * block, block) for j in range(chosen)]
        for g in range(groups)
    ]
    for g in range(groups):
        for p in range(plan.pairs):
            keys = jnp.concatenate([k_ref[p, pl.ds(s, block), :] for s in starts[g]], axis=0)
            score = lax.dot_general(
                q_ref[p, g], keys, (((1,), (1,)), ((), ())), preferred_element_type=f32
            )
            e_ref[p, g] = jnp.exp2(score * scale).astype(bf16)
    for g in range(groups):
        rows = slice(g * block, (g + 1) * block)
        for p in range(plan.pairs):
            cols = slice(p * LANES, (p + 1) * LANES)
            values = jnp.concatenate([wide_v[p, pl.ds(s, block), :] for s in starts[g]], axis=0)
            both = jnp.dot(e_ref[p, g], values, preferred_element_type=f32)
            both = both[:, :LANES] / both[:, LANES:]
            a[rows, cols] = halves((block, LANES), both[:block], both[block:])
    for g in range(groups):
        rows = slice(g * block, (g + 1) * block)
        for p in range(plan.pairs):
            cols = slice(p * LANES, (p + 1) * LANES)
            items = slice((g * plan.pairs + p) * N, (g * plan.pairs + p + 1) * N)
            a[rows, cols] = a[rows, cols] + read_out(
                c_ref[rows, cols], local[items, :].astype(f32), block
            )
        if (g + 1) % per == 0:
            done = slice((g + 1 - per) * block, (g + 1) * block)
            leaving.append(copies.start(a.at[done], a_out.at[done]))
    finish(leaving)


def attend(plan, slot, lists, x, weights, local):
    tokens, width = x.shape
    every = tokens * plan.merge
    groups, chosen = lists.shape
    block = tokens // groups
    cols = plan.pairs * LANES
    return pl.pallas_call(
        functools.partial(attend_kernel, plan, slot),
        in_specs=[smem] + [hbm] * (2 + len(weights)),
        out_specs=(hbm,) * 2,
        scratch_shapes=[
            pltpu.VMEM((tokens, width), bf16),
            pltpu.VMEM(local.shape[1:], bf16),
            pltpu.VMEM((width, 4 * cols), bf16),
            pltpu.VMEM((plan.pairs, groups, 2 * block, LANES), bf16),
            pltpu.VMEM((plan.pairs, tokens, LANES), bf16),
            pltpu.VMEM((plan.pairs, tokens, 2 * LANES), bf16),
            pltpu.VMEM((plan.pairs, groups, 2 * block, chosen * block), bf16),
            pltpu.VMEM((tokens, cols), f32),
            pltpu.VMEM((tokens, cols), bf16),
            Copies.scratch(),
        ],
        out_shape=(
            jax.ShapeDtypeStruct((tokens, cols), f32),
            jax.ShapeDtypeStruct((tokens, cols), bf16),
        ),
        compiler_params=params(60),
        cost_estimate=cost(
            6 * tokens * width * 3 * cols,
            4 * (tokens * width + 5 * width * cols + local.size),
            2 * plan.pairs * tokens * chosen * block,
        ),
        name="attend",
    )(lists, x, local, *weights)


def read_out(readers, state, block):
    half = first_half(state.shape)
    wide = jnp.concatenate([jnp.where(half, state, 0.0), jnp.where(half, 0.0, state)], axis=0)
    return jnp.dot(readers, wide.astype(bf16), preferred_element_type=f32) * (
        1.0 / (N * math.sqrt(block))
    )


def mix_kernel(plan, groups, decay_in, *refs):
    a_ins, refs = refs[: plan.merge], refs[plan.merge :]
    c_ins, refs = refs[: plan.merge], refs[plan.merge :]
    s_in, back_in, refs = refs[0], refs[1], refs[2:]
    out_refs, (decay, a, c, state, back, mixed, out, sems) = refs[:-8], refs[-8:]
    copies = Copies(sems)
    tokens = back.shape[0]
    block = tokens // groups
    width = a.shape[2]
    here = groups // 4
    many = here * plan.pairs * N

    arriving = []
    decaying = copies.start(decay_in, decay)
    for i in range(4):
        rows = slice(i * here * block, (i + 1) * here * block)
        items = slice(i * many, (i + 1) * many)
        arriving.append([copies.start(s_in.at[items], state.at[items])])
        for s in range(plan.merge):
            arriving[-1] += [
                copies.start(c_ins[s].at[rows], c.at[s, rows, :]),
                copies.start(a_ins[s].at[rows], a.at[s, rows, :]),
            ]
    local = tokens // plan.peers
    order = list(range(1, plan.peers)) + [0]
    turning = []
    for k in order:
        rows = slice(k * local, (k + 1) * local)
        turning.append(copies.start(back_in.at[rows], back.at[rows]))

    decaying.wait()
    for g in range(groups):
        if g % here == 0:
            finish(arriving[g // here])
        rows = slice(g * block, (g + 1) * block)
        for p in range(plan.pairs):
            cols = slice(p * LANES, (p + 1) * LANES)
            at = (g * plan.pairs + p) * N
            readers = jnp.concatenate([c[s, rows, cols] for s in range(plan.merge)], axis=0)
            read = read_out(readers, state[at : at + N, :].astype(f32), block)
            item = slice(g * plan.pairs + p, g * plan.pairs + p + 1)
            for s in range(plan.merge):
                there = slice(s * width + p * LANES, s * width + (p + 1) * LANES)
                mixed[rows, there] = (
                    a[s, rows, cols]
                    + decay[2 + s, item, :] * read[s * block : (s + 1) * block]
                ).astype(bf16)

    leaving = []
    for k, turned in zip(order, turning):
        turned.wait()
        placed = jnp.dot(
            back[k * local : (k + 1) * local, :], mixed[...], preferred_element_type=f32
        ).astype(bf16)
        for s in range(plan.merge):
            i = s * plan.peers + k
            out[i] = placed[:, s * width : (s + 1) * width]
            leaving.append(copies.start(out.at[i], out_refs[i]))
    finish(leaving)


def mix(plan, decays, attended, readers, state, back, groups):
    tokens = back.shape[0]
    width = attended[0].shape[1]
    count = plan.merge * plan.peers
    return pl.pallas_call(
        functools.partial(mix_kernel, plan, groups),
        in_specs=[hbm] * (2 * plan.merge + 3),
        out_specs=(hbm,) * count,
        out_shape=(jax.ShapeDtypeStruct((tokens // plan.peers, width), bf16),) * count,
        scratch_shapes=[
            pltpu.VMEM(decays.shape, f32),
            pltpu.VMEM((plan.merge, tokens, width), f32),
            pltpu.VMEM((plan.merge, tokens, width), bf16),
            pltpu.VMEM(state.shape, bf16),
            pltpu.VMEM(back.shape, bf16),
            pltpu.VMEM((tokens, plan.merge * width), bf16),
            pltpu.VMEM((count, tokens // plan.peers, width), bf16),
            Copies.scratch(),
        ],
        compiler_params=params(52),
        cost_estimate=cost(4 * tokens * tokens * width, 2 * tokens * tokens + 16 * tokens * width),
        name="mix",
    )(decays, *attended, *readers, state, back)


def out_kernel(plan, sources, w_ref, *refs):
    part_refs, base_refs, out_ref = refs[: len(sources)], refs[len(sources) : -3], refs[-3]
    kept, sems = refs[-2:]
    copies = Copies(sems)
    depth = part_refs[0].shape[1]
    core, me = plan.core(), lax.axis_index("head")
    owners = []
    for s, k in sources:
        owner = lax.rem(me - k + plan.peers, plan.peers) * plan.merge
        owners.append(owner + (core if s == 0 else 1 - core))
    leaving = []
    step = min(128, out_ref.shape[0])
    for at in range(0, out_ref.shape[0], step):
        there = slice(at, at + step)
        total = base_refs[0][there, :] if base_refs else 0.0
        for owner, part in zip(owners, part_refs):
            rows = pl.ds(pl.multiple_of(owner * depth, depth), depth)
            total = total + jnp.dot(part[there, :], w_ref[rows, :], preferred_element_type=f32)
        if base_refs:
            kept[there, :] = total.astype(out_ref.dtype)
            leaving.append(copies.start(kept.at[there], out_ref.at[there]))
        else:
            out_ref[there, :] = total.astype(out_ref.dtype)
    finish(leaving)


def project_out(plan, w, parts, base, kind):
    local, width = next(iter(parts.values())).shape[0], w.shape[1]
    return pl.pallas_call(
        functools.partial(out_kernel, plan, list(parts)),
        in_specs=[vmem] * (1 + len(parts) + len(base)),
        out_specs=hbm if base else vmem,
        out_shape=jax.ShapeDtypeStruct((local, width), kind),
        scratch_shapes=[pltpu.VMEM((local, width), kind), Copies.scratch()],
        compiler_params=params(),
        cost_estimate=cost(0, 4 * local),
        name="project_out",
    )(w, *parts.values(), *base)


def body(frames_in, in_weight, out_weight, block_ids, block_lists, decays):
    local_tokens = frames_in.shape[1]
    heads_here = decays.shape[1]
    groups = block_lists.shape[0]
    me = lax.axis_index("head")
    plan = Plan(lax.axis_size("tm"), lax.axis_size("head"), heads_here, frames_in.shape[2])

    own = frames_in[0]
    arriving = [plan.to_peer(own, plan.peers - k, False) for k in range(1, plan.peers)]
    owns = [own] + [plan.swap(own)] * (plan.merge - 1)
    rates = [decays[0]] + [plan.swap(decays[0])] * (plan.merge - 1)
    block = reorder(plan, in_weight)
    if plan.merge == 2:
        block = reorder(plan, plan.swap(in_weight), [block])
    ids = jnp.roll(block_ids, -me * local_tokens)
    ids, rates = lax.optimization_barrier((ids, rates))
    tables = decay_tables(plan, rates, groups)
    rank = rank_tokens(ids, groups)

    def fill(slot, arriving, part):
        if slot == 1:
            arriving = [plan.swap(tokens) for tokens in arriving]
        return place_tokens([slot], rank, local_tokens, arriving, [part])

    if plan.ringed:
        blocks, crossed = [block], []
        half = block.shape[0] // 2
        for k in range(plan.along - 1):
            with_ = ()
            if k == 0:
                places = back_tokens(rank)
                with_ = (places, tables)
            if k == min(1, plan.along - 2):
                rank, owns, _ = lax.optimization_barrier((rank, owns, blocks[-1]))
                part = with_ = place_tokens(list(range(plan.merge)), rank, 0, owns, [])
            if k == plan.along - 2:
                arriving, _ = lax.optimization_barrier((arriving, blocks[-1]))
                x = [fill(s, arriving, part) for s in range(plan.merge)]
            passed, across, with_ = lax.optimization_barrier(
                (plan.round(blocks[-1]), plan.cross(blocks[-1]), with_)
            )
            if k == plan.along - 2:
                tables, passed, across, x[0] = lax.optimization_barrier(
                    (tables, passed, across, x[0])
                )
                tables, passed, across = lax.optimization_barrier(
                    (hold(tables), passed, across)
                )
            blocks.append(passed)
            crossed.append(across)
        last = [plan.cross(blocks[-1][:half]), plan.round(crossed[-1][half:])]
        weights = blocks + crossed + last
    else:
        weights = [
            lax.all_gather(block, "tm", axis=0, tiled=True, axis_index_groups=plan.groups())
        ]
        places = back_tokens(rank)
        part = place_tokens(list(range(plan.merge)), rank, 0, owns, [])
        x = [fill(s, arriving, part) for s in range(plan.merge)]
    if plan.ringed:
        v, b, x_last = project(plan, x, weights[:-2])
        local, total = block_updates(plan, tables, v, b, x_last, last, groups)
    else:
        v, b, x_last = project(plan, x, weights)
        local, total = block_updates(plan, tables, v, b, x_last, [], groups)

    def exchange(blocks):
        return lax.all_to_all(
            blocks, "tm", split_axis=0, concat_axis=0, tiled=True,
            axis_index_groups=plan.groups(),
        )

    share = local.shape[1] // plan.chips
    arrived = exchange(total)
    attended = [attend(plan, 0, block_lists, x[0], weights, local)]
    arrived, attended = lax.optimization_barrier((arrived, attended))
    states = scan_states(plan, arrived, share)
    x, states = lax.optimization_barrier((x, states))
    if plan.merge == 2:
        attended.append(attend(plan, 1, block_lists, x[1], weights, local))
    state = exchange(states).reshape(-1, LANES)

    bases, readers = ([a[i] for a in attended] for i in range(2))
    mixed = mix(plan, tables, bases, readers, state, places, groups)
    moved = {
        (s, k): plan.to_peer(mixed[s * plan.peers + k], k, s == 1)
        for s in range(plan.merge)
        for k in range(1, plan.peers)
    }
    near = {(0, 0): mixed[0]}
    if plan.merge == 2:
        near[1, 0] = plan.swap(mixed[plan.peers])
    result = project_out(plan, out_weight, near, [], f32)
    last = {key: moved.pop(key) for key in list(moved)[-1:]}
    if moved:
        result = project_out(plan, out_weight, moved, [result], f32)
    return project_out(plan, out_weight, last, [result], bf16)[None]


def solution(mesh):
    return jax.shard_map(
        body,
        mesh=mesh,
        in_specs=(P("tm", "head", None), P("tm", "head"), P(), P(), P(), P("tm", "head", None)),
        out_specs=P("tm", "head", None),
        check_vma=False,
    )
```

```python
import functools
import math

import jax
import jax.numpy as jnp
from jax import lax
from jax.experimental import pallas as pl
from jax.experimental.pallas import tpu as pltpu
from jax.sharding import PartitionSpec as P

HD = 64
N = 64
LANES = 2 * HD
PIECES = 5
EARLY = (2, 3)
LATE = (0, 1, 4)

epsilon = 1e-06

vmem = pl.BlockSpec(memory_space=pltpu.VMEM)
smem = pl.BlockSpec(memory_space=pltpu.SMEM)

hbm = pl.BlockSpec(memory_space=pltpu.HBM)

f32 = jnp.float32
bf16 = jnp.bfloat16


def params(mib=12):
    return pltpu.CompilerParams(vmem_limit_bytes=mib << 20)


def cost(flops, nbytes, transcendentals=0):
    return pl.CostEstimate(
        flops=int(flops), bytes_accessed=int(nbytes), transcendentals=int(transcendentals)
    )


def first_half(shape):
    return lax.broadcasted_iota(jnp.int32, shape, len(shape) - 1) < HD


class Plan:
    def __init__(self, frames, peers, heads_here, width):
        self.merge = 2 if frames % 2 == 0 and heads_here % 4 == 0 else 1
        self.frames, self.peers = frames, peers
        self.heads = heads_here // self.merge
        self.pairs = self.heads // 2
        self.chips = frames // self.merge
        self.across = 2 if self.chips % 2 == 0 else 1
        self.along = self.chips // self.across
        self.ringed = self.across == 2 and 2 <= self.along <= 8 and width % (self.chips * LANES) == 0

    def core(self):
        return lax.rem(lax.axis_index("tm"), self.merge)

    def chip(self):
        return lax.div(lax.axis_index("tm"), self.merge)

    def swap(self, block):
        return lax.ppermute(block, "tm", [(t, t ^ 1) for t in range(self.frames)])

    def round(self, block):
        a, b, c = self.along, self.across, self.merge
        pairs = [(t, (t + b * c) % (a * b * c)) for t in range(self.frames)]
        return lax.ppermute(block, "tm", pairs)

    def cross(self, block):
        c = self.merge
        pairs = [(t, (t // c ^ 1) * c + t % c) for t in range(self.frames)]
        return lax.ppermute(block, "tm", pairs)

    def last_chip(self):
        a, b = lax.div(self.chip(), self.across), lax.rem(self.chip(), self.across)
        return lax.rem(a + 1, self.along) * self.across + (self.across - 1 - b)

    def places(self, refs):
        if len(refs) == 1:
            return [(refs[0], slice(None))]
        rows = refs[0].shape[0]
        a, b = lax.div(self.chip(), self.across), lax.rem(self.chip(), self.across)
        n = self.along
        made = []
        for i, ref in enumerate(refs):
            k, flip = (i, 0) if i < n else (min(i - n, n - 1), 1)
            there = lax.rem(a - k + n, n) * self.across
            at = (there + (1 - b if flip else b)) * rows
            at = at + (rows // 2 if i == 2 * n else 0)
            made.append((ref, pl.ds(pl.multiple_of(at, rows // 2), ref.shape[0])))
        return made

    def to_peer(self, block, k, other):
        if not other:
            pairs = [(j, (j + k) % self.peers) for j in range(self.peers)]
            return lax.ppermute(block, "head", pairs)
        if k == 0:
            return self.swap(block)
        pairs = [
            (t * self.peers + j, (t ^ 1) * self.peers + (j + k) % self.peers)
            for t in range(self.frames)
            for j in range(self.peers)
        ]
        return lax.ppermute(block, ("tm", "head"), pairs)

    def groups(self):
        if self.merge == 1:
            return None
        return [[j * self.merge + c for j in range(self.chips)] for c in range(self.merge)]

    def decay(self, refs, slot, pair, g):
        head = self.core() * self.heads + 2 * pair
        return halves((1, LANES), refs[slot][head, g], refs[slot][head + 1, g])


class Copies:
    room = 48

    def __init__(self, sems):
        self.sems, self.count = sems, 0

    def start(self, src, dst):
        copy = pltpu.make_async_copy(src, dst, self.sems.at[self.count])
        copy.start()
        self.count += 1
        return copy

    @staticmethod
    def scratch():
        return pltpu.SemaphoreType.DMA((Copies.room,))


def finish(copies):
    for copy in copies:
        copy.wait()


def halves(shape, one, two):
    return jnp.where(first_half(shape), one, two)


def reorder_kernel(plan, *refs):
    w_ref, out_ref = refs[0], refs[-1]
    rows = w_ref.shape[0]
    width = plan.heads * PIECES * HD
    first = plan.core() == 0

    def chosen(at):
        one = w_ref[:, at : at + HD]
        if plan.merge == 1:
            return one
        return jnp.where(first, one, w_ref[:, width + at : width + at + HD])

    order = [(p, i) for i in EARLY for p in range(plan.pairs)]
    order += [(p, i) for p in range(plan.pairs) for i in LATE]
    for n, (p, i) in enumerate(order):
        block = jnp.concatenate(
            [chosen(((2 * p + h) * PIECES + i) * HD) for h in range(2)], axis=1
        )
        cols = slice(n * LANES, (n + 1) * LANES)
        if len(refs) == 2:
            out_ref[:, cols] = block
        else:
            mine = refs[1][:, cols]
            out_ref[:rows, cols] = jnp.where(first, mine, block)
            out_ref[rows:, cols] = jnp.where(first, block, mine)


def reorder(plan, w, mine=()):
    rows = w.shape[0] * (1 + len(mine))
    return pl.pallas_call(
        functools.partial(reorder_kernel, plan),
        out_shape=jax.ShapeDtypeStruct((rows, plan.heads * PIECES * HD), bf16),
        compiler_params=params(),
        cost_estimate=cost(0, 4 * rows),
        name="reorder",
    )(w, *mine)


def normalise(part, out, at):
    step = min(128, part.shape[0])

    def norm(c, _):
        start = pl.multiple_of(c * step, step)
        wide = part[pl.ds(start, step), :].astype(f32)
        scale = lax.rsqrt(jnp.mean(wide * wide, axis=-1, keepdims=True) + epsilon)
        out[pl.ds(at + start, step), :] = (wide * scale).astype(bf16)
        return 0

    lax.fori_loop(0, part.shape[0] // step, norm, 0)


def rank_kernel(groups, ids_ref, row_ref):
    tokens = ids_ref.shape[1]
    block = tokens // groups
    label = lax.broadcasted_iota(jnp.int32, (groups, tokens), 0)
    held = label == ids_ref[...]
    held_bf = jnp.where(held, 1.0, 0.0).astype(bf16)
    counts = []
    for c in range(tokens // 256):
        before = lax.broadcasted_iota(jnp.int32, (tokens, 256), 0) < (
            lax.broadcasted_iota(jnp.int32, (tokens, 256), 1) + c * 256
        )
        counts.append(
            jnp.dot(held_bf, jnp.where(before, 1.0, 0.0).astype(bf16), preferred_element_type=f32)
        )
    count = jnp.concatenate(counts, axis=1)
    row_ref[...] = jnp.sum(
        jnp.where(held, count + (label * block).astype(f32), 0.0), axis=0, keepdims=True
    )


def rank_tokens(ids, groups):
    tokens = ids.shape[0]
    return pl.pallas_call(
        functools.partial(rank_kernel, groups),
        out_shape=jax.ShapeDtypeStruct((1, tokens), f32),
        compiler_params=params(),
        cost_estimate=cost(0, 4 * tokens),
        name="rank_tokens",
    )(ids.reshape(1, tokens))


def back_kernel(row_ref, back_ref):
    tokens = back_ref.shape[0]
    lane = lax.broadcasted_iota(jnp.int32, (LANES, LANES), 1)
    for at in range(0, tokens, LANES):
        place = jnp.broadcast_to(row_ref[:, at : at + LANES], (LANES, LANES)).T
        for t in range(0, tokens, LANES):
            back_ref[at : at + LANES, t : t + LANES] = jnp.where(
                (lane + t).astype(f32) == place, 1.0, 0.0
            ).astype(bf16)


def back_tokens(rank):
    return pl.pallas_call(
        back_kernel,
        out_shape=jax.ShapeDtypeStruct((rank.shape[1], rank.shape[1]), bf16),
        compiler_params=params(),
        cost_estimate=cost(0, 4 * LANES),
        name="back_tokens",
    )(rank)


def hold(values):
    def kernel(in_ref, out_ref):
        out_ref[...] = in_ref[...]

    return pl.pallas_call(
        kernel,
        out_shape=jax.ShapeDtypeStruct(values.shape, values.dtype),
        compiler_params=params(),
        cost_estimate=cost(2e10, 4 * LANES),
        name="hold",
    )(values)


def picks(rank, at, rows):
    places = lax.broadcasted_iota(jnp.int32, (rows, rank.shape[1]), 0) + at
    return jnp.where(places.astype(f32) == rank, 1.0, 0.0).astype(bf16)


def place_kernel(slots, parts, start, rank_ref, *refs):
    frame_refs, refs = refs[: len(slots) * parts], refs[len(slots) * parts :]
    base_refs, (x_ref, normed) = refs[:-2], refs[-2:]
    tokens = rank_ref.shape[1]
    count = normed.shape[1]
    step = 256
    for i in range(len(slots)):
        at = 0
        for ref in frame_refs[i * parts : (i + 1) * parts]:
            rows = ref.shape[0]
            normalise(ref, normed.at[i], at)
            at += rows
    for at in range(0, tokens, step):
        pick = picks(rank_ref[:, start : start + count], at, step)
        for i, slot in enumerate(slots):
            placed = jnp.dot(pick, normed[i], preferred_element_type=f32).astype(bf16)
            for base in base_refs:
                placed = base[slot * tokens + at : slot * tokens + at + step, :] + placed
            x_ref[i * tokens + at : i * tokens + at + step, :] = placed


def place_tokens(slots, rank, start, frames, base):
    tokens = rank.shape[1]
    width = frames[0].shape[1]
    parts = len(frames) // len(slots)
    count = parts * frames[0].shape[0]
    return pl.pallas_call(
        functools.partial(place_kernel, slots, parts, start),
        out_shape=jax.ShapeDtypeStruct((len(slots) * tokens, width), bf16),
        scratch_shapes=[pltpu.VMEM((len(slots), count, width), bf16)],
        compiler_params=params(),
        cost_estimate=cost(0, 4 * tokens),
        name="place_tokens",
    )(rank, *frames, *base)


def project_kernel(plan, *refs):
    x_refs, refs = refs[: plan.merge], refs[plan.merge :]
    w_refs, (v_ref, b_ref, rest_ref, w, turned) = refs[:-5], refs[-5:]
    tokens, width = x_refs[0].shape
    step = 256
    cols = plan.pairs * LANES
    if len(w_refs) > 1:
        w[...] = jnp.zeros_like(w)
        turned[...] = jnp.zeros_like(turned)
    for ref, rows in plan.places(w_refs):
        w[rows, :] = ref[:, :cols]
        turned[rows, :] = ref[:, cols : 2 * cols]
    maps = jnp.concatenate(
        [
            turned[at : at + LANES, :].astype(f32).T.astype(bf16)
            for at in range(0, turned.shape[0], LANES)
        ],
        axis=1,
    )
    count = rest_ref.shape[1]
    there = plan.last_chip() * count
    for s, x_ref in enumerate(x_refs):
        for at in range(0, tokens, step):
            rows = slice(s * tokens + at, s * tokens + at + step)
            x = x_ref[at : at + step, :]
            v_ref[rows, :] = jnp.dot(x, w[...], preferred_element_type=f32)
            b_ref[:, rows] = lax.dot_general(
                maps, x, (((1,), (1,)), ((), ())), preferred_element_type=f32
            )
    for s, x_ref in enumerate(x_refs):
        for at in range(0, tokens, step):
            here = slice(at, at + step)
            rest = x_ref[here, :count]
            for c in range(count, width, count):
                rest = jnp.where(there == c, x_ref[here, c : c + count], rest)
            rest_ref[s * tokens + at : s * tokens + at + step, :] = rest


def project(plan, x, weights):
    every, width = x[0].shape[0] * plan.merge, x[0].shape[1]
    cols = plan.pairs * LANES
    count = max(LANES, width // plan.chips)
    return pl.pallas_call(
        functools.partial(project_kernel, plan),
        out_shape=(
            jax.ShapeDtypeStruct((every, cols), f32),
            jax.ShapeDtypeStruct((cols, every), f32),
            jax.ShapeDtypeStruct((every, count), bf16),
        ),
        scratch_shapes=[pltpu.VMEM((width, cols), bf16), pltpu.VMEM((width, cols), bf16)],
        compiler_params=params(),
        cost_estimate=cost(0, 4 * width),
        name="project",
    )(*x, *weights)


def update_kernel(plan, groups, decay_ref, *refs):
    v_ref, b_ref, x_ref, last_refs, (left, total_out, total_ref, u, sems) = (
        refs[0], refs[1], refs[2], refs[3:-5], refs[-5:]
    )
    copies = Copies(sems)
    leaving = []
    every = v_ref.shape[0]
    tokens = every // plan.merge
    block = tokens // groups
    step = 256
    here = step // block
    cols = plan.pairs * LANES
    if last_refs:
        w = jnp.concatenate([ref[:, : 2 * cols] for ref in last_refs], axis=0)
        maps = w[:, cols:].astype(f32).T.astype(bf16)
        w = w[:, :cols]

    lane = lax.div(lax.broadcasted_iota(jnp.int32, (LANES, step), 1), block)
    for at in range(0, every, step):
        there = slice(at, at + step)
        values, b = v_ref[there, :], b_ref[:, there]
        if last_refs:
            x = x_ref[there, :]
            values = values + jnp.dot(x, w, preferred_element_type=f32)
            b = b + lax.dot_general(
                maps, x, (((1,), (1,)), ((), ())), preferred_element_type=f32
            )
        values = values.astype(bf16)
        for p in range(plan.pairs):
            mine = b[p * LANES : (p + 1) * LANES]
            wide = jnp.concatenate(
                [jnp.where(lane == i, mine, 0.0).astype(bf16) for i in range(here)], axis=0
            )
            outer = jnp.dot(
                wide, values[:, p * LANES : (p + 1) * LANES], preferred_element_type=f32
            )
            for i in range(here):
                m = outer[i * 2 * N : (i + 1) * 2 * N]
                row = ((at % tokens // block + i) * plan.pairs + p) * N
                u[at // tokens, row : row + N, :] = halves((N, LANES), m[:N], m[N:])

    peers = total_ref.shape[0]
    share = u.shape[1] // peers
    items = max(1, share // N)
    size = min(N, share)
    first = plan.core() == 0
    for d in range(peers):
        for i in range(items):
            row = d * share + i * N
            rows = slice(row, row + size)
            item = slice(row // N, row // N + 1)
            last, product = decay_ref[0, item, :], decay_ref[1, item, :]
            if plan.merge == 2:
                one, two = u[0, rows, :], u[1, rows, :]
                one, two = (
                    one + jnp.where(first, 0.0, last) * two,
                    two + jnp.where(first, last, 0.0) * one,
                )
                left[0, rows, :] = one.astype(bf16)
                left[1, rows, :] = two.astype(bf16)
                total = jnp.where(first, two, one)
            else:
                total = u[0, rows, :]
                left[0, rows, :] = total.astype(bf16)
            total_ref[d, i * size : (i + 1) * size, :] = total.astype(bf16)
            for n in range(3):
                piece = product.astype(bf16)
                at = share + n * items + i
                total_ref[d, at : at + 1, :] = piece
                product = product - piece.astype(f32)
        if (d + 1) % (peers // 4) == 0:
            done = slice(d + 1 - peers // 4, d + 1)
            leaving.append(copies.start(total_ref.at[done], total_out.at[done]))
    finish(leaving)


def share_rows(share):
    return share + 16 * -(-3 * max(1, share // N) // 16)


def block_updates(plan, decays, v, b, x, last, groups):
    every, cols = v.shape
    rows = plan.pairs * groups * N
    share = rows // plan.chips
    return pl.pallas_call(
        functools.partial(update_kernel, plan, groups),
        in_specs=[vmem] * (4 + len(last)),
        out_specs=(vmem, hbm),
        out_shape=(
            jax.ShapeDtypeStruct((plan.merge, rows, LANES), bf16),
            jax.ShapeDtypeStruct((plan.chips, share_rows(share), LANES), bf16),
        ),
        scratch_shapes=[
            pltpu.VMEM((plan.chips, share_rows(share), LANES), bf16),
            pltpu.VMEM((plan.merge, rows, LANES), f32),
            Copies.scratch(),
        ],
        compiler_params=params(),
        cost_estimate=cost(4 * every * 256 * 2 * cols, 6 * every * cols),
        name="block_updates",
    )(decays, v, b, x, *last)


def decay_kernel(plan, groups, *refs):
    rate_refs, out_ref = refs[:-1], refs[-1]
    first = plan.core() == 0
    for g in range(groups):
        for p in range(plan.pairs):
            row = slice(g * plan.pairs + p, g * plan.pairs + p + 1)
            slots = [plan.decay(rate_refs, s, p, g) for s in range(plan.merge)]
            together, last = slots[0], slots[0]
            if plan.merge == 2:
                together = slots[0] * slots[1]
                last = jnp.where(first, slots[1], slots[0])
                slots = [
                    jnp.where(first, slots[0], together),
                    jnp.where(first, together, slots[1]),
                ]
            for i, value in enumerate([last, together] + slots):
                out_ref[i, row, :] = value


def decay_tables(plan, rates, groups):
    return pl.pallas_call(
        functools.partial(decay_kernel, plan, groups),
        in_specs=[smem] * plan.merge,
        out_shape=jax.ShapeDtypeStruct((2 + plan.merge, plan.pairs * groups, LANES), f32),
        compiler_params=params(),
        cost_estimate=cost(0, 4 * LANES),
        name="decay_tables",
    )(*rates)


def scan_kernel(plan, u_ref, s_ref):
    share = s_ref.shape[1]
    size = min(share, N)
    items = share // size
    for i in range(items):
        at = slice(i * size, (i + 1) * size)
        state = jnp.zeros((size, LANES), f32)
        for j in range(plan.chips):
            s_ref[j, at, :] = state.astype(bf16)
            decay = jnp.zeros((1, LANES), f32)
            for n in range(3):
                row = share + n * items + i
                decay = decay + u_ref[j, row : row + 1, :].astype(f32)
            state = decay * state + u_ref[j, at, :].astype(f32)


def scan_states(plan, update, share):
    return pl.pallas_call(
        functools.partial(scan_kernel, plan),
        out_shape=jax.ShapeDtypeStruct((plan.chips, share, LANES), bf16),
        compiler_params=params(),
        cost_estimate=cost(2 * update.size, 4 * update.size),
        name="scan_states",
    )(update)


def attend_kernel(plan, slot, *refs):
    lists_ref, x_in, local_in, refs = refs[0], refs[1], refs[2], refs[3:]
    w_refs, refs = refs[:-12], refs[-12:]
    a_out, c_out, x, local, w, q_ref, k_ref, wide_v, e_ref, a, c_ref, sems = refs
    copies = Copies(sems)
    tokens = x.shape[0]
    groups, chosen = lists_ref.shape
    block = tokens // groups
    step = 256
    per = step // block
    wide = plan.pairs * LANES

    weights = []
    for ref, rows in plan.places(w_refs):
        weights.append(copies.start(ref.at[:, :wide], w.at[rows, :wide]))
        weights.append(copies.start(ref.at[:, 2 * wide :], w.at[rows, wide:]))
    arriving = []
    for at in range(0, tokens, step):
        arriving.append(copies.start(x_in.at[at : at + step], x.at[at : at + step]))
    later = copies.start(local_in.at[slot], local)

    same = lax.div(lax.broadcasted_iota(jnp.int32, (2 * LANES, 2 * LANES), 0), HD) == lax.div(
        lax.broadcasted_iota(jnp.int32, (2 * LANES, 2 * LANES), 1), HD
    )
    same = jnp.where(same, 1.0, 0.0).astype(bf16)

    def head_norm(values):
        square = values * values
        high = square.astype(bf16)
        low = (square - high.astype(f32)).astype(bf16)
        total = jnp.dot(high, same, preferred_element_type=f32)
        total = total + jnp.dot(low, same, preferred_element_type=f32)
        return values * lax.rsqrt(total * (1.0 / HD) + epsilon)

    half = first_half((step, LANES))
    finish(weights)
    for at in range(0, tokens, step):
        rows = slice(at, at + step)
        arriving[at // step].wait()
        every = jnp.dot(x[rows, :], w[...], preferred_element_type=f32).astype(bf16)
        for p in range(plan.pairs):
            cols = slice(p * LANES, (p + 1) * LANES)
            wide_v[p, rows, :LANES] = every[:, cols]
            first = wide + 3 * p * LANES
            c_ref[rows, cols] = every[:, first + 2 * LANES : first + 3 * LANES]
            both = head_norm(every[:, first : first + 2 * LANES].astype(f32))
            k_ref[p, rows, :] = both[:, LANES:].astype(bf16)
            q = both[:, :LANES]
            one = jnp.where(half, q, 0.0).astype(bf16)
            two = jnp.where(half, 0.0, q).astype(bf16)
            for i in range(per):
                part = slice(i * block, (i + 1) * block)
                q_ref[p, at // block + i] = jnp.concatenate([one[part], two[part]], axis=0)
    leaving = [copies.start(c_ref, c_out)]
    later.wait()
    for p in range(plan.pairs):
        wide_v[p, :, LANES:] = jnp.ones((tokens, LANES), bf16)

    scale = math.log2(math.e) / math.sqrt(HD)
    starts = [
        [pl.multiple_of(lists_ref[g, j] * block, block) for j in range(chosen)]
        for g in range(groups)
    ]
    for g in range(groups):
        for p in range(plan.pairs):
            keys = jnp.concatenate([k_ref[p, pl.ds(s, block), :] for s in starts[g]], axis=0)
            score = lax.dot_general(
                q_ref[p, g], keys, (((1,), (1,)), ((), ())), preferred_element_type=f32
            )
            e_ref[p, g] = jnp.exp2(score * scale).astype(bf16)
    for g in range(groups):
        rows = slice(g * block, (g + 1) * block)
        for p in range(plan.pairs):
            cols = slice(p * LANES, (p + 1) * LANES)
            values = jnp.concatenate([wide_v[p, pl.ds(s, block), :] for s in starts[g]], axis=0)
            both = jnp.dot(e_ref[p, g], values, preferred_element_type=f32)
            both = both[:, :LANES] / both[:, LANES:]
            a[rows, cols] = halves((block, LANES), both[:block], both[block:])
    for g in range(groups):
        rows = slice(g * block, (g + 1) * block)
        for p in range(plan.pairs):
            cols = slice(p * LANES, (p + 1) * LANES)
            items = slice((g * plan.pairs + p) * N, (g * plan.pairs + p + 1) * N)
            a[rows, cols] = a[rows, cols] + read_out(
                c_ref[rows, cols], local[items, :].astype(f32), block
            )
        if (g + 1) % per == 0:
            done = slice((g + 1 - per) * block, (g + 1) * block)
            leaving.append(copies.start(a.at[done], a_out.at[done]))
    finish(leaving)


def attend(plan, slot, lists, x, weights, local):
    tokens, width = x.shape
    every = tokens * plan.merge
    groups, chosen = lists.shape
    block = tokens // groups
    cols = plan.pairs * LANES
    return pl.pallas_call(
        functools.partial(attend_kernel, plan, slot),
        in_specs=[smem] + [hbm] * (2 + len(weights)),
        out_specs=(hbm,) * 2,
        scratch_shapes=[
            pltpu.VMEM((tokens, width), bf16),
            pltpu.VMEM(local.shape[1:], bf16),
            pltpu.VMEM((width, 4 * cols), bf16),
            pltpu.VMEM((plan.pairs, groups, 2 * block, LANES), bf16),
            pltpu.VMEM((plan.pairs, tokens, LANES), bf16),
            pltpu.VMEM((plan.pairs, tokens, 2 * LANES), bf16),
            pltpu.VMEM((plan.pairs, groups, 2 * block, chosen * block), bf16),
            pltpu.VMEM((tokens, cols), f32),
            pltpu.VMEM((tokens, cols), bf16),
            Copies.scratch(),
        ],
        out_shape=(
            jax.ShapeDtypeStruct((tokens, cols), f32),
            jax.ShapeDtypeStruct((tokens, cols), bf16),
        ),
        compiler_params=params(60),
        cost_estimate=cost(
            6 * tokens * width * 3 * cols,
            4 * (tokens * width + 5 * width * cols + local.size),
            2 * plan.pairs * tokens * chosen * block,
        ),
        name="attend",
    )(lists, x, local, *weights)


def read_out(readers, state, block):
    half = first_half(state.shape)
    wide = jnp.concatenate([jnp.where(half, state, 0.0), jnp.where(half, 0.0, state)], axis=0)
    return jnp.dot(readers, wide.astype(bf16), preferred_element_type=f32) * (
        1.0 / (N * math.sqrt(block))
    )


def mix_kernel(plan, groups, decay_in, *refs):
    a_ins, refs = refs[: plan.merge], refs[plan.merge :]
    c_ins, refs = refs[: plan.merge], refs[plan.merge :]
    s_in, back_in, refs = refs[0], refs[1], refs[2:]
    out_refs, (decay, a, c, state, back, mixed, out, sems) = refs[:-8], refs[-8:]
    copies = Copies(sems)
    tokens = back.shape[0]
    block = tokens // groups
    width = a.shape[2]
    here = groups // 4
    many = here * plan.pairs * N

    arriving = []
    decaying = copies.start(decay_in, decay)
    for i in range(4):
        rows = slice(i * here * block, (i + 1) * here * block)
        items = slice(i * many, (i + 1) * many)
        arriving.append([copies.start(s_in.at[items], state.at[items])])
        for s in range(plan.merge):
            arriving[-1] += [
                copies.start(c_ins[s].at[rows], c.at[s, rows, :]),
                copies.start(a_ins[s].at[rows], a.at[s, rows, :]),
            ]
    local = tokens // plan.peers
    order = list(range(1, plan.peers)) + [0]
    turning = []
    for k in order:
        rows = slice(k * local, (k + 1) * local)
        turning.append(copies.start(back_in.at[rows], back.at[rows]))

    decaying.wait()
    for g in range(groups):
        if g % here == 0:
            finish(arriving[g // here])
        rows = slice(g * block, (g + 1) * block)
        for p in range(plan.pairs):
            cols = slice(p * LANES, (p + 1) * LANES)
            at = (g * plan.pairs + p) * N
            readers = jnp.concatenate([c[s, rows, cols] for s in range(plan.merge)], axis=0)
            read = read_out(readers, state[at : at + N, :].astype(f32), block)
            item = slice(g * plan.pairs + p, g * plan.pairs + p + 1)
            for s in range(plan.merge):
                there = slice(s * width + p * LANES, s * width + (p + 1) * LANES)
                mixed[rows, there] = (
                    a[s, rows, cols]
                    + decay[2 + s, item, :] * read[s * block : (s + 1) * block]
                ).astype(bf16)

    leaving = []
    for k, turned in zip(order, turning):
        turned.wait()
        placed = jnp.dot(
            back[k * local : (k + 1) * local, :], mixed[...], preferred_element_type=f32
        ).astype(bf16)
        for s in range(plan.merge):
            i = s * plan.peers + k
            out[i] = placed[:, s * width : (s + 1) * width]
            leaving.append(copies.start(out.at[i], out_refs[i]))
    finish(leaving)


def mix(plan, decays, attended, readers, state, back, groups):
    tokens = back.shape[0]
    width = attended[0].shape[1]
    count = plan.merge * plan.peers
    return pl.pallas_call(
        functools.partial(mix_kernel, plan, groups),
        in_specs=[hbm] * (2 * plan.merge + 3),
        out_specs=(hbm,) * count,
        out_shape=(jax.ShapeDtypeStruct((tokens // plan.peers, width), bf16),) * count,
        scratch_shapes=[
            pltpu.VMEM(decays.shape, f32),
            pltpu.VMEM((plan.merge, tokens, width), f32),
            pltpu.VMEM((plan.merge, tokens, width), bf16),
            pltpu.VMEM(state.shape, bf16),
            pltpu.VMEM(back.shape, bf16),
            pltpu.VMEM((tokens, plan.merge * width), bf16),
            pltpu.VMEM((count, tokens // plan.peers, width), bf16),
            Copies.scratch(),
        ],
        compiler_params=params(52),
        cost_estimate=cost(4 * tokens * tokens * width, 2 * tokens * tokens + 16 * tokens * width),
        name="mix",
    )(decays, *attended, *readers, state, back)


def out_kernel(plan, sources, w_ref, *refs):
    part_refs, base_refs, out_ref = refs[: len(sources)], refs[len(sources) : -3], refs[-3]
    kept, sems = refs[-2:]
    copies = Copies(sems)
    depth = part_refs[0].shape[1]
    core, me = plan.core(), lax.axis_index("head")
    owners = []
    for s, k in sources:
        owner = lax.rem(me - k + plan.peers, plan.peers) * plan.merge
        owners.append(owner + (core if s == 0 else 1 - core))
    leaving = []
    step = min(128, out_ref.shape[0])
    for at in range(0, out_ref.shape[0], step):
        there = slice(at, at + step)
        total = base_refs[0][there, :] if base_refs else 0.0
        for owner, part in zip(owners, part_refs):
            rows = pl.ds(pl.multiple_of(owner * depth, depth), depth)
            total = total + jnp.dot(part[there, :], w_ref[rows, :], preferred_element_type=f32)
        if base_refs:
            kept[there, :] = total.astype(out_ref.dtype)
            leaving.append(copies.start(kept.at[there], out_ref.at[there]))
        else:
            out_ref[there, :] = total.astype(out_ref.dtype)
    finish(leaving)


def project_out(plan, w, parts, base, kind):
    local, width = next(iter(parts.values())).shape[0], w.shape[1]
    return pl.pallas_call(
        functools.partial(out_kernel, plan, list(parts)),
        in_specs=[vmem] * (1 + len(parts) + len(base)),
        out_specs=hbm if base else vmem,
        out_shape=jax.ShapeDtypeStruct((local, width), kind),
        scratch_shapes=[pltpu.VMEM((local, width), kind), Copies.scratch()],
        compiler_params=params(),
        cost_estimate=cost(0, 4 * local),
        name="project_out",
    )(w, *parts.values(), *base)


def body(frames_in, in_weight, out_weight, block_ids, block_lists, decays):
    local_tokens = frames_in.shape[1]
    heads_here = decays.shape[1]
    groups = block_lists.shape[0]
    me = lax.axis_index("head")
    plan = Plan(lax.axis_size("tm"), lax.axis_size("head"), heads_here, frames_in.shape[2])

    own = frames_in[0]
    arriving = [plan.to_peer(own, plan.peers - k, False) for k in range(1, plan.peers)]
    owns = [own] + [plan.swap(own)] * (plan.merge - 1)
    rates = [decays[0]] + [plan.swap(decays[0])] * (plan.merge - 1)
    block = reorder(plan, in_weight)
    if plan.merge == 2:
        block = reorder(plan, plan.swap(in_weight), [block])
    ids = jnp.roll(block_ids, -me * local_tokens)
    ids, rates = lax.optimization_barrier((ids, rates))
    tables = decay_tables(plan, rates, groups)
    rank = rank_tokens(ids, groups)

    def fill(slot, arriving, part):
        if slot == 1:
            arriving = [plan.swap(tokens) for tokens in arriving]
        return place_tokens([slot], rank, local_tokens, arriving, [part])

    if plan.ringed:
        blocks, crossed = [block], []
        half = block.shape[0] // 2
        for k in range(plan.along - 1):
            with_ = ()
            if k == 0:
                places = back_tokens(rank)
                with_ = (places, tables)
            if k == min(1, plan.along - 2):
                rank, owns, _ = lax.optimization_barrier((rank, owns, blocks[-1]))
                part = with_ = place_tokens(list(range(plan.merge)), rank, 0, owns, [])
            if k == plan.along - 2:
                arriving, _ = lax.optimization_barrier((arriving, blocks[-1]))
                x = [fill(s, arriving, part) for s in range(plan.merge)]
            passed, across, with_ = lax.optimization_barrier(
                (plan.round(blocks[-1]), plan.cross(blocks[-1]), with_)
            )
            if k == plan.along - 2:
                tables, passed, across, x[0] = lax.optimization_barrier(
                    (tables, passed, across, x[0])
                )
                tables, passed, across = lax.optimization_barrier(
                    (hold(tables), passed, across)
                )
            blocks.append(passed)
            crossed.append(across)
        last = [plan.cross(blocks[-1][:half]), plan.round(crossed[-1][half:])]
        weights = blocks + crossed + last
    else:
        weights = [
            lax.all_gather(block, "tm", axis=0, tiled=True, axis_index_groups=plan.groups())
        ]
        places = back_tokens(rank)
        part = place_tokens(list(range(plan.merge)), rank, 0, owns, [])
        x = [fill(s, arriving, part) for s in range(plan.merge)]
    if plan.ringed:
        v, b, x_last = project(plan, x, weights[:-2])
        local, total = block_updates(plan, tables, v, b, x_last, last, groups)
    else:
        v, b, x_last = project(plan, x, weights)
        local, total = block_updates(plan, tables, v, b, x_last, [], groups)

    def exchange(blocks):
        return lax.all_to_all(
            blocks, "tm", split_axis=0, concat_axis=0, tiled=True,
            axis_index_groups=plan.groups(),
        )

    share = local.shape[1] // plan.chips
    arrived = exchange(total)
    attended = [attend(plan, 0, block_lists, x[0], weights, local)]
    arrived, attended = lax.optimization_barrier((arrived, attended))
    states = scan_states(plan, arrived, share)
    x, states = lax.optimization_barrier((x, states))
    if plan.merge == 2:
        attended.append(attend(plan, 1, block_lists, x[1], weights, local))
    state = exchange(states).reshape(-1, LANES)

    bases, readers = ([a[i] for a in attended] for i in range(2))
    mixed = mix(plan, tables, bases, readers, state, places, groups)
    moved = {
        (s, k): plan.to_peer(mixed[s * plan.peers + k], k, s == 1)
        for s in range(plan.merge)
        for k in range(1, plan.peers)
    }
    near = {(0, 0): mixed[0]}
    if plan.merge == 2:
        near[1, 0] = plan.swap(mixed[plan.peers])
    result = project_out(plan, out_weight, near, [], f32)
    last = {key: moved.pop(key) for key in list(moved)[-1:]}
    if moved:
        result = project_out(plan, out_weight, moved, [result], f32)
    return project_out(plan, out_weight, last, [result], bf16)[None]


def solution(mesh):
    return jax.shard_map(
        body,
        mesh=mesh,
        in_specs=(P("tm", "head", None), P("tm", "head"), P(), P(), P(), P("tm", "head", None)),
        out_specs=P("tm", "head", None),
        check_vma=False,
    )
```

```python
import functools
import math

import jax
import jax.numpy as jnp
from jax import lax
from jax.experimental import pallas as pl
from jax.experimental.pallas import tpu as pltpu
from jax.sharding import PartitionSpec as P

HD = 64
N = 64
LANES = 2 * HD
PIECES = 5
EARLY = (2, 3)
LATE = (0, 1, 4)

epsilon = 1e-06

vmem = pl.BlockSpec(memory_space=pltpu.VMEM)
smem = pl.BlockSpec(memory_space=pltpu.SMEM)

hbm = pl.BlockSpec(memory_space=pltpu.HBM)

f32 = jnp.float32
bf16 = jnp.bfloat16


def params(mib=16):
    return pltpu.CompilerParams(vmem_limit_bytes=mib << 20)


def cost(flops, nbytes, transcendentals=0):
    return pl.CostEstimate(
        flops=int(flops), bytes_accessed=int(nbytes), transcendentals=int(transcendentals)
    )


def first_half(shape):
    return lax.broadcasted_iota(jnp.int32, shape, len(shape) - 1) < HD


class Plan:
    def __init__(self, frames, peers, heads_here, width):
        self.merge = 2 if frames % 2 == 0 and heads_here % 4 == 0 else 1
        self.frames, self.peers = frames, peers
        self.heads = heads_here // self.merge
        self.pairs = self.heads // 2
        self.chips = frames // self.merge
        self.across = 2 if self.chips % 2 == 0 else 1
        self.along = self.chips // self.across
        self.ringed = self.across == 2 and 2 <= self.along <= 8 and width % (self.chips * LANES) == 0

    def core(self):
        return lax.rem(lax.axis_index("tm"), self.merge)

    def chip(self):
        return lax.div(lax.axis_index("tm"), self.merge)

    def swap(self, block):
        return lax.ppermute(block, "tm", [(t, t ^ 1) for t in range(self.frames)])

    def round(self, block):
        a, b, c = self.along, self.across, self.merge
        pairs = [(t, (t + b * c) % (a * b * c)) for t in range(self.frames)]
        return lax.ppermute(block, "tm", pairs)

    def cross(self, block):
        c = self.merge
        pairs = [(t, (t // c ^ 1) * c + t % c) for t in range(self.frames)]
        return lax.ppermute(block, "tm", pairs)

    def last_chip(self):
        a, b = lax.div(self.chip(), self.across), lax.rem(self.chip(), self.across)
        return lax.rem(a + 1, self.along) * self.across + (self.across - 1 - b)

    def places(self, refs):
        if len(refs) == 1:
            return [(refs[0], slice(None))]
        rows = refs[0].shape[0]
        a, b = lax.div(self.chip(), self.across), lax.rem(self.chip(), self.across)
        n = self.along
        made = []
        for i, ref in enumerate(refs):
            k, flip = (i, 0) if i < n else (min(i - n, n - 1), 1)
            there = lax.rem(a - k + n, n) * self.across
            at = (there + (1 - b if flip else b)) * rows
            at = at + (rows // 2 if i == 2 * n else 0)
            made.append((ref, pl.ds(pl.multiple_of(at, rows // 2), ref.shape[0])))
        return made

    def to_peer(self, block, k, other):
        if not other:
            pairs = [(j, (j + k) % self.peers) for j in range(self.peers)]
            return lax.ppermute(block, "head", pairs)
        if k == 0:
            return self.swap(block)
        pairs = [
            (t * self.peers + j, (t ^ 1) * self.peers + (j + k) % self.peers)
            for t in range(self.frames)
            for j in range(self.peers)
        ]
        return lax.ppermute(block, ("tm", "head"), pairs)

    def groups(self):
        if self.merge == 1:
            return None
        return [[j * self.merge + c for j in range(self.chips)] for c in range(self.merge)]

    def decay(self, refs, slot, pair, g):
        head = self.core() * self.heads + 2 * pair
        return halves((1, LANES), refs[slot][head, g], refs[slot][head + 1, g])


class Copies:
    room = 48

    def __init__(self, sems):
        self.sems, self.count = sems, 0

    def start(self, src, dst):
        copy = pltpu.make_async_copy(src, dst, self.sems.at[self.count])
        copy.start()
        self.count += 1
        return copy

    @staticmethod
    def scratch():
        return pltpu.SemaphoreType.DMA((Copies.room,))


def finish(copies):
    for copy in copies:
        copy.wait()


def halves(shape, one, two):
    return jnp.where(first_half(shape), one, two)


def reorder_kernel(plan, *refs):
    w_ref, out_ref = refs[0], refs[-1]
    rows = w_ref.shape[0]
    width = plan.heads * PIECES * HD
    first = plan.core() == 0

    def chosen(at):
        one = w_ref[:, at : at + HD]
        if plan.merge == 1:
            return one
        return jnp.where(first, one, w_ref[:, width + at : width + at + HD])

    order = [(p, i) for i in EARLY for p in range(plan.pairs)]
    order += [(p, i) for p in range(plan.pairs) for i in LATE]
    for n, (p, i) in enumerate(order):
        block = jnp.concatenate(
            [chosen(((2 * p + h) * PIECES + i) * HD) for h in range(2)], axis=1
        )
        cols = slice(n * LANES, (n + 1) * LANES)
        if len(refs) == 2:
            out_ref[:, cols] = block
        else:
            mine = refs[1][:, cols]
            out_ref[:rows, cols] = jnp.where(first, mine, block)
            out_ref[rows:, cols] = jnp.where(first, block, mine)


def reorder(plan, w, mine=()):
    rows = w.shape[0] * (1 + len(mine))
    return pl.pallas_call(
        functools.partial(reorder_kernel, plan),
        out_shape=jax.ShapeDtypeStruct((rows, plan.heads * PIECES * HD), bf16),
        compiler_params=params(),
        cost_estimate=cost(0, 4 * rows),
        name="reorder",
    )(w, *mine)


def normalise(part, out, at):
    step = min(128, part.shape[0])

    def norm(c, _):
        start = pl.multiple_of(c * step, step)
        wide = part[pl.ds(start, step), :].astype(f32)
        scale = lax.rsqrt(jnp.mean(wide * wide, axis=-1, keepdims=True) + epsilon)
        out[pl.ds(at + start, step), :] = (wide * scale).astype(bf16)
        return 0

    lax.fori_loop(0, part.shape[0] // step, norm, 0)


def rank_kernel(groups, ids_ref, row_ref):
    tokens = ids_ref.shape[1]
    block = tokens // groups
    label = lax.broadcasted_iota(jnp.int32, (groups, tokens), 0)
    held = label == ids_ref[...]
    held_bf = jnp.where(held, 1.0, 0.0).astype(bf16)
    counts = []
    for c in range(tokens // 256):
        before = lax.broadcasted_iota(jnp.int32, (tokens, 256), 0) < (
            lax.broadcasted_iota(jnp.int32, (tokens, 256), 1) + c * 256
        )
        counts.append(
            jnp.dot(held_bf, jnp.where(before, 1.0, 0.0).astype(bf16), preferred_element_type=f32)
        )
    count = jnp.concatenate(counts, axis=1)
    row_ref[...] = jnp.sum(
        jnp.where(held, count + (label * block).astype(f32), 0.0), axis=0, keepdims=True
    )


def rank_tokens(ids, groups):
    tokens = ids.shape[0]
    return pl.pallas_call(
        functools.partial(rank_kernel, groups),
        out_shape=jax.ShapeDtypeStruct((1, tokens), f32),
        compiler_params=params(),
        cost_estimate=cost(0, 4 * tokens),
        name="rank_tokens",
    )(ids.reshape(1, tokens))


def back_kernel(row_ref, back_ref):
    tokens = back_ref.shape[0]
    lane = lax.broadcasted_iota(jnp.int32, (LANES, LANES), 1)
    for at in range(0, tokens, LANES):
        place = jnp.broadcast_to(row_ref[:, at : at + LANES], (LANES, LANES)).T
        for t in range(0, tokens, LANES):
            back_ref[at : at + LANES, t : t + LANES] = jnp.where(
                (lane + t).astype(f32) == place, 1.0, 0.0
            ).astype(bf16)


def back_tokens(rank):
    return pl.pallas_call(
        back_kernel,
        out_shape=jax.ShapeDtypeStruct((rank.shape[1], rank.shape[1]), bf16),
        compiler_params=params(),
        cost_estimate=cost(0, 4 * LANES),
        name="back_tokens",
    )(rank)


def hold(values):
    def kernel(in_ref, out_ref):
        out_ref[...] = in_ref[...]

    return pl.pallas_call(
        kernel,
        out_shape=jax.ShapeDtypeStruct(values.shape, values.dtype),
        compiler_params=params(),
        cost_estimate=cost(2e10, 4 * LANES),
        name="hold",
    )(values)


def picks(rank, at, rows):
    places = lax.broadcasted_iota(jnp.int32, (rows, rank.shape[1]), 0) + at
    return jnp.where(places.astype(f32) == rank, 1.0, 0.0).astype(bf16)


def place_kernel(slots, parts, start, bases, rank_ref, *refs):
    frame_refs, refs = refs[: len(slots) * parts], refs[len(slots) * parts :]
    base_refs, before_refs, (x_ref, normed) = refs[:bases], refs[bases:-2], refs[-2:]
    tokens = rank_ref.shape[1]
    count = normed.shape[1]
    step = 256
    done = 0
    for ref in before_refs:
        x_ref[done : done + ref.shape[0], :] = ref[...]
        done += ref.shape[0]
    for i in range(len(slots)):
        at = 0
        for ref in frame_refs[i * parts : (i + 1) * parts]:
            normalise(ref, normed.at[i], at)
            at += ref.shape[0]
    for at in range(0, tokens, step):
        pick = picks(rank_ref[:, start : start + count], at, step)
        for i, slot in enumerate(slots):
            placed = jnp.dot(pick, normed[i], preferred_element_type=f32).astype(bf16)
            for base in base_refs:
                placed = base[slot * tokens + at : slot * tokens + at + step, :] + placed
            x_ref[done + i * tokens + at : done + i * tokens + at + step, :] = placed


def place_tokens(slots, rank, start, frames, base, before=()):
    tokens = rank.shape[1]
    width = frames[0].shape[1]
    parts = len(frames) // len(slots)
    count = parts * frames[0].shape[0]
    rows = len(slots) * tokens + sum(b.shape[0] for b in before)
    return pl.pallas_call(
        functools.partial(place_kernel, slots, parts, start, len(base)),
        out_shape=jax.ShapeDtypeStruct((rows, width), bf16),
        scratch_shapes=[pltpu.VMEM((len(slots), count, width), bf16)],
        compiler_params=params(),
        cost_estimate=cost(0, 4 * tokens),
        name="place_tokens",
    )(rank, *frames, *base, *before)


def project_kernel(plan, x_ref, *refs):
    w_refs, (v_ref, b_ref, rest_ref, w, turned) = refs[:-5], refs[-5:]
    every = x_ref.shape[0]
    step = 256
    cols = plan.pairs * LANES
    if len(w_refs) > 1:
        w[...] = jnp.zeros_like(w)
        turned[...] = jnp.zeros_like(turned)
    for ref, rows in plan.places(w_refs):
        w[rows, :] = ref[:, :cols]
        turned[rows, :] = ref[:, cols : 2 * cols]
    maps = jnp.concatenate(
        [
            turned[at : at + LANES, :].astype(f32).T.astype(bf16)
            for at in range(0, turned.shape[0], LANES)
        ],
        axis=1,
    )
    for at in range(0, every, step):
        x = x_ref[at : at + step, :]
        v_ref[at : at + step, :] = jnp.dot(x, w[...], preferred_element_type=f32)
        b_ref[:, at : at + step] = lax.dot_general(
            maps, x, (((1,), (1,)), ((), ())), preferred_element_type=f32
        )
    count = rest_ref.shape[1]
    there = plan.last_chip() * count
    for at in range(0, every, step):
        rest = x_ref[at : at + step, :count]
        for c in range(count, x_ref.shape[1], count):
            rest = jnp.where(there == c, x_ref[at : at + step, c : c + count], rest)
        rest_ref[at : at + step, :] = rest


def project(plan, x, weights):
    every, width = x.shape
    cols = plan.pairs * LANES
    count = max(LANES, width // plan.chips)
    return pl.pallas_call(
        functools.partial(project_kernel, plan),
        out_shape=(
            jax.ShapeDtypeStruct((every, cols), f32),
            jax.ShapeDtypeStruct((cols, every), f32),
            jax.ShapeDtypeStruct((every, count), bf16),
        ),
        scratch_shapes=[pltpu.VMEM((width, cols), bf16), pltpu.VMEM((width, cols), bf16)],
        compiler_params=params(),
        cost_estimate=cost(0, 4 * width),
        name="project",
    )(x, *weights)


def update_kernel(plan, groups, decay_ref, *refs):
    v_ref, b_ref, x_ref, last_refs, (left, total_out, total_ref, u, sems) = (
        refs[0], refs[1], refs[2], refs[3:-5], refs[-5:]
    )
    copies = Copies(sems)
    leaving = []
    every = v_ref.shape[0]
    tokens = every // plan.merge
    block = tokens // groups
    step = 256
    here = step // block
    cols = plan.pairs * LANES
    if last_refs:
        w = jnp.concatenate([ref[:, : 2 * cols] for ref in last_refs], axis=0)
        maps = w[:, cols:].astype(f32).T.astype(bf16)
        w = w[:, :cols]

    lane = lax.div(lax.broadcasted_iota(jnp.int32, (LANES, step), 1), block)
    for at in range(0, every, step):
        there = slice(at, at + step)
        values, b = v_ref[there, :], b_ref[:, there]
        if last_refs:
            x = x_ref[there, :]
            values = values + jnp.dot(x, w, preferred_element_type=f32)
            b = b + lax.dot_general(
                maps, x, (((1,), (1,)), ((), ())), preferred_element_type=f32
            )
        values = values.astype(bf16)
        for p in range(plan.pairs):
            mine = b[p * LANES : (p + 1) * LANES]
            wide = jnp.concatenate(
                [jnp.where(lane == i, mine, 0.0).astype(bf16) for i in range(here)], axis=0
            )
            outer = jnp.dot(
                wide, values[:, p * LANES : (p + 1) * LANES], preferred_element_type=f32
            )
            for i in range(here):
                m = outer[i * 2 * N : (i + 1) * 2 * N]
                row = ((at % tokens // block + i) * plan.pairs + p) * N
                u[at // tokens, row : row + N, :] = halves((N, LANES), m[:N], m[N:])

    peers = total_ref.shape[0]
    share = u.shape[1] // peers
    items = max(1, share // N)
    size = min(N, share)
    first = plan.core() == 0
    for d in range(peers):
        for i in range(items):
            row = d * share + i * N
            rows = slice(row, row + size)
            item = slice(row // N, row // N + 1)
            last, product = decay_ref[0, item, :], decay_ref[1, item, :]
            if plan.merge == 2:
                one, two = u[0, rows, :], u[1, rows, :]
                one, two = (
                    one + jnp.where(first, 0.0, last) * two,
                    two + jnp.where(first, last, 0.0) * one,
                )
                left[0, rows, :] = one.astype(bf16)
                left[1, rows, :] = two.astype(bf16)
                total = jnp.where(first, two, one)
            else:
                total = u[0, rows, :]
                left[0, rows, :] = total.astype(bf16)
            total_ref[d, i * size : (i + 1) * size, :] = total.astype(bf16)
            for n in range(3):
                piece = product.astype(bf16)
                at = share + n * items + i
                total_ref[d, at : at + 1, :] = piece
                product = product - piece.astype(f32)
        if (d + 1) % (peers // 4) == 0:
            done = slice(d + 1 - peers // 4, d + 1)
            leaving.append(copies.start(total_ref.at[done], total_out.at[done]))
    finish(leaving)


def share_rows(share):
    return share + 16 * -(-3 * max(1, share // N) // 16)


def block_updates(plan, decays, v, b, x, last, groups):
    every, cols = v.shape
    rows = plan.pairs * groups * N
    share = rows // plan.chips
    return pl.pallas_call(
        functools.partial(update_kernel, plan, groups),
        in_specs=[vmem] * (4 + len(last)),
        out_specs=(vmem, hbm),
        out_shape=(
            jax.ShapeDtypeStruct((plan.merge, rows, LANES), bf16),
            jax.ShapeDtypeStruct((plan.chips, share_rows(share), LANES), bf16),
        ),
        scratch_shapes=[
            pltpu.VMEM((plan.chips, share_rows(share), LANES), bf16),
            pltpu.VMEM((plan.merge, rows, LANES), f32),
            Copies.scratch(),
        ],
        compiler_params=params(),
        cost_estimate=cost(4 * every * 256 * 2 * cols, 6 * every * cols),
        name="block_updates",
    )(decays, v, b, x, *last)


def decay_kernel(plan, groups, *refs):
    rate_refs, out_ref = refs[:-1], refs[-1]
    first = plan.core() == 0
    for g in range(groups):
        for p in range(plan.pairs):
            row = slice(g * plan.pairs + p, g * plan.pairs + p + 1)
            slots = [plan.decay(rate_refs, s, p, g) for s in range(plan.merge)]
            together, last = slots[0], slots[0]
            if plan.merge == 2:
                together = slots[0] * slots[1]
                last = jnp.where(first, slots[1], slots[0])
                slots = [
                    jnp.where(first, slots[0], together),
                    jnp.where(first, together, slots[1]),
                ]
            for i, value in enumerate([last, together] + slots):
                out_ref[i, row, :] = value


def decay_tables(plan, rates, groups):
    return pl.pallas_call(
        functools.partial(decay_kernel, plan, groups),
        in_specs=[smem] * plan.merge,
        out_shape=jax.ShapeDtypeStruct((2 + plan.merge, plan.pairs * groups, LANES), f32),
        compiler_params=params(),
        cost_estimate=cost(0, 4 * LANES),
        name="decay_tables",
    )(*rates)


def scan_kernel(plan, u_ref, s_ref):
    share = s_ref.shape[1]
    size = min(share, N)
    items = share // size
    for i in range(items):
        at = slice(i * size, (i + 1) * size)
        state = jnp.zeros((size, LANES), f32)
        for j in range(plan.chips):
            s_ref[j, at, :] = state.astype(bf16)
            decay = jnp.zeros((1, LANES), f32)
            for n in range(3):
                row = share + n * items + i
                decay = decay + u_ref[j, row : row + 1, :].astype(f32)
            state = decay * state + u_ref[j, at, :].astype(f32)


def scan_states(plan, update, share):
    return pl.pallas_call(
        functools.partial(scan_kernel, plan),
        out_shape=jax.ShapeDtypeStruct((plan.chips, share, LANES), bf16),
        compiler_params=params(),
        cost_estimate=cost(2 * update.size, 4 * update.size),
        name="scan_states",
    )(update)


def attend_kernel(plan, slot, *refs):
    lists_ref, x_in, local_in, refs = refs[0], refs[1], refs[2], refs[3:]
    w_refs, refs = refs[:-12], refs[-12:]
    a_out, c_out, x, local, w, q_ref, k_ref, wide_v, e_ref, a, c_ref, sems = refs
    copies = Copies(sems)
    tokens = x.shape[0]
    groups, chosen = lists_ref.shape
    block = tokens // groups
    step = 256
    per = step // block
    wide = plan.pairs * LANES

    weights = []
    for ref, rows in plan.places(w_refs):
        weights.append(copies.start(ref.at[:, :wide], w.at[rows, :wide]))
        weights.append(copies.start(ref.at[:, 2 * wide :], w.at[rows, wide:]))
    arriving = []
    for at in range(0, tokens, step):
        from_ = slice(slot * tokens + at, slot * tokens + at + step)
        arriving.append(copies.start(x_in.at[from_], x.at[at : at + step]))
    later = copies.start(local_in.at[slot], local)

    same = lax.div(lax.broadcasted_iota(jnp.int32, (2 * LANES, 2 * LANES), 0), HD) == lax.div(
        lax.broadcasted_iota(jnp.int32, (2 * LANES, 2 * LANES), 1), HD
    )
    same = jnp.where(same, 1.0, 0.0).astype(bf16)

    def head_norm(values):
        square = values * values
        high = square.astype(bf16)
        low = (square - high.astype(f32)).astype(bf16)
        total = jnp.dot(high, same, preferred_element_type=f32)
        total = total + jnp.dot(low, same, preferred_element_type=f32)
        return values * lax.rsqrt(total * (1.0 / HD) + epsilon)

    half = first_half((step, LANES))
    finish(weights)
    for at in range(0, tokens, step):
        rows = slice(at, at + step)
        arriving[at // step].wait()
        every = jnp.dot(x[rows, :], w[...], preferred_element_type=f32).astype(bf16)
        for p in range(plan.pairs):
            cols = slice(p * LANES, (p + 1) * LANES)
            wide_v[p, rows, :LANES] = every[:, cols]
            first = wide + 3 * p * LANES
            c_ref[rows, cols] = every[:, first + 2 * LANES : first + 3 * LANES]
            both = head_norm(every[:, first : first + 2 * LANES].astype(f32))
            k_ref[p, rows, :] = both[:, LANES:].astype(bf16)
            q = both[:, :LANES]
            one = jnp.where(half, q, 0.0).astype(bf16)
            two = jnp.where(half, 0.0, q).astype(bf16)
            for i in range(per):
                part = slice(i * block, (i + 1) * block)
                q_ref[p, at // block + i] = jnp.concatenate([one[part], two[part]], axis=0)
    leaving = [copies.start(c_ref, c_out)]
    later.wait()
    for p in range(plan.pairs):
        wide_v[p, :, LANES:] = jnp.ones((tokens, LANES), bf16)

    scale = math.log2(math.e) / math.sqrt(HD)
    starts = [
        [pl.multiple_of(lists_ref[g, j] * block, block) for j in range(chosen)]
        for g in range(groups)
    ]
    for g in range(groups):
        for p in range(plan.pairs):
            keys = jnp.concatenate([k_ref[p, pl.ds(s, block), :] for s in starts[g]], axis=0)
            score = lax.dot_general(
                q_ref[p, g], keys, (((1,), (1,)), ((), ())), preferred_element_type=f32
            )
            e_ref[p, g] = jnp.exp2(score * scale).astype(bf16)
    for g in range(groups):
        rows = slice(g * block, (g + 1) * block)
        for p in range(plan.pairs):
            cols = slice(p * LANES, (p + 1) * LANES)
            values = jnp.concatenate([wide_v[p, pl.ds(s, block), :] for s in starts[g]], axis=0)
            both = jnp.dot(e_ref[p, g], values, preferred_element_type=f32)
            both = both[:, :LANES] / both[:, LANES:]
            a[rows, cols] = halves((block, LANES), both[:block], both[block:])
    for g in range(groups):
        rows = slice(g * block, (g + 1) * block)
        for p in range(plan.pairs):
            cols = slice(p * LANES, (p + 1) * LANES)
            items = slice((g * plan.pairs + p) * N, (g * plan.pairs + p + 1) * N)
            a[rows, cols] = a[rows, cols] + read_out(
                c_ref[rows, cols], local[items, :].astype(f32), block
            )
        if (g + 1) % per == 0:
            done = slice((g + 1 - per) * block, (g + 1) * block)
            leaving.append(copies.start(a.at[done], a_out.at[done]))
    finish(leaving)


def attend(plan, slot, lists, x, weights, local):
    every, width = x.shape
    groups, chosen = lists.shape
    tokens = every // plan.merge
    block = tokens // groups
    cols = plan.pairs * LANES
    return pl.pallas_call(
        functools.partial(attend_kernel, plan, slot),
        in_specs=[smem] + [hbm] * (2 + len(weights)),
        out_specs=(hbm,) * 2,
        scratch_shapes=[
            pltpu.VMEM((tokens, width), bf16),
            pltpu.VMEM(local.shape[1:], bf16),
            pltpu.VMEM((width, 4 * cols), bf16),
            pltpu.VMEM((plan.pairs, groups, 2 * block, LANES), bf16),
            pltpu.VMEM((plan.pairs, tokens, LANES), bf16),
            pltpu.VMEM((plan.pairs, tokens, 2 * LANES), bf16),
            pltpu.VMEM((plan.pairs, groups, 2 * block, chosen * block), bf16),
            pltpu.VMEM((tokens, cols), f32),
            pltpu.VMEM((tokens, cols), bf16),
            Copies.scratch(),
        ],
        out_shape=(
            jax.ShapeDtypeStruct((tokens, cols), f32),
            jax.ShapeDtypeStruct((tokens, cols), bf16),
        ),
        compiler_params=params(60),
        cost_estimate=cost(
            6 * tokens * width * 3 * cols,
            4 * (tokens * width + 5 * width * cols + local.size),
            2 * plan.pairs * tokens * chosen * block,
        ),
        name="attend",
    )(lists, x, local, *weights)


def read_out(readers, state, block):
    half = first_half(state.shape)
    wide = jnp.concatenate([jnp.where(half, state, 0.0), jnp.where(half, 0.0, state)], axis=0)
    return jnp.dot(readers, wide.astype(bf16), preferred_element_type=f32) * (
        1.0 / (N * math.sqrt(block))
    )


def mix_kernel(plan, groups, decay_in, *refs):
    a_ins, refs = refs[: plan.merge], refs[plan.merge :]
    c_ins, refs = refs[: plan.merge], refs[plan.merge :]
    s_in, back_in, refs = refs[0], refs[1], refs[2:]
    out_refs, (decay, a, c, state, back, mixed, out, sems) = refs[:-8], refs[-8:]
    copies = Copies(sems)
    tokens = back.shape[0]
    block = tokens // groups
    width = a.shape[2]
    here = groups // 4
    many = here * plan.pairs * N

    arriving = []
    decaying = copies.start(decay_in, decay)
    for i in range(4):
        rows = slice(i * here * block, (i + 1) * here * block)
        items = slice(i * many, (i + 1) * many)
        arriving.append([copies.start(s_in.at[items], state.at[items])])
        for s in range(plan.merge):
            arriving[-1] += [
                copies.start(c_ins[s].at[rows], c.at[s, rows, :]),
                copies.start(a_ins[s].at[rows], a.at[s, rows, :]),
            ]
    local = tokens // plan.peers
    order = list(range(1, plan.peers)) + [0]
    turning = []
    for k in order:
        rows = slice(k * local, (k + 1) * local)
        turning.append(copies.start(back_in.at[rows], back.at[rows]))

    decaying.wait()
    for g in range(groups):
        if g % here == 0:
            finish(arriving[g // here])
        rows = slice(g * block, (g + 1) * block)
        for p in range(plan.pairs):
            cols = slice(p * LANES, (p + 1) * LANES)
            at = (g * plan.pairs + p) * N
            readers = jnp.concatenate([c[s, rows, cols] for s in range(plan.merge)], axis=0)
            read = read_out(readers, state[at : at + N, :].astype(f32), block)
            item = slice(g * plan.pairs + p, g * plan.pairs + p + 1)
            for s in range(plan.merge):
                there = slice(s * width + p * LANES, s * width + (p + 1) * LANES)
                mixed[rows, there] = (
                    a[s, rows, cols]
                    + decay[2 + s, item, :] * read[s * block : (s + 1) * block]
                ).astype(bf16)

    leaving = []
    for k, turned in zip(order, turning):
        turned.wait()
        placed = jnp.dot(
            back[k * local : (k + 1) * local, :], mixed[...], preferred_element_type=f32
        ).astype(bf16)
        for s in range(plan.merge):
            i = s * plan.peers + k
            out[i] = placed[:, s * width : (s + 1) * width]
            leaving.append(copies.start(out.at[i], out_refs[i]))
    finish(leaving)


def mix(plan, decays, attended, readers, state, back, groups):
    tokens = back.shape[0]
    width = attended[0].shape[1]
    count = plan.merge * plan.peers
    return pl.pallas_call(
        functools.partial(mix_kernel, plan, groups),
        in_specs=[hbm] * (2 * plan.merge + 3),
        out_specs=(hbm,) * count,
        out_shape=(jax.ShapeDtypeStruct((tokens // plan.peers, width), bf16),) * count,
        scratch_shapes=[
            pltpu.VMEM(decays.shape, f32),
            pltpu.VMEM((plan.merge, tokens, width), f32),
            pltpu.VMEM((plan.merge, tokens, width), bf16),
            pltpu.VMEM(state.shape, bf16),
            pltpu.VMEM(back.shape, bf16),
            pltpu.VMEM((tokens, plan.merge * width), bf16),
            pltpu.VMEM((count, tokens // plan.peers, width), bf16),
            Copies.scratch(),
        ],
        compiler_params=params(52),
        cost_estimate=cost(4 * tokens * tokens * width, 2 * tokens * tokens + 16 * tokens * width),
        name="mix",
    )(decays, *attended, *readers, state, back)


def out_kernel(plan, sources, w_ref, *refs):
    part_refs, base_refs, out_ref = refs[: len(sources)], refs[len(sources) : -3], refs[-3]
    kept, sems = refs[-2:]
    copies = Copies(sems)
    depth = part_refs[0].shape[1]
    core, me = plan.core(), lax.axis_index("head")
    owners = []
    for s, k in sources:
        owner = lax.rem(me - k + plan.peers, plan.peers) * plan.merge
        owners.append(owner + (core if s == 0 else 1 - core))
    leaving = []
    step = min(128, out_ref.shape[0])
    for at in range(0, out_ref.shape[0], step):
        there = slice(at, at + step)
        total = base_refs[0][there, :] if base_refs else 0.0
        for owner, part in zip(owners, part_refs):
            rows = pl.ds(pl.multiple_of(owner * depth, depth), depth)
            total = total + jnp.dot(part[there, :], w_ref[rows, :], preferred_element_type=f32)
        if base_refs:
            kept[there, :] = total.astype(out_ref.dtype)
            leaving.append(copies.start(kept.at[there], out_ref.at[there]))
        else:
            out_ref[there, :] = total.astype(out_ref.dtype)
    finish(leaving)


def project_out(plan, w, parts, base, kind):
    local, width = next(iter(parts.values())).shape[0], w.shape[1]
    return pl.pallas_call(
        functools.partial(out_kernel, plan, list(parts)),
        in_specs=[vmem] * (1 + len(parts) + len(base)),
        out_specs=hbm if base else vmem,
        out_shape=jax.ShapeDtypeStruct((local, width), kind),
        scratch_shapes=[pltpu.VMEM((local, width), kind), Copies.scratch()],
        compiler_params=params(),
        cost_estimate=cost(0, 4 * local),
        name="project_out",
    )(w, *parts.values(), *base)


def body(frames_in, in_weight, out_weight, block_ids, block_lists, decays):
    local_tokens = frames_in.shape[1]
    heads_here = decays.shape[1]
    groups = block_lists.shape[0]
    me = lax.axis_index("head")
    plan = Plan(lax.axis_size("tm"), lax.axis_size("head"), heads_here, frames_in.shape[2])

    own = frames_in[0]
    arriving = [plan.to_peer(own, plan.peers - k, False) for k in range(1, plan.peers)]
    owns = [own] + [plan.swap(own)] * (plan.merge - 1)
    rates = [decays[0]] + [plan.swap(decays[0])] * (plan.merge - 1)
    block = reorder(plan, in_weight)
    if plan.merge == 2:
        block = reorder(plan, plan.swap(in_weight), [block])
    ids = jnp.roll(block_ids, -me * local_tokens)
    ids, rates = lax.optimization_barrier((ids, rates))
    tables = decay_tables(plan, rates, groups)
    rank = rank_tokens(ids, groups)

    def fill(slot, arriving, part, before):
        if slot == 1:
            arriving = [plan.swap(tokens) for tokens in arriving]
        return place_tokens([slot], rank, local_tokens, arriving, [part], before)

    if plan.ringed:
        blocks, crossed = [block], []
        half = block.shape[0] // 2
        for k in range(plan.along - 1):
            with_ = ()
            if k == 0:
                places = back_tokens(rank)
                with_ = (places, tables)
            if k == min(1, plan.along - 2):
                rank, owns, _ = lax.optimization_barrier((rank, owns, blocks[-1]))
                part = with_ = place_tokens(list(range(plan.merge)), rank, 0, owns, [])
            if k == plan.along - 2:
                arriving, _ = lax.optimization_barrier((arriving, blocks[-1]))
                x = fill(0, arriving, part, [])
            passed, across, with_ = lax.optimization_barrier(
                (plan.round(blocks[-1]), plan.cross(blocks[-1]), with_)
            )
            if k == plan.along - 2:
                tables, passed, across, x = lax.optimization_barrier(
                    (tables, passed, across, x)
                )
                if plan.merge == 2:
                    x = fill(1, arriving, part, [x])
                tables, passed, across = lax.optimization_barrier(
                    (hold(tables), passed, across)
                )
            blocks.append(passed)
            crossed.append(across)
        last = [plan.cross(blocks[-1][:half]), plan.round(crossed[-1][half:])]
        weights = blocks + crossed + last
    else:
        weights = [
            lax.all_gather(block, "tm", axis=0, tiled=True, axis_index_groups=plan.groups())
        ]
        places = back_tokens(rank)
        part = place_tokens(list(range(plan.merge)), rank, 0, owns, [])
        x = fill(0, arriving, part, [])
        if plan.merge == 2:
            x = fill(1, arriving, part, [x])
    if plan.ringed:
        v, b, x_last = project(plan, x, weights[:-2])
        local, total = block_updates(plan, tables, v, b, x_last, last, groups)
    else:
        v, b, x_last = project(plan, x, weights)
        local, total = block_updates(plan, tables, v, b, x_last, [], groups)

    def exchange(blocks):
        return lax.all_to_all(
            blocks, "tm", split_axis=0, concat_axis=0, tiled=True,
            axis_index_groups=plan.groups(),
        )

    share = local.shape[1] // plan.chips
    arrived = exchange(total)
    attended = [attend(plan, 0, block_lists, x, weights, local)]
    arrived, attended = lax.optimization_barrier((arrived, attended))
    states = scan_states(plan, arrived, share)
    x, states = lax.optimization_barrier((x, states))
    if plan.merge == 2:
        attended.append(attend(plan, 1, block_lists, x, weights, local))
    state = exchange(states).reshape(-1, LANES)

    bases, readers = ([a[i] for a in attended] for i in range(2))
    mixed = mix(plan, tables, bases, readers, state, places, groups)
    moved = {
        (s, k): plan.to_peer(mixed[s * plan.peers + k], k, s == 1)
        for s in range(plan.merge)
        for k in range(1, plan.peers)
    }
    near = {(0, 0): mixed[0]}
    if plan.merge == 2:
        near[1, 0] = plan.swap(mixed[plan.peers])
    result = project_out(plan, out_weight, near, [], f32)
    last = {key: moved.pop(key) for key in list(moved)[-1:]}
    if moved:
        result = project_out(plan, out_weight, moved, [result], f32)
    return project_out(plan, out_weight, last, [result], bf16)[None]


def solution(mesh):
    return jax.shard_map(
        body,
        mesh=mesh,
        in_specs=(P("tm", "head", None), P("tm", "head"), P(), P(), P(), P("tm", "head", None)),
        out_specs=P("tm", "head", None),
        check_vma=False,
    )
```
